32 devices in a mesh: dp: 4 (over y, x), rows: 8 (over z, core).
Axes of the slice: x: 2, y: 2, z: 4, core: 2. Of those that a mesh axis runs over, the one named last changes fastest.
Arguments:
- events: bfloat16 [16384, 512], P(('dp', 'rows')), may hold values from -6 to 6
- cotangent: bfloat16 [16384, 512], P(('dp', 'rows')), may hold values from -6 to 6
- lengths: int32 [32], P(('dp', 'rows')), may hold values from 128 to 512
- event_slot: int32 [32, 512], P(('dp', 'rows')), may hold values from 0 to 511, as said below
- slot_row: int32 [32, 32, 16], P(('dp', 'rows')), may hold values from 0 to 511, as said below
- slot_count: int32 [32, 32], P(('dp', 'rows')), may hold values from 1 to 16, as said below
- w_in: bfloat16 [512, 2048], replicated, may hold values from -0.25 to 0.25
- w_out: bfloat16 [512, 512], replicated, may hold values from -0.25 to 0.25
- item_table: float32 [16384, 512], P(('dp', 'rows')), may hold values from -6 to 6
- accumulator: float32 [16384], P(('dp', 'rows')), may hold values from 0.5 to 8
Outputs:
- grad_in: float32 [512, 2048], P('rows')
- grad_out: float32 [512, 512], P('rows')
- table_new: float32 [16384, 512], P(('dp', 'rows'))
- accum_new: float32 [16384], P(('dp', 'rows'))
The draws below stay inside these ranges and needn't reach their ends.
Inputs may be any that keep to these rules, and one draw needn't show every extreme that they name: `event_slot`: slot s of a history belongs to shard s // 16, place s % 16; events only name slots whose place is below that history's slot_count for the shard, and every such slot is named by at least one event of the history. `slot_row`: within one history and shard the used slots name distinct rows; unused slots hold 0. `slot_count`: for one shard drawn from the seed every history uses all 16 slots, and some history uses all 16 slots of the last shard.
All inputs are finite; a program needn't handle non-finite values.
Results may differ from the reference program's by a relative error of at most 0.0081.
Values sent between devices are 32-bit elements; how exact they have to be, the bound alone decides.
No kernel may reach another device: no remote copies, remote signals or barrier semaphores. Data moves between devices by JAX's collectives and lax.ppermute only.
A program may use at most 64 MiB of HBM per device.

```python
import math
import jax
import jax.numpy as jnp
from jax import lax

D = 512
HEADS = 4
TOK_DEV = 512
ROWS_DEV = 512
SEQS = 32
OWNERS = 32
CAP = 16
TOKENS = 16384
ROWS_TOTAL = 16384


def shared_counts(key):
    key_count, key_hot, key_full = jax.random.split(jax.random.fold_in(key, 11), 3)
    counts = jax.random.randint(key_count, (SEQS, OWNERS), 1, CAP + 1)
    hot_owner = jax.random.randint(key_hot, (), 0, OWNERS)
    counts = jnp.where(jnp.arange(OWNERS)[None, :] == hot_owner, CAP, counts)
    full_history = jax.random.randint(key_full, (), 0, SEQS)
    last_full = (jnp.arange(SEQS)[:, None] == full_history) & (jnp.arange(OWNERS)[None, :] == OWNERS - 1)
    counts = jnp.where(last_full, CAP, counts)
    return counts.astype(jnp.int32)


def draw_slot_count(key, part):
    return shared_counts(key)


def draw_slot_row(key, part):
    counts = shared_counts(key)
    key_hot, key_flip, key_near, key_far = jax.random.split(jax.random.fold_in(key, 12), 4)
    hot_start = jax.random.randint(key_hot, (1, OWNERS, 1), 0, ROWS_DEV - CAP - 7)
    near_start = hot_start + jax.random.randint(key_near, (SEQS, OWNERS, 1), 0, 8)
    far_start = jax.random.randint(key_far, (SEQS, OWNERS, 1), 0, ROWS_DEV - CAP + 1)
    coin_flip = jax.random.randint(key_flip, (SEQS, OWNERS, 1), 0, 2)
    window_start = jnp.where(coin_flip == 1, near_start, far_start)
    slot_index = jnp.arange(CAP)[None, None, :]
    rows_named = window_start + slot_index
    return jnp.where(slot_index < counts[:, :, None], rows_named, 0).astype(jnp.int32)


def draw_event_slot(key, part):
    counts = shared_counts(key)
    starts = jnp.cumsum(counts, axis=1) - counts
    totals = jnp.sum(counts, axis=1)
    history_keys = jax.random.split(jax.random.fold_in(key, 13), SEQS)
    shuffled = jax.vmap(lambda one_key: jax.random.permutation(one_key, TOK_DEV))(history_keys)
    live_index = shuffled % totals[:, None]
    owner_of = jnp.sum((starts[:, None, :] <= live_index[:, :, None]).astype(jnp.int32), axis=-1) - 1
    offset = live_index - jnp.take_along_axis(starts, owner_of, axis=1)
    return (owner_of * CAP + offset).astype(jnp.int32)


def draw_lengths(key, part):
    key_len, key_pick = jax.random.split(jax.random.fold_in(key, 14))
    lengths_drawn = jax.random.randint(key_len, (SEQS,), TOK_DEV // 4, TOK_DEV + 1)
    longest = jax.random.randint(key_pick, (), 0, SEQS)
    positions = jnp.arange(SEQS)
    lengths_drawn = jnp.where(positions == longest, TOK_DEV, lengths_drawn)
    lengths_drawn = jnp.where(positions == (longest + 1) % SEQS, TOK_DEV // 4, lengths_drawn)
    return lengths_drawn.astype(jnp.int32)


def level_of(key, shape, cuts, smallest, top_value):
    loudness, own = 1.0, jax.random.fold_in(key, 6)
    for dim, parts in cuts:
        heights = jnp.exp(jax.random.uniform(jax.random.fold_in(own, dim), (parts,), jnp.float32, smallest / len(cuts), top_value / len(cuts)))
        loudness = loudness * jnp.repeat(heights, shape[dim] // parts).reshape([-1 if axis == dim else 1 for axis in range(len(shape))])
    return loudness


def scatter_about(stream_key, dims, spread, limit, pieces=(), held_as=jnp.bfloat16):
    drawn = jax.random.normal(stream_key, dims, jnp.float32) * spread
    if len(pieces) > 0:
        drawn = level_of(stream_key, dims, pieces, -0.22, 0.18) * drawn
    return jnp.clip(drawn, min=-limit, max=limit).astype(held_as)


def setup_inputs(seed: int = 0) -> dict:
    streams_of = jax.random.split(jax.random.key(seed), 11)
    events = scatter_about(streams_of[0], (TOKENS, D), 1.0, 6.0, ((0, 32),))
    cotangent = scatter_about(streams_of[1], (TOKENS, D), 1.0, 6.0, ((0, 32),))
    lengths = draw_lengths(jax.random.fold_in(streams_of[10], 71), 0)
    event_slot = draw_event_slot(jax.random.fold_in(streams_of[10], 71), 0)
    slot_row = draw_slot_row(jax.random.fold_in(streams_of[10], 71), 0)
    slot_count = draw_slot_count(jax.random.fold_in(streams_of[10], 71), 0)
    w_in = scatter_about(streams_of[6], (D, 4 * D), D ** -0.5, 0.25)
    w_out = scatter_about(streams_of[7], (D, D), D ** -0.5, 0.25)
    item_table = scatter_about(streams_of[8], (ROWS_TOTAL, D), 1.0, 6.0, ((0, 32),), jnp.float32)
    accumulator = jnp.clip(jnp.exp(math.log(8.0) - 2.7725887 * jax.random.uniform(streams_of[9], (ROWS_TOTAL,), jnp.float32) ** level_of(streams_of[9], (ROWS_TOTAL,), ((0, 32),), -0.2, 0.2)), 0.5, 8.0)
    return {"events": events, "cotangent": cotangent, "lengths": lengths, "event_slot": event_slot, "slot_row": slot_row, "slot_count": slot_count, "w_in": w_in, "w_out": w_out, "item_table": item_table, "accumulator": accumulator}


norm_eps = 1e-05
adagrad_eps = 1e-10
learning_rate = 0.1

def rounded(values):
    return lax.optimization_barrier(values.astype(jnp.bfloat16)).astype(jnp.float32)

def layer_grads(events, cotangent, length, w_in, w_out):
    tokens, model_width = events.shape
    head_dim = model_width // HEADS
    block_rows = min(512, tokens)
    num_blocks = tokens // block_rows
    inputs_f = events.astype(jnp.float32)
    centered = inputs_f - lax.optimization_barrier(jnp.mean(inputs_f, axis=-1, keepdims=True))
    inv_std = lax.rsqrt(lax.optimization_barrier(jnp.mean(centered * centered, axis=-1, keepdims=True)) + norm_eps)
    normed = centered * inv_std
    normed_b = normed.astype(jnp.bfloat16)
    preact = jnp.dot(normed_b, w_in, preferred_element_type=jnp.float32)
    gate_sig = jax.nn.sigmoid(preact)
    hidden = rounded(preact * gate_sig)
    user_part = hidden[:, :model_width]
    value_heads = hidden[:, model_width:2 * model_width].reshape(tokens, HEADS, head_dim)
    query_heads = hidden[:, 2 * model_width:3 * model_width].reshape(tokens, HEADS, head_dim)
    key_heads = hidden[:, 3 * model_width:].reshape(tokens, HEADS, head_dim)
    is_valid = jnp.arange(tokens) < length
    masked = jnp.where(is_valid[:, None], cotangent, jnp.zeros_like(cotangent))
    inv_len = 1.0 / length.astype(jnp.float32)
    score_scale = head_dim ** (-0.5)
    positions = jnp.arange(tokens)

    def scores(blk_index):
        query_blk = lax.dynamic_slice_in_dim(query_heads, blk_index * block_rows, block_rows, 0)
        raw_scores = jnp.einsum('qhd,khd->hqk', query_blk, key_heads) * score_scale
        causal = (blk_index * block_rows + jnp.arange(block_rows))[:, None] >= positions[None, :]
        return (query_blk, raw_scores, causal)

    def forward_block(blk_index):
        query_blk, raw_scores, causal = scores(blk_index)
        att_weights = rounded(jnp.where(causal, raw_scores * jax.nn.sigmoid(raw_scores), 0.0) * inv_len)
        return jnp.einsum('hqk,khd->qhd', att_weights, value_heads).reshape(block_rows, model_width)
    attended = lax.map(forward_block, jnp.arange(num_blocks)).reshape(tokens, model_width)
    att_centered = attended - lax.optimization_barrier(jnp.mean(attended, axis=-1, keepdims=True))
    att_inv = lax.rsqrt(lax.optimization_barrier(jnp.mean(att_centered * att_centered, axis=-1, keepdims=True)) + norm_eps)
    att_normed = att_centered * att_inv
    mixed_b = (att_normed * user_part).astype(jnp.bfloat16)
    grad_mixed = lax.dot_general(masked, w_out, (((1,), (1,)), ((), ())), preferred_element_type=jnp.float32)
    grad_user = grad_mixed * att_normed
    grad_norm_att = grad_mixed * user_part
    grad_att = rounded(att_inv * (grad_norm_att - lax.optimization_barrier(jnp.mean(grad_norm_att, axis=-1, keepdims=True)) - att_normed * lax.optimization_barrier(jnp.mean(grad_norm_att * att_normed, axis=-1, keepdims=True))))
    grad_att = grad_att.reshape(tokens, HEADS, head_dim)

    def backward_block(running, blk_index):
        grad_keys, grad_values = running
        query_blk, raw_scores, causal = scores(blk_index)
        score_sig = jax.nn.sigmoid(raw_scores)
        att_weights = rounded(jnp.where(causal, raw_scores * score_sig, 0.0) * inv_len)
        grad_blk = lax.dynamic_slice_in_dim(grad_att, blk_index * block_rows, block_rows, 0)
        grad_weights = jnp.einsum('qhd,khd->hqk', grad_blk, value_heads)
        grad_values = grad_values + jnp.einsum('hqk,qhd->khd', att_weights, grad_blk)
        grad_raw = rounded(jnp.where(causal, grad_weights * score_sig * (1.0 + raw_scores * (1.0 - score_sig)), 0.0) * (inv_len * score_scale))
        grad_query = jnp.einsum('hqk,khd->qhd', grad_raw, key_heads)
        grad_keys = grad_keys + jnp.einsum('hqk,qhd->khd', grad_raw, query_blk)
        return ((grad_keys, grad_values), grad_query)
    empty_grad = jnp.zeros((tokens, HEADS, head_dim), jnp.float32)
    (grad_keys, grad_values), grad_queries = lax.scan(backward_block, (empty_grad, empty_grad), jnp.arange(num_blocks))
    grad_hidden = jnp.concatenate([grad_user, grad_values.reshape(tokens, model_width), grad_queries.reshape(tokens, model_width), grad_keys.reshape(tokens, model_width)], axis=1)
    grad_pre = (grad_hidden * gate_sig * (1.0 + preact * (1.0 - gate_sig))).astype(jnp.bfloat16)
    grad_normed = lax.dot_general(grad_pre, w_in, (((1,), (1,)), ((), ())), preferred_element_type=jnp.float32)
    grad_events = masked.astype(jnp.float32) + inv_std * (grad_normed - lax.optimization_barrier(jnp.mean(grad_normed, axis=-1, keepdims=True)) - normed * lax.optimization_barrier(jnp.mean(grad_normed * normed, axis=-1, keepdims=True)))
    return (grad_events, normed_b, grad_pre, mixed_b, masked)

def reference(events, cotangent, lengths, event_slot, slot_row, slot_count, w_in, w_out, item_table, accumulator):
    model_width = events.shape[1]
    history_events = events.reshape(SEQS, TOK_DEV, model_width)
    history_grads = cotangent.reshape(SEQS, TOK_DEV, model_width)

    def per_history(running, inputs):
        hist_events, hist_grads, length, slots = inputs
        grad_events, normed_b, grad_pre, mixed_b, masked = layer_grads(hist_events, hist_grads, length, w_in, w_out)
        term_in = lax.dot_general(normed_b, grad_pre, (((0,), (0,)), ((), ())), preferred_element_type=jnp.float32)
        term_out = lax.dot_general(mixed_b, masked, (((0,), (0,)), ((), ())), preferred_element_type=jnp.float32)
        slot_sums = jax.ops.segment_sum(grad_events, slots.astype(jnp.int32), num_segments=TOK_DEV)
        return (running + jnp.concatenate([term_in, term_out], axis=1), slot_sums)
    summed, slot_sums = lax.scan(per_history, jnp.zeros((model_width, 5 * model_width), jnp.float32), (history_events, history_grads, lengths, event_slot))
    summed = summed / TOK_DEV
    is_live = jnp.arange(CAP)[None, None, :] < slot_count[:, :, None]
    row_data = jnp.where(is_live[..., None], slot_sums.reshape(SEQS, OWNERS, CAP, model_width), 0.0)
    global_rows = (jnp.arange(OWNERS).astype(jnp.int32)[None, :, None] * ROWS_DEV + slot_row).astype(jnp.int32)
    table_grad = jax.ops.segment_sum(row_data.reshape(-1, model_width), global_rows.reshape(-1), num_segments=ROWS_TOTAL)
    accum_new = accumulator + lax.optimization_barrier(jnp.mean(table_grad * table_grad, axis=-1))
    table_new = item_table - learning_rate * table_grad / (jnp.sqrt(accum_new)[:, None] + adagrad_eps)
    return (summed[:, :4 * model_width], summed[:, 4 * model_width:], table_new, accum_new)
```

```python
import functools

import jax
import jax.numpy as jnp
from jax import lax
from jax.experimental import pallas as pl
from jax.experimental.pallas import tpu as pltpu
from jax.sharding import PartitionSpec as P

HEADS = 4

norm_eps = 1e-05
adagrad_eps = 1e-10
learning_rate = 0.1

f32, bf16 = jnp.float32, jnp.bfloat16
VMEM_BYTES = 56 * 1024 * 1024
STEP = 256


def dot_nn(a, b):
    return lax.dot_general(a, b, (((1,), (0,)), ((), ())), preferred_element_type=f32)


def dot_nt(a, b):
    return lax.dot_general(a, b, (((1,), (1,)), ((), ())), preferred_element_type=f32)


def dot_tn(a, b):
    return lax.dot_general(a, b, (((0,), (0,)), ((), ())), preferred_element_type=f32)


def standardize(x):
    centered = x - jnp.mean(x, axis=-1, keepdims=True)
    inv = lax.rsqrt(jnp.mean(centered * centered, axis=-1, keepdims=True) + norm_eps)
    return centered * inv, inv


def masked_rows(cot, start, length):
    row = start + lax.broadcasted_iota(jnp.int32, cot.shape, 0)
    return jnp.where(row < length, cot.astype(f32), 0.0)


def forward_kernel(len_ref, ev_ref, cot_ref, win_ref, wout_ref,
                   term_ref, hid_ref, dsilu_ref, gatt_ref, gpre_ref,
                   normed_ref, user_ref, duser_ref, att_ref, mixed_ref, masked_ref):
    tokens, width = ev_ref.shape
    hd = width // HEADS
    length = len_ref[0]
    inv_len = 1.0 / length.astype(f32)
    scale = hd ** -0.5
    steps = tokens // STEP

    for i in range(steps):
        rows = pl.ds(i * STEP, STEP)
        xhat, _ = standardize(ev_ref[rows, :].astype(f32))
        normed_ref[rows, :] = xhat.astype(bf16)
        masked_ref[rows, :] = masked_rows(cot_ref[rows, :], i * STEP, length).astype(bf16)

    def project(i, c):
        rows = pl.ds(i * STEP, STEP)
        pre = dot_nn(normed_ref[rows, :], win_ref[:, c * width:(c + 1) * width])
        sig = 0.5 + 0.5 * jnp.tanh(0.5 * pre)
        hid = pre * sig
        dsilu = sig * (1.0 + (pre - hid))
        if c == 0:
            user_ref[rows, :] = hid.astype(bf16)
            duser_ref[rows, :] = dsilu
        else:
            cols = slice((c - 1) * width, c * width)
            hid_ref[rows, cols] = hid.astype(bf16)
            dsilu_ref[rows, cols] = dsilu.astype(bf16)

    for c in range(4):
        for i in range(steps):
            project(i, c)

    tri = lax.broadcasted_iota(jnp.int32, (STEP, STEP), 0) >= lax.broadcasted_iota(jnp.int32, (STEP, STEP), 1)
    for h in range(HEADS):
        v_cols = slice(h * hd, (h + 1) * hd)
        q_cols = slice(width + h * hd, width + (h + 1) * hd)
        k_cols = slice(2 * width + h * hd, 2 * width + (h + 1) * hd)
        for i in range(steps):
            rows = pl.ds(i * STEP, STEP)
            query = hid_ref[rows, q_cols]
            total = None
            for j in range(i + 1):
                keys = pl.ds(j * STEP, STEP)
                half = dot_nt(query, hid_ref[keys, k_cols]) * (0.5 * scale)
                weights = (half + half * jnp.tanh(half)) * inv_len
                if i == j:
                    weights = jnp.where(tri, weights, 0.0)
                part = dot_nn(weights.astype(bf16), hid_ref[keys, v_cols])
                total = part if total is None else total + part
            att_ref[rows, v_cols] = total

    for i in range(steps):
        rows = pl.ds(i * STEP, STEP)
        ahat, inv = standardize(att_ref[rows, :])
        user = user_ref[rows, :].astype(f32)
        mixed_ref[rows, :] = (ahat * user).astype(bf16)
        grad_mixed = dot_nt(masked_ref[rows, :], wout_ref[...])
        gpre_ref[rows, :] = (grad_mixed * ahat * duser_ref[rows, :]).astype(bf16)
        e = grad_mixed * user
        gatt_ref[rows, :] = (inv * (e - jnp.mean(e, axis=-1, keepdims=True)
                                    - ahat * jnp.mean(e * ahat, axis=-1, keepdims=True))).astype(bf16)

    term_ref[:, :width] = dot_tn(mixed_ref[...], masked_ref[...])
    term_ref[:, width:] = dot_tn(normed_ref[...], gpre_ref[...])


def backward_kernel(len_ref, ev_ref, cot_ref, win_ref, slot_ref, hid_ref, dsilu_ref, gatt_ref, gpre_u_ref,
                    term_ref, send_ref,
                    normed_ref, gpre_ref, hi_ref, lo_ref):
    tokens, width = ev_ref.shape
    hd = width // HEADS
    length = len_ref[0]
    inv_len = 1.0 / length.astype(f32)
    scale = hd ** -0.5
    steps = tokens // STEP

    tri = lax.broadcasted_iota(jnp.int32, (STEP, STEP), 0) <= lax.broadcasted_iota(jnp.int32, (STEP, STEP), 1)
    for h in range(HEADS):
        v_cols = slice(h * hd, (h + 1) * hd)
        q_cols = slice(width + h * hd, width + (h + 1) * hd)
        k_cols = slice(2 * width + h * hd, 2 * width + (h + 1) * hd)
        grad_q = [None] * steps
        for j in range(steps):
            keys = pl.ds(j * STEP, STEP)
            key, value = hid_ref[keys, k_cols], hid_ref[keys, v_cols]
            grad_k = grad_v = None
            for i in range(j, steps):
                rows = pl.ds(i * STEP, STEP)
                query, gatt = hid_ref[rows, q_cols], gatt_ref[rows, v_cols]
                half = dot_nt(key, query) * (0.5 * scale)
                sig2 = 1.0 + jnp.tanh(half)
                silu = half * sig2
                dsilu = sig2 * ((1.0 + half) + (half - silu))
                weights = silu * inv_len
                gscore = dot_nt(value, gatt) * dsilu * (0.5 * inv_len * scale)
                if i == j:
                    weights = jnp.where(tri, weights, 0.0)
                    gscore = jnp.where(tri, gscore, 0.0)
                weights, gscore = weights.astype(bf16), gscore.astype(bf16)
                pv, pk, pq = dot_nn(weights, gatt), dot_nn(gscore, query), dot_tn(gscore, key)
                grad_v = pv if grad_v is None else grad_v + pv
                grad_k = pk if grad_k is None else grad_k + pk
                grad_q[i] = pq if grad_q[i] is None else grad_q[i] + pq
            gpre_ref[keys, v_cols] = (grad_v * dsilu_ref[keys, v_cols].astype(f32)).astype(bf16)
            gpre_ref[keys, k_cols] = (grad_k * dsilu_ref[keys, k_cols].astype(f32)).astype(bf16)
        for i in range(steps):
            rows = pl.ds(i * STEP, STEP)
            gpre_ref[rows, q_cols] = (grad_q[i] * dsilu_ref[rows, q_cols].astype(f32)).astype(bf16)

    for i in range(steps):
        rows = pl.ds(i * STEP, STEP)
        xhat, inv = standardize(ev_ref[rows, :].astype(f32))
        normed_ref[rows, :] = xhat.astype(bf16)
        grad_normed = dot_nt(gpre_u_ref[rows, :], win_ref[:, :width]) + dot_nt(gpre_ref[rows, :], win_ref[:, width:])
        grad = masked_rows(cot_ref[rows, :], i * STEP, length) + inv * (
            grad_normed - jnp.mean(grad_normed, axis=-1, keepdims=True)
            - xhat * jnp.mean(grad_normed * xhat, axis=-1, keepdims=True))
        high = grad.astype(bf16)
        hi_ref[rows, :] = high
        lo_ref[rows, :] = (grad - high.astype(f32)).astype(bf16)

    term_ref[...] = dot_tn(normed_ref[...], gpre_ref[...])
    send_ref[...] = one_hot_rows(slot_ref, send_ref.shape[0], hi_ref, lo_ref)


def one_hot_rows(ids_ref, rows, hi_ref, lo_ref):
    named = lax.broadcasted_iota(jnp.int32, (rows, ids_ref.shape[1]), 0) == ids_ref[...]
    onehot = jnp.where(named, 1.0, 0.0).astype(bf16)
    return dot_nn(onehot, hi_ref[...]) + dot_nn(onehot, lo_ref[...])


def table_kernel(ids_ref, recv_ref, table_ref, accum_ref, table_new_ref, accum_new_ref, hi_ref, lo_ref):
    high = recv_ref[...].astype(bf16)
    hi_ref[...] = high
    lo_ref[...] = (recv_ref[...] - high.astype(f32)).astype(bf16)
    grad = one_hot_rows(ids_ref, table_ref.shape[0], hi_ref, lo_ref)
    accum_new = accum_ref[...] + jnp.mean(grad * grad, axis=-1, keepdims=True)
    accum_new_ref[...] = accum_new
    table_new_ref[...] = table_ref[...] - learning_rate * grad / (jnp.sqrt(accum_new) + adagrad_eps)


def vmem():
    return pl.BlockSpec(memory_space=pltpu.VMEM)


def smem():
    return pl.BlockSpec(memory_space=pltpu.SMEM)


def shape(*dims, dtype=f32):
    return jax.ShapeDtypeStruct(dims, dtype)


def forward_part(lengths, events, cotangent, w_in, w_out):
    tokens, width = events.shape
    return pl.pallas_call(
        forward_kernel,
        name="forward_part",
        in_specs=[smem()] + [vmem()] * 4,
        out_specs=[vmem()] * 5,
        out_shape=[
            shape(width, 2 * width),
            shape(tokens, 3 * width, dtype=bf16),
            shape(tokens, 3 * width, dtype=bf16),
            shape(tokens, width, dtype=bf16),
            shape(tokens, width, dtype=bf16),
        ],
        scratch_shapes=[
            pltpu.VMEM((tokens, width), bf16),
            pltpu.VMEM((tokens, width), bf16),
            pltpu.VMEM((tokens, width), f32),
            pltpu.VMEM((tokens, width), f32),
            pltpu.VMEM((tokens, width), bf16),
            pltpu.VMEM((tokens, width), bf16),
        ],
        compiler_params=pltpu.CompilerParams(vmem_limit_bytes=VMEM_BYTES),
    )(lengths, events, cotangent, w_in, w_out)


def backward_part(lengths, events, cotangent, w_in, event_slot, hid, dsilu, gatt, gpre_u):
    tokens, width = events.shape
    return pl.pallas_call(
        backward_kernel,
        name="backward_part",
        in_specs=[smem()] + [vmem()] * 8,
        out_specs=[vmem()] * 2,
        out_shape=[shape(width, 3 * width), shape(event_slot.shape[1], width)],
        scratch_shapes=[
            pltpu.VMEM((tokens, width), bf16),
            pltpu.VMEM((tokens, 3 * width), bf16),
            pltpu.VMEM((tokens, width), bf16),
            pltpu.VMEM((tokens, width), bf16),
        ],
        compiler_params=pltpu.CompilerParams(vmem_limit_bytes=VMEM_BYTES),
    )(lengths, events, cotangent, w_in, event_slot, hid, dsilu, gatt, gpre_u)


def table_part(ids, recv, table, accum):
    rows, width = table.shape
    return pl.pallas_call(
        table_kernel,
        name="table_part",
        in_specs=[vmem()] * 4,
        out_specs=[vmem()] * 2,
        out_shape=[shape(rows, width), shape(rows, 1)],
        scratch_shapes=[pltpu.VMEM(recv.shape, bf16), pltpu.VMEM(recv.shape, bf16)],
        compiler_params=pltpu.CompilerParams(vmem_limit_bytes=VMEM_BYTES),
    )(ids, recv, table, accum)


def body(events, cotangent, lengths, event_slot, slot_row, slot_count, w_in, w_out, item_table, accumulator):
    tokens, width = events.shape
    owners = slot_count.shape[1]
    me = lax.axis_index(("dp", "rows"))
    ids = lax.all_gather(slot_row[0].reshape(-1), ("dp", "rows"), axis=0, tiled=False)
    ids = lax.dynamic_index_in_dim(ids.reshape(owners, owners, -1), me, 1, keepdims=False).reshape(1, -1)

    def summed(term):
        return lax.psum(lax.psum_scatter(term, "rows", scatter_dimension=0, tiled=True), "dp") / tokens

    first, hid, dsilu, gatt, gpre_u = forward_part(lengths, events, cotangent, w_in, w_out)
    second, send = backward_part(lengths, events, cotangent, w_in, event_slot, hid, dsilu, gatt, gpre_u)
    recv = lax.all_to_all(send.reshape(owners, -1, width), ("dp", "rows"), split_axis=0, concat_axis=0, tiled=True)
    first, second = summed(first), summed(second)
    table_new, accum_new = table_part(ids, recv.reshape(-1, width), item_table, accumulator[:, None])
    grad_in = jnp.concatenate([first[:, width:], second], axis=1)
    return grad_in, first[:, :width], table_new, accum_new[:, 0]


def solution(mesh):
    whole = P(("dp", "rows"))
    in_specs = (whole,) * 6 + (P(), P(), whole, whole)
    out_specs = (P("rows"), P("rows"), whole, whole)
    return jax.shard_map(body, mesh=mesh, in_specs=in_specs, out_specs=out_specs, check_vma=False)
```

```python
import functools

import jax
import jax.numpy as jnp
from jax import lax
from jax.experimental import pallas as pl
from jax.experimental.pallas import tpu as pltpu
from jax.sharding import PartitionSpec as P

HEADS = 4

norm_eps = 1e-05
adagrad_eps = 1e-10
learning_rate = 0.1

f32, bf16 = jnp.float32, jnp.bfloat16
VMEM_BYTES = 56 * 1024 * 1024
STEP = 256
LANES = 128
ID_ROWS = 8


def dot_nn(a, b):
    return lax.dot_general(a, b, (((1,), (0,)), ((), ())), preferred_element_type=f32)


def dot_nt(a, b):
    return lax.dot_general(a, b, (((1,), (1,)), ((), ())), preferred_element_type=f32)


def dot_tn(a, b):
    return lax.dot_general(a, b, (((0,), (0,)), ((), ())), preferred_element_type=f32)


def standardize(x):
    centered = x - jnp.mean(x, axis=-1, keepdims=True)
    inv = lax.rsqrt(jnp.mean(centered * centered, axis=-1, keepdims=True) + norm_eps)
    return centered * inv, inv


def masked_rows(cot, start, length):
    row = start + lax.broadcasted_iota(jnp.int32, cot.shape, 0)
    return jnp.where(row < length, cot.astype(f32), 0.0)


def owner_order(width, rows, dp):
    chips = rows // 2
    piece = width // (rows * dp)
    at = lax.broadcasted_iota(jnp.int32, (width, 1), 0)
    side, rest = at // (width // 2), at % (width // 2)
    part, rest = rest // (chips * piece), rest % (chips * piece)
    chip, row = rest // piece, rest % piece
    core = lax.rem(lax.axis_index("rows"), 2)
    core = jnp.where(side == 0, core, 1 - core)
    wanted = ((chip * 2 + core) * dp + part) * piece + row
    return jnp.where(lax.broadcasted_iota(jnp.int32, (width, width), 1) == wanted, 1.0, 0.0).astype(bf16)


def forward_kernel(rows_size, dp_size, len_ref, ev_ref, cot_ref, win_ref, wout_ref,
                   keep_ref, send_ref, hid_ref, dsilu_ref, gatt_ref, gpre_ref, normed_t_ref,
                   normed_ref, user_ref, duser_ref, att_ref, mixed_ref, masked_ref):
    tokens, width = ev_ref.shape
    hd = width // HEADS
    length = len_ref[0]
    inv_len = 1.0 / length.astype(f32)
    scale = hd ** -0.5
    steps = tokens // STEP

    for i in range(steps):
        rows = pl.ds(i * STEP, STEP)
        xhat, _ = standardize(ev_ref[rows, :].astype(f32))
        normed_ref[rows, :] = xhat.astype(bf16)
        masked_ref[rows, :] = masked_rows(cot_ref[rows, :], i * STEP, length).astype(bf16)

    def project(i, c):
        rows = pl.ds(i * STEP, STEP)
        pre = dot_nn(normed_ref[rows, :], win_ref[:, c * width:(c + 1) * width])
        sig = 0.5 + 0.5 * jnp.tanh(0.5 * pre)
        hid = pre * sig
        dsilu = sig * (1.0 + (pre - hid))
        if c == 0:
            user_ref[rows, :] = hid.astype(bf16)
            duser_ref[rows, :] = dsilu
        else:
            cols = slice((c - 1) * width, c * width)
            hid_ref[rows, cols] = hid.astype(bf16)
            dsilu_ref[rows, cols] = dsilu.astype(bf16)

    for c in range(4):
        for i in range(steps):
            project(i, c)

    tri = lax.broadcasted_iota(jnp.int32, (STEP, STEP), 0) >= lax.broadcasted_iota(jnp.int32, (STEP, STEP), 1)
    for h in range(HEADS):
        v_cols = slice(h * hd, (h + 1) * hd)
        q_cols = slice(width + h * hd, width + (h + 1) * hd)
        k_cols = slice(2 * width + h * hd, 2 * width + (h + 1) * hd)
        for i in range(steps):
            rows = pl.ds(i * STEP, STEP)
            query = hid_ref[rows, q_cols]
            total = None
            for j in range(i + 1):
                keys = pl.ds(j * STEP, STEP)
                half = dot_nt(query, hid_ref[keys, k_cols]) * (0.5 * scale)
                weights = (half + half * jnp.tanh(half)) * inv_len
                if i == j:
                    weights = jnp.where(tri, weights, 0.0)
                part = dot_nn(weights.astype(bf16), hid_ref[keys, v_cols])
                total = part if total is None else total + part
            att_ref[rows, v_cols] = total

    for i in range(steps):
        rows = pl.ds(i * STEP, STEP)
        ahat, inv = standardize(att_ref[rows, :])
        user = user_ref[rows, :].astype(f32)
        mixed_ref[rows, :] = (ahat * user).astype(bf16)
        grad_mixed = dot_nt(masked_ref[rows, :], wout_ref[...])
        gpre_ref[rows, :] = (grad_mixed * ahat * duser_ref[rows, :]).astype(bf16)
        e = grad_mixed * user
        gatt_ref[rows, :] = (inv * (e - jnp.mean(e, axis=-1, keepdims=True)
                                    - ahat * jnp.mean(e * ahat, axis=-1, keepdims=True))).astype(bf16)

    order = owner_order(width, rows_size, dp_size)
    normed_t_ref[...] = dot_nt(order, normed_ref[...]).astype(bf16)
    mixed_t = dot_nt(order, mixed_ref[...]).astype(bf16)
    half = width // 2
    for ref, start in ((send_ref, half), (keep_ref, 0)):
        ref[:, :width] = dot_nn(mixed_t[start:start + half], masked_ref[...])
        ref[:, width:] = dot_nn(normed_t_ref[start:start + half, :], gpre_ref[...])


def attention_kernel(len_ref, hid_ref, dsilu_ref, gatt_ref, normed_t_ref, keep_ref, send_ref, gpre_ref):
    tokens, width = gatt_ref.shape
    hd = width // HEADS
    inv_len = 1.0 / len_ref[0].astype(f32)
    scale = hd ** -0.5
    steps = tokens // STEP

    tri = lax.broadcasted_iota(jnp.int32, (STEP, STEP), 0) <= lax.broadcasted_iota(jnp.int32, (STEP, STEP), 1)
    for h in range(HEADS):
        v_cols = slice(h * hd, (h + 1) * hd)
        q_cols = slice(width + h * hd, width + (h + 1) * hd)
        k_cols = slice(2 * width + h * hd, 2 * width + (h + 1) * hd)
        grad_q = [None] * steps
        for j in range(steps):
            keys = pl.ds(j * STEP, STEP)
            key, value = hid_ref[keys, k_cols], hid_ref[keys, v_cols]
            grad_k = grad_v = None
            for i in range(j, steps):
                rows = pl.ds(i * STEP, STEP)
                query, gatt = hid_ref[rows, q_cols], gatt_ref[rows, v_cols]
                half = dot_nt(key, query) * (0.5 * scale)
                sig2 = 1.0 + jnp.tanh(half)
                silu = half * sig2
                dsilu = sig2 * ((1.0 + half) + (half - silu))
                weights = silu * inv_len
                gscore = dot_nt(value, gatt) * dsilu * (0.5 * inv_len * scale)
                if i == j:
                    weights = jnp.where(tri, weights, 0.0)
                    gscore = jnp.where(tri, gscore, 0.0)
                weights, gscore = weights.astype(bf16), gscore.astype(bf16)
                pv, pk, pq = dot_nn(weights, gatt), dot_nn(gscore, query), dot_tn(gscore, key)
                grad_v = pv if grad_v is None else grad_v + pv
                grad_k = pk if grad_k is None else grad_k + pk
                grad_q[i] = pq if grad_q[i] is None else grad_q[i] + pq
            gpre_ref[keys, v_cols] = (grad_v * dsilu_ref[keys, v_cols].astype(f32)).astype(bf16)
            gpre_ref[keys, k_cols] = (grad_k * dsilu_ref[keys, k_cols].astype(f32)).astype(bf16)
        for i in range(steps):
            rows = pl.ds(i * STEP, STEP)
            gpre_ref[rows, q_cols] = (grad_q[i] * dsilu_ref[rows, q_cols].astype(f32)).astype(bf16)

    half = width // 2
    for ref, start in ((send_ref, half), (keep_ref, 0)):
        ref[...] = dot_nn(normed_t_ref[start:start + half, :], gpre_ref[...])


def events_kernel(len_ref, ev_ref, cot_ref, win_ref, slot_ref, slot_row_ref, gpre_u_ref, gpre_ref,
                  send_ref, hi_ref, lo_ref, rows_ref):
    tokens, width = ev_ref.shape
    owners, capacity = slot_row_ref.shape
    length = len_ref[0]
    for i in range(tokens // STEP):
        rows = pl.ds(i * STEP, STEP)
        xhat, inv = standardize(ev_ref[rows, :].astype(f32))
        grad_normed = dot_nt(gpre_u_ref[rows, :], win_ref[:, :width]) + dot_nt(gpre_ref[rows, :], win_ref[:, width:])
        grad = masked_rows(cot_ref[rows, :], i * STEP, length) + inv * (
            grad_normed - jnp.mean(grad_normed, axis=-1, keepdims=True)
            - xhat * jnp.mean(grad_normed * xhat, axis=-1, keepdims=True))
        high = grad.astype(bf16)
        hi_ref[rows, :] = high
        lo_ref[rows, :] = (grad - high.astype(f32)).astype(bf16)

    rows_ref[...] = one_hot_rows(slot_ref[...], rows_ref.shape[0], hi_ref, lo_ref)
    me = lax.axis_index(("dp", "rows"))
    lane = lax.broadcasted_iota(jnp.int32, (capacity, LANES), 1)
    place = lax.broadcasted_iota(jnp.int32, (capacity, LANES), 0) + lax.rem(me, LANES // capacity) * capacity
    spread = jnp.where(lane == place, 1.0, 0.0).astype(bf16)
    ids = slot_row_ref[...]
    ids = 16.0 * dot_nn((ids // 16).astype(bf16), spread) + dot_nn((ids % 16).astype(bf16), spread)
    tiles = width // LANES
    for o in range(owners):
        for t in range(tiles):
            send_ref[o, t * capacity:(t + 1) * capacity, :] = rows_ref[o * capacity:(o + 1) * capacity, t * LANES:(t + 1) * LANES]
        send_ref[o, tiles * capacity:, :] = jnp.broadcast_to(ids[o:o + 1, :], (ID_ROWS, LANES))


def one_hot_rows(ids, rows, hi_ref, lo_ref):
    named = lax.broadcasted_iota(jnp.int32, (rows, ids.shape[1]), 0) == ids
    onehot = jnp.where(named, 1.0, 0.0).astype(bf16)
    return dot_nn(onehot, hi_ref[...]) + dot_nn(onehot, lo_ref[...])


def table_kernel(recv_ref, table_ref, accum_ref, table_new_ref, accum_new_ref, rows_ref, hi_ref, lo_ref):
    owners = recv_ref.shape[0]
    rows, width = table_ref.shape
    tiles = width // LANES
    capacity = (recv_ref.shape[1] - ID_ROWS) // tiles
    for o in range(owners):
        for t in range(tiles):
            rows_ref[o * capacity:(o + 1) * capacity, t * LANES:(t + 1) * LANES] = recv_ref[o, t * capacity:(t + 1) * capacity, :]
    group = LANES // capacity
    ids = [sum(recv_ref[o, tiles * capacity:, :] for o in range(g, g + group)) for g in range(0, owners, group)]
    ids = jnp.concatenate(ids, axis=1)[:1, :].astype(jnp.int32)
    high = rows_ref[...].astype(bf16)
    hi_ref[...] = high
    lo_ref[...] = (rows_ref[...] - high.astype(f32)).astype(bf16)
    grad = one_hot_rows(ids, rows, hi_ref, lo_ref)
    accum = jnp.transpose(jnp.broadcast_to(accum_ref[...].reshape(1, rows), (8, rows)))[:, :1]
    accum_new = accum + jnp.mean(grad * grad, axis=-1, keepdims=True)
    accum_new_ref[...] = jnp.transpose(jnp.broadcast_to(accum_new, (rows, LANES)))[:1, :].reshape(rows)
    table_new_ref[...] = table_ref[...] - learning_rate * grad / (jnp.sqrt(accum_new) + adagrad_eps)


def split_first_kernel(keep_ref, recv_ref, send_a_ref, keep_a_ref, send_b_ref, keep_b_ref):
    d = lax.axis_index("dp")
    x, y = lax.rem(d, 2), d // 2
    half = keep_ref.shape[-1] // 2
    lo, hi = slice(0, half), slice(half, 2 * half)
    for s in range(2):
        send_a_ref[s] = keep_ref[s, 1 - x, :, lo] + recv_ref[s, 1 - x, :, lo]
        send_b_ref[s] = keep_ref[1 - y, s, :, hi] + recv_ref[1 - y, s, :, hi]
        keep_a_ref[s] = keep_ref[s, x, :, lo] + recv_ref[s, x, :, lo]
        keep_b_ref[s] = keep_ref[y, s, :, hi] + recv_ref[y, s, :, hi]


def split_second_kernel(keep_a_ref, recv_a_ref, keep_b_ref, recv_b_ref, send_a_ref, next_a_ref, send_b_ref, next_b_ref):
    d = lax.axis_index("dp")
    x, y = lax.rem(d, 2), d // 2
    send_a_ref[...] = keep_a_ref[1 - y] + recv_a_ref[1 - y]
    send_b_ref[...] = keep_b_ref[1 - x] + recv_b_ref[1 - x]
    next_a_ref[...] = keep_a_ref[y] + recv_a_ref[y]
    next_b_ref[...] = keep_b_ref[x] + recv_b_ref[x]


def chips_kernel(keep_a_ref, recv_a_ref, keep_b_ref, recv_b_ref, *out_refs):
    chips = len(out_refs)
    chip = lax.axis_index("rows") // 2
    half = keep_a_ref.shape[-1]
    for k, out_ref in enumerate(out_refs):
        at = lax.rem(chip + k, chips)
        out_ref[:, :half] = keep_a_ref[at] + recv_a_ref[at]
        out_ref[:, half:] = keep_b_ref[at] + recv_b_ref[at]


def total_kernel(tokens, *refs):
    total = refs[0][...]
    for ref in refs[1:-1]:
        total = total + ref[...]
    refs[-1][...] = total * (1.0 / tokens)


def gather_kernel(*refs):
    *pieces, grad_in_ref, grad_out_ref = refs
    dp = len(pieces) // 2
    d = lax.axis_index("dp")
    width = grad_out_ref.shape[-1]
    for k in range(dp):
        at = jnp.bitwise_xor(d, k)
        grad_out_ref[at] = pieces[k][:, :width]
        grad_in_ref[at, :, :width] = pieces[k][:, width:]
        grad_in_ref[at, :, width:] = pieces[dp + k][...]


def vmem():
    return pl.BlockSpec(memory_space=pltpu.VMEM)


def smem():
    return pl.BlockSpec(memory_space=pltpu.SMEM)


def shape(*dims, dtype=f32):
    return jax.ShapeDtypeStruct(dims, dtype)


def call(kernel, name, out_shape, args, scalars=0, scratch=()):
    return pl.pallas_call(
        kernel,
        name=name,
        in_specs=[smem()] * scalars + [vmem()] * (len(args) - scalars),
        out_specs=[vmem()] * len(out_shape),
        out_shape=out_shape,
        scratch_shapes=[pltpu.VMEM(dims, dtype) for dims, dtype in scratch],
        compiler_params=pltpu.CompilerParams(vmem_limit_bytes=VMEM_BYTES),
    )(*args)


def body(rows_size, dp_size, events, cotangent, lengths, event_slot, slot_row, slot_count, w_in, w_out, item_table, accumulator):
    tokens, width = events.shape
    owners, capacity = slot_row.shape[1:]
    chips = rows_size // 2
    piece = width // (rows_size * dp_size)
    flip = lambda bit, size: [(i, i ^ bit) for i in range(size)]
    other_core = lambda v: lax.ppermute(v, "rows", flip(1, rows_size))
    over_dp = lambda v, bit: lax.ppermute(v, "dp", flip(bit, dp_size))
    over_chips = lambda v, k: lax.ppermute(v, "rows", [(i, (i + 2 * k) % rows_size) for i in range(rows_size)])

    def summed(keep, recv):
        cols = keep.shape[1]
        views = [v.reshape(2, 2, chips * piece, cols) for v in (keep, recv)]
        send_a, keep_a, send_b, keep_b = call(
            split_first_kernel, "split_first", [shape(2, chips * piece, cols // 2)] * 4, views)
        recv_a, recv_b = over_dp(send_a, 1), over_dp(send_b, 2)
        send_a, keep_a, send_b, keep_b = call(
            split_second_kernel, "split_second", [shape(chips * piece, cols // 2)] * 4, [keep_a, recv_a, keep_b, recv_b])
        recv_a, recv_b = over_dp(send_a, 2), over_dp(send_b, 1)
        views = [v.reshape(chips, piece, cols // 2) for v in (keep_a, recv_a, keep_b, recv_b)]
        blocks = call(chips_kernel, "by_chip", [shape(piece, cols)] * chips, views)
        blocks = [blocks[0]] + [over_chips(blocks[k], k) for k in range(1, chips)]
        (total,) = call(functools.partial(total_kernel, tokens), "total", [shape(piece, cols)], blocks)
        return [total] + [over_dp(total, k) for k in range(1, dp_size)]

    sides = lambda cols: [shape(width // 2, cols)] * 2
    keep1, send1, hid, dsilu, gatt, gpre_u, normed_t = call(
        functools.partial(forward_kernel, rows_size, dp_size), "forward_part",
        sides(2 * width) + [
            shape(tokens, 3 * width, dtype=bf16),
            shape(tokens, 3 * width, dtype=bf16),
            shape(tokens, width, dtype=bf16),
            shape(tokens, width, dtype=bf16),
            shape(width, tokens, dtype=bf16),
        ],
        (lengths, events, cotangent, w_in, w_out), 1,
        [((tokens, width), bf16), ((tokens, width), bf16), ((tokens, width), f32), ((tokens, width), f32),
         ((tokens, width), bf16), ((tokens, width), bf16)])
    recv1 = other_core(send1)
    keep2, send2, gpre = call(
        attention_kernel, "attention_part", sides(3 * width) + [shape(tokens, 3 * width, dtype=bf16)],
        (lengths, hid, dsilu, gatt, normed_t), 1)
    recv2 = other_core(send2)
    pay_rows = capacity * (width // LANES) + ID_ROWS
    (send,) = call(
        events_kernel, "events_part", [shape(owners, pay_rows, LANES)],
        (lengths, events, cotangent, w_in, event_slot, slot_row[0], gpre_u, gpre), 1,
        [((tokens, width), bf16), ((tokens, width), bf16), ((owners * capacity, width), f32)])
    recv = lax.all_to_all(send, ("dp", "rows"), split_axis=0, concat_axis=0, tiled=True)
    pieces = summed(keep1, recv1) + summed(keep2, recv2)
    grad_in, grad_out = call(
        gather_kernel, "gather", [shape(dp_size, piece, 4 * width), shape(dp_size, piece, width)], pieces)
    slots = owners * capacity
    table_new, accum_new = call(
        table_kernel, "table_part", [shape(*item_table.shape), shape(*accumulator.shape)],
        (recv, item_table, accumulator), 0,
        [((slots, width), f32), ((slots, width), bf16), ((slots, width), bf16)])
    return grad_in.reshape(-1, 4 * width), grad_out.reshape(-1, width), table_new, accum_new


def solution(mesh):
    whole = P(("dp", "rows"))
    in_specs = (whole,) * 6 + (P(), P(), whole, whole)
    out_specs = (P("rows"), P("rows"), whole, whole)
    run = functools.partial(body, mesh.shape["rows"], mesh.shape["dp"])
    return jax.shard_map(run, mesh=mesh, in_specs=in_specs, out_specs=out_specs, check_vma=False)
```

```python
import functools

import jax
import jax.numpy as jnp
from jax import lax
from jax.experimental import pallas as pl
from jax.experimental.pallas import tpu as pltpu
from jax.sharding import PartitionSpec as P

HEADS = 4

norm_eps = 1e-05
adagrad_eps = 1e-10
learning_rate = 0.1

f32, bf16 = jnp.float32, jnp.bfloat16
VMEM_BYTES = 32 * 1024 * 1024
STEP = 256
LANES = 128
ID_ROWS = 8


def dot_nn(a, b):
    return lax.dot_general(a, b, (((1,), (0,)), ((), ())), preferred_element_type=f32)


def dot_nt(a, b):
    return lax.dot_general(a, b, (((1,), (1,)), ((), ())), preferred_element_type=f32)


def dot_tn(a, b):
    return lax.dot_general(a, b, (((0,), (0,)), ((), ())), preferred_element_type=f32)


def standardize(x):
    centered = x - jnp.mean(x, axis=-1, keepdims=True)
    inv = lax.rsqrt(jnp.mean(centered * centered, axis=-1, keepdims=True) + norm_eps)
    return centered * inv, inv


def masked_rows(cot, start, length):
    row = start + lax.broadcasted_iota(jnp.int32, cot.shape, 0)
    return jnp.where(row < length, cot.astype(f32), 0.0)


def owner_order(width, rows, dp):
    chips = rows // 2
    piece = width // (rows * dp)
    at = lax.broadcasted_iota(jnp.int32, (width, 1), 0)
    side, rest = at // (width // 2), at % (width // 2)
    part, rest = rest // (chips * piece), rest % (chips * piece)
    chip, row = rest // piece, rest % piece
    core = lax.rem(lax.axis_index("rows"), 2)
    core = jnp.where(side == 0, core, 1 - core)
    wanted = ((chip * 2 + core) * dp + part) * piece + row
    return jnp.where(lax.broadcasted_iota(jnp.int32, (width, width), 1) == wanted, 1.0, 0.0).astype(bf16)


def forward_kernel(rows_size, dp_size, len_ref, ev_hbm, cot_hbm, win_hbm, wout_hbm,
                   keep_ref, send_ref, hid_ref, dsilu_ref, gatt_ref, gpre_ref, normed_t_ref,
                   ev_ref, cot_ref, win_ref, normed_ref, user_ref, duser_ref, att_ref, mixed_ref, masked_ref, dval_ref, weights_ref,
                   wout_ref, arrived):
    tokens, width = ev_ref.shape
    copies = [pltpu.make_async_copy(ev_hbm, ev_ref, arrived.at[0])]
    for c in range(4):
        cols = pl.ds(c * width, width)
        copies.append(pltpu.make_async_copy(win_hbm.at[:, cols], win_ref.at[:, cols], arrived.at[1 + c]))
    copies.append(pltpu.make_async_copy(cot_hbm, cot_ref, arrived.at[5]))
    copies.append(pltpu.make_async_copy(wout_hbm, wout_ref, arrived.at[6]))
    for copy in copies:
        copy.start()
    hd = width // HEADS
    length = len_ref[0]
    inv_len = 1.0 / length.astype(f32)
    scale = hd ** -0.5
    steps = tokens // STEP

    copies[0].wait()
    for i in range(steps):
        rows = pl.ds(i * STEP, STEP)
        xhat, _ = standardize(ev_ref[rows, :].astype(f32))
        normed_ref[rows, :] = xhat.astype(bf16)

    def project(i, c):
        rows = pl.ds(i * STEP, STEP)
        pre = dot_nn(normed_ref[rows, :], win_ref[:, c * width:(c + 1) * width])
        sig = 0.5 + 0.5 * jnp.tanh(0.5 * pre)
        hid = pre * sig
        dsilu = sig * (1.0 + (pre - hid))
        if c == 0:
            user_ref[rows, :] = hid.astype(bf16)
            duser_ref[rows, :] = dsilu
        else:
            cols = slice((c - 1) * width, c * width)
            hid_ref[rows, cols] = hid.astype(bf16)
            if c == 1:
                dval_ref[rows, :] = dsilu
            else:
                dsilu_ref[rows, (c - 2) * width:(c - 1) * width] = dsilu.astype(bf16)

    for c in range(4):
        copies[1 + c].wait()
        for i in range(steps):
            project(i, c)

    tri = lax.broadcasted_iota(jnp.int32, (STEP, STEP), 0) >= lax.broadcasted_iota(jnp.int32, (STEP, STEP), 1)
    for h in range(HEADS):
        v_cols = slice(h * hd, (h + 1) * hd)
        q_cols = slice(width + h * hd, width + (h + 1) * hd)
        k_cols = slice(2 * width + h * hd, 2 * width + (h + 1) * hd)
        for i in range(steps):
            rows = pl.ds(i * STEP, STEP)
            query = hid_ref[rows, q_cols]
            total = None
            for j in range(i + 1):
                keys = pl.ds(j * STEP, STEP)
                half = dot_nt(query, hid_ref[keys, k_cols]) * (0.5 * scale)
                weights = (half + half * jnp.tanh(half)) * inv_len
                if i == j:
                    weights = jnp.where(tri, weights, 0.0)
                weights = weights.astype(bf16)
                weights_ref[h, rows, keys] = weights
                part = dot_nn(weights, hid_ref[keys, v_cols])
                total = part if total is None else total + part
            att_ref[rows, v_cols] = total

    copies[5].wait()
    copies[6].wait()
    for i in range(steps):
        rows = pl.ds(i * STEP, STEP)
        masked_ref[rows, :] = masked_rows(cot_ref[rows, :], i * STEP, length).astype(bf16)
        ahat, inv = standardize(att_ref[rows, :])
        user = user_ref[rows, :].astype(f32)
        mixed_ref[rows, :] = (ahat * user).astype(bf16)
        grad_mixed = dot_nt(masked_ref[rows, :], wout_ref[...])
        gpre_ref[rows, :width] = (grad_mixed * ahat * duser_ref[rows, :]).astype(bf16)
        e = grad_mixed * user
        gatt_ref[rows, :] = (inv * (e - jnp.mean(e, axis=-1, keepdims=True)
                                    - ahat * jnp.mean(e * ahat, axis=-1, keepdims=True))).astype(bf16)

    for h in range(HEADS):
        v_cols = slice(h * hd, (h + 1) * hd)
        for j in range(steps):
            keys, rest = pl.ds(j * STEP, STEP), pl.ds(j * STEP, tokens - j * STEP)
            grad_v = dot_tn(weights_ref[h, rest, keys], gatt_ref[rest, v_cols])
            gpre_ref[keys, width + h * hd:width + (h + 1) * hd] = (grad_v * dval_ref[keys, v_cols]).astype(bf16)

    order = owner_order(width, rows_size, dp_size)
    normed_t_ref[...] = dot_nt(order, normed_ref[...]).astype(bf16)
    mixed_t = dot_nt(order, mixed_ref[...]).astype(bf16)
    half = width // 2
    for ref, start in ((send_ref, half), (keep_ref, 0)):
        ref[:, :width] = dot_nn(mixed_t[start:start + half], masked_ref[...])
        ref[:, width:] = dot_nn(normed_t_ref[start:start + half, :], gpre_ref[...])


def attention_kernel(len_ref, hid_ref, dsilu_ref, gatt_ref, normed_t_ref, keep_ref, send_ref, gpre_ref):
    tokens, width = gatt_ref.shape
    hd = width // HEADS
    inv_len = 1.0 / len_ref[0].astype(f32)
    scale = hd ** -0.5
    steps = tokens // STEP

    tri = lax.broadcasted_iota(jnp.int32, (STEP, STEP), 0) <= lax.broadcasted_iota(jnp.int32, (STEP, STEP), 1)
    for h in range(HEADS):
        v_cols = slice(h * hd, (h + 1) * hd)
        q_cols = slice(width + h * hd, width + (h + 1) * hd)
        k_cols = slice(2 * width + h * hd, 2 * width + (h + 1) * hd)
        grad_q = [None] * steps
        for j in range(steps):
            keys = pl.ds(j * STEP, STEP)
            key, value = hid_ref[keys, k_cols], hid_ref[keys, v_cols]
            grad_k = None
            for i in range(j, steps):
                rows = pl.ds(i * STEP, STEP)
                query, gatt = hid_ref[rows, q_cols], gatt_ref[rows, v_cols]
                half = dot_nt(key, query) * (0.5 * scale)
                sig2 = 1.0 + jnp.tanh(half)
                silu = half * sig2
                dsilu = sig2 * ((1.0 + half) + (half - silu))
                gscore = dot_nt(value, gatt) * dsilu * (0.5 * inv_len * scale)
                if i == j:
                    gscore = jnp.where(tri, gscore, 0.0)
                gscore = gscore.astype(bf16)
                pk, pq = dot_nn(gscore, query), dot_tn(gscore, key)
                grad_k = pk if grad_k is None else grad_k + pk
                grad_q[i] = pq if grad_q[i] is None else grad_q[i] + pq
            gpre_ref[keys, q_cols] = (grad_k * dsilu_ref[keys, q_cols].astype(f32)).astype(bf16)
        for i in range(steps):
            rows = pl.ds(i * STEP, STEP)
            gpre_ref[rows, v_cols] = (grad_q[i] * dsilu_ref[rows, v_cols].astype(f32)).astype(bf16)

    half = width // 2
    for ref, start in ((send_ref, half), (keep_ref, 0)):
        ref[...] = dot_nn(normed_t_ref[start:start + half, :], gpre_ref[...])


def events_kernel(len_ref, ev_ref, cot_ref, win_ref, slot_ref, slot_row_ref, gpre_uv_ref, gpre_qk_ref,
                  send_ref, hi_ref, lo_ref, rows_ref):
    tokens, width = ev_ref.shape
    capacity, owners = slot_row_ref.shape
    length = len_ref[0]
    for i in range(tokens // STEP):
        rows = pl.ds(i * STEP, STEP)
        xhat, inv = standardize(ev_ref[rows, :].astype(f32))
        grad_normed = dot_nt(gpre_uv_ref[rows, :], win_ref[:, :2 * width]) + dot_nt(gpre_qk_ref[rows, :], win_ref[:, 2 * width:])
        grad = masked_rows(cot_ref[rows, :], i * STEP, length) + inv * (
            grad_normed - jnp.mean(grad_normed, axis=-1, keepdims=True)
            - xhat * jnp.mean(grad_normed * xhat, axis=-1, keepdims=True))
        high = grad.astype(bf16)
        hi_ref[rows, :] = high
        lo_ref[rows, :] = (grad - high.astype(f32)).astype(bf16)

    rows_ref[...] = one_hot_rows(slot_ref[...], rows_ref.shape[0], hi_ref, lo_ref)
    me = lax.axis_index(("dp", "rows"))
    lane = lax.broadcasted_iota(jnp.int32, (capacity, LANES), 1)
    place = lax.broadcasted_iota(jnp.int32, (capacity, LANES), 0) + lax.rem(me, LANES // capacity) * capacity
    spread = jnp.where(lane == place, 1.0, 0.0).astype(bf16)
    ids = slot_row_ref[...]
    ids = 16.0 * dot_tn((ids // 16).astype(bf16), spread) + dot_tn((ids % 16).astype(bf16), spread)
    tiles = width // LANES
    for o in range(owners):
        for t in range(tiles):
            send_ref[o, t * capacity:(t + 1) * capacity, :] = rows_ref[o * capacity:(o + 1) * capacity, t * LANES:(t + 1) * LANES]
        send_ref[o, tiles * capacity:, :] = jnp.broadcast_to(ids[o:o + 1, :], (ID_ROWS, LANES))


def one_hot_rows(ids, rows, hi_ref, lo_ref):
    named = lax.broadcasted_iota(jnp.int32, (rows, ids.shape[1]), 0) == ids
    onehot = jnp.where(named, 1.0, 0.0).astype(bf16)
    return dot_nn(onehot, hi_ref[...]) + dot_nn(onehot, lo_ref[...])


def table_kernel(recv_ref, table_ref, accum_ref, table_new_ref, accum_new_ref, rows_ref, hi_ref, lo_ref):
    owners = recv_ref.shape[0]
    rows, width = table_ref.shape
    tiles = width // LANES
    capacity = (recv_ref.shape[1] - ID_ROWS) // tiles
    for o in range(owners):
        for t in range(tiles):
            rows_ref[o * capacity:(o + 1) * capacity, t * LANES:(t + 1) * LANES] = recv_ref[o, t * capacity:(t + 1) * capacity, :]
    group = LANES // capacity
    ids = [sum(recv_ref[o, tiles * capacity:, :] for o in range(g, g + group)) for g in range(0, owners, group)]
    ids = jnp.concatenate(ids, axis=1)[:1, :].astype(jnp.int32)
    high = rows_ref[...].astype(bf16)
    hi_ref[...] = high
    lo_ref[...] = (rows_ref[...] - high.astype(f32)).astype(bf16)
    grad = one_hot_rows(ids, rows, hi_ref, lo_ref)
    accum = jnp.transpose(jnp.broadcast_to(accum_ref[...].reshape(1, rows), (8, rows)))[:, :1]
    accum_new = accum + jnp.mean(grad * grad, axis=-1, keepdims=True)
    accum_new_ref[...] = jnp.transpose(jnp.broadcast_to(accum_new, (rows, LANES)))[:1, :].reshape(rows)
    table_new_ref[...] = table_ref[...] - learning_rate * grad / (jnp.sqrt(accum_new) + adagrad_eps)


def vmem():
    return pl.BlockSpec(memory_space=pltpu.VMEM)


def shape(*dims, dtype=f32):
    return jax.ShapeDtypeStruct(dims, dtype)


def call(kernel, name, out_shape, args, scalars=0, scratch=(), flops=0, far=0):
    place = [None] * scalars + [pltpu.HBM] * far + [pltpu.VMEM] * (len(args) - scalars - far)
    args = [a if p is None else pltpu.with_memory_space_constraint(a, p) for a, p in zip(args, place)]
    return pl.pallas_call(
        kernel,
        name=name,
        in_specs=[pl.BlockSpec(memory_space=p or pltpu.SMEM) for p in place],
        out_specs=[vmem()] * len(out_shape),
        out_shape=out_shape,
        scratch_shapes=[pltpu.VMEM(dims, dtype) for dims, dtype in scratch] + [pltpu.SemaphoreType.DMA((7,))] * (far > 0),
        compiler_params=pltpu.CompilerParams(vmem_limit_bytes=VMEM_BYTES),
        cost_estimate=pl.CostEstimate(flops=flops, bytes_accessed=1 << 20, transcendentals=0),
    )(*args)


def body(rows_size, dp_size, events, cotangent, lengths, event_slot, slot_row, slot_count, w_in, w_out, item_table, accumulator):
    tokens, width = events.shape
    owners, capacity = slot_row.shape[1:]
    chips = rows_size // 2
    piece = width // (rows_size * dp_size)
    cores = [(i, i ^ 1) for i in range(rows_size)]
    lines = [list(range(c, rows_size, 2)) for c in range(2)]

    def exchange(v, axis, groups=None):
        return lax.all_to_all(v, axis, split_axis=0, concat_axis=0, axis_index_groups=groups, tiled=True)

    def after(value, *others):
        return lax.optimization_barrier((value, *others))[0]

    def over_dp(both):
        return exchange(both.reshape(dp_size, chips * piece, both.shape[1]), "dp")

    def over_chips(parts):
        return exchange(jnp.sum(parts, axis=0).reshape(chips, piece, -1), "rows", lines)

    def gathered(parts):
        part = jnp.sum(parts, axis=0) * (1.0 / tokens)
        return exchange(jnp.broadcast_to(part, (dp_size, *part.shape)), "dp").reshape(dp_size * piece, -1)

    local = lambda *dims, dtype=f32: pltpu.VMEM(dims, dtype)
    sides = lambda cols: [local(width // 2, cols)] * 2
    keep1, send1, hid, dsilu, gatt, gpre_uv, normed_t, events, cotangent, w_in = call(
        functools.partial(forward_kernel, rows_size, dp_size), "forward_part",
        sides(3 * width) + [
            local(tokens, 3 * width, dtype=bf16),
            local(tokens, 2 * width, dtype=bf16),
            local(tokens, width, dtype=bf16),
            local(tokens, 2 * width, dtype=bf16),
            local(width, tokens, dtype=bf16),
            local(tokens, width, dtype=bf16),
            local(tokens, width, dtype=bf16),
            local(*w_in.shape, dtype=bf16),
        ],
        (lengths, events, cotangent, w_in, w_out), 1,
        [((tokens, width), bf16), ((tokens, width), bf16), ((tokens, width), f32), ((tokens, width), f32),
         ((tokens, width), bf16), ((tokens, width), bf16), ((tokens, width), f32), ((HEADS, tokens, tokens), bf16),
         (w_out.shape, bf16)],
        flops=100_000_000_000, far=4)
    recv1 = lax.ppermute(send1, "rows", cores)
    keep2, send2, gpre_qk = call(
        attention_kernel, "attention_part", sides(2 * width) + [local(tokens, 2 * width, dtype=bf16)],
        (lengths, hid, dsilu, gatt, normed_t), 1, flops=100_000_000_000)
    recv2 = lax.ppermute(send2, "rows", cores)
    pay_rows = capacity * (width // LANES) + ID_ROWS
    both1 = keep1 + recv1
    gpre_uv = after(gpre_uv, both1)
    parts1 = over_dp(both1)
    (send,) = call(
        events_kernel, "events_part", [local(owners, pay_rows, LANES)],
        (lengths, events, cotangent, w_in, event_slot, slot_row[0].T, gpre_uv, gpre_qk), 1,
        [((tokens, width), bf16), ((tokens, width), bf16), ((owners * capacity, width), f32)], flops=100_000_000_000)
    recv = exchange(send, ("dp", "rows"))
    both2 = after(keep2, send) + recv2
    parts2 = over_dp(both2)
    parts1 = over_chips(after(parts1, both2))
    parts2 = over_chips(after(parts2, parts1))
    first = gathered(parts1)
    second = gathered(parts2)
    grad_in = jnp.concatenate([first[:, width:], second], axis=1)
    slots = owners * capacity
    table_new, accum_new = call(
        table_kernel, "table_part", [shape(*item_table.shape), shape(*accumulator.shape)],
        (recv, item_table, accumulator), 0,
        [((slots, width), f32), ((slots, width), bf16), ((slots, width), bf16)], flops=10_000_000_000)
    return grad_in, first[:, :width], table_new, accum_new


def solution(mesh):
    whole = P(("dp", "rows"))
    in_specs = (whole,) * 6 + (P(), P(), whole, whole)
    out_specs = (P("rows"), P("rows"), whole, whole)
    run = functools.partial(body, mesh.shape["rows"], mesh.shape["dp"])
    return jax.shard_map(run, mesh=mesh, in_specs=in_specs, out_specs=out_specs, check_vma=False)
```

```python
import functools

import jax
import jax.numpy as jnp
from jax import lax
from jax.experimental import pallas as pl
from jax.experimental.pallas import tpu as pltpu
from jax.sharding import PartitionSpec as P

HEADS = 4

norm_eps = 1e-05
adagrad_eps = 1e-10
learning_rate = 0.1

f32, bf16 = jnp.float32, jnp.bfloat16
VMEM_BYTES = 16 * 1024 * 1024
STEP = 256
LANES = 128
ID_ROWS = 8


def dot_nn(a, b):
    return lax.dot_general(a, b, (((1,), (0,)), ((), ())), preferred_element_type=f32)


def dot_nt(a, b):
    return lax.dot_general(a, b, (((1,), (1,)), ((), ())), preferred_element_type=f32)


def dot_tn(a, b):
    return lax.dot_general(a, b, (((0,), (0,)), ((), ())), preferred_element_type=f32)


def standardize(x):
    centered = x - jnp.mean(x, axis=-1, keepdims=True)
    inv = lax.rsqrt(jnp.mean(centered * centered, axis=-1, keepdims=True) + norm_eps)
    return centered * inv, inv


def masked_rows(cot, start, length):
    row = start + lax.broadcasted_iota(jnp.int32, cot.shape, 0)
    return jnp.where(row < length, cot.astype(f32), 0.0)


def owner_order(width, rows, dp):
    chips = rows // 2
    piece = width // (rows * dp)
    at = lax.broadcasted_iota(jnp.int32, (width, 1), 0)
    side, rest = at // (width // 2), at % (width // 2)
    part, rest = rest // (chips * piece), rest % (chips * piece)
    chip, row = rest // piece, rest % piece
    core = lax.rem(lax.axis_index("rows"), 2)
    core = jnp.where(side == 0, core, 1 - core)
    wanted = ((chip * 2 + core) * dp + part) * piece + row
    return jnp.where(lax.broadcasted_iota(jnp.int32, (width, width), 1) == wanted, 1.0, 0.0).astype(bf16)


def forward_kernel(rows_size, dp_size, len_ref, ev_hbm, cot_hbm, win_hbm, wout_hbm,
                   keep_ref, send_ref, hid_ref, dsilu_ref, gatt_ref, gpre_ref, normed_t_ref,
                   ev_ref, cot_ref, win_ref, normed_ref, user_ref, duser_ref, att_ref, mixed_ref, masked_ref, dval_ref, weights_ref,
                   wout_ref, arrived):
    tokens, width = ev_ref.shape
    copies = [pltpu.make_async_copy(ev_hbm, ev_ref, arrived.at[0])]
    for c in range(4):
        cols = pl.ds(c * width, width)
        copies.append(pltpu.make_async_copy(win_hbm.at[:, cols], win_ref.at[:, cols], arrived.at[1 + c]))
    copies.append(pltpu.make_async_copy(cot_hbm, cot_ref, arrived.at[5]))
    copies.append(pltpu.make_async_copy(wout_hbm, wout_ref, arrived.at[6]))
    for copy in copies:
        copy.start()
    hd = width // HEADS
    length = len_ref[0]
    inv_len = 1.0 / length.astype(f32)
    scale = hd ** -0.5
    steps = tokens // STEP

    copies[0].wait()
    for i in range(steps):
        rows = pl.ds(i * STEP, STEP)
        xhat, _ = standardize(ev_ref[rows, :].astype(f32))
        normed_ref[rows, :] = xhat.astype(bf16)

    def project(i, c):
        rows = pl.ds(i * STEP, STEP)
        pre = dot_nn(normed_ref[rows, :], win_ref[:, c * width:(c + 1) * width])
        sig = 0.5 + 0.5 * jnp.tanh(0.5 * pre)
        hid = pre * sig
        dsilu = sig * (1.0 + (pre - hid))
        if c == 0:
            user_ref[rows, :] = hid.astype(bf16)
            duser_ref[rows, :] = dsilu
        else:
            cols = slice((c - 1) * width, c * width)
            hid_ref[rows, cols] = hid.astype(bf16)
            if c == 1:
                dval_ref[rows, :] = dsilu
            else:
                dsilu_ref[rows, (c - 2) * width:(c - 1) * width] = dsilu.astype(bf16)

    for c in range(4):
        copies[1 + c].wait()
        for i in range(steps):
            project(i, c)

    tri = lax.broadcasted_iota(jnp.int32, (STEP, STEP), 0) >= lax.broadcasted_iota(jnp.int32, (STEP, STEP), 1)
    for h in range(HEADS):
        v_cols = slice(h * hd, (h + 1) * hd)
        q_cols = slice(width + h * hd, width + (h + 1) * hd)
        k_cols = slice(2 * width + h * hd, 2 * width + (h + 1) * hd)
        for i in range(steps):
            rows = pl.ds(i * STEP, STEP)
            query = hid_ref[rows, q_cols]
            total = None
            for j in range(i + 1):
                keys = pl.ds(j * STEP, STEP)
                half = dot_nt(query, hid_ref[keys, k_cols]) * (0.5 * scale)
                weights = (half + half * jnp.tanh(half)) * inv_len
                if i == j:
                    weights = jnp.where(tri, weights, 0.0)
                weights = weights.astype(bf16)
                weights_ref[h, rows, keys] = weights
                part = dot_nn(weights, hid_ref[keys, v_cols])
                total = part if total is None else total + part
            att_ref[rows, v_cols] = total

    copies[5].wait()
    copies[6].wait()
    for i in range(steps):
        rows = pl.ds(i * STEP, STEP)
        masked_ref[rows, :] = masked_rows(cot_ref[rows, :], i * STEP, length).astype(bf16)
        ahat, inv = standardize(att_ref[rows, :])
        user = user_ref[rows, :].astype(f32)
        mixed_ref[rows, :] = (ahat * user).astype(bf16)
        grad_mixed = dot_nt(masked_ref[rows, :], wout_ref[...])
        gpre_ref[rows, :width] = (grad_mixed * ahat * duser_ref[rows, :]).astype(bf16)
        e = grad_mixed * user
        gatt_ref[rows, :] = (inv * (e - jnp.mean(e, axis=-1, keepdims=True)
                                    - ahat * jnp.mean(e * ahat, axis=-1, keepdims=True))).astype(bf16)

    for h in range(HEADS):
        v_cols = slice(h * hd, (h + 1) * hd)
        for j in range(steps):
            keys, rest = pl.ds(j * STEP, STEP), pl.ds(j * STEP, tokens - j * STEP)
            grad_v = dot_tn(weights_ref[h, rest, keys], gatt_ref[rest, v_cols])
            gpre_ref[keys, width + h * hd:width + (h + 1) * hd] = (grad_v * dval_ref[keys, v_cols]).astype(bf16)

    order = owner_order(width, rows_size, dp_size)
    normed_t_ref[...] = dot_nt(order, normed_ref[...]).astype(bf16)
    mixed_t = dot_nt(order, mixed_ref[...]).astype(bf16)
    half = width // 2
    for ref, start in ((send_ref, half), (keep_ref, 0)):
        ref[:, :width] = dot_nn(mixed_t[start:start + half], masked_ref[...])
        ref[:, width:] = dot_nn(normed_t_ref[start:start + half, :], gpre_ref[...])


def attention_kernel(len_ref, hid_ref, dsilu_ref, gatt_ref, normed_t_ref, keep_ref, send_ref, gpre_ref):
    tokens, width = gatt_ref.shape
    hd = width // HEADS
    inv_len = 1.0 / len_ref[0].astype(f32)
    scale = hd ** -0.5
    steps = tokens // STEP

    tri = lax.broadcasted_iota(jnp.int32, (STEP, STEP), 0) <= lax.broadcasted_iota(jnp.int32, (STEP, STEP), 1)
    for h in range(HEADS):
        v_cols = slice(h * hd, (h + 1) * hd)
        q_cols = slice(width + h * hd, width + (h + 1) * hd)
        k_cols = slice(2 * width + h * hd, 2 * width + (h + 1) * hd)
        grad_q = [None] * steps
        for j in range(steps):
            keys = pl.ds(j * STEP, STEP)
            key, value = hid_ref[keys, k_cols], hid_ref[keys, v_cols]
            grad_k = None
            for i in range(j, steps):
                rows = pl.ds(i * STEP, STEP)
                query, gatt = hid_ref[rows, q_cols], gatt_ref[rows, v_cols]
                half = dot_nt(key, query) * (0.5 * scale)
                sig2 = 1.0 + jnp.tanh(half)
                silu = half * sig2
                dsilu = sig2 * ((1.0 + half) + (half - silu))
                gscore = dot_nt(value, gatt) * dsilu * (0.5 * inv_len * scale)
                if i == j:
                    gscore = jnp.where(tri, gscore, 0.0)
                gscore = gscore.astype(bf16)
                pk, pq = dot_nn(gscore, query), dot_tn(gscore, key)
                grad_k = pk if grad_k is None else grad_k + pk
                grad_q[i] = pq if grad_q[i] is None else grad_q[i] + pq
            gpre_ref[keys, q_cols] = (grad_k * dsilu_ref[keys, q_cols].astype(f32)).astype(bf16)
        for i in range(steps):
            rows = pl.ds(i * STEP, STEP)
            gpre_ref[rows, v_cols] = (grad_q[i] * dsilu_ref[rows, v_cols].astype(f32)).astype(bf16)

    half = width // 2
    for ref, start in ((send_ref, half), (keep_ref, 0)):
        ref[...] = dot_nn(normed_t_ref[start:start + half, :], gpre_ref[...])


def events_kernel(len_ref, ev_ref, cot_ref, win_ref, slot_ref, slot_row_ref, gpre_uv_ref, gpre_qk_ref,
                  send_ref, hi_ref, lo_ref, rows_ref):
    tokens, width = ev_ref.shape
    capacity, owners = slot_row_ref.shape
    length = len_ref[0]
    for i in range(tokens // STEP):
        rows = pl.ds(i * STEP, STEP)
        xhat, inv = standardize(ev_ref[rows, :].astype(f32))
        grad_normed = dot_nt(gpre_uv_ref[rows, :], win_ref[:, :2 * width]) + dot_nt(gpre_qk_ref[rows, :], win_ref[:, 2 * width:])
        grad = masked_rows(cot_ref[rows, :], i * STEP, length) + inv * (
            grad_normed - jnp.mean(grad_normed, axis=-1, keepdims=True)
            - xhat * jnp.mean(grad_normed * xhat, axis=-1, keepdims=True))
        high = grad.astype(bf16)
        hi_ref[rows, :] = high
        lo_ref[rows, :] = (grad - high.astype(f32)).astype(bf16)

    rows_ref[...] = one_hot_rows(slot_ref[...], rows_ref.shape[0], hi_ref, lo_ref)
    me = lax.axis_index(("dp", "rows"))
    lane = lax.broadcasted_iota(jnp.int32, (capacity, LANES), 1)
    place = lax.broadcasted_iota(jnp.int32, (capacity, LANES), 0) + lax.rem(me, LANES // capacity) * capacity
    spread = jnp.where(lane == place, 1.0, 0.0).astype(bf16)
    ids = slot_row_ref[...]
    ids = 16.0 * dot_tn((ids // 16).astype(bf16), spread) + dot_tn((ids % 16).astype(bf16), spread)
    tiles = width // LANES
    for o in range(owners):
        for t in range(tiles):
            send_ref[o, t * capacity:(t + 1) * capacity, :] = rows_ref[o * capacity:(o + 1) * capacity, t * LANES:(t + 1) * LANES]
        send_ref[o, tiles * capacity:, :] = jnp.broadcast_to(ids[o:o + 1, :], (ID_ROWS, LANES))


def one_hot_rows(ids, rows, hi_ref, lo_ref):
    named = lax.broadcasted_iota(jnp.int32, (rows, ids.shape[1]), 0) == ids
    onehot = jnp.where(named, 1.0, 0.0).astype(bf16)
    return dot_nn(onehot, hi_ref[...]) + dot_nn(onehot, lo_ref[...])


def table_kernel(recv_ref, table_ref, accum_ref, table_new_ref, accum_new_ref, rows_ref, hi_ref, lo_ref):
    owners = recv_ref.shape[0]
    rows, width = table_ref.shape
    tiles = width // LANES
    capacity = (recv_ref.shape[1] - ID_ROWS) // tiles
    for o in range(owners):
        for t in range(tiles):
            rows_ref[o * capacity:(o + 1) * capacity, t * LANES:(t + 1) * LANES] = recv_ref[o, t * capacity:(t + 1) * capacity, :]
    group = LANES // capacity
    ids = [sum(recv_ref[o, tiles * capacity:, :] for o in range(g, g + group)) for g in range(0, owners, group)]
    ids = jnp.concatenate(ids, axis=1)[:1, :].astype(jnp.int32)
    high = rows_ref[...].astype(bf16)
    hi_ref[...] = high
    lo_ref[...] = (rows_ref[...] - high.astype(f32)).astype(bf16)
    grad = one_hot_rows(ids, rows, hi_ref, lo_ref)
    accum = jnp.transpose(jnp.broadcast_to(accum_ref[...].reshape(1, rows), (8, rows)))[:, :1]
    accum_new = accum + jnp.mean(grad * grad, axis=-1, keepdims=True)
    accum_new_ref[...] = jnp.transpose(jnp.broadcast_to(accum_new, (rows, LANES)))[:1, :].reshape(rows)
    table_new_ref[...] = table_ref[...] - learning_rate * grad / (jnp.sqrt(accum_new) + adagrad_eps)


def split_first_kernel(keep_ref, recv_ref, send_a_ref, keep_a_ref, send_b_ref, keep_b_ref):
    d = lax.axis_index("dp")
    x, y = lax.rem(d, 2), d // 2
    half = keep_ref.shape[-1] // 2
    lo, hi = slice(0, half), slice(half, 2 * half)
    for s in range(2):
        send_a_ref[s] = keep_ref[s, 1 - x, :, lo] + recv_ref[s, 1 - x, :, lo]
        send_b_ref[s] = keep_ref[1 - y, s, :, hi] + recv_ref[1 - y, s, :, hi]
        keep_a_ref[s] = keep_ref[s, x, :, lo] + recv_ref[s, x, :, lo]
        keep_b_ref[s] = keep_ref[y, s, :, hi] + recv_ref[y, s, :, hi]


def split_second_kernel(keep_a_ref, recv_a_ref, keep_b_ref, recv_b_ref, send_a_ref, next_a_ref, send_b_ref, next_b_ref):
    d = lax.axis_index("dp")
    x, y = lax.rem(d, 2), d // 2
    send_a_ref[...] = keep_a_ref[1 - y] + recv_a_ref[1 - y]
    send_b_ref[...] = keep_b_ref[1 - x] + recv_b_ref[1 - x]
    next_a_ref[...] = keep_a_ref[y] + recv_a_ref[y]
    next_b_ref[...] = keep_b_ref[x] + recv_b_ref[x]


def chips_kernel(keep_a_ref, recv_a_ref, keep_b_ref, recv_b_ref, *out_refs):
    chips = len(out_refs)
    chip = lax.axis_index("rows") // 2
    half = keep_a_ref.shape[-1]
    for k, out_ref in enumerate(out_refs):
        at = lax.rem(chip + k, chips)
        out_ref[:, :half] = keep_a_ref[at] + recv_a_ref[at]
        out_ref[:, half:] = keep_b_ref[at] + recv_b_ref[at]


def total_kernel(tokens, *refs):
    *pieces, out_ref = refs
    half = len(pieces) // 2
    start = 0
    for group in (pieces[:half], pieces[half:]):
        total = group[0][...]
        for ref in group[1:]:
            total = total + ref[...]
        end = start + total.shape[-1]
        out_ref[:, start:end] = total * (1.0 / tokens)
        start = end


def gather_kernel(*refs):
    *pieces, grad_in_ref, grad_out_ref = refs
    d = lax.axis_index("dp")
    width = grad_out_ref.shape[-1]
    for k, piece in enumerate(pieces):
        at = jnp.bitwise_xor(d, k)
        grad_out_ref[at] = piece[:, :width]
        grad_in_ref[at] = piece[:, width:]


def vmem():
    return pl.BlockSpec(memory_space=pltpu.VMEM)


def shape(*dims, dtype=f32):
    return jax.ShapeDtypeStruct(dims, dtype)


def call(kernel, name, out_shape, args, scalars=0, scratch=(), flops=0, far=0):
    place = [None] * scalars + [pltpu.HBM] * far + [pltpu.VMEM] * (len(args) - scalars - far)
    args = [a if p is None else pltpu.with_memory_space_constraint(a, p) for a, p in zip(args, place)]
    return pl.pallas_call(
        kernel,
        name=name,
        in_specs=[pl.BlockSpec(memory_space=p or pltpu.SMEM) for p in place],
        out_specs=[vmem()] * len(out_shape),
        out_shape=list(out_shape),
        scratch_shapes=[pltpu.VMEM(dims, dtype) for dims, dtype in scratch] + [pltpu.SemaphoreType.DMA((7,))] * (far > 0),
        compiler_params=pltpu.CompilerParams(vmem_limit_bytes=VMEM_BYTES),
        cost_estimate=pl.CostEstimate(flops=flops, bytes_accessed=1 << 16, transcendentals=0),
    )(*args)


def body(rows_size, dp_size, events, cotangent, lengths, event_slot, slot_row, slot_count, w_in, w_out, item_table, accumulator):
    tokens, width = events.shape
    owners, capacity = slot_row.shape[1:]
    chips = rows_size // 2
    piece = width // (rows_size * dp_size)
    cores = [(i, i ^ 1) for i in range(rows_size)]
    over_dp = lambda v, bit: lax.ppermute(v, "dp", [(i, i ^ bit) for i in range(dp_size)])
    over_chips = lambda v, k: lax.ppermute(v, "rows", [(i, (i + 2 * k) % rows_size) for i in range(rows_size)])
    after = lambda value, *others: lax.optimization_barrier((value, *others))[0]
    strip = chips * piece

    def split_first(keep, recv):
        cols = keep.shape[1]
        views = [v.reshape(2, 2, strip, cols) for v in (keep, recv)]
        return call(split_first_kernel, "split_first", [local(2, strip, cols // 2)] * 4, views)

    def split_second(send_a, keep_a, send_b, keep_b):
        recv_a, recv_b = over_dp(send_a, 1), over_dp(send_b, 2)
        return call(split_second_kernel, "split_second", [local(strip, keep_a.shape[-1])] * 4, (keep_a, recv_a, keep_b, recv_b))

    def by_chip(send_a, keep_a, send_b, keep_b):
        cols = keep_a.shape[-1]
        recv_a, recv_b = over_dp(send_a, 2), over_dp(send_b, 1)
        views = [v.reshape(chips, piece, cols) for v in (keep_a, recv_a, keep_b, recv_b)]
        return call(chips_kernel, "by_chip", [local(piece, 2 * cols)] * chips, views)

    def meet(blocks):
        return [blocks[0]] + [over_chips(blocks[k], k) for k in range(1, chips)]

    local = lambda *dims, dtype=f32: pltpu.VMEM(dims, dtype)
    sides = lambda cols: [local(width // 2, cols)] * 2
    keep1, send1, hid, dsilu, gatt, gpre_uv, normed_t, events, cotangent, w_in = call(
        functools.partial(forward_kernel, rows_size, dp_size), "forward_part",
        sides(3 * width) + [
            local(tokens, 3 * width, dtype=bf16),
            local(tokens, 2 * width, dtype=bf16),
            local(tokens, width, dtype=bf16),
            local(tokens, 2 * width, dtype=bf16),
            local(width, tokens, dtype=bf16),
            local(tokens, width, dtype=bf16),
            local(tokens, width, dtype=bf16),
            local(*w_in.shape, dtype=bf16),
        ],
        (lengths, events, cotangent, w_in, w_out), 1,
        [((tokens, width), bf16), ((tokens, width), bf16), ((tokens, width), f32), ((tokens, width), f32),
         ((tokens, width), bf16), ((tokens, width), bf16), ((tokens, width), f32), ((HEADS, tokens, tokens), bf16),
         (w_out.shape, bf16)],
        flops=100_000_000_000, far=4)
    recv1 = lax.ppermute(send1, "rows", cores)
    keep2, send2, gpre_qk = call(
        attention_kernel, "attention_part", sides(2 * width) + [local(tokens, 2 * width, dtype=bf16)],
        (lengths, hid, dsilu, gatt, normed_t), 1, flops=100_000_000_000)
    recv2 = lax.ppermute(send2, "rows", cores)
    pay_rows = capacity * (width // LANES) + ID_ROWS
    first = list(split_first(keep1, after(recv1, keep2)))
    gpre_uv = after(gpre_uv, *first)
    (send,) = call(
        events_kernel, "events_part", [local(owners, pay_rows, LANES)],
        (lengths, events, cotangent, w_in, event_slot, slot_row[0].T, gpre_uv, gpre_qk), 1,
        [((tokens, width), bf16), ((tokens, width), bf16), ((owners * capacity, width), f32)], flops=100_000_000_000)
    recv = lax.all_to_all(send, ("dp", "rows"), split_axis=0, concat_axis=0, tiled=True)
    first[1] = after(first[1], send)
    first = list(split_second(*first))
    second = list(split_first(after(keep2, *first), recv2))
    first[1] = after(first[1], *second)
    first = by_chip(*first)
    second[1] = after(second[1], *first)
    second = list(split_second(*second))
    second = by_chip(*second)
    (total,) = call(functools.partial(total_kernel, tokens), "total", [local(piece, 5 * width)], meet(first) + meet(second))
    pieces = [total] + [over_dp(total, k) for k in range(1, dp_size)]
    grad_in, grad_out = call(
        gather_kernel, "gather", [shape(dp_size, piece, 4 * width), shape(dp_size, piece, width)], pieces)
    slots = owners * capacity
    table_new, accum_new = call(
        table_kernel, "table_part", [shape(*item_table.shape), shape(*accumulator.shape)],
        (recv, item_table, accumulator), 0,
        [((slots, width), f32), ((slots, width), bf16), ((slots, width), bf16)])
    return grad_in.reshape(-1, 4 * width), grad_out.reshape(-1, width), table_new, accum_new


def solution(mesh):
    whole = P(("dp", "rows"))
    in_specs = (whole,) * 6 + (P(), P(), whole, whole)
    out_specs = (P("rows"), P("rows"), whole, whole)
    run = functools.partial(body, mesh.shape["rows"], mesh.shape["dp"])
    return jax.shard_map(run, mesh=mesh, in_specs=in_specs, out_specs=out_specs, check_vma=False)
```

```python
import functools

import jax
import jax.numpy as jnp
from jax import lax
from jax.experimental import pallas as pl
from jax.experimental.pallas import tpu as pltpu
from jax.sharding import PartitionSpec as P

HEADS = 4

norm_eps = 1e-05
adagrad_eps = 1e-10
learning_rate = 0.1

f32, bf16 = jnp.float32, jnp.bfloat16
VMEM_BYTES = 16 * 1024 * 1024
STEP = 256
LANES = 128
ID_ROWS = 8


def dot_nn(a, b):
    return lax.dot_general(a, b, (((1,), (0,)), ((), ())), preferred_element_type=f32)


def dot_nt(a, b):
    return lax.dot_general(a, b, (((1,), (1,)), ((), ())), preferred_element_type=f32)


def dot_tn(a, b):
    return lax.dot_general(a, b, (((0,), (0,)), ((), ())), preferred_element_type=f32)


def standardize(x):
    centered = x - jnp.mean(x, axis=-1, keepdims=True)
    inv = lax.rsqrt(jnp.mean(centered * centered, axis=-1, keepdims=True) + norm_eps)
    return centered * inv, inv


def masked_rows(cot, start, length):
    row = start + lax.broadcasted_iota(jnp.int32, cot.shape, 0)
    return jnp.where(row < length, cot.astype(f32), 0.0)


def owner_order(width, rows, dp):
    chips = rows // 2
    piece = width // (rows * dp)
    at = lax.broadcasted_iota(jnp.int32, (width, 1), 0)
    side, rest = at // (width // 2), at % (width // 2)
    part, rest = rest // (chips * piece), rest % (chips * piece)
    chip, row = rest // piece, rest % piece
    core = lax.rem(lax.axis_index("rows"), 2)
    core = jnp.where(side == 0, core, 1 - core)
    wanted = ((chip * 2 + core) * dp + part) * piece + row
    return jnp.where(lax.broadcasted_iota(jnp.int32, (width, width), 1) == wanted, 1.0, 0.0).astype(bf16)


def forward_kernel(rows_size, dp_size, len_ref, ev_hbm, cot_hbm, win_hbm, wout_hbm,
                   keep_ref, send_ref, hid_ref, dsilu_ref, gatt_ref, gpre_ref, normed_t_ref,
                   ev_ref, cot_ref, win_ref, normed_ref, user_ref, duser_ref, att_ref, mixed_ref, masked_ref, dval_ref, weights_ref,
                   wout_ref, arrived):
    tokens, width = ev_ref.shape
    copies = [pltpu.make_async_copy(ev_hbm, ev_ref, arrived.at[0])]
    for c in range(4):
        cols = pl.ds(c * width, width)
        copies.append(pltpu.make_async_copy(win_hbm.at[:, cols], win_ref.at[:, cols], arrived.at[1 + c]))
    copies.append(pltpu.make_async_copy(cot_hbm, cot_ref, arrived.at[5]))
    copies.append(pltpu.make_async_copy(wout_hbm, wout_ref, arrived.at[6]))
    for copy in copies:
        copy.start()
    hd = width // HEADS
    length = len_ref[0]
    inv_len = 1.0 / length.astype(f32)
    scale = hd ** -0.5
    steps = tokens // STEP

    copies[0].wait()
    for i in range(steps):
        rows = pl.ds(i * STEP, STEP)
        xhat, _ = standardize(ev_ref[rows, :].astype(f32))
        normed_ref[rows, :] = xhat.astype(bf16)

    def project(i, c):
        rows = pl.ds(i * STEP, STEP)
        pre = dot_nn(normed_ref[rows, :], win_ref[:, c * width:(c + 1) * width])
        sig = 0.5 + 0.5 * jnp.tanh(0.5 * pre)
        hid = pre * sig
        dsilu = sig * (1.0 + (pre - hid))
        if c == 0:
            user_ref[rows, :] = hid.astype(bf16)
            duser_ref[rows, :] = dsilu
        else:
            cols = slice((c - 1) * width, c * width)
            hid_ref[rows, cols] = hid.astype(bf16)
            if c == 1:
                dval_ref[rows, :] = dsilu
            else:
                dsilu_ref[rows, (c - 2) * width:(c - 1) * width] = dsilu.astype(bf16)

    for c in range(4):
        copies[1 + c].wait()
        for i in range(steps):
            project(i, c)

    tri = lax.broadcasted_iota(jnp.int32, (STEP, STEP), 0) >= lax.broadcasted_iota(jnp.int32, (STEP, STEP), 1)
    for h in range(HEADS):
        v_cols = slice(h * hd, (h + 1) * hd)
        q_cols = slice(width + h * hd, width + (h + 1) * hd)
        k_cols = slice(2 * width + h * hd, 2 * width + (h + 1) * hd)
        for i in range(steps):
            rows = pl.ds(i * STEP, STEP)
            query = hid_ref[rows, q_cols]
            total = None
            for j in range(i + 1):
                keys = pl.ds(j * STEP, STEP)
                half = dot_nt(query, hid_ref[keys, k_cols]) * (0.5 * scale)
                weights = (half + half * jnp.tanh(half)) * inv_len
                if i == j:
                    weights = jnp.where(tri, weights, 0.0)
                weights = weights.astype(bf16)
                weights_ref[h, rows, keys] = weights
                part = dot_nn(weights, hid_ref[keys, v_cols])
                total = part if total is None else total + part
            att_ref[rows, v_cols] = total

    copies[5].wait()
    copies[6].wait()
    for i in range(steps):
        rows = pl.ds(i * STEP, STEP)
        masked_ref[rows, :] = masked_rows(cot_ref[rows, :], i * STEP, length).astype(bf16)
        ahat, inv = standardize(att_ref[rows, :])
        user = user_ref[rows, :].astype(f32)
        mixed_ref[rows, :] = (ahat * user).astype(bf16)
        grad_mixed = dot_nt(masked_ref[rows, :], wout_ref[...])
        gpre_ref[rows, :width] = (grad_mixed * ahat * duser_ref[rows, :]).astype(bf16)
        e = grad_mixed * user
        gatt_ref[rows, :] = (inv * (e - jnp.mean(e, axis=-1, keepdims=True)
                                    - ahat * jnp.mean(e * ahat, axis=-1, keepdims=True))).astype(bf16)

    for h in range(HEADS):
        v_cols = slice(h * hd, (h + 1) * hd)
        for j in range(steps):
            keys, rest = pl.ds(j * STEP, STEP), pl.ds(j * STEP, tokens - j * STEP)
            grad_v = dot_tn(weights_ref[h, rest, keys], gatt_ref[rest, v_cols])
            gpre_ref[keys, width + h * hd:width + (h + 1) * hd] = (grad_v * dval_ref[keys, v_cols]).astype(bf16)

    order = owner_order(width, rows_size, dp_size)
    normed_t_ref[...] = dot_nt(order, normed_ref[...]).astype(bf16)
    mixed_t = dot_nt(order, mixed_ref[...]).astype(bf16)
    half = width // 2
    for ref, start in ((send_ref, half), (keep_ref, 0)):
        ref[:, :width] = dot_nn(mixed_t[start:start + half], masked_ref[...])
        ref[:, width:] = dot_nn(normed_t_ref[start:start + half, :], gpre_ref[...])


def attention_kernel(len_ref, hid_ref, dsilu_ref, gatt_ref, normed_t_ref, keep_ref, send_ref, gpre_ref):
    tokens, width = gatt_ref.shape
    hd = width // HEADS
    inv_len = 1.0 / len_ref[0].astype(f32)
    scale = hd ** -0.5
    steps = tokens // STEP

    tri = lax.broadcasted_iota(jnp.int32, (STEP, STEP), 0) <= lax.broadcasted_iota(jnp.int32, (STEP, STEP), 1)
    for h in range(HEADS):
        v_cols = slice(h * hd, (h + 1) * hd)
        q_cols = slice(width + h * hd, width + (h + 1) * hd)
        k_cols = slice(2 * width + h * hd, 2 * width + (h + 1) * hd)
        grad_q = [None] * steps
        for j in range(steps):
            keys = pl.ds(j * STEP, STEP)
            key, value = hid_ref[keys, k_cols], hid_ref[keys, v_cols]
            grad_k = None
            for i in range(j, steps):
                rows = pl.ds(i * STEP, STEP)
                query, gatt = hid_ref[rows, q_cols], gatt_ref[rows, v_cols]
                half = dot_nt(key, query) * (0.5 * scale)
                sig2 = 1.0 + jnp.tanh(half)
                silu = half * sig2
                dsilu = sig2 * ((1.0 + half) + (half - silu))
                gscore = dot_nt(value, gatt) * dsilu * (0.5 * inv_len * scale)
                if i == j:
                    gscore = jnp.where(tri, gscore, 0.0)
                gscore = gscore.astype(bf16)
                pk, pq = dot_nn(gscore, query), dot_tn(gscore, key)
                grad_k = pk if grad_k is None else grad_k + pk
                grad_q[i] = pq if grad_q[i] is None else grad_q[i] + pq
            gpre_ref[keys, q_cols] = (grad_k * dsilu_ref[keys, q_cols].astype(f32)).astype(bf16)
        for i in range(steps):
            rows = pl.ds(i * STEP, STEP)
            gpre_ref[rows, v_cols] = (grad_q[i] * dsilu_ref[rows, v_cols].astype(f32)).astype(bf16)

    half = width // 2
    for ref, start in ((send_ref, half), (keep_ref, 0)):
        ref[...] = dot_nn(normed_t_ref[start:start + half, :], gpre_ref[...])


def events_kernel(len_ref, ev_ref, cot_ref, win_ref, slot_ref, slot_row_ref, gpre_uv_ref, gpre_qk_ref,
                  send_ref, hi_ref, lo_ref, rows_ref):
    tokens, width = ev_ref.shape
    capacity, owners = slot_row_ref.shape
    length = len_ref[0]
    for i in range(tokens // STEP):
        rows = pl.ds(i * STEP, STEP)
        xhat, inv = standardize(ev_ref[rows, :].astype(f32))
        grad_normed = dot_nt(gpre_uv_ref[rows, :], win_ref[:, :2 * width]) + dot_nt(gpre_qk_ref[rows, :], win_ref[:, 2 * width:])
        grad = masked_rows(cot_ref[rows, :], i * STEP, length) + inv * (
            grad_normed - jnp.mean(grad_normed, axis=-1, keepdims=True)
            - xhat * jnp.mean(grad_normed * xhat, axis=-1, keepdims=True))
        high = grad.astype(bf16)
        hi_ref[rows, :] = high
        lo_ref[rows, :] = (grad - high.astype(f32)).astype(bf16)

    rows_ref[...] = one_hot_rows(slot_ref[...], rows_ref.shape[0], hi_ref, lo_ref)
    me = lax.axis_index(("dp", "rows"))
    lane = lax.broadcasted_iota(jnp.int32, (capacity, LANES), 1)
    place = lax.broadcasted_iota(jnp.int32, (capacity, LANES), 0) + lax.rem(me, LANES // capacity) * capacity
    spread = jnp.where(lane == place, 1.0, 0.0).astype(bf16)
    ids = slot_row_ref[...]
    ids = 16.0 * dot_tn((ids // 16).astype(bf16), spread) + dot_tn((ids % 16).astype(bf16), spread)
    tiles = width // LANES
    for o in range(owners):
        for t in range(tiles):
            send_ref[o, t * capacity:(t + 1) * capacity, :] = rows_ref[o * capacity:(o + 1) * capacity, t * LANES:(t + 1) * LANES]
        send_ref[o, tiles * capacity:, :] = jnp.broadcast_to(ids[o:o + 1, :], (ID_ROWS, LANES))


def one_hot_rows(ids, rows, hi_ref, lo_ref):
    named = lax.broadcasted_iota(jnp.int32, (rows, ids.shape[1]), 0) == ids
    onehot = jnp.where(named, 1.0, 0.0).astype(bf16)
    return dot_nn(onehot, hi_ref[...]) + dot_nn(onehot, lo_ref[...])


def table_kernel(recv_ref, table_ref, accum_ref, table_new_ref, accum_new_ref, rows_ref, hi_ref, lo_ref):
    owners = recv_ref.shape[0]
    rows, width = table_ref.shape
    tiles = width // LANES
    capacity = (recv_ref.shape[1] - ID_ROWS) // tiles
    for o in range(owners):
        for t in range(tiles):
            rows_ref[o * capacity:(o + 1) * capacity, t * LANES:(t + 1) * LANES] = recv_ref[o, t * capacity:(t + 1) * capacity, :]
    group = LANES // capacity
    ids = [sum(recv_ref[o, tiles * capacity:, :] for o in range(g, g + group)) for g in range(0, owners, group)]
    ids = jnp.concatenate(ids, axis=1)[:1, :].astype(jnp.int32)
    high = rows_ref[...].astype(bf16)
    hi_ref[...] = high
    lo_ref[...] = (rows_ref[...] - high.astype(f32)).astype(bf16)
    grad = one_hot_rows(ids, rows, hi_ref, lo_ref)
    accum = jnp.transpose(jnp.broadcast_to(accum_ref[...].reshape(1, rows), (8, rows)))[:, :1]
    accum_new = accum + jnp.mean(grad * grad, axis=-1, keepdims=True)
    accum_new_ref[...] = jnp.transpose(jnp.broadcast_to(accum_new, (rows, LANES)))[:1, :].reshape(rows)
    table_new_ref[...] = table_ref[...] - learning_rate * grad / (jnp.sqrt(accum_new) + adagrad_eps)


def split_first_kernel(keep_ref, recv_ref, send_a_ref, keep_a_ref, send_b_ref, keep_b_ref):
    d = lax.axis_index("dp")
    x, y = lax.rem(d, 2), d // 2
    half = keep_ref.shape[-1] // 2
    lo, hi = slice(0, half), slice(half, 2 * half)
    for s in range(2):
        send_a_ref[s] = keep_ref[s, 1 - x, :, lo] + recv_ref[s, 1 - x, :, lo]
        send_b_ref[s] = keep_ref[1 - y, s, :, hi] + recv_ref[1 - y, s, :, hi]
        keep_a_ref[s] = keep_ref[s, x, :, lo] + recv_ref[s, x, :, lo]
        keep_b_ref[s] = keep_ref[y, s, :, hi] + recv_ref[y, s, :, hi]


def split_second_kernel(keep_a_ref, recv_a_ref, keep_b_ref, recv_b_ref, send_a_ref, next_a_ref, send_b_ref, next_b_ref):
    d = lax.axis_index("dp")
    x, y = lax.rem(d, 2), d // 2
    send_a_ref[...] = keep_a_ref[1 - y] + recv_a_ref[1 - y]
    send_b_ref[...] = keep_b_ref[1 - x] + recv_b_ref[1 - x]
    next_a_ref[...] = keep_a_ref[y] + recv_a_ref[y]
    next_b_ref[...] = keep_b_ref[x] + recv_b_ref[x]


def chips_kernel(keep_a_ref, recv_a_ref, keep_b_ref, recv_b_ref, *out_refs):
    chips = len(out_refs)
    chip = lax.axis_index("rows") // 2
    half = keep_a_ref.shape[-1]
    for k, out_ref in enumerate(out_refs):
        at = lax.rem(chip + k, chips)
        out_ref[:, :half] = keep_a_ref[at] + recv_a_ref[at]
        out_ref[:, half:] = keep_b_ref[at] + recv_b_ref[at]


def total_kernel(tokens, *refs):
    *pieces, out_ref = refs
    half = len(pieces) // 2
    start = 0
    for group in (pieces[:half], pieces[half:]):
        total = group[0][...]
        for ref in group[1:]:
            total = total + ref[...]
        end = start + total.shape[-1]
        out_ref[:, start:end] = total * (1.0 / tokens)
        start = end


def gather_kernel(*refs):
    *pieces, grad_in_ref, grad_out_ref = refs
    d = lax.axis_index("dp")
    width = grad_out_ref.shape[-1]
    for k, piece in enumerate(pieces):
        at = jnp.bitwise_xor(d, k)
        grad_out_ref[at] = piece[:, :width]
        grad_in_ref[at] = piece[:, width:]


def vmem():
    return pl.BlockSpec(memory_space=pltpu.VMEM)


def shape(*dims, dtype=f32):
    return jax.ShapeDtypeStruct(dims, dtype)


def call(kernel, name, out_shape, args, scalars=0, scratch=(), far=0):
    place = [None] * scalars + [pltpu.HBM] * far + [pltpu.VMEM] * (len(args) - scalars - far)
    args = [a if p is None else pltpu.with_memory_space_constraint(a, p) for a, p in zip(args, place)]
    return pl.pallas_call(
        kernel,
        name=name,
        in_specs=[pl.BlockSpec(memory_space=p or pltpu.SMEM) for p in place],
        out_specs=[vmem()] * len(out_shape),
        out_shape=list(out_shape),
        scratch_shapes=[pltpu.VMEM(dims, dtype) for dims, dtype in scratch] + [pltpu.SemaphoreType.DMA((7,))] * (far > 0),
        compiler_params=pltpu.CompilerParams(vmem_limit_bytes=VMEM_BYTES),
        cost_estimate=pl.CostEstimate(flops=100_000_000_000, bytes_accessed=1 << 16, transcendentals=0),
    )(*args)


def body(rows_size, dp_size, events, cotangent, lengths, event_slot, slot_row, slot_count, w_in, w_out, item_table, accumulator):
    tokens, width = events.shape
    owners, capacity = slot_row.shape[1:]
    chips = rows_size // 2
    piece = width // (rows_size * dp_size)
    cores = [(i, i ^ 1) for i in range(rows_size)]
    over_dp = lambda v, bit: lax.ppermute(v, "dp", [(i, i ^ bit) for i in range(dp_size)])
    over_chips = lambda v, k: lax.ppermute(v, "rows", [(i, (i + 2 * k) % rows_size) for i in range(rows_size)])
    after = lambda value, *others: lax.optimization_barrier((value, *others))[0]
    strip = chips * piece

    def split_first(keep, recv):
        cols = keep.shape[1]
        views = [v.reshape(2, 2, strip, cols) for v in (keep, recv)]
        return call(split_first_kernel, "split_first", [local(2, strip, cols // 2)] * 4, views)

    def split_second(send_a, keep_a, send_b, keep_b):
        recv_a, recv_b = over_dp(send_a, 1), over_dp(send_b, 2)
        return call(split_second_kernel, "split_second", [local(strip, keep_a.shape[-1])] * 4, (keep_a, recv_a, keep_b, recv_b))

    def by_chip(send_a, keep_a, send_b, keep_b):
        cols = keep_a.shape[-1]
        recv_a, recv_b = over_dp(send_a, 2), over_dp(send_b, 1)
        views = [v.reshape(chips, piece, cols) for v in (keep_a, recv_a, keep_b, recv_b)]
        return call(chips_kernel, "by_chip", [local(piece, 2 * cols)] * chips, views)

    def meet(blocks):
        return [blocks[0]] + [over_chips(blocks[k], k) for k in range(1, chips)]

    local = lambda *dims, dtype=f32: pltpu.VMEM(dims, dtype)
    sides = lambda cols: [local(width // 2, cols)] * 2
    keep1, send1, hid, dsilu, gatt, gpre_uv, normed_t, events, cotangent, w_in = call(
        functools.partial(forward_kernel, rows_size, dp_size), "forward_part",
        sides(3 * width) + [
            local(tokens, 3 * width, dtype=bf16),
            local(tokens, 2 * width, dtype=bf16),
            local(tokens, width, dtype=bf16),
            local(tokens, 2 * width, dtype=bf16),
            local(width, tokens, dtype=bf16),
            local(tokens, width, dtype=bf16),
            local(tokens, width, dtype=bf16),
            local(*w_in.shape, dtype=bf16),
        ],
        (lengths, events, cotangent, w_in, w_out), 1,
        [((tokens, width), bf16), ((tokens, width), bf16), ((tokens, width), f32), ((tokens, width), f32),
         ((tokens, width), bf16), ((tokens, width), bf16), ((tokens, width), f32), ((HEADS, tokens, tokens), bf16),
         (w_out.shape, bf16)], far=4)
    recv1 = lax.ppermute(send1, "rows", cores)
    keep2, send2, gpre_qk = call(
        attention_kernel, "attention_part", sides(2 * width) + [local(tokens, 2 * width, dtype=bf16)],
        (lengths, hid, dsilu, gatt, normed_t), 1)
    recv2 = lax.ppermute(send2, "rows", cores)
    pay_rows = capacity * (width // LANES) + ID_ROWS
    first = list(split_first(keep1, after(recv1, keep2)))
    gpre_uv = after(gpre_uv, *first)
    (send,) = call(
        events_kernel, "events_part", [local(owners, pay_rows, LANES)],
        (lengths, events, cotangent, w_in, event_slot, slot_row[0].T, gpre_uv, gpre_qk), 1,
        [((tokens, width), bf16), ((tokens, width), bf16), ((owners * capacity, width), f32)])
    recv = lax.all_to_all(send, ("dp", "rows"), split_axis=0, concat_axis=0, tiled=True)
    first[1] = after(first[1], send)
    first = list(split_second(*first))
    second = list(split_first(after(keep2, *first), recv2))
    first[1] = after(first[1], *second)
    first = by_chip(*first)
    second[1] = after(second[1], *first)
    second = list(split_second(*second))
    second = by_chip(*second)
    (total,) = call(functools.partial(total_kernel, tokens), "total", [local(piece, 5 * width)], meet(first) + meet(second))
    pieces = [total] + [over_dp(total, k) for k in range(1, dp_size)]
    slots = owners * capacity
    table_new, accum_new = call(
        table_kernel, "table_part", [shape(*item_table.shape), shape(*accumulator.shape)],
        (recv, item_table, accumulator), 0,
        [((slots, width), f32), ((slots, width), bf16), ((slots, width), bf16)])
    pieces[1] = after(pieces[1], accum_new)
    grad_in, grad_out = call(
        gather_kernel, "gather", [shape(dp_size, piece, 4 * width), shape(dp_size, piece, width)], pieces)
    return grad_in.reshape(-1, 4 * width), grad_out.reshape(-1, width), table_new, accum_new


def solution(mesh):
    whole = P(("dp", "rows"))
    in_specs = (whole,) * 6 + (P(), P(), whole, whole)
    out_specs = (P("rows"), P("rows"), whole, whole)
    run = functools.partial(body, mesh.shape["rows"], mesh.shape["dp"])
    return jax.shard_map(run, mesh=mesh, in_specs=in_specs, out_specs=out_specs, check_vma=False)
```

```python
import functools

import jax
import jax.numpy as jnp
from jax import lax
from jax.experimental import pallas as pl
from jax.experimental.pallas import tpu as pltpu
from jax.sharding import PartitionSpec as P

HEADS = 4

norm_eps = 1e-05
adagrad_eps = 1e-10
learning_rate = 0.1

f32, bf16 = jnp.float32, jnp.bfloat16
VMEM_BYTES = 16 * 1024 * 1024
STEP = 256
LANES = 128
ID_ROWS = 8


def dot_nn(a, b):
    return lax.dot_general(a, b, (((1,), (0,)), ((), ())), preferred_element_type=f32)


def dot_nt(a, b):
    return lax.dot_general(a, b, (((1,), (1,)), ((), ())), preferred_element_type=f32)


def dot_tn(a, b):
    return lax.dot_general(a, b, (((0,), (0,)), ((), ())), preferred_element_type=f32)


def standardize(x):
    centered = x - jnp.mean(x, axis=-1, keepdims=True)
    inv = lax.rsqrt(jnp.mean(centered * centered, axis=-1, keepdims=True) + norm_eps)
    return centered * inv, inv


def masked_rows(cot, start, length):
    row = start + lax.broadcasted_iota(jnp.int32, cot.shape, 0)
    return jnp.where(row < length, cot.astype(f32), 0.0)


def owner_order(width, rows, dp):
    chips = rows // 2
    piece = width // (rows * dp)
    at = lax.broadcasted_iota(jnp.int32, (width, 1), 0)
    side, rest = at // (width // 2), at % (width // 2)
    part, rest = rest // (chips * piece), rest % (chips * piece)
    chip, row = rest // piece, rest % piece
    core = lax.rem(lax.axis_index("rows"), 2)
    core = jnp.where(side == 0, core, 1 - core)
    wanted = ((chip * 2 + core) * dp + part) * piece + row
    return jnp.where(lax.broadcasted_iota(jnp.int32, (width, width), 1) == wanted, 1.0, 0.0).astype(bf16)


def forward_kernel(rows_size, dp_size, len_ref, ev_hbm, cot_hbm, win_hbm, wout_hbm,
                   keep_ref, send_ref, hid_ref, dsilu_ref, gatt_ref, gpre_ref, normed_t_ref,
                   ev_ref, cot_ref, win_ref, normed_ref, user_ref, duser_ref, att_ref, mixed_ref, masked_ref, dval_ref, weights_ref,
                   wout_ref, arrived):
    tokens, width = ev_ref.shape
    copies = [pltpu.make_async_copy(ev_hbm, ev_ref, arrived.at[0])]
    for c in range(4):
        cols = pl.ds(c * width, width)
        copies.append(pltpu.make_async_copy(win_hbm.at[:, cols], win_ref.at[:, cols], arrived.at[1 + c]))
    copies.append(pltpu.make_async_copy(cot_hbm, cot_ref, arrived.at[5]))
    copies.append(pltpu.make_async_copy(wout_hbm, wout_ref, arrived.at[6]))
    for copy in copies:
        copy.start()
    hd = width // HEADS
    length = len_ref[0]
    inv_len = 1.0 / length.astype(f32)
    scale = hd ** -0.5
    steps = tokens // STEP

    copies[0].wait()
    for i in range(steps):
        rows = pl.ds(i * STEP, STEP)
        xhat, _ = standardize(ev_ref[rows, :].astype(f32))
        normed_ref[rows, :] = xhat.astype(bf16)

    def project(i, c):
        rows = pl.ds(i * STEP, STEP)
        pre = dot_nn(normed_ref[rows, :], win_ref[:, c * width:(c + 1) * width])
        sig = 0.5 + 0.5 * jnp.tanh(0.5 * pre)
        hid = pre * sig
        dsilu = sig * (1.0 + (pre - hid))
        if c == 0:
            user_ref[rows, :] = hid.astype(bf16)
            duser_ref[rows, :] = dsilu
        else:
            cols = slice((c - 1) * width, c * width)
            hid_ref[rows, cols] = hid.astype(bf16)
            if c == 1:
                dval_ref[rows, :] = dsilu
            else:
                dsilu_ref[rows, (c - 2) * width:(c - 1) * width] = dsilu.astype(bf16)

    for c in range(4):
        copies[1 + c].wait()
        for i in range(steps):
            project(i, c)

    tri = lax.broadcasted_iota(jnp.int32, (STEP, STEP), 0) >= lax.broadcasted_iota(jnp.int32, (STEP, STEP), 1)
    for h in range(HEADS):
        v_cols = slice(h * hd, (h + 1) * hd)
        q_cols = slice(width + h * hd, width + (h + 1) * hd)
        k_cols = slice(2 * width + h * hd, 2 * width + (h + 1) * hd)
        for i in range(steps):
            rows = pl.ds(i * STEP, STEP)
            query = hid_ref[rows, q_cols]
            total = None
            for j in range(i + 1):
                keys = pl.ds(j * STEP, STEP)
                half = dot_nt(query, hid_ref[keys, k_cols]) * (0.5 * scale)
                weights = (half + half * jnp.tanh(half)) * inv_len
                if i == j:
                    weights = jnp.where(tri, weights, 0.0)
                weights = weights.astype(bf16)
                weights_ref[h, rows, keys] = weights
                part = dot_nn(weights, hid_ref[keys, v_cols])
                total = part if total is None else total + part
            att_ref[rows, v_cols] = total

    copies[5].wait()
    copies[6].wait()
    for i in range(steps):
        rows = pl.ds(i * STEP, STEP)
        masked_ref[rows, :] = masked_rows(cot_ref[rows, :], i * STEP, length).astype(bf16)
        ahat, inv = standardize(att_ref[rows, :])
        user = user_ref[rows, :].astype(f32)
        mixed_ref[rows, :] = (ahat * user).astype(bf16)
        grad_mixed = dot_nt(masked_ref[rows, :], wout_ref[...])
        gpre_ref[rows, :width] = (grad_mixed * ahat * duser_ref[rows, :]).astype(bf16)
        e = grad_mixed * user
        gatt_ref[rows, :] = (inv * (e - jnp.mean(e, axis=-1, keepdims=True)
                                    - ahat * jnp.mean(e * ahat, axis=-1, keepdims=True))).astype(bf16)

    for h in range(HEADS):
        v_cols = slice(h * hd, (h + 1) * hd)
        for j in range(steps):
            keys, rest = pl.ds(j * STEP, STEP), pl.ds(j * STEP, tokens - j * STEP)
            grad_v = dot_tn(weights_ref[h, rest, keys], gatt_ref[rest, v_cols])
            gpre_ref[keys, width + h * hd:width + (h + 1) * hd] = (grad_v * dval_ref[keys, v_cols]).astype(bf16)

    order = owner_order(width, rows_size, dp_size)
    normed_t_ref[...] = dot_nt(order, normed_ref[...]).astype(bf16)
    mixed_t = dot_nt(order, mixed_ref[...]).astype(bf16)
    half = width // 2
    for ref, start in ((send_ref, half), (keep_ref, 0)):
        ref[:, :width] = dot_nn(mixed_t[start:start + half], masked_ref[...])
        ref[:, width:] = dot_nn(normed_t_ref[start:start + half, :], gpre_ref[...])


def attention_kernel(len_ref, hid_ref, dsilu_ref, gatt_ref, normed_t_ref, keep_ref, send_ref, gpre_ref):
    tokens, width = gatt_ref.shape
    hd = width // HEADS
    inv_len = 1.0 / len_ref[0].astype(f32)
    scale = hd ** -0.5
    steps = tokens // STEP

    tri = lax.broadcasted_iota(jnp.int32, (STEP, STEP), 0) <= lax.broadcasted_iota(jnp.int32, (STEP, STEP), 1)
    for h in range(HEADS):
        v_cols = slice(h * hd, (h + 1) * hd)
        q_cols = slice(width + h * hd, width + (h + 1) * hd)
        k_cols = slice(2 * width + h * hd, 2 * width + (h + 1) * hd)
        grad_q = [None] * steps
        for j in range(steps):
            keys = pl.ds(j * STEP, STEP)
            key, value = hid_ref[keys, k_cols], hid_ref[keys, v_cols]
            grad_k = None
            for i in range(j, steps):
                rows = pl.ds(i * STEP, STEP)
                query, gatt = hid_ref[rows, q_cols], gatt_ref[rows, v_cols]
                half = dot_nt(key, query) * (0.5 * scale)
                sig2 = 1.0 + jnp.tanh(half)
                silu = half * sig2
                dsilu = sig2 * ((1.0 + half) + (half - silu))
                gscore = dot_nt(value, gatt) * dsilu * (0.5 * inv_len * scale)
                if i == j:
                    gscore = jnp.where(tri, gscore, 0.0)
                gscore = gscore.astype(bf16)
                pk, pq = dot_nn(gscore, query), dot_tn(gscore, key)
                grad_k = pk if grad_k is None else grad_k + pk
                grad_q[i] = pq if grad_q[i] is None else grad_q[i] + pq
            gpre_ref[keys, q_cols] = (grad_k * dsilu_ref[keys, q_cols].astype(f32)).astype(bf16)
        for i in range(steps):
            rows = pl.ds(i * STEP, STEP)
            gpre_ref[rows, v_cols] = (grad_q[i] * dsilu_ref[rows, v_cols].astype(f32)).astype(bf16)

    half = width // 2
    for ref, start in ((send_ref, half), (keep_ref, 0)):
        ref[...] = dot_nn(normed_t_ref[start:start + half, :], gpre_ref[...])


def events_kernel(len_ref, ev_ref, cot_ref, win_ref, slot_ref, slot_row_ref, gpre_uv_ref, gpre_qk_ref,
                  send_ref, hi_ref, lo_ref, rows_ref):
    tokens, width = ev_ref.shape
    capacity, owners = slot_row_ref.shape
    length = len_ref[0]
    for i in range(tokens // STEP):
        rows = pl.ds(i * STEP, STEP)
        xhat, inv = standardize(ev_ref[rows, :].astype(f32))
        grad_normed = dot_nt(gpre_uv_ref[rows, :], win_ref[:, :2 * width]) + dot_nt(gpre_qk_ref[rows, :], win_ref[:, 2 * width:])
        grad = masked_rows(cot_ref[rows, :], i * STEP, length) + inv * (
            grad_normed - jnp.mean(grad_normed, axis=-1, keepdims=True)
            - xhat * jnp.mean(grad_normed * xhat, axis=-1, keepdims=True))
        high = grad.astype(bf16)
        hi_ref[rows, :] = high
        lo_ref[rows, :] = (grad - high.astype(f32)).astype(bf16)

    rows_ref[...] = one_hot_rows(slot_ref[...], rows_ref.shape[0], hi_ref, lo_ref)
    me = lax.axis_index(("dp", "rows"))
    lane = lax.broadcasted_iota(jnp.int32, (capacity, LANES), 1)
    place = lax.broadcasted_iota(jnp.int32, (capacity, LANES), 0) + lax.rem(me, LANES // capacity) * capacity
    spread = jnp.where(lane == place, 1.0, 0.0).astype(bf16)
    ids = slot_row_ref[...]
    ids = 16.0 * dot_tn((ids // 16).astype(bf16), spread) + dot_tn((ids % 16).astype(bf16), spread)
    tiles = width // LANES
    for o in range(owners):
        for t in range(tiles):
            send_ref[o, t * capacity:(t + 1) * capacity, :] = rows_ref[o * capacity:(o + 1) * capacity, t * LANES:(t + 1) * LANES]
        send_ref[o, tiles * capacity:, :] = jnp.broadcast_to(ids[o:o + 1, :], (ID_ROWS, LANES))


def one_hot_rows(ids, rows, hi_ref, lo_ref):
    named = lax.broadcasted_iota(jnp.int32, (rows, ids.shape[1]), 0) == ids
    onehot = jnp.where(named, 1.0, 0.0).astype(bf16)
    return dot_nn(onehot, hi_ref[...]) + dot_nn(onehot, lo_ref[...])


def table_kernel(recv_ref, table_ref, accum_ref, table_new_ref, accum_new_ref, rows_ref, hi_ref, lo_ref):
    owners = recv_ref.shape[0]
    rows, width = table_ref.shape
    tiles = width // LANES
    capacity = (recv_ref.shape[1] - ID_ROWS) // tiles
    for o in range(owners):
        for t in range(tiles):
            rows_ref[o * capacity:(o + 1) * capacity, t * LANES:(t + 1) * LANES] = recv_ref[o, t * capacity:(t + 1) * capacity, :]
    group = LANES // capacity
    ids = [sum(recv_ref[o, tiles * capacity:, :] for o in range(g, g + group)) for g in range(0, owners, group)]
    ids = jnp.concatenate(ids, axis=1)[:1, :].astype(jnp.int32)
    high = rows_ref[...].astype(bf16)
    hi_ref[...] = high
    lo_ref[...] = (rows_ref[...] - high.astype(f32)).astype(bf16)
    grad = one_hot_rows(ids, rows, hi_ref, lo_ref)
    accum = jnp.transpose(jnp.broadcast_to(accum_ref[...].reshape(1, rows), (8, rows)))[:, :1]
    accum_new = accum + jnp.mean(grad * grad, axis=-1, keepdims=True)
    accum_new_ref[...] = jnp.transpose(jnp.broadcast_to(accum_new, (rows, LANES)))[:1, :].reshape(rows)
    table_new_ref[...] = table_ref[...] - learning_rate * grad / (jnp.sqrt(accum_new) + adagrad_eps)


def split_first_kernel(keep_ref, recv_ref, send_a_ref, keep_a_ref, send_b_ref, keep_b_ref):
    d = lax.axis_index("dp")
    x, y = lax.rem(d, 2), d // 2
    half = keep_ref.shape[-1] // 2
    lo, hi = slice(0, half), slice(half, 2 * half)
    for s in range(2):
        send_a_ref[s] = keep_ref[s, 1 - x, :, lo] + recv_ref[s, 1 - x, :, lo]
        send_b_ref[s] = keep_ref[1 - y, s, :, hi] + recv_ref[1 - y, s, :, hi]
        keep_a_ref[s] = keep_ref[s, x, :, lo] + recv_ref[s, x, :, lo]
        keep_b_ref[s] = keep_ref[y, s, :, hi] + recv_ref[y, s, :, hi]


def split_second_kernel(keep_a_ref, recv_a_ref, keep_b_ref, recv_b_ref, send_a_ref, next_a_ref, send_b_ref, next_b_ref):
    d = lax.axis_index("dp")
    x, y = lax.rem(d, 2), d // 2
    send_a_ref[...] = keep_a_ref[1 - y] + recv_a_ref[1 - y]
    send_b_ref[...] = keep_b_ref[1 - x] + recv_b_ref[1 - x]
    next_a_ref[...] = keep_a_ref[y] + recv_a_ref[y]
    next_b_ref[...] = keep_b_ref[x] + recv_b_ref[x]


def chips_kernel(keep_a_ref, recv_a_ref, keep_b_ref, recv_b_ref, *out_refs):
    chips = len(out_refs)
    chip = lax.axis_index("rows") // 2
    half = keep_a_ref.shape[-1]
    for k, out_ref in enumerate(out_refs):
        at = lax.rem(chip + k, chips)
        out_ref[:, :half] = keep_a_ref[at] + recv_a_ref[at]
        out_ref[:, half:] = keep_b_ref[at] + recv_b_ref[at]


def total_kernel(tokens, *refs):
    *pieces, out_ref = refs
    half = len(pieces) // 2
    start = 0
    for group in (pieces[:half], pieces[half:]):
        total = group[0][...]
        for ref in group[1:]:
            total = total + ref[...]
        end = start + total.shape[-1]
        out_ref[:, start:end] = total * (1.0 / tokens)
        start = end


def gather_kernel(*refs):
    *pieces, grad_in_ref, grad_out_ref = refs
    d = lax.axis_index("dp")
    width = grad_out_ref.shape[-1]
    for k, piece in enumerate(pieces):
        at = jnp.bitwise_xor(d, k)
        grad_out_ref[at] = piece[:, :width]
        grad_in_ref[at] = piece[:, width:]


def vmem():
    return pl.BlockSpec(memory_space=pltpu.VMEM)


def shape(*dims, dtype=f32):
    return jax.ShapeDtypeStruct(dims, dtype)


def call(kernel, name, out_shape, args, scalars=0, scratch=(), far=0, long=False):
    place = [None] * scalars + [pltpu.HBM] * far + [pltpu.VMEM] * (len(args) - scalars - far)
    args = [a if p is None else pltpu.with_memory_space_constraint(a, p) for a, p in zip(args, place)]
    return pl.pallas_call(
        kernel,
        name=name,
        in_specs=[pl.BlockSpec(memory_space=p or pltpu.SMEM) for p in place],
        out_specs=[vmem()] * len(out_shape),
        out_shape=list(out_shape),
        scratch_shapes=[pltpu.VMEM(dims, dtype) for dims, dtype in scratch] + [pltpu.SemaphoreType.DMA((7,))] * (far > 0),
        compiler_params=pltpu.CompilerParams(vmem_limit_bytes=VMEM_BYTES),
        cost_estimate=pl.CostEstimate(flops=100_000_000_000 if long else 1_000_000_000, bytes_accessed=1 << 16, transcendentals=0),
    )(*args)


def body(rows_size, dp_size, events, cotangent, lengths, event_slot, slot_row, slot_count, w_in, w_out, item_table, accumulator):
    tokens, width = events.shape
    owners, capacity = slot_row.shape[1:]
    chips = rows_size // 2
    piece = width // (rows_size * dp_size)
    cores = [(i, i ^ 1) for i in range(rows_size)]
    over_dp = lambda v, bit: lax.ppermute(v, "dp", [(i, i ^ bit) for i in range(dp_size)])
    over_chips = lambda v, k: lax.ppermute(v, "rows", [(i, (i + 2 * k) % rows_size) for i in range(rows_size)])
    after = lambda value, *others: lax.optimization_barrier((value, *others))[0]
    strip = chips * piece

    def split_first(keep, recv):
        cols = keep.shape[1]
        views = [v.reshape(2, 2, strip, cols) for v in (keep, recv)]
        return call(split_first_kernel, "split_first", [local(2, strip, cols // 2)] * 4, views)

    def split_second(send_a, keep_a, send_b, keep_b, long=False):
        recv_a, recv_b = over_dp(send_a, 1), over_dp(send_b, 2)
        return call(split_second_kernel, "split_second", [local(strip, keep_a.shape[-1])] * 4, (keep_a, recv_a, keep_b, recv_b), long=long)

    def by_chip(send_a, keep_a, send_b, keep_b):
        cols = keep_a.shape[-1]
        recv_a, recv_b = over_dp(send_a, 2), over_dp(send_b, 1)
        views = [v.reshape(chips, piece, cols) for v in (keep_a, recv_a, keep_b, recv_b)]
        return call(chips_kernel, "by_chip", [local(piece, 2 * cols)] * chips, views)

    def meet(blocks):
        return [blocks[0]] + [over_chips(blocks[k], k) for k in range(1, chips)]

    local = lambda *dims, dtype=f32: pltpu.VMEM(dims, dtype)
    sides = lambda cols: [local(width // 2, cols)] * 2
    keep1, send1, hid, dsilu, gatt, gpre_uv, normed_t, events, cotangent, w_in = call(
        functools.partial(forward_kernel, rows_size, dp_size), "forward_part",
        sides(3 * width) + [
            local(tokens, 3 * width, dtype=bf16),
            local(tokens, 2 * width, dtype=bf16),
            local(tokens, width, dtype=bf16),
            local(tokens, 2 * width, dtype=bf16),
            local(width, tokens, dtype=bf16),
            local(tokens, width, dtype=bf16),
            local(tokens, width, dtype=bf16),
            local(*w_in.shape, dtype=bf16),
        ],
        (lengths, events, cotangent, w_in, w_out), 1,
        [((tokens, width), bf16), ((tokens, width), bf16), ((tokens, width), f32), ((tokens, width), f32),
         ((tokens, width), bf16), ((tokens, width), bf16), ((tokens, width), f32), ((HEADS, tokens, tokens), bf16),
         (w_out.shape, bf16)], far=4, long=True)
    recv1 = lax.ppermute(send1, "rows", cores)
    keep2, send2, gpre_qk = call(
        attention_kernel, "attention_part", sides(2 * width) + [local(tokens, 2 * width, dtype=bf16)],
        (lengths, hid, dsilu, gatt, normed_t), 1, long=True)
    recv2 = lax.ppermute(send2, "rows", cores)
    pay_rows = capacity * (width // LANES) + ID_ROWS
    first = list(split_first(keep1, after(recv1, keep2)))
    gpre_uv = after(gpre_uv, *first)
    (send,) = call(
        events_kernel, "events_part", [local(owners, pay_rows, LANES)],
        (lengths, events, cotangent, w_in, event_slot, slot_row[0].T, gpre_uv, gpre_qk), 1,
        [((tokens, width), bf16), ((tokens, width), bf16), ((owners * capacity, width), f32)], long=True)
    recv = lax.all_to_all(send, ("dp", "rows"), split_axis=0, concat_axis=0, tiled=True)
    first[1] = after(first[1], send)
    first = list(split_second(*first, long=True))
    second = list(split_first(after(keep2, *first), recv2))
    first[1] = after(first[1], *second)
    first = by_chip(*first)
    second[1] = after(second[1], *first)
    second = list(split_second(*second))
    second = by_chip(*second)
    (total,) = call(functools.partial(total_kernel, tokens), "total", [local(piece, 5 * width)], meet(first) + meet(second))
    pieces = [total] + [over_dp(total, k) for k in range(1, dp_size)]
    slots = owners * capacity
    table_new, accum_new = call(
        table_kernel, "table_part", [shape(*item_table.shape), shape(*accumulator.shape)],
        (recv, item_table, accumulator), 0,
        [((slots, width), f32), ((slots, width), bf16), ((slots, width), bf16)])
    pieces[1] = after(pieces[1], accum_new)
    grad_in, grad_out = call(
        gather_kernel, "gather", [shape(dp_size, piece, 4 * width), shape(dp_size, piece, width)], pieces)
    return grad_in.reshape(-1, 4 * width), grad_out.reshape(-1, width), table_new, accum_new


def solution(mesh):
    whole = P(("dp", "rows"))
    in_specs = (whole,) * 6 + (P(), P(), whole, whole)
    out_specs = (P("rows"), P("rows"), whole, whole)
    run = functools.partial(body, mesh.shape["rows"], mesh.shape["dp"])
    return jax.shard_map(run, mesh=mesh, in_specs=in_specs, out_specs=out_specs, check_vma=False)
```

```python
import functools

import jax
import jax.numpy as jnp
from jax import lax
from jax.experimental import pallas as pl
from jax.experimental.pallas import tpu as pltpu
from jax.sharding import PartitionSpec as P

HEADS = 4

norm_eps = 1e-05
adagrad_eps = 1e-10
learning_rate = 0.1

f32, bf16 = jnp.float32, jnp.bfloat16
MIB = 1024 * 1024
STEP = 256
LANES = 128
ID_ROWS = 8


def dot_nn(a, b):
    return lax.dot_general(a, b, (((1,), (0,)), ((), ())), preferred_element_type=f32)


def dot_nt(a, b):
    return lax.dot_general(a, b, (((1,), (1,)), ((), ())), preferred_element_type=f32)


def dot_tn(a, b):
    return lax.dot_general(a, b, (((0,), (0,)), ((), ())), preferred_element_type=f32)


def standardize(x):
    centered = x - jnp.mean(x, axis=-1, keepdims=True)
    inv = lax.rsqrt(jnp.mean(centered * centered, axis=-1, keepdims=True) + norm_eps)
    return centered * inv, inv


def masked_rows(cot, start, length):
    row = start + lax.broadcasted_iota(jnp.int32, cot.shape, 0)
    return jnp.where(row < length, cot.astype(f32), 0.0)


def owner_order(width, rows, dp):
    chips = rows // 2
    piece = width // (rows * dp)
    at = lax.broadcasted_iota(jnp.int32, (width, 1), 0)
    side, rest = at // (width // 2), at % (width // 2)
    part, rest = rest // (chips * piece), rest % (chips * piece)
    chip, row = rest // piece, rest % piece
    core = lax.rem(lax.axis_index("rows"), 2)
    core = jnp.where(side == 0, core, 1 - core)
    wanted = ((chip * 2 + core) * dp + part) * piece + row
    return jnp.where(lax.broadcasted_iota(jnp.int32, (width, width), 1) == wanted, 1.0, 0.0).astype(bf16)


def forward_kernel(rows_size, dp_size, len_ref, ev_hbm, cot_hbm, win_hbm, wout_hbm,
                   keep_ref, send_ref, hid_ref, dsilu_ref, gatt_ref, gpre_ref, normed_t_ref,
                   ev_ref, cot_ref, win_ref, normed_ref, user_ref, duser_ref, att_ref, mixed_ref, masked_ref, dval_ref, weights_ref,
                   wout_ref, arrived):
    tokens, width = ev_ref.shape
    copies = [pltpu.make_async_copy(ev_hbm, ev_ref, arrived.at[0])]
    for c in range(4):
        cols = pl.ds(c * width, width)
        copies.append(pltpu.make_async_copy(win_hbm.at[:, cols], win_ref.at[:, cols], arrived.at[1 + c]))
    copies.append(pltpu.make_async_copy(cot_hbm, cot_ref, arrived.at[5]))
    copies.append(pltpu.make_async_copy(wout_hbm, wout_ref, arrived.at[6]))
    for copy in copies:
        copy.start()
    hd = width // HEADS
    length = len_ref[0]
    inv_len = 1.0 / length.astype(f32)
    scale = hd ** -0.5
    steps = tokens // STEP

    copies[0].wait()
    for i in range(steps):
        rows = pl.ds(i * STEP, STEP)
        xhat, _ = standardize(ev_ref[rows, :].astype(f32))
        normed_ref[rows, :] = xhat.astype(bf16)

    def project(i, c):
        rows = pl.ds(i * STEP, STEP)
        pre = dot_nn(normed_ref[rows, :], win_ref[:, c * width:(c + 1) * width])
        sig = 0.5 + 0.5 * jnp.tanh(0.5 * pre)
        hid = pre * sig
        dsilu = sig * (1.0 + (pre - hid))
        if c == 0:
            user_ref[rows, :] = hid.astype(bf16)
            duser_ref[rows, :] = dsilu
        else:
            cols = slice((c - 1) * width, c * width)
            hid_ref[rows, cols] = hid.astype(bf16)
            if c == 1:
                dval_ref[rows, :] = dsilu
            else:
                dsilu_ref[rows, (c - 2) * width:(c - 1) * width] = dsilu.astype(bf16)

    for c in range(4):
        copies[1 + c].wait()
        for i in range(steps):
            project(i, c)

    tri = lax.broadcasted_iota(jnp.int32, (STEP, STEP), 0) >= lax.broadcasted_iota(jnp.int32, (STEP, STEP), 1)
    for h in range(HEADS):
        v_cols = slice(h * hd, (h + 1) * hd)
        q_cols = slice(width + h * hd, width + (h + 1) * hd)
        k_cols = slice(2 * width + h * hd, 2 * width + (h + 1) * hd)
        for i in range(steps):
            rows = pl.ds(i * STEP, STEP)
            query = hid_ref[rows, q_cols]
            total = None
            for j in range(i + 1):
                keys = pl.ds(j * STEP, STEP)
                half = dot_nt(query, hid_ref[keys, k_cols]) * (0.5 * scale)
                weights = (half + half * jnp.tanh(half)) * inv_len
                if i == j:
                    weights = jnp.where(tri, weights, 0.0)
                weights = weights.astype(bf16)
                weights_ref[h, rows, keys] = weights
                part = dot_nn(weights, hid_ref[keys, v_cols])
                total = part if total is None else total + part
            att_ref[rows, v_cols] = total

    copies[5].wait()
    copies[6].wait()
    for i in range(steps):
        rows = pl.ds(i * STEP, STEP)
        masked_ref[rows, :] = masked_rows(cot_ref[rows, :], i * STEP, length).astype(bf16)
        ahat, inv = standardize(att_ref[rows, :])
        user = user_ref[rows, :].astype(f32)
        mixed_ref[rows, :] = (ahat * user).astype(bf16)
        grad_mixed = dot_nt(masked_ref[rows, :], wout_ref[...])
        gpre_ref[rows, :width] = (grad_mixed * ahat * duser_ref[rows, :]).astype(bf16)
        e = grad_mixed * user
        gatt_ref[rows, :] = (inv * (e - jnp.mean(e, axis=-1, keepdims=True)
                                    - ahat * jnp.mean(e * ahat, axis=-1, keepdims=True))).astype(bf16)

    for h in range(HEADS):
        v_cols = slice(h * hd, (h + 1) * hd)
        for j in range(steps):
            keys, rest = pl.ds(j * STEP, STEP), pl.ds(j * STEP, tokens - j * STEP)
            grad_v = dot_tn(weights_ref[h, rest, keys], gatt_ref[rest, v_cols])
            gpre_ref[keys, width + h * hd:width + (h + 1) * hd] = (grad_v * dval_ref[keys, v_cols]).astype(bf16)

    order = owner_order(width, rows_size, dp_size)
    normed_t_ref[...] = dot_nt(order, normed_ref[...]).astype(bf16)
    mixed_t = dot_nt(order, mixed_ref[...]).astype(bf16)
    half = width // 2
    for ref, start in ((send_ref, half), (keep_ref, 0)):
        ref[:, :width] = dot_nn(mixed_t[start:start + half], masked_ref[...])
        ref[:, width:] = dot_nn(normed_t_ref[start:start + half, :], gpre_ref[...])


def attention_kernel(len_ref, hid_ref, dsilu_ref, gatt_ref, normed_t_ref, keep_ref, send_ref, gpre_ref):
    tokens, width = gatt_ref.shape
    hd = width // HEADS
    inv_len = 1.0 / len_ref[0].astype(f32)
    scale = hd ** -0.5
    steps = tokens // STEP

    tri = lax.broadcasted_iota(jnp.int32, (STEP, STEP), 0) <= lax.broadcasted_iota(jnp.int32, (STEP, STEP), 1)
    for h in range(HEADS):
        v_cols = slice(h * hd, (h + 1) * hd)
        q_cols = slice(width + h * hd, width + (h + 1) * hd)
        k_cols = slice(2 * width + h * hd, 2 * width + (h + 1) * hd)
        grad_q = [None] * steps
        for j in range(steps):
            keys = pl.ds(j * STEP, STEP)
            key, value = hid_ref[keys, k_cols], hid_ref[keys, v_cols]
            grad_k = None
            for i in range(j, steps):
                rows = pl.ds(i * STEP, STEP)
                query, gatt = hid_ref[rows, q_cols], gatt_ref[rows, v_cols]
                half = dot_nt(key, query) * (0.5 * scale)
                sig2 = 1.0 + jnp.tanh(half)
                silu = half * sig2
                dsilu = sig2 * ((1.0 + half) + (half - silu))
                gscore = dot_nt(value, gatt) * dsilu * (0.5 * inv_len * scale)
                if i == j:
                    gscore = jnp.where(tri, gscore, 0.0)
                gscore = gscore.astype(bf16)
                pk, pq = dot_nn(gscore, query), dot_tn(gscore, key)
                grad_k = pk if grad_k is None else grad_k + pk
                grad_q[i] = pq if grad_q[i] is None else grad_q[i] + pq
            gpre_ref[keys, q_cols] = (grad_k * dsilu_ref[keys, q_cols].astype(f32)).astype(bf16)
        for i in range(steps):
            rows = pl.ds(i * STEP, STEP)
            gpre_ref[rows, v_cols] = (grad_q[i] * dsilu_ref[rows, v_cols].astype(f32)).astype(bf16)

    half = width // 2
    for ref, start in ((send_ref, half), (keep_ref, 0)):
        ref[...] = dot_nn(normed_t_ref[start:start + half, :], gpre_ref[...])


def events_kernel(len_ref, ev_ref, cot_ref, win_ref, slot_ref, slot_row_ref, gpre_uv_ref, gpre_qk_ref,
                  send_ref, hi_ref, lo_ref, rows_ref):
    tokens, width = ev_ref.shape
    capacity, owners = slot_row_ref.shape
    length = len_ref[0]
    for i in range(tokens // STEP):
        rows = pl.ds(i * STEP, STEP)
        xhat, inv = standardize(ev_ref[rows, :].astype(f32))
        grad_normed = dot_nt(gpre_uv_ref[rows, :], win_ref[:, :2 * width]) + dot_nt(gpre_qk_ref[rows, :], win_ref[:, 2 * width:])
        grad = masked_rows(cot_ref[rows, :], i * STEP, length) + inv * (
            grad_normed - jnp.mean(grad_normed, axis=-1, keepdims=True)
            - xhat * jnp.mean(grad_normed * xhat, axis=-1, keepdims=True))
        high = grad.astype(bf16)
        hi_ref[rows, :] = high
        lo_ref[rows, :] = (grad - high.astype(f32)).astype(bf16)

    rows_ref[...] = one_hot_rows(slot_ref[...], rows_ref.shape[0], hi_ref, lo_ref)
    me = lax.axis_index(("dp", "rows"))
    lane = lax.broadcasted_iota(jnp.int32, (capacity, LANES), 1)
    place = lax.broadcasted_iota(jnp.int32, (capacity, LANES), 0) + lax.rem(me, LANES // capacity) * capacity
    spread = jnp.where(lane == place, 1.0, 0.0).astype(bf16)
    ids = slot_row_ref[...]
    ids = 16.0 * dot_tn((ids // 16).astype(bf16), spread) + dot_tn((ids % 16).astype(bf16), spread)
    tiles = width // LANES
    for o in range(owners):
        for t in range(tiles):
            send_ref[o, t * capacity:(t + 1) * capacity, :] = rows_ref[o * capacity:(o + 1) * capacity, t * LANES:(t + 1) * LANES]
        send_ref[o, tiles * capacity:, :] = jnp.broadcast_to(ids[o:o + 1, :], (ID_ROWS, LANES))


def one_hot_rows(ids, rows, hi_ref, lo_ref):
    named = lax.broadcasted_iota(jnp.int32, (rows, ids.shape[1]), 0) == ids
    onehot = jnp.where(named, 1.0, 0.0).astype(bf16)
    return dot_nn(onehot, hi_ref[...]) + dot_nn(onehot, lo_ref[...])


def table_kernel(recv_ref, table_ref, accum_ref, table_new_ref, accum_new_ref, rows_ref, hi_ref, lo_ref):
    owners = recv_ref.shape[0]
    rows, width = table_ref.shape
    tiles = width // LANES
    capacity = (recv_ref.shape[1] - ID_ROWS) // tiles
    for o in range(owners):
        for t in range(tiles):
            rows_ref[o * capacity:(o + 1) * capacity, t * LANES:(t + 1) * LANES] = recv_ref[o, t * capacity:(t + 1) * capacity, :]
    group = LANES // capacity
    ids = [sum(recv_ref[o, tiles * capacity:, :] for o in range(g, g + group)) for g in range(0, owners, group)]
    ids = jnp.concatenate(ids, axis=1)[:1, :].astype(jnp.int32)
    high = rows_ref[...].astype(bf16)
    hi_ref[...] = high
    lo_ref[...] = (rows_ref[...] - high.astype(f32)).astype(bf16)
    grad = one_hot_rows(ids, rows, hi_ref, lo_ref)
    accum = jnp.transpose(jnp.broadcast_to(accum_ref[...].reshape(1, rows), (8, rows)))[:, :1]
    accum_new = accum + jnp.mean(grad * grad, axis=-1, keepdims=True)
    accum_new_ref[...] = jnp.transpose(jnp.broadcast_to(accum_new, (rows, LANES)))[:1, :].reshape(rows)
    table_new_ref[...] = table_ref[...] - learning_rate * grad / (jnp.sqrt(accum_new) + adagrad_eps)


def place_on_dp():
    d = lax.axis_index("dp")
    return lax.rem(d, 2), d // 2


def split_first(x, y, keep_ref, recv_ref):
    half = keep_ref.shape[-1] // 2
    part = lambda i, j, cols: keep_ref[i, j, :, cols] + recv_ref[i, j, :, cols]
    lo, hi = slice(0, half), slice(half, 2 * half)
    return ([part(s, 1 - x, lo) for s in range(2)], [part(1 - y, s, hi) for s in range(2)],
            [part(s, x, lo) for s in range(2)], [part(y, s, hi) for s in range(2)])


def first_kernel(keep_ref, recv_ref, to_x_ref, to_y_ref, keep_a_ref, keep_b_ref):
    parts = split_first(*place_on_dp(), keep_ref, recv_ref)
    for ref, pair in zip((to_x_ref, to_y_ref, keep_a_ref, keep_b_ref), parts):
        for s in range(2):
            ref[s] = pair[s]


def second_kernel(keep_a_ref, from_x_ref, keep_b_ref, from_y_ref, keep_ref, recv_ref,
                  to_x_ref, to_y_ref, next_a_ref, next_b_ref, keep2_a_ref, keep2_b_ref):
    x, y = place_on_dp()
    half = keep_a_ref.shape[-1]
    to_y_ref[:, :half] = keep_a_ref[1 - y] + from_x_ref[1 - y]
    to_x_ref[:, :half] = keep_b_ref[1 - x] + from_y_ref[1 - x]
    next_a_ref[...] = keep_a_ref[y] + from_x_ref[y]
    next_b_ref[...] = keep_b_ref[x] + from_y_ref[x]
    send_x, send_y, keep2_a, keep2_b = split_first(x, y, keep_ref, recv_ref)
    half2 = keep_ref.shape[-1] // 2
    for s in range(2):
        to_x_ref[:, half + s * half2:half + (s + 1) * half2] = send_x[s]
        to_y_ref[:, half + s * half2:half + (s + 1) * half2] = send_y[s]
        keep2_a_ref[s] = keep2_a[s]
        keep2_b_ref[s] = keep2_b[s]


def chip_parts(out_refs, keep_a, recv_a, keep_b, recv_b):
    chips = len(out_refs)
    chip = lax.axis_index("rows") // 2
    half = out_refs[0].shape[-1] // 2
    for k, out_ref in enumerate(out_refs):
        at = lax.rem(chip + k, chips)
        out_ref[:, :half] = keep_a(at) + recv_a(at)
        out_ref[:, half:] = keep_b(at) + recv_b(at)


def third_kernel(chips, next_a_ref, next_b_ref, from_x_ref, from_y_ref, keep2_a_ref, keep2_b_ref, *out_refs):
    x, y = place_on_dp()
    half, half2 = next_a_ref.shape[-1], keep2_a_ref.shape[-1]
    lo = slice(0, half)
    chip_parts(out_refs[:chips], lambda at: next_a_ref[at], lambda at: from_y_ref[at, :, lo],
               lambda at: next_b_ref[at], lambda at: from_x_ref[at, :, lo])
    to_x_ref, to_y_ref, next2_a_ref, next2_b_ref = out_refs[chips:]
    blocks = [slice(half + s * half2, half + (s + 1) * half2) for s in range(2)]
    sum_a = [keep2_a_ref[s] + from_x_ref[:, :, blocks[s]] for s in range(2)]
    sum_b = [keep2_b_ref[s] + from_y_ref[:, :, blocks[s]] for s in range(2)]
    to_y_ref[...] = jnp.where(y == 0, sum_a[1], sum_a[0])
    next2_a_ref[...] = jnp.where(y == 0, sum_a[0], sum_a[1])
    to_x_ref[...] = jnp.where(x == 0, sum_b[1], sum_b[0])
    next2_b_ref[...] = jnp.where(x == 0, sum_b[0], sum_b[1])


def sum_of(refs):
    total = refs[0][...]
    for ref in refs[1:]:
        total = total + ref[...]
    return total


def fourth_kernel(chips, tokens, *refs):
    blocks, (next2_a_ref, next2_b_ref, from_x_ref, from_y_ref) = refs[:chips], refs[chips:chips + 4]
    total_ref, *out_refs = refs[chips + 4:]
    total_ref[...] = sum_of(blocks) * (1.0 / tokens)
    chip_parts(out_refs, lambda at: next2_a_ref[at], lambda at: from_y_ref[at],
               lambda at: next2_b_ref[at], lambda at: from_x_ref[at])


def total_kernel(tokens, *refs):
    refs[-1][...] = sum_of(refs[:-1]) * (1.0 / tokens)


def gather_kernel(*refs):
    *pieces, grad_in_ref, grad_out_ref = refs
    dp = len(pieces) // 2
    d = lax.axis_index("dp")
    width = grad_out_ref.shape[-1]
    for k in range(dp):
        at = jnp.bitwise_xor(d, k)
        first = pieces[k].shape[-1]
        grad_out_ref[at] = pieces[k][:, :width]
        grad_in_ref[at, :, :first - width] = pieces[k][:, width:]
        grad_in_ref[at, :, first - width:] = pieces[dp + k][...]


def vmem():
    return pl.BlockSpec(memory_space=pltpu.VMEM)


def shape(*dims, dtype=f32):
    return jax.ShapeDtypeStruct(dims, dtype)


def call(kernel, name, out_shape, args, scalars=0, scratch=(), far=0, long=False, grant=4):
    place = [None] * scalars + [pltpu.HBM] * far + [pltpu.VMEM] * (len(args) - scalars - far)
    args = [a if p is None else pltpu.with_memory_space_constraint(a, p) for a, p in zip(args, place)]
    return pl.pallas_call(
        kernel,
        name=name,
        in_specs=[pl.BlockSpec(memory_space=p or pltpu.SMEM) for p in place],
        out_specs=[vmem()] * len(out_shape),
        out_shape=list(out_shape),
        scratch_shapes=[pltpu.VMEM(dims, dtype) for dims, dtype in scratch] + [pltpu.SemaphoreType.DMA((7,))] * (far > 0),
        compiler_params=pltpu.CompilerParams(vmem_limit_bytes=grant * MIB),
        cost_estimate=pl.CostEstimate(flops=100_000_000_000 if long else 1_000_000_000, bytes_accessed=1 << 16, transcendentals=0),
    )(*args)


def body(rows_size, dp_size, events, cotangent, lengths, event_slot, slot_row, slot_count, w_in, w_out, item_table, accumulator):
    tokens, width = events.shape
    owners, capacity = slot_row.shape[1:]
    chips = rows_size // 2
    piece = width // (rows_size * dp_size)
    cores = [(i, i ^ 1) for i in range(rows_size)]
    over_dp = lambda v, bit: lax.ppermute(v, "dp", [(i, i ^ bit) for i in range(dp_size)])
    over_chips = lambda v, k: lax.ppermute(v, "rows", [(i, (i + 2 * k) % rows_size) for i in range(rows_size)])
    after = lambda value, *others: lax.optimization_barrier((value, *others))[0]
    strip = chips * piece

    def to_chips(blocks):
        return [blocks[0]] + [over_chips(blocks[k], k) for k in range(1, chips)]

    def gathered(total):
        return [total] + [over_dp(total, k) for k in range(1, dp_size)]

    by_dp = lambda v: v.reshape(2, 2, strip, v.shape[-1])
    by_chip = lambda v: v.reshape(*v.shape[:-2], chips, piece, v.shape[-1])
    local = lambda *dims, dtype=f32: pltpu.VMEM(dims, dtype)
    sides = lambda cols: [local(width // 2, cols)] * 2
    keep1, send1, hid, dsilu, gatt, gpre_uv, normed_t, events, cotangent, w_in = call(
        functools.partial(forward_kernel, rows_size, dp_size), "forward_part",
        sides(3 * width) + [
            local(tokens, 3 * width, dtype=bf16),
            local(tokens, 2 * width, dtype=bf16),
            local(tokens, width, dtype=bf16),
            local(tokens, 2 * width, dtype=bf16),
            local(width, tokens, dtype=bf16),
            local(tokens, width, dtype=bf16),
            local(tokens, width, dtype=bf16),
            local(*w_in.shape, dtype=bf16),
        ],
        (lengths, events, cotangent, w_in, w_out), 1,
        [((tokens, width), bf16), ((tokens, width), bf16), ((tokens, width), f32), ((tokens, width), f32),
         ((tokens, width), bf16), ((tokens, width), bf16), ((tokens, width), f32), ((HEADS, tokens, tokens), bf16),
         (w_out.shape, bf16)], far=4, long=True, grant=16)
    recv1 = lax.ppermute(send1, "rows", cores)
    keep2, send2, gpre_qk = call(
        attention_kernel, "attention_part", sides(2 * width) + [local(tokens, 2 * width, dtype=bf16)],
        (lengths, hid, dsilu, gatt, normed_t), 1, long=True, grant=10)
    recv2 = lax.ppermute(send2, "rows", cores)
    pay_rows = capacity * (width // LANES) + ID_ROWS
    half1, half2 = 3 * width // 2, width
    to_x, to_y, keep_a, keep_b = call(
        first_kernel, "first_sums", [local(2, strip, half1)] * 4, (by_dp(keep1), by_dp(after(recv1, keep2))))
    gpre_uv = after(gpre_uv, to_x, to_y)
    (send,) = call(
        events_kernel, "events_part", [local(owners, pay_rows, LANES)],
        (lengths, events, cotangent, w_in, event_slot, slot_row[0].T, gpre_uv, gpre_qk), 1,
        [((tokens, width), bf16), ((tokens, width), bf16), ((owners * capacity, width), f32)], long=True, grant=10)
    recv = lax.all_to_all(send, ("dp", "rows"), split_axis=0, concat_axis=0, tiled=True)
    from_x, from_y = over_dp(to_x, 1), over_dp(to_y, 2)
    to_x, to_y, next_a, next_b, keep2_a, keep2_b = call(
        second_kernel, "second_sums",
        [local(strip, half1 + 2 * half2)] * 2 + [local(strip, half1)] * 2 + [local(2, strip, half2)] * 2,
        (after(keep_a, send), from_x, keep_b, from_y, by_dp(keep2), by_dp(recv2)), long=True)
    from_x, from_y = over_dp(to_x, 1), over_dp(to_y, 2)
    *blocks, to_x, to_y, next2_a, next2_b = call(
        functools.partial(third_kernel, chips), "third_sums",
        [local(piece, 2 * half1)] * chips + [local(chips, piece, half2)] * 4,
        [by_chip(v) for v in (next_a, next_b, from_x, from_y, keep2_a, keep2_b)])
    from_x, from_y = over_dp(to_x, 1), over_dp(to_y, 2)
    total, *blocks = call(
        functools.partial(fourth_kernel, chips, tokens), "fourth_sums",
        [local(piece, 2 * half1)] + [local(piece, 2 * half2)] * chips,
        to_chips(blocks) + [next2_a, next2_b, from_x, from_y])
    pieces = gathered(total)
    blocks = to_chips(blocks)
    blocks[0] = after(blocks[0], *pieces)
    (total,) = call(functools.partial(total_kernel, tokens), "last_sums", [local(piece, 2 * half2)], blocks)
    pieces += gathered(total)
    slots = owners * capacity
    table_new, accum_new = call(
        table_kernel, "table_part", [shape(*item_table.shape), shape(*accumulator.shape)],
        (recv, item_table, accumulator), 0,
        [((slots, width), f32), ((slots, width), bf16), ((slots, width), bf16)], grant=10)
    pieces[-1] = after(pieces[-1], accum_new)
    grad_in, grad_out = call(
        gather_kernel, "gather", [shape(dp_size, piece, 4 * width), shape(dp_size, piece, width)], pieces)
    return grad_in.reshape(-1, 4 * width), grad_out.reshape(-1, width), table_new, accum_new


def solution(mesh):
    whole = P(("dp", "rows"))
    in_specs = (whole,) * 6 + (P(), P(), whole, whole)
    out_specs = (P("rows"), P("rows"), whole, whole)
    run = functools.partial(body, mesh.shape["rows"], mesh.shape["dp"])
    return jax.shard_map(run, mesh=mesh, in_specs=in_specs, out_specs=out_specs, check_vma=False)
```

```python
import functools

import jax
import jax.numpy as jnp
from jax import lax
from jax.experimental import pallas as pl
from jax.experimental.pallas import tpu as pltpu
from jax.sharding import PartitionSpec as P

HEADS = 4

norm_eps = 1e-05
adagrad_eps = 1e-10
learning_rate = 0.1

f32, bf16 = jnp.float32, jnp.bfloat16
MIB = 1024 * 1024
STEP = 256
LANES = 128
ID_ROWS = 8


def dot_nn(a, b):
    return lax.dot_general(a, b, (((1,), (0,)), ((), ())), preferred_element_type=f32)


def dot_nt(a, b):
    return lax.dot_general(a, b, (((1,), (1,)), ((), ())), preferred_element_type=f32)


def dot_tn(a, b):
    return lax.dot_general(a, b, (((0,), (0,)), ((), ())), preferred_element_type=f32)


def standardize(x):
    centered = x - jnp.mean(x, axis=-1, keepdims=True)
    inv = lax.rsqrt(jnp.mean(centered * centered, axis=-1, keepdims=True) + norm_eps)
    return centered * inv, inv


def masked_rows(cot, start, length):
    row = start + lax.broadcasted_iota(jnp.int32, cot.shape, 0)
    return jnp.where(row < length, cot.astype(f32), 0.0)


def owner_order(width, rows, dp):
    chips = rows // 2
    piece = width // (rows * dp)
    at = lax.broadcasted_iota(jnp.int32, (width, 1), 0)
    side, rest = at // (width // 2), at % (width // 2)
    part, rest = rest // (chips * piece), rest % (chips * piece)
    chip, row = rest // piece, rest % piece
    core = lax.rem(lax.axis_index("rows"), 2)
    core = jnp.where(side == 0, core, 1 - core)
    wanted = ((chip * 2 + core) * dp + part) * piece + row
    return jnp.where(lax.broadcasted_iota(jnp.int32, (width, width), 1) == wanted, 1.0, 0.0).astype(bf16)


def forward_kernel(rows_size, dp_size, len_ref, ev_hbm, cot_hbm, win_hbm, wout_hbm,
                   keep_ref, send_ref, hid_ref, dsilu_ref, gatt_ref, gpre_ref, normed_t_ref,
                   ev_ref, cot_ref, win_ref, normed_ref, user_ref, duser_ref, att_ref, mixed_ref, masked_ref, dval_ref, weights_ref,
                   wout_ref, arrived):
    tokens, width = ev_ref.shape
    copies = [pltpu.make_async_copy(ev_hbm, ev_ref, arrived.at[0])]
    for c in range(4):
        cols = pl.ds(c * width, width)
        copies.append(pltpu.make_async_copy(win_hbm.at[:, cols], win_ref.at[:, cols], arrived.at[1 + c]))
    copies.append(pltpu.make_async_copy(cot_hbm, cot_ref, arrived.at[5]))
    copies.append(pltpu.make_async_copy(wout_hbm, wout_ref, arrived.at[6]))
    for copy in copies:
        copy.start()
    hd = width // HEADS
    length = len_ref[0]
    inv_len = 1.0 / length.astype(f32)
    scale = hd ** -0.5
    steps = tokens // STEP

    copies[0].wait()
    for i in range(steps):
        rows = pl.ds(i * STEP, STEP)
        xhat, _ = standardize(ev_ref[rows, :].astype(f32))
        normed_ref[rows, :] = xhat.astype(bf16)

    def project(i, c):
        rows = pl.ds(i * STEP, STEP)
        pre = dot_nn(normed_ref[rows, :], win_ref[:, c * width:(c + 1) * width])
        sig = 0.5 + 0.5 * jnp.tanh(0.5 * pre)
        hid = pre * sig
        dsilu = sig * (1.0 + (pre - hid))
        if c == 0:
            user_ref[rows, :] = hid.astype(bf16)
            duser_ref[rows, :] = dsilu
        else:
            cols = slice((c - 1) * width, c * width)
            hid_ref[rows, cols] = hid.astype(bf16)
            if c == 1:
                dval_ref[rows, :] = dsilu
            else:
                dsilu_ref[rows, (c - 2) * width:(c - 1) * width] = dsilu.astype(bf16)

    for c in range(4):
        copies[1 + c].wait()
        for i in range(steps):
            project(i, c)

    tri = lax.broadcasted_iota(jnp.int32, (STEP, STEP), 0) >= lax.broadcasted_iota(jnp.int32, (STEP, STEP), 1)
    for h in range(HEADS):
        v_cols = slice(h * hd, (h + 1) * hd)
        q_cols = slice(width + h * hd, width + (h + 1) * hd)
        k_cols = slice(2 * width + h * hd, 2 * width + (h + 1) * hd)
        for i in range(steps):
            rows = pl.ds(i * STEP, STEP)
            query = hid_ref[rows, q_cols]
            total = None
            for j in range(i + 1):
                keys = pl.ds(j * STEP, STEP)
                half = dot_nt(query, hid_ref[keys, k_cols]) * (0.5 * scale)
                weights = (half + half * jnp.tanh(half)) * inv_len
                if i == j:
                    weights = jnp.where(tri, weights, 0.0)
                weights = weights.astype(bf16)
                weights_ref[h, rows, keys] = weights
                part = dot_nn(weights, hid_ref[keys, v_cols])
                total = part if total is None else total + part
            att_ref[rows, v_cols] = total

    copies[5].wait()
    copies[6].wait()
    for i in range(steps):
        rows = pl.ds(i * STEP, STEP)
        masked_ref[rows, :] = masked_rows(cot_ref[rows, :], i * STEP, length).astype(bf16)
        ahat, inv = standardize(att_ref[rows, :])
        user = user_ref[rows, :].astype(f32)
        mixed_ref[rows, :] = (ahat * user).astype(bf16)
        grad_mixed = dot_nt(masked_ref[rows, :], wout_ref[...])
        gpre_ref[rows, :width] = (grad_mixed * ahat * duser_ref[rows, :]).astype(bf16)
        e = grad_mixed * user
        gatt_ref[rows, :] = (inv * (e - jnp.mean(e, axis=-1, keepdims=True)
                                    - ahat * jnp.mean(e * ahat, axis=-1, keepdims=True))).astype(bf16)

    for h in range(HEADS):
        v_cols = slice(h * hd, (h + 1) * hd)
        for j in range(steps):
            keys, rest = pl.ds(j * STEP, STEP), pl.ds(j * STEP, tokens - j * STEP)
            grad_v = dot_tn(weights_ref[h, rest, keys], gatt_ref[rest, v_cols])
            gpre_ref[keys, width + h * hd:width + (h + 1) * hd] = (grad_v * dval_ref[keys, v_cols]).astype(bf16)

    order = owner_order(width, rows_size, dp_size)
    normed_t_ref[...] = dot_nt(order, normed_ref[...]).astype(bf16)
    mixed_t = dot_nt(order, mixed_ref[...]).astype(bf16)
    half = width // 2
    for ref, start in ((send_ref, half), (keep_ref, 0)):
        ref[:, :width] = dot_nn(mixed_t[start:start + half], masked_ref[...])
        ref[:, width:] = dot_nn(normed_t_ref[start:start + half, :], gpre_ref[...])


def attention_kernel(len_ref, hid_ref, dsilu_ref, gatt_ref, normed_t_ref, keep_ref, send_ref, gpre_ref):
    tokens, width = gatt_ref.shape
    hd = width // HEADS
    inv_len = 1.0 / len_ref[0].astype(f32)
    scale = hd ** -0.5
    steps = tokens // STEP

    tri = lax.broadcasted_iota(jnp.int32, (STEP, STEP), 0) <= lax.broadcasted_iota(jnp.int32, (STEP, STEP), 1)
    for h in range(HEADS):
        v_cols = slice(h * hd, (h + 1) * hd)
        q_cols = slice(width + h * hd, width + (h + 1) * hd)
        k_cols = slice(2 * width + h * hd, 2 * width + (h + 1) * hd)
        grad_q = [None] * steps
        for j in range(steps):
            keys = pl.ds(j * STEP, STEP)
            key, value = hid_ref[keys, k_cols], hid_ref[keys, v_cols]
            grad_k = None
            for i in range(j, steps):
                rows = pl.ds(i * STEP, STEP)
                query, gatt = hid_ref[rows, q_cols], gatt_ref[rows, v_cols]
                half = dot_nt(key, query) * (0.5 * scale)
                sig2 = 1.0 + jnp.tanh(half)
                silu = half * sig2
                dsilu = sig2 * ((1.0 + half) + (half - silu))
                gscore = dot_nt(value, gatt) * dsilu * (0.5 * inv_len * scale)
                if i == j:
                    gscore = jnp.where(tri, gscore, 0.0)
                gscore = gscore.astype(bf16)
                pk, pq = dot_nn(gscore, query), dot_tn(gscore, key)
                grad_k = pk if grad_k is None else grad_k + pk
                grad_q[i] = pq if grad_q[i] is None else grad_q[i] + pq
            gpre_ref[keys, q_cols] = (grad_k * dsilu_ref[keys, q_cols].astype(f32)).astype(bf16)
        for i in range(steps):
            rows = pl.ds(i * STEP, STEP)
            gpre_ref[rows, v_cols] = (grad_q[i] * dsilu_ref[rows, v_cols].astype(f32)).astype(bf16)

    half = width // 2
    for ref, start in ((send_ref, half), (keep_ref, 0)):
        ref[...] = dot_nn(normed_t_ref[start:start + half, :], gpre_ref[...])


def events_kernel(len_ref, ev_ref, cot_ref, win_ref, slot_ref, slot_row_ref, gpre_uv_ref, gpre_qk_ref,
                  send_ref, hi_ref, lo_ref, rows_ref):
    tokens, width = ev_ref.shape
    capacity, owners = slot_row_ref.shape
    length = len_ref[0]
    for i in range(tokens // STEP):
        rows = pl.ds(i * STEP, STEP)
        xhat, inv = standardize(ev_ref[rows, :].astype(f32))
        grad_normed = dot_nt(gpre_uv_ref[rows, :], win_ref[:, :2 * width]) + dot_nt(gpre_qk_ref[rows, :], win_ref[:, 2 * width:])
        grad = masked_rows(cot_ref[rows, :], i * STEP, length) + inv * (
            grad_normed - jnp.mean(grad_normed, axis=-1, keepdims=True)
            - xhat * jnp.mean(grad_normed * xhat, axis=-1, keepdims=True))
        high = grad.astype(bf16)
        hi_ref[rows, :] = high
        lo_ref[rows, :] = (grad - high.astype(f32)).astype(bf16)

    rows_ref[...] = one_hot_rows(slot_ref[...], rows_ref.shape[0], hi_ref, lo_ref)
    me = lax.axis_index(("dp", "rows"))
    lane = lax.broadcasted_iota(jnp.int32, (capacity, LANES), 1)
    place = lax.broadcasted_iota(jnp.int32, (capacity, LANES), 0) + lax.rem(me, LANES // capacity) * capacity
    spread = jnp.where(lane == place, 1.0, 0.0).astype(bf16)
    ids = slot_row_ref[...]
    ids = 16.0 * dot_tn((ids // 16).astype(bf16), spread) + dot_tn((ids % 16).astype(bf16), spread)
    tiles = width // LANES
    for o in range(owners):
        for t in range(tiles):
            send_ref[o, t * capacity:(t + 1) * capacity, :] = rows_ref[o * capacity:(o + 1) * capacity, t * LANES:(t + 1) * LANES]
        send_ref[o, tiles * capacity:, :] = jnp.broadcast_to(ids[o:o + 1, :], (ID_ROWS, LANES))


def one_hot_rows(ids, rows, hi_ref, lo_ref):
    named = lax.broadcasted_iota(jnp.int32, (rows, ids.shape[1]), 0) == ids
    onehot = jnp.where(named, 1.0, 0.0).astype(bf16)
    return dot_nn(onehot, hi_ref[...]) + dot_nn(onehot, lo_ref[...])


def table_kernel(recv_ref, table_ref, accum_ref, table_new_ref, accum_new_ref, rows_ref, hi_ref, lo_ref):
    owners = recv_ref.shape[0]
    rows, width = table_ref.shape
    tiles = width // LANES
    capacity = (recv_ref.shape[1] - ID_ROWS) // tiles
    for o in range(owners):
        for t in range(tiles):
            rows_ref[o * capacity:(o + 1) * capacity, t * LANES:(t + 1) * LANES] = recv_ref[o, t * capacity:(t + 1) * capacity, :]
    group = LANES // capacity
    ids = [sum(recv_ref[o, tiles * capacity:, :] for o in range(g, g + group)) for g in range(0, owners, group)]
    ids = jnp.concatenate(ids, axis=1)[:1, :].astype(jnp.int32)
    high = rows_ref[...].astype(bf16)
    hi_ref[...] = high
    lo_ref[...] = (rows_ref[...] - high.astype(f32)).astype(bf16)
    grad = one_hot_rows(ids, rows, hi_ref, lo_ref)
    accum = jnp.transpose(jnp.broadcast_to(accum_ref[...].reshape(1, rows), (8, rows)))[:, :1]
    accum_new = accum + jnp.mean(grad * grad, axis=-1, keepdims=True)
    accum_new_ref[...] = jnp.transpose(jnp.broadcast_to(accum_new, (rows, LANES)))[:1, :].reshape(rows)
    table_new_ref[...] = table_ref[...] - learning_rate * grad / (jnp.sqrt(accum_new) + adagrad_eps)


def place_on_dp():
    d = lax.axis_index("dp")
    return lax.rem(d, 2), d // 2


def split_first(x, y, keep_ref, recv_ref):
    half = keep_ref.shape[-1] // 2
    part = lambda i, j, cols: keep_ref[i, j, :, cols] + recv_ref[i, j, :, cols]
    lo, hi = slice(0, half), slice(half, 2 * half)
    return ([part(s, 1 - x, lo) for s in range(2)], [part(1 - y, s, hi) for s in range(2)],
            [part(s, x, lo) for s in range(2)], [part(y, s, hi) for s in range(2)])


def first_kernel(keep_ref, recv_ref, to_x_ref, to_y_ref, keep_a_ref, keep_b_ref):
    parts = split_first(*place_on_dp(), keep_ref, recv_ref)
    for ref, pair in zip((to_x_ref, to_y_ref, keep_a_ref, keep_b_ref), parts):
        for s in range(2):
            ref[s] = pair[s]


def second_kernel(keep_a_ref, from_x_ref, keep_b_ref, from_y_ref, keep_ref, recv_ref,
                  to_x_ref, to_y_ref, next_a_ref, next_b_ref, keep2_a_ref, keep2_b_ref):
    x, y = place_on_dp()
    half = keep_a_ref.shape[-1]
    to_y_ref[:, :half] = keep_a_ref[1 - y] + from_x_ref[1 - y]
    to_x_ref[:, :half] = keep_b_ref[1 - x] + from_y_ref[1 - x]
    next_a_ref[...] = keep_a_ref[y] + from_x_ref[y]
    next_b_ref[...] = keep_b_ref[x] + from_y_ref[x]
    send_x, send_y, keep2_a, keep2_b = split_first(x, y, keep_ref, recv_ref)
    half2 = keep_ref.shape[-1] // 2
    for s in range(2):
        to_x_ref[:, half + s * half2:half + (s + 1) * half2] = send_x[s]
        to_y_ref[:, half + s * half2:half + (s + 1) * half2] = send_y[s]
        keep2_a_ref[s] = keep2_a[s]
        keep2_b_ref[s] = keep2_b[s]


def chip_parts(out_refs, keep_a, recv_a, keep_b, recv_b):
    chips = len(out_refs)
    chip = lax.axis_index("rows") // 2
    half = out_refs[0].shape[-1] // 2
    for k, out_ref in enumerate(out_refs):
        at = lax.rem(chip + k, chips)
        out_ref[:, :half] = keep_a(at) + recv_a(at)
        out_ref[:, half:] = keep_b(at) + recv_b(at)


def third_kernel(chips, next_a_ref, next_b_ref, from_x_ref, from_y_ref, keep2_a_ref, keep2_b_ref, *out_refs):
    x, y = place_on_dp()
    half, half2 = next_a_ref.shape[-1], keep2_a_ref.shape[-1]
    lo = slice(0, half)
    chip_parts(out_refs[:chips], lambda at: next_a_ref[at], lambda at: from_y_ref[at, :, lo],
               lambda at: next_b_ref[at], lambda at: from_x_ref[at, :, lo])
    to_x_ref, to_y_ref, next2_a_ref, next2_b_ref = out_refs[chips:]
    blocks = [slice(half + s * half2, half + (s + 1) * half2) for s in range(2)]
    sum_a = [keep2_a_ref[s] + from_x_ref[:, :, blocks[s]] for s in range(2)]
    sum_b = [keep2_b_ref[s] + from_y_ref[:, :, blocks[s]] for s in range(2)]
    to_y_ref[...] = jnp.where(y == 0, sum_a[1], sum_a[0])
    next2_a_ref[...] = jnp.where(y == 0, sum_a[0], sum_a[1])
    to_x_ref[...] = jnp.where(x == 0, sum_b[1], sum_b[0])
    next2_b_ref[...] = jnp.where(x == 0, sum_b[0], sum_b[1])


def sum_of(refs):
    total = refs[0][...]
    for ref in refs[1:]:
        total = total + ref[...]
    return total


def fourth_kernel(chips, tokens, *refs):
    blocks, (next2_a_ref, next2_b_ref, from_x_ref, from_y_ref) = refs[:chips], refs[chips:chips + 4]
    total_ref, *out_refs = refs[chips + 4:]
    total_ref[...] = sum_of(blocks) * (1.0 / tokens)
    chip_parts(out_refs, lambda at: next2_a_ref[at], lambda at: from_y_ref[at],
               lambda at: next2_b_ref[at], lambda at: from_x_ref[at])


def total_kernel(tokens, *refs):
    refs[-1][...] = sum_of(refs[:-1]) * (1.0 / tokens)


def gather_kernel(*refs):
    *pieces, grad_in_ref, grad_out_ref = refs
    dp = len(pieces) // 2
    d = lax.axis_index("dp")
    width = grad_out_ref.shape[-1]
    for k in range(dp):
        at = jnp.bitwise_xor(d, k)
        first = pieces[k].shape[-1]
        grad_out_ref[at] = pieces[k][:, :width]
        grad_in_ref[at, :, :first - width] = pieces[k][:, width:]
        grad_in_ref[at, :, first - width:] = pieces[dp + k][...]


def vmem():
    return pl.BlockSpec(memory_space=pltpu.VMEM)


def shape(*dims, dtype=f32):
    return jax.ShapeDtypeStruct(dims, dtype)


def call(kernel, name, out_shape, args, scalars=0, scratch=(), far=0, long=False, grant=4, tied=True):
    place = [None] * scalars + [pltpu.HBM] * far + [pltpu.VMEM] * (len(args) - scalars - far)
    args = [a if p is None or not tied else pltpu.with_memory_space_constraint(a, p) for a, p in zip(args, place)]
    return pl.pallas_call(
        kernel,
        name=name,
        in_specs=[pl.BlockSpec(memory_space=p or pltpu.SMEM) for p in place],
        out_specs=[vmem()] * len(out_shape),
        out_shape=list(out_shape),
        scratch_shapes=[pltpu.VMEM(dims, dtype) for dims, dtype in scratch] + [pltpu.SemaphoreType.DMA((7,))] * (far > 0),
        compiler_params=pltpu.CompilerParams(vmem_limit_bytes=grant * MIB),
        cost_estimate=pl.CostEstimate(flops=100_000_000_000 if long else 1_000_000_000, bytes_accessed=1 << 16, transcendentals=0),
    )(*args)


def body(rows_size, dp_size, events, cotangent, lengths, event_slot, slot_row, slot_count, w_in, w_out, item_table, accumulator):
    tokens, width = events.shape
    owners, capacity = slot_row.shape[1:]
    chips = rows_size // 2
    piece = width // (rows_size * dp_size)
    cores = [(i, i ^ 1) for i in range(rows_size)]
    over_dp = lambda v, bit: lax.ppermute(v, "dp", [(i, i ^ bit) for i in range(dp_size)])
    over_chips = lambda v, k: lax.ppermute(v, "rows", [(i, (i + 2 * k) % rows_size) for i in range(rows_size)])
    after = lambda value, *others: lax.optimization_barrier((value, *others))[0]
    strip = chips * piece

    def to_chips(blocks):
        return [blocks[0]] + [over_chips(blocks[k], k) for k in range(1, chips)]

    def gathered(total):
        return [total] + [over_dp(total, k) for k in range(1, dp_size)]

    by_dp = lambda v: v.reshape(2, 2, strip, v.shape[-1])
    by_chip = lambda v: v.reshape(*v.shape[:-2], chips, piece, v.shape[-1])
    local = lambda *dims, dtype=f32: pltpu.VMEM(dims, dtype)
    sides = lambda cols: [local(width // 2, cols)] * 2
    keep1, send1, hid, dsilu, gatt, gpre_uv, normed_t, events, cotangent, w_in = call(
        functools.partial(forward_kernel, rows_size, dp_size), "forward_part",
        sides(3 * width) + [
            local(tokens, 3 * width, dtype=bf16),
            local(tokens, 2 * width, dtype=bf16),
            local(tokens, width, dtype=bf16),
            local(tokens, 2 * width, dtype=bf16),
            local(width, tokens, dtype=bf16),
            local(tokens, width, dtype=bf16),
            local(tokens, width, dtype=bf16),
            local(*w_in.shape, dtype=bf16),
        ],
        (lengths, events, cotangent, w_in, w_out), 1,
        [((tokens, width), bf16), ((tokens, width), bf16), ((tokens, width), f32), ((tokens, width), f32),
         ((tokens, width), bf16), ((tokens, width), bf16), ((tokens, width), f32), ((HEADS, tokens, tokens), bf16),
         (w_out.shape, bf16)], far=4, long=True, grant=16)
    recv1 = lax.ppermute(send1, "rows", cores)
    keep2, send2, gpre_qk = call(
        attention_kernel, "attention_part", sides(2 * width) + [local(tokens, 2 * width, dtype=bf16)],
        (lengths, hid, dsilu, gatt, normed_t), 1, long=True, grant=10)
    recv2 = lax.ppermute(send2, "rows", cores)
    pay_rows = capacity * (width // LANES) + ID_ROWS
    half1, half2 = 3 * width // 2, width
    to_x, to_y, keep_a, keep_b = call(
        first_kernel, "first_sums", [local(2, strip, half1)] * 4, (by_dp(keep1), by_dp(after(recv1, keep2))))
    gpre_uv = after(gpre_uv, to_x, to_y)
    (send,) = call(
        events_kernel, "events_part", [local(owners, pay_rows, LANES)],
        (lengths, events, cotangent, w_in, event_slot, slot_row[0].T, gpre_uv, gpre_qk), 1,
        [((tokens, width), bf16), ((tokens, width), bf16), ((owners * capacity, width), f32)], long=True, grant=10)
    from_x, from_y = over_dp(to_x, 1), over_dp(to_y, 2)
    to_x, to_y, next_a, next_b, keep2_a, keep2_b = call(
        second_kernel, "second_sums",
        [shape(strip, half1 + 2 * half2)] * 2 + [shape(strip, half1)] * 2 + [shape(2, strip, half2)] * 2,
        (after(keep_a, send), from_x, keep_b, from_y, by_dp(keep2), by_dp(recv2)), grant=10)
    send = after(send, to_x, to_y)
    recv = lax.all_to_all(send, ("dp", "rows"), split_axis=0, concat_axis=0, tiled=True)
    from_x, from_y = over_dp(to_x, 1), over_dp(to_y, 2)
    *blocks, to_x, to_y, next2_a, next2_b = call(
        functools.partial(third_kernel, chips), "third_sums",
        [local(piece, 2 * half1)] * chips + [local(chips, piece, half2)] * 4,
        [by_chip(v) for v in (next_a, next_b, from_x, from_y, keep2_a, keep2_b)], long=True, grant=10, tied=False)
    from_x, from_y = over_dp(to_x, 1), over_dp(to_y, 2)
    total, *blocks = call(
        functools.partial(fourth_kernel, chips, tokens), "fourth_sums",
        [local(piece, 2 * half1)] + [local(piece, 2 * half2)] * chips,
        to_chips(blocks) + [next2_a, next2_b, from_x, from_y])
    pieces = gathered(total)
    blocks = to_chips(blocks)
    blocks[0] = after(blocks[0], *pieces)
    (total,) = call(functools.partial(total_kernel, tokens), "last_sums", [local(piece, 2 * half2)], blocks)
    pieces += gathered(total)
    slots = owners * capacity
    table_new, accum_new = call(
        table_kernel, "table_part", [shape(*item_table.shape), shape(*accumulator.shape)],
        (recv, item_table, accumulator), 0,
        [((slots, width), f32), ((slots, width), bf16), ((slots, width), bf16)], grant=10)
    pieces[-1] = after(pieces[-1], accum_new)
    grad_in, grad_out = call(
        gather_kernel, "gather", [shape(dp_size, piece, 4 * width), shape(dp_size, piece, width)], pieces)
    return grad_in.reshape(-1, 4 * width), grad_out.reshape(-1, width), table_new, accum_new


def solution(mesh):
    whole = P(("dp", "rows"))
    in_specs = (whole,) * 6 + (P(), P(), whole, whole)
    out_specs = (P("rows"), P("rows"), whole, whole)
    run = functools.partial(body, mesh.shape["rows"], mesh.shape["dp"])
    return jax.shard_map(run, mesh=mesh, in_specs=in_specs, out_specs=out_specs, check_vma=False)
```

```python
import functools

import jax
import jax.numpy as jnp
from jax import lax
from jax.experimental import pallas as pl
from jax.experimental.pallas import tpu as pltpu
from jax.sharding import PartitionSpec as P

HEADS = 4

norm_eps = 1e-05
adagrad_eps = 1e-10
learning_rate = 0.1

f32, bf16 = jnp.float32, jnp.bfloat16
MIB = 1024 * 1024
STEP = 256
LANES = 128
ID_ROWS = 8


def dot_nn(a, b):
    return lax.dot_general(a, b, (((1,), (0,)), ((), ())), preferred_element_type=f32)


def dot_nt(a, b):
    return lax.dot_general(a, b, (((1,), (1,)), ((), ())), preferred_element_type=f32)


def dot_tn(a, b):
    return lax.dot_general(a, b, (((0,), (0,)), ((), ())), preferred_element_type=f32)


def standardize(x):
    centered = x - jnp.mean(x, axis=-1, keepdims=True)
    inv = lax.rsqrt(jnp.mean(centered * centered, axis=-1, keepdims=True) + norm_eps)
    return centered * inv, inv


def masked_rows(cot, start, length):
    row = start + lax.broadcasted_iota(jnp.int32, cot.shape, 0)
    return jnp.where(row < length, cot.astype(f32), 0.0)


def owner_order(width, rows, dp):
    chips = rows // 2
    piece = width // (rows * dp)
    at = lax.broadcasted_iota(jnp.int32, (width, 1), 0)
    side, rest = at // (width // 2), at % (width // 2)
    part, rest = rest // (chips * piece), rest % (chips * piece)
    chip, row = rest // piece, rest % piece
    core = lax.rem(lax.axis_index("rows"), 2)
    core = jnp.where(side == 0, core, 1 - core)
    wanted = ((chip * 2 + core) * dp + part) * piece + row
    return jnp.where(lax.broadcasted_iota(jnp.int32, (width, width), 1) == wanted, 1.0, 0.0).astype(bf16)


def forward_kernel(rows_size, dp_size, len_ref, ev_hbm, cot_hbm, win_hbm, wout_hbm,
                   keep_ref, send_ref, hid_ref, dsilu_ref, gatt_ref, gpre_ref, normed_t_ref,
                   ev_ref, cot_ref, win_ref, normed_ref, user_ref, duser_ref, att_ref, mixed_ref, masked_ref, dval_ref, weights_ref,
                   wout_ref, arrived):
    tokens, width = ev_ref.shape
    copies = [pltpu.make_async_copy(ev_hbm, ev_ref, arrived.at[0])]
    for c in range(4):
        cols = pl.ds(c * width, width)
        copies.append(pltpu.make_async_copy(win_hbm.at[:, cols], win_ref.at[:, cols], arrived.at[1 + c]))
    copies.append(pltpu.make_async_copy(cot_hbm, cot_ref, arrived.at[5]))
    copies.append(pltpu.make_async_copy(wout_hbm, wout_ref, arrived.at[6]))
    for copy in copies:
        copy.start()
    hd = width // HEADS
    length = len_ref[0]
    inv_len = 1.0 / length.astype(f32)
    scale = hd ** -0.5
    steps = tokens // STEP

    copies[0].wait()
    for i in range(steps):
        rows = pl.ds(i * STEP, STEP)
        xhat, _ = standardize(ev_ref[rows, :].astype(f32))
        normed_ref[rows, :] = xhat.astype(bf16)

    def project(i, c):
        rows = pl.ds(i * STEP, STEP)
        pre = dot_nn(normed_ref[rows, :], win_ref[:, c * width:(c + 1) * width])
        sig = 0.5 + 0.5 * jnp.tanh(0.5 * pre)
        hid = pre * sig
        dsilu = sig * (1.0 + (pre - hid))
        if c == 0:
            user_ref[rows, :] = hid.astype(bf16)
            duser_ref[rows, :] = dsilu
        else:
            cols = slice((c - 1) * width, c * width)
            hid_ref[rows, cols] = hid.astype(bf16)
            if c == 1:
                dval_ref[rows, :] = dsilu
            else:
                dsilu_ref[rows, (c - 2) * width:(c - 1) * width] = dsilu.astype(bf16)

    for c in range(4):
        copies[1 + c].wait()
        for i in range(steps):
            project(i, c)

    tri = lax.broadcasted_iota(jnp.int32, (STEP, STEP), 0) >= lax.broadcasted_iota(jnp.int32, (STEP, STEP), 1)
    for h in range(HEADS):
        v_cols = slice(h * hd, (h + 1) * hd)
        q_cols = slice(width + h * hd, width + (h + 1) * hd)
        k_cols = slice(2 * width + h * hd, 2 * width + (h + 1) * hd)
        for i in range(steps):
            rows = pl.ds(i * STEP, STEP)
            query = hid_ref[rows, q_cols]
            total = None
            for j in range(i + 1):
                keys = pl.ds(j * STEP, STEP)
                half = dot_nt(query, hid_ref[keys, k_cols]) * (0.5 * scale)
                weights = (half + half * jnp.tanh(half)) * inv_len
                if i == j:
                    weights = jnp.where(tri, weights, 0.0)
                weights = weights.astype(bf16)
                weights_ref[h, rows, keys] = weights
                part = dot_nn(weights, hid_ref[keys, v_cols])
                total = part if total is None else total + part
            att_ref[rows, v_cols] = total

    copies[5].wait()
    copies[6].wait()
    for i in range(steps):
        rows = pl.ds(i * STEP, STEP)
        masked_ref[rows, :] = masked_rows(cot_ref[rows, :], i * STEP, length).astype(bf16)
        ahat, inv = standardize(att_ref[rows, :])
        user = user_ref[rows, :].astype(f32)
        mixed_ref[rows, :] = (ahat * user).astype(bf16)
        grad_mixed = dot_nt(masked_ref[rows, :], wout_ref[...])
        gpre_ref[rows, :width] = (grad_mixed * ahat * duser_ref[rows, :]).astype(bf16)
        e = grad_mixed * user
        gatt_ref[rows, :] = (inv * (e - jnp.mean(e, axis=-1, keepdims=True)
                                    - ahat * jnp.mean(e * ahat, axis=-1, keepdims=True))).astype(bf16)

    for h in range(HEADS):
        v_cols = slice(h * hd, (h + 1) * hd)
        for j in range(steps):
            keys, rest = pl.ds(j * STEP, STEP), pl.ds(j * STEP, tokens - j * STEP)
            grad_v = dot_tn(weights_ref[h, rest, keys], gatt_ref[rest, v_cols])
            gpre_ref[keys, width + h * hd:width + (h + 1) * hd] = (grad_v * dval_ref[keys, v_cols]).astype(bf16)

    order = owner_order(width, rows_size, dp_size)
    normed_t_ref[...] = dot_nt(order, normed_ref[...]).astype(bf16)
    mixed_t = dot_nt(order, mixed_ref[...]).astype(bf16)
    half = width // 2
    for ref, start in ((send_ref, half), (keep_ref, 0)):
        ref[:, :width] = dot_nn(mixed_t[start:start + half], masked_ref[...])
        ref[:, width:] = dot_nn(normed_t_ref[start:start + half, :], gpre_ref[...])


def attention_kernel(len_ref, hid_ref, dsilu_ref, gatt_ref, normed_t_ref, keep_ref, send_ref, gpre_ref):
    tokens, width = gatt_ref.shape
    hd = width // HEADS
    inv_len = 1.0 / len_ref[0].astype(f32)
    scale = hd ** -0.5
    steps = tokens // STEP

    tri = lax.broadcasted_iota(jnp.int32, (STEP, STEP), 0) <= lax.broadcasted_iota(jnp.int32, (STEP, STEP), 1)
    for h in range(HEADS):
        v_cols = slice(h * hd, (h + 1) * hd)
        q_cols = slice(width + h * hd, width + (h + 1) * hd)
        k_cols = slice(2 * width + h * hd, 2 * width + (h + 1) * hd)
        grad_q = [None] * steps
        for j in range(steps):
            keys = pl.ds(j * STEP, STEP)
            key, value = hid_ref[keys, k_cols], hid_ref[keys, v_cols]
            grad_k = None
            for i in range(j, steps):
                rows = pl.ds(i * STEP, STEP)
                query, gatt = hid_ref[rows, q_cols], gatt_ref[rows, v_cols]
                half = dot_nt(key, query) * (0.5 * scale)
                sig2 = 1.0 + jnp.tanh(half)
                silu = half * sig2
                dsilu = sig2 * ((1.0 + half) + (half - silu))
                gscore = dot_nt(value, gatt) * dsilu * (0.5 * inv_len * scale)
                if i == j:
                    gscore = jnp.where(tri, gscore, 0.0)
                gscore = gscore.astype(bf16)
                pk, pq = dot_nn(gscore, query), dot_tn(gscore, key)
                grad_k = pk if grad_k is None else grad_k + pk
                grad_q[i] = pq if grad_q[i] is None else grad_q[i] + pq
            gpre_ref[keys, q_cols] = (grad_k * dsilu_ref[keys, q_cols].astype(f32)).astype(bf16)
        for i in range(steps):
            rows = pl.ds(i * STEP, STEP)
            gpre_ref[rows, v_cols] = (grad_q[i] * dsilu_ref[rows, v_cols].astype(f32)).astype(bf16)

    half = width // 2
    for ref, start in ((send_ref, half), (keep_ref, 0)):
        ref[...] = dot_nn(normed_t_ref[start:start + half, :], gpre_ref[...])


def events_kernel(len_ref, ev_ref, cot_ref, win_ref, slot_ref, slot_row_ref, gpre_uv_ref, gpre_qk_ref,
                  send_ref, hi_ref, lo_ref, rows_ref):
    tokens, width = ev_ref.shape
    capacity, owners = slot_row_ref.shape
    length = len_ref[0]
    for i in range(tokens // STEP):
        rows = pl.ds(i * STEP, STEP)
        xhat, inv = standardize(ev_ref[rows, :].astype(f32))
        grad_normed = dot_nt(gpre_uv_ref[rows, :], win_ref[:, :2 * width]) + dot_nt(gpre_qk_ref[rows, :], win_ref[:, 2 * width:])
        grad = masked_rows(cot_ref[rows, :], i * STEP, length) + inv * (
            grad_normed - jnp.mean(grad_normed, axis=-1, keepdims=True)
            - xhat * jnp.mean(grad_normed * xhat, axis=-1, keepdims=True))
        high = grad.astype(bf16)
        hi_ref[rows, :] = high
        lo_ref[rows, :] = (grad - high.astype(f32)).astype(bf16)

    rows_ref[...] = one_hot_rows(slot_ref[...], rows_ref.shape[0], hi_ref, lo_ref)
    me = lax.axis_index(("dp", "rows"))
    lane = lax.broadcasted_iota(jnp.int32, (capacity, LANES), 1)
    place = lax.broadcasted_iota(jnp.int32, (capacity, LANES), 0) + lax.rem(me, LANES // capacity) * capacity
    spread = jnp.where(lane == place, 1.0, 0.0).astype(bf16)
    ids = slot_row_ref[...]
    ids = 16.0 * dot_tn((ids // 16).astype(bf16), spread) + dot_tn((ids % 16).astype(bf16), spread)
    tiles = width // LANES
    for o in range(owners):
        for t in range(tiles):
            send_ref[o, t * capacity:(t + 1) * capacity, :] = rows_ref[o * capacity:(o + 1) * capacity, t * LANES:(t + 1) * LANES]
        send_ref[o, tiles * capacity:, :] = jnp.broadcast_to(ids[o:o + 1, :], (ID_ROWS, LANES))


def one_hot_rows(ids, rows, hi_ref, lo_ref):
    named = lax.broadcasted_iota(jnp.int32, (rows, ids.shape[1]), 0) == ids
    onehot = jnp.where(named, 1.0, 0.0).astype(bf16)
    return dot_nn(onehot, hi_ref[...]) + dot_nn(onehot, lo_ref[...])


def table_kernel(recv_ref, table_ref, accum_ref, table_new_ref, accum_new_ref, rows_ref, hi_ref, lo_ref):
    owners = recv_ref.shape[0]
    rows, width = table_ref.shape
    tiles = width // LANES
    capacity = (recv_ref.shape[1] - ID_ROWS) // tiles
    for o in range(owners):
        for t in range(tiles):
            rows_ref[o * capacity:(o + 1) * capacity, t * LANES:(t + 1) * LANES] = recv_ref[o, t * capacity:(t + 1) * capacity, :]
    group = LANES // capacity
    ids = [sum(recv_ref[o, tiles * capacity:, :] for o in range(g, g + group)) for g in range(0, owners, group)]
    ids = jnp.concatenate(ids, axis=1)[:1, :].astype(jnp.int32)
    high = rows_ref[...].astype(bf16)
    hi_ref[...] = high
    lo_ref[...] = (rows_ref[...] - high.astype(f32)).astype(bf16)
    grad = one_hot_rows(ids, rows, hi_ref, lo_ref)
    accum = jnp.transpose(jnp.broadcast_to(accum_ref[...].reshape(1, rows), (8, rows)))[:, :1]
    accum_new = accum + jnp.mean(grad * grad, axis=-1, keepdims=True)
    accum_new_ref[...] = jnp.transpose(jnp.broadcast_to(accum_new, (rows, LANES)))[:1, :].reshape(rows)
    table_new_ref[...] = table_ref[...] - learning_rate * grad / (jnp.sqrt(accum_new) + adagrad_eps)


def place_on_dp():
    d = lax.axis_index("dp")
    return lax.rem(d, 2), d // 2


def split_first(x, y, keep_ref, recv_ref):
    half = keep_ref.shape[-1] // 2
    part = lambda i, j, cols: keep_ref[i, j, :, cols] + recv_ref[i, j, :, cols]
    lo, hi = slice(0, half), slice(half, 2 * half)
    return ([part(s, 1 - x, lo) for s in range(2)], [part(1 - y, s, hi) for s in range(2)],
            [part(s, x, lo) for s in range(2)], [part(y, s, hi) for s in range(2)])


def first_kernel(keep_ref, recv_ref, to_x_ref, to_y_ref, keep_a_ref, keep_b_ref):
    parts = split_first(*place_on_dp(), keep_ref, recv_ref)
    for ref, pair in zip((to_x_ref, to_y_ref, keep_a_ref, keep_b_ref), parts):
        for s in range(2):
            ref[s] = pair[s]


def second_kernel(keep_a_ref, from_x_ref, keep_b_ref, from_y_ref, keep_ref, recv_ref,
                  to_x_ref, to_y_ref, next_a_ref, next_b_ref, keep2_a_ref, keep2_b_ref):
    x, y = place_on_dp()
    half = keep_a_ref.shape[-1]
    to_y_ref[:, :half] = keep_a_ref[1 - y] + from_x_ref[1 - y]
    to_x_ref[:, :half] = keep_b_ref[1 - x] + from_y_ref[1 - x]
    next_a_ref[...] = keep_a_ref[y] + from_x_ref[y]
    next_b_ref[...] = keep_b_ref[x] + from_y_ref[x]
    send_x, send_y, keep2_a, keep2_b = split_first(x, y, keep_ref, recv_ref)
    half2 = keep_ref.shape[-1] // 2
    for s in range(2):
        to_x_ref[:, half + s * half2:half + (s + 1) * half2] = send_x[s]
        to_y_ref[:, half + s * half2:half + (s + 1) * half2] = send_y[s]
        keep2_a_ref[s] = keep2_a[s]
        keep2_b_ref[s] = keep2_b[s]


def chip_bit(bit):
    return (lax.axis_index("rows") // 2) // (1 << bit) % 2


def halve(bit, send_ref, keep_ref, block):
    mine = chip_bit(bit)
    for i in range(send_ref.shape[0]):
        send_ref[i] = block(2 * i + 1 - mine)
        keep_ref[i] = block(2 * i + mine)


def third_kernel(next_a_ref, next_b_ref, from_x_ref, from_y_ref, keep2_a_ref, keep2_b_ref,
                 send_ref, keep_ref, to_x_ref, to_y_ref, next2_a_ref, next2_b_ref):
    x, y = place_on_dp()
    half, half2 = next_a_ref.shape[-1], keep2_a_ref.shape[-1]
    lo = slice(0, half)
    halve(0, send_ref, keep_ref, lambda at: jnp.concatenate(
        [next_a_ref[at] + from_y_ref[at, :, lo], next_b_ref[at] + from_x_ref[at, :, lo]], axis=1))
    blocks = [slice(half + s * half2, half + (s + 1) * half2) for s in range(2)]
    sum_a = [keep2_a_ref[s] + from_x_ref[:, :, blocks[s]] for s in range(2)]
    sum_b = [keep2_b_ref[s] + from_y_ref[:, :, blocks[s]] for s in range(2)]
    to_y_ref[...] = jnp.where(y == 0, sum_a[1], sum_a[0])
    next2_a_ref[...] = jnp.where(y == 0, sum_a[0], sum_a[1])
    to_x_ref[...] = jnp.where(x == 0, sum_b[1], sum_b[0])
    next2_b_ref[...] = jnp.where(x == 0, sum_b[0], sum_b[1])


def chips_kernel(tokens, bit, bit2, first, *refs):
    refs = list(refs)
    take = lambda n: [refs.pop(0) for _ in range(n)]
    inputs = take(2) if first else []
    inputs2 = take(4 if bit2 == 0 else 2)
    if first:
        keep_in, recv_in = inputs
        if bit is None:
            (total_ref,) = take(1)
            total_ref[...] = (keep_in[0] + recv_in[0]) * (1.0 / tokens)
        else:
            send_ref, keep_ref = take(2)
            halve(bit, send_ref, keep_ref, lambda at: keep_in[at] + recv_in[at])
    if bit2 is None:
        keep_in, recv_in = inputs2
        (total_ref,) = take(1)
        total_ref[...] = (keep_in[0] + recv_in[0]) * (1.0 / tokens)
    else:
        send_ref, keep_ref = take(2)
        if bit2 == 0:
            next_a, next_b, from_x, from_y = inputs2
            halve(0, send_ref, keep_ref, lambda at: jnp.concatenate(
                [next_a[at] + from_y[at], next_b[at] + from_x[at]], axis=1))
        else:
            keep_in, recv_in = inputs2
            halve(bit2, send_ref, keep_ref, lambda at: keep_in[at] + recv_in[at])


def gather_kernel(*refs):
    *pieces, grad_in_ref, grad_out_ref = refs
    dp = len(pieces) // 2
    d = lax.axis_index("dp")
    width = grad_out_ref.shape[-1]
    for k in range(dp):
        at = jnp.bitwise_xor(d, k)
        first = pieces[k].shape[-1]
        grad_out_ref[at] = pieces[k][:, :width]
        grad_in_ref[at, :, :first - width] = pieces[k][:, width:]
        grad_in_ref[at, :, first - width:] = pieces[dp + k][...]


def vmem():
    return pl.BlockSpec(memory_space=pltpu.VMEM)


def shape(*dims, dtype=f32):
    return jax.ShapeDtypeStruct(dims, dtype)


def call(kernel, name, out_shape, args, scalars=0, scratch=(), far=0, long=False, grant=4, apart=(), either=()):
    place = [None] * scalars + [pltpu.HBM] * far + [pltpu.VMEM] * (len(args) - scalars - far)
    held = [None if i in either else pltpu.HBM if i in apart else p for i, p in enumerate(place)]
    args = [a if p is None else pltpu.with_memory_space_constraint(a, p) for a, p in zip(args, held)]
    return pl.pallas_call(
        kernel,
        name=name,
        in_specs=[pl.BlockSpec(memory_space=p or pltpu.SMEM) for p in place],
        out_specs=[vmem()] * len(out_shape),
        out_shape=list(out_shape),
        scratch_shapes=[pltpu.VMEM(dims, dtype) for dims, dtype in scratch] + [pltpu.SemaphoreType.DMA((7,))] * (far > 0),
        compiler_params=pltpu.CompilerParams(vmem_limit_bytes=grant * MIB),
        cost_estimate=pl.CostEstimate(flops=100_000_000_000 if long else 1_000_000_000, bytes_accessed=1 << 16, transcendentals=0),
    )(*args)


def body(rows_size, dp_size, events, cotangent, lengths, event_slot, slot_row, slot_count, w_in, w_out, item_table, accumulator):
    tokens, width = events.shape
    owners, capacity = slot_row.shape[1:]
    chips = rows_size // 2
    piece = width // (rows_size * dp_size)
    cores = [(i, i ^ 1) for i in range(rows_size)]
    over_dp = lambda v, bit: lax.ppermute(v, "dp", [(i, i ^ bit) for i in range(dp_size)])
    over_chips = lambda v, bit: lax.ppermute(v, "rows", [(i, i ^ (2 << bit)) for i in range(rows_size)])
    after = lambda value, *others: lax.optimization_barrier((value, *others))[0]
    strip = chips * piece

    def gathered(total):
        return [total] + [over_dp(total, k) for k in range(1, dp_size)]

    by_dp = lambda v: v.reshape(2, 2, strip, v.shape[-1])
    by_chip = lambda v: v.reshape(*v.shape[:-2], chips, piece, v.shape[-1])
    bits = chips.bit_length() - 1
    far_off = lambda *dims, dtype=f32: pltpu.HBM(dims, dtype)
    local = lambda *dims, dtype=f32: pltpu.VMEM(dims, dtype)
    sides = lambda cols: [local(width // 2, cols)] * 2
    keep1, send1, hid, dsilu, gatt, gpre_uv, normed_t, events, cotangent, w_in = call(
        functools.partial(forward_kernel, rows_size, dp_size), "forward_part",
        sides(3 * width) + [
            local(tokens, 3 * width, dtype=bf16),
            local(tokens, 2 * width, dtype=bf16),
            local(tokens, width, dtype=bf16),
            local(tokens, 2 * width, dtype=bf16),
            local(width, tokens, dtype=bf16),
            local(tokens, width, dtype=bf16),
            local(tokens, width, dtype=bf16),
            local(*w_in.shape, dtype=bf16),
        ],
        (lengths, events, cotangent, w_in, w_out), 1,
        [((tokens, width), bf16), ((tokens, width), bf16), ((tokens, width), f32), ((tokens, width), f32),
         ((tokens, width), bf16), ((tokens, width), bf16), ((tokens, width), f32), ((HEADS, tokens, tokens), bf16),
         (w_out.shape, bf16)], far=4, long=True, grant=16)
    recv1 = lax.ppermute(send1, "rows", cores)
    keep2, send2, gpre_qk = call(
        attention_kernel, "attention_part", [far_off(width // 2, 2 * width)] * 2 + [local(tokens, 2 * width, dtype=bf16)],
        (lengths, hid, dsilu, gatt, normed_t), 1, long=True, grant=10)
    recv2 = lax.ppermute(send2, "rows", cores)
    pay_rows = capacity * (width // LANES) + ID_ROWS
    half1, half2 = 3 * width // 2, width
    to_x, to_y, keep_a, keep_b = call(
        first_kernel, "first_sums", [far_off(2, strip, half1)] * 4, (by_dp(keep1), by_dp(after(recv1, keep2))))
    gpre_uv = after(gpre_uv, to_x, to_y)
    (send,) = call(
        events_kernel, "events_part", [local(owners, pay_rows, LANES)],
        (lengths, events, cotangent, w_in, event_slot, slot_row[0].T, gpre_uv, gpre_qk), 1,
        [((tokens, width), bf16), ((tokens, width), bf16), ((owners * capacity, width), f32)], long=True, grant=10)
    recv = lax.all_to_all(send, ("dp", "rows"), split_axis=0, concat_axis=0, tiled=True)
    from_x, from_y = over_dp(to_x, 1), over_dp(to_y, 2)
    to_x, to_y, next_a, next_b, keep2_a, keep2_b = call(
        second_kernel, "second_sums",
        [local(strip, half1 + 2 * half2)] * 2 + [local(strip, half1)] * 2 + [local(2, strip, half2)] * 2,
        (after(keep_a, send), from_x, keep_b, from_y, by_dp(keep2), by_dp(recv2)), long=True, grant=10, apart=(0, 2, 4), either=(1, 3, 5))
    from_x, from_y = over_dp(to_x, 1), over_dp(to_y, 2)
    send1, keep1, to_x, to_y, next_a, next_b = call(
        third_kernel, "third_sums", [local(chips // 2, piece, 2 * half1)] * 2 + [local(chips, piece, half2)] * 4,
        [by_chip(v) for v in (next_a, next_b, from_x, from_y, keep2_a, keep2_b)])
    first = [keep1, over_chips(send1, 0)]
    second = [next_a, next_b, over_dp(to_x, 1), over_dp(to_y, 2)]
    pieces, at = [], 1
    while second is not None:
        bit, bit2 = at if at < bits else None, at - 1 if at - 1 < bits else None
        outs = []
        if first is not None:
            outs += [local(piece, 2 * half1)] if bit is None else [local(chips >> (bit + 1), piece, 2 * half1)] * 2
        outs += [local(piece, 2 * half2)] if bit2 is None else [local(chips >> (bit2 + 1), piece, 2 * half2)] * 2
        outs = list(call(
            functools.partial(chips_kernel, tokens, bit, bit2, first is not None), "chip_sums", outs, (first or []) + second))
        if first is not None:
            if bit is None:
                first, pieces = None, gathered(outs.pop(0))
            else:
                first = [outs[1], over_chips(outs[0], bit)]
                outs = outs[2:]
        if bit2 is None:
            second, pieces = None, pieces + gathered(outs[0])
        else:
            second = [outs[1], over_chips(outs[0], bit2)]
        at += 1
    slots = owners * capacity
    table_new, accum_new = call(
        table_kernel, "table_part", [shape(*item_table.shape), shape(*accumulator.shape)],
        (recv, item_table, accumulator), 0,
        [((slots, width), f32), ((slots, width), bf16), ((slots, width), bf16)], grant=10)
    pieces[-1] = after(pieces[-1], accum_new)
    grad_in, grad_out = call(
        gather_kernel, "gather", [shape(dp_size, piece, 4 * width), shape(dp_size, piece, width)], pieces)
    return grad_in.reshape(-1, 4 * width), grad_out.reshape(-1, width), table_new, accum_new


def solution(mesh):
    whole = P(("dp", "rows"))
    in_specs = (whole,) * 6 + (P(), P(), whole, whole)
    out_specs = (P("rows"), P("rows"), whole, whole)
    run = functools.partial(body, mesh.shape["rows"], mesh.shape["dp"])
    return jax.shard_map(run, mesh=mesh, in_specs=in_specs, out_specs=out_specs, check_vma=False)
```

```python
import functools

import jax
import jax.numpy as jnp
from jax import lax
from jax.experimental import pallas as pl
from jax.experimental.pallas import tpu as pltpu
from jax.sharding import PartitionSpec as P

HEADS = 4

norm_eps = 1e-05
adagrad_eps = 1e-10
learning_rate = 0.1

f32, bf16 = jnp.float32, jnp.bfloat16
MIB = 1024 * 1024
STEP = 256
LANES = 128
ID_ROWS = 8


def dot_nn(a, b):
    return lax.dot_general(a, b, (((1,), (0,)), ((), ())), preferred_element_type=f32)


def dot_nt(a, b):
    return lax.dot_general(a, b, (((1,), (1,)), ((), ())), preferred_element_type=f32)


def dot_tn(a, b):
    return lax.dot_general(a, b, (((0,), (0,)), ((), ())), preferred_element_type=f32)


def standardize(x):
    centered = x - jnp.mean(x, axis=-1, keepdims=True)
    inv = lax.rsqrt(jnp.mean(centered * centered, axis=-1, keepdims=True) + norm_eps)
    return centered * inv, inv


def masked_rows(cot, start, length):
    row = start + lax.broadcasted_iota(jnp.int32, cot.shape, 0)
    return jnp.where(row < length, cot.astype(f32), 0.0)


def owner_order(width, rows, dp):
    chips = rows // 2
    piece = width // (rows * dp)
    at = lax.broadcasted_iota(jnp.int32, (width, 1), 0)
    side, rest = at // (width // 2), at % (width // 2)
    part, rest = rest // (chips * piece), rest % (chips * piece)
    chip, row = rest // piece, rest % piece
    core = lax.rem(lax.axis_index("rows"), 2)
    core = jnp.where(side == 0, core, 1 - core)
    wanted = ((chip * 2 + core) * dp + part) * piece + row
    return jnp.where(lax.broadcasted_iota(jnp.int32, (width, width), 1) == wanted, 1.0, 0.0).astype(bf16)


def forward_kernel(rows_size, dp_size, len_ref, ev_hbm, cot_hbm, win_hbm, wout_hbm,
                   keep_ref, send_ref, hid_ref, dsilu_ref, gatt_ref, gpre_ref, normed_t_ref,
                   ev_ref, cot_ref, win_ref, normed_ref, user_ref, duser_ref, att_ref, mixed_ref, masked_ref, dval_ref, weights_ref,
                   wout_ref, arrived):
    tokens, width = ev_ref.shape
    copies = [pltpu.make_async_copy(ev_hbm, ev_ref, arrived.at[0])]
    for c in range(4):
        cols = pl.ds(c * width, width)
        copies.append(pltpu.make_async_copy(win_hbm.at[:, cols], win_ref.at[:, cols], arrived.at[1 + c]))
    copies.append(pltpu.make_async_copy(cot_hbm, cot_ref, arrived.at[5]))
    copies.append(pltpu.make_async_copy(wout_hbm, wout_ref, arrived.at[6]))
    for copy in copies:
        copy.start()
    hd = width // HEADS
    length = len_ref[0]
    inv_len = 1.0 / length.astype(f32)
    scale = hd ** -0.5
    steps = tokens // STEP

    copies[0].wait()
    for i in range(steps):
        rows = pl.ds(i * STEP, STEP)
        xhat, _ = standardize(ev_ref[rows, :].astype(f32))
        normed_ref[rows, :] = xhat.astype(bf16)

    def project(i, c):
        rows = pl.ds(i * STEP, STEP)
        pre = dot_nn(normed_ref[rows, :], win_ref[:, c * width:(c + 1) * width])
        sig = 0.5 + 0.5 * jnp.tanh(0.5 * pre)
        hid = pre * sig
        dsilu = sig * (1.0 + (pre - hid))
        if c == 0:
            user_ref[rows, :] = hid.astype(bf16)
            duser_ref[rows, :] = dsilu
        else:
            cols = slice((c - 1) * width, c * width)
            hid_ref[rows, cols] = hid.astype(bf16)
            if c == 1:
                dval_ref[rows, :] = dsilu
            else:
                dsilu_ref[rows, (c - 2) * width:(c - 1) * width] = dsilu.astype(bf16)

    for c in range(4):
        copies[1 + c].wait()
        for i in range(steps):
            project(i, c)

    tri = lax.broadcasted_iota(jnp.int32, (STEP, STEP), 0) >= lax.broadcasted_iota(jnp.int32, (STEP, STEP), 1)
    for h in range(HEADS):
        v_cols = slice(h * hd, (h + 1) * hd)
        q_cols = slice(width + h * hd, width + (h + 1) * hd)
        k_cols = slice(2 * width + h * hd, 2 * width + (h + 1) * hd)
        for i in range(steps):
            rows = pl.ds(i * STEP, STEP)
            query = hid_ref[rows, q_cols]
            total = None
            for j in range(i + 1):
                keys = pl.ds(j * STEP, STEP)
                half = dot_nt(query, hid_ref[keys, k_cols]) * (0.5 * scale)
                weights = (half + half * jnp.tanh(half)) * inv_len
                if i == j:
                    weights = jnp.where(tri, weights, 0.0)
                weights = weights.astype(bf16)
                weights_ref[h, rows, keys] = weights
                part = dot_nn(weights, hid_ref[keys, v_cols])
                total = part if total is None else total + part
            att_ref[rows, v_cols] = total

    copies[5].wait()
    copies[6].wait()
    for i in range(steps):
        rows = pl.ds(i * STEP, STEP)
        masked_ref[rows, :] = masked_rows(cot_ref[rows, :], i * STEP, length).astype(bf16)
        ahat, inv = standardize(att_ref[rows, :])
        user = user_ref[rows, :].astype(f32)
        mixed_ref[rows, :] = (ahat * user).astype(bf16)
        grad_mixed = dot_nt(masked_ref[rows, :], wout_ref[...])
        gpre_ref[rows, :width] = (grad_mixed * ahat * duser_ref[rows, :]).astype(bf16)
        e = grad_mixed * user
        gatt_ref[rows, :] = (inv * (e - jnp.mean(e, axis=-1, keepdims=True)
                                    - ahat * jnp.mean(e * ahat, axis=-1, keepdims=True))).astype(bf16)

    for h in range(HEADS):
        v_cols = slice(h * hd, (h + 1) * hd)
        for j in range(steps):
            keys, rest = pl.ds(j * STEP, STEP), pl.ds(j * STEP, tokens - j * STEP)
            grad_v = dot_tn(weights_ref[h, rest, keys], gatt_ref[rest, v_cols])
            gpre_ref[keys, width + h * hd:width + (h + 1) * hd] = (grad_v * dval_ref[keys, v_cols]).astype(bf16)

    order = owner_order(width, rows_size, dp_size)
    normed_t_ref[...] = dot_nt(order, normed_ref[...]).astype(bf16)
    mixed_t = dot_nt(order, mixed_ref[...]).astype(bf16)
    half = width // 2
    for ref, start in ((send_ref, half), (keep_ref, 0)):
        ref[:, :width] = dot_nn(mixed_t[start:start + half], masked_ref[...])
        ref[:, width:] = dot_nn(normed_t_ref[start:start + half, :], gpre_ref[...])


def attention_kernel(heads, len_ref, hid_ref, dsilu_ref, gatt_ref, *refs):
    *refs, gpre_ref = refs
    tokens, width = gatt_ref.shape
    hd = width // HEADS
    inv_len = 1.0 / len_ref[0].astype(f32)
    scale = hd ** -0.5
    steps = tokens // STEP
    base = gpre_ref.shape[1] // 2
    past = heads[0] * hd if refs else 0
    if refs:
        normed_t_ref, before_ref, keep_ref, send_ref = refs
        gpre_ref[:, :past] = before_ref[:, :past]
        gpre_ref[:, base:base + past] = before_ref[:, past:]

    tri = lax.broadcasted_iota(jnp.int32, (STEP, STEP), 0) <= lax.broadcasted_iota(jnp.int32, (STEP, STEP), 1)
    for h in heads:
        v_cols = slice(h * hd, (h + 1) * hd)
        q_cols = slice(width + h * hd, width + (h + 1) * hd)
        k_cols = slice(2 * width + h * hd, 2 * width + (h + 1) * hd)
        at = past + (h - heads[0]) * hd
        out_q, out_k = slice(at, at + hd), slice(base + at, base + at + hd)
        grad_q = [None] * steps
        for j in range(steps):
            keys = pl.ds(j * STEP, STEP)
            key, value = hid_ref[keys, k_cols], hid_ref[keys, v_cols]
            grad_k = None
            for i in range(j, steps):
                rows = pl.ds(i * STEP, STEP)
                query, gatt = hid_ref[rows, q_cols], gatt_ref[rows, v_cols]
                half = dot_nt(key, query) * (0.5 * scale)
                sig2 = 1.0 + jnp.tanh(half)
                silu = half * sig2
                dsilu = sig2 * ((1.0 + half) + (half - silu))
                gscore = dot_nt(value, gatt) * dsilu * (0.5 * inv_len * scale)
                if i == j:
                    gscore = jnp.where(tri, gscore, 0.0)
                gscore = gscore.astype(bf16)
                pk, pq = dot_nn(gscore, query), dot_tn(gscore, key)
                grad_k = pk if grad_k is None else grad_k + pk
                grad_q[i] = pq if grad_q[i] is None else grad_q[i] + pq
            gpre_ref[keys, out_k] = (grad_k * dsilu_ref[keys, q_cols].astype(f32)).astype(bf16)
        for i in range(steps):
            rows = pl.ds(i * STEP, STEP)
            gpre_ref[rows, out_q] = (grad_q[i] * dsilu_ref[rows, v_cols].astype(f32)).astype(bf16)

    if refs:
        half = width // 2
        for ref, start in ((send_ref, half), (keep_ref, 0)):
            ref[...] = dot_nn(normed_t_ref[start:start + half, :], gpre_ref[...])


def events_kernel(len_ref, ev_ref, cot_ref, win_ref, slot_ref, slot_row_ref, gpre_uv_ref, gpre_qk_ref,
                  send_ref, hi_ref, lo_ref, rows_ref):
    tokens, width = ev_ref.shape
    capacity, owners = slot_row_ref.shape
    length = len_ref[0]
    for i in range(tokens // STEP):
        rows = pl.ds(i * STEP, STEP)
        xhat, inv = standardize(ev_ref[rows, :].astype(f32))
        grad_normed = dot_nt(gpre_uv_ref[rows, :], win_ref[:, :2 * width]) + dot_nt(gpre_qk_ref[rows, :], win_ref[:, 2 * width:])
        grad = masked_rows(cot_ref[rows, :], i * STEP, length) + inv * (
            grad_normed - jnp.mean(grad_normed, axis=-1, keepdims=True)
            - xhat * jnp.mean(grad_normed * xhat, axis=-1, keepdims=True))
        high = grad.astype(bf16)
        hi_ref[rows, :] = high
        lo_ref[rows, :] = (grad - high.astype(f32)).astype(bf16)

    rows_ref[...] = one_hot_rows(slot_ref[...], rows_ref.shape[0], hi_ref, lo_ref)
    me = lax.axis_index(("dp", "rows"))
    lane = lax.broadcasted_iota(jnp.int32, (capacity, LANES), 1)
    place = lax.broadcasted_iota(jnp.int32, (capacity, LANES), 0) + lax.rem(me, LANES // capacity) * capacity
    spread = jnp.where(lane == place, 1.0, 0.0).astype(bf16)
    ids = slot_row_ref[...]
    ids = 16.0 * dot_tn((ids // 16).astype(bf16), spread) + dot_tn((ids % 16).astype(bf16), spread)
    tiles = width // LANES
    for o in range(owners):
        for t in range(tiles):
            send_ref[o, t * capacity:(t + 1) * capacity, :] = rows_ref[o * capacity:(o + 1) * capacity, t * LANES:(t + 1) * LANES]
        send_ref[o, tiles * capacity:, :] = jnp.broadcast_to(ids[o:o + 1, :], (ID_ROWS, LANES))


def one_hot_rows(ids, rows, hi_ref, lo_ref):
    named = lax.broadcasted_iota(jnp.int32, (rows, ids.shape[1]), 0) == ids
    onehot = jnp.where(named, 1.0, 0.0).astype(bf16)
    return dot_nn(onehot, hi_ref[...]) + dot_nn(onehot, lo_ref[...])


def table_kernel(recv_ref, table_ref, accum_ref, table_new_ref, accum_new_ref, rows_ref, hi_ref, lo_ref):
    owners = recv_ref.shape[0]
    rows, width = table_ref.shape
    tiles = width // LANES
    capacity = (recv_ref.shape[1] - ID_ROWS) // tiles
    for o in range(owners):
        for t in range(tiles):
            rows_ref[o * capacity:(o + 1) * capacity, t * LANES:(t + 1) * LANES] = recv_ref[o, t * capacity:(t + 1) * capacity, :]
    group = LANES // capacity
    ids = [sum(recv_ref[o, tiles * capacity:, :] for o in range(g, g + group)) for g in range(0, owners, group)]
    ids = jnp.concatenate(ids, axis=1)[:1, :].astype(jnp.int32)
    high = rows_ref[...].astype(bf16)
    hi_ref[...] = high
    lo_ref[...] = (rows_ref[...] - high.astype(f32)).astype(bf16)
    grad = one_hot_rows(ids, rows, hi_ref, lo_ref)
    accum = jnp.transpose(jnp.broadcast_to(accum_ref[...].reshape(1, rows), (8, rows)))[:, :1]
    accum_new = accum + jnp.mean(grad * grad, axis=-1, keepdims=True)
    accum_new_ref[...] = jnp.transpose(jnp.broadcast_to(accum_new, (rows, LANES)))[:1, :].reshape(rows)
    table_new_ref[...] = table_ref[...] - learning_rate * grad / (jnp.sqrt(accum_new) + adagrad_eps)


def place_on_dp():
    d = lax.axis_index("dp")
    return lax.rem(d, 2), d // 2


def split_first(x, y, keep_ref, recv_ref):
    half = keep_ref.shape[-1] // 2
    part = lambda i, j, cols: keep_ref[i, j, :, cols] + recv_ref[i, j, :, cols]
    lo, hi = slice(0, half), slice(half, 2 * half)
    return ([part(s, 1 - x, lo) for s in range(2)], [part(1 - y, s, hi) for s in range(2)],
            [part(s, x, lo) for s in range(2)], [part(y, s, hi) for s in range(2)])


def first_kernel(keep_ref, recv_ref, to_x_ref, to_y_ref, keep_a_ref, keep_b_ref):
    parts = split_first(*place_on_dp(), keep_ref, recv_ref)
    for ref, pair in zip((to_x_ref, to_y_ref, keep_a_ref, keep_b_ref), parts):
        for s in range(2):
            ref[s] = pair[s]


def second_kernel(keep_a_ref, from_x_ref, keep_b_ref, from_y_ref, keep_ref, recv_ref,
                  to_x_ref, to_y_ref, next_a_ref, next_b_ref, keep2_a_ref, keep2_b_ref):
    x, y = place_on_dp()
    half = keep_a_ref.shape[-1]
    to_y_ref[:, :half] = keep_a_ref[1 - y] + from_x_ref[1 - y]
    to_x_ref[:, :half] = keep_b_ref[1 - x] + from_y_ref[1 - x]
    next_a_ref[...] = keep_a_ref[y] + from_x_ref[y]
    next_b_ref[...] = keep_b_ref[x] + from_y_ref[x]
    send_x, send_y, keep2_a, keep2_b = split_first(x, y, keep_ref, recv_ref)
    half2 = keep_ref.shape[-1] // 2
    for s in range(2):
        to_x_ref[:, half + s * half2:half + (s + 1) * half2] = send_x[s]
        to_y_ref[:, half + s * half2:half + (s + 1) * half2] = send_y[s]
        keep2_a_ref[s] = keep2_a[s]
        keep2_b_ref[s] = keep2_b[s]


def chip_bit(bit):
    return (lax.axis_index("rows") // 2) // (1 << bit) % 2


def halve(bit, send_ref, keep_ref, block):
    mine = chip_bit(bit)
    for i in range(send_ref.shape[0]):
        send_ref[i] = block(2 * i + 1 - mine)
        keep_ref[i] = block(2 * i + mine)


def third_kernel(next_a_ref, next_b_ref, from_x_ref, from_y_ref, keep2_a_ref, keep2_b_ref,
                 send_ref, keep_ref, to_x_ref, to_y_ref, next2_a_ref, next2_b_ref):
    x, y = place_on_dp()
    half, half2 = next_a_ref.shape[-1], keep2_a_ref.shape[-1]
    lo = slice(0, half)
    halve(0, send_ref, keep_ref, lambda at: jnp.concatenate(
        [next_a_ref[at] + from_y_ref[at, :, lo], next_b_ref[at] + from_x_ref[at, :, lo]], axis=1))
    blocks = [slice(half + s * half2, half + (s + 1) * half2) for s in range(2)]
    sum_a = [keep2_a_ref[s] + from_x_ref[:, :, blocks[s]] for s in range(2)]
    sum_b = [keep2_b_ref[s] + from_y_ref[:, :, blocks[s]] for s in range(2)]
    to_y_ref[...] = jnp.where(y == 0, sum_a[1], sum_a[0])
    next2_a_ref[...] = jnp.where(y == 0, sum_a[0], sum_a[1])
    to_x_ref[...] = jnp.where(x == 0, sum_b[1], sum_b[0])
    next2_b_ref[...] = jnp.where(x == 0, sum_b[0], sum_b[1])


def chips_kernel(tokens, bit, bit2, first, *refs):
    refs = list(refs)
    take = lambda n: [refs.pop(0) for _ in range(n)]
    inputs = take(2) if first else []
    inputs2 = take(4 if bit2 == 0 else 2)
    if first:
        keep_in, recv_in = inputs
        if bit is None:
            (total_ref,) = take(1)
            total_ref[...] = (keep_in[0] + recv_in[0]) * (1.0 / tokens)
        else:
            send_ref, keep_ref = take(2)
            halve(bit, send_ref, keep_ref, lambda at: keep_in[at] + recv_in[at])
    if bit2 is None:
        keep_in, recv_in = inputs2
        (total_ref,) = take(1)
        total_ref[...] = (keep_in[0] + recv_in[0]) * (1.0 / tokens)
    else:
        send_ref, keep_ref = take(2)
        if bit2 == 0:
            next_a, next_b, from_x, from_y = inputs2
            halve(0, send_ref, keep_ref, lambda at: jnp.concatenate(
                [next_a[at] + from_y[at], next_b[at] + from_x[at]], axis=1))
        else:
            keep_in, recv_in = inputs2
            halve(bit2, send_ref, keep_ref, lambda at: keep_in[at] + recv_in[at])


def gather_kernel(*refs):
    *pieces, grad_in_ref, grad_out_ref = refs
    dp = len(pieces) // 2
    d = lax.axis_index("dp")
    width = grad_out_ref.shape[-1]
    for k in range(dp):
        at = jnp.bitwise_xor(d, k)
        first = pieces[k].shape[-1]
        grad_out_ref[at] = pieces[k][:, :width]
        grad_in_ref[at, :, :first - width] = pieces[k][:, width:]
        grad_in_ref[at, :, first - width:] = pieces[dp + k][...]


def vmem():
    return pl.BlockSpec(memory_space=pltpu.VMEM)


def shape(*dims, dtype=f32):
    return jax.ShapeDtypeStruct(dims, dtype)


def call(kernel, name, out_shape, args, scalars=0, scratch=(), far=0, long=False, grant=4, apart=(), either=()):
    place = [None] * scalars + [pltpu.HBM] * far + [pltpu.VMEM] * (len(args) - scalars - far)
    held = [None if i in either else pltpu.HBM if i in apart else p for i, p in enumerate(place)]
    args = [a if p is None else pltpu.with_memory_space_constraint(a, p) for a, p in zip(args, held)]
    return pl.pallas_call(
        kernel,
        name=name,
        in_specs=[pl.BlockSpec(memory_space=p or pltpu.SMEM) for p in place],
        out_specs=[vmem()] * len(out_shape),
        out_shape=list(out_shape),
        scratch_shapes=[pltpu.VMEM(dims, dtype) for dims, dtype in scratch] + [pltpu.SemaphoreType.DMA((7,))] * (far > 0),
        compiler_params=pltpu.CompilerParams(vmem_limit_bytes=grant * MIB),
        cost_estimate=pl.CostEstimate(flops=100_000_000_000 if long else 1_000_000_000, bytes_accessed=1 << 16, transcendentals=0),
    )(*args)


def body(rows_size, dp_size, events, cotangent, lengths, event_slot, slot_row, slot_count, w_in, w_out, item_table, accumulator):
    tokens, width = events.shape
    owners, capacity = slot_row.shape[1:]
    chips = rows_size // 2
    piece = width // (rows_size * dp_size)
    cores = [(i, i ^ 1) for i in range(rows_size)]
    over_dp = lambda v, bit: lax.ppermute(v, "dp", [(i, i ^ bit) for i in range(dp_size)])
    over_chips = lambda v, bit: lax.ppermute(v, "rows", [(i, i ^ (2 << bit)) for i in range(rows_size)])
    after = lambda value, *others: lax.optimization_barrier((value, *others))[0]
    strip = chips * piece

    def gathered(total):
        return [total] + [over_dp(total, k) for k in range(1, dp_size)]

    by_dp = lambda v: v.reshape(2, 2, strip, v.shape[-1])
    by_chip = lambda v: v.reshape(*v.shape[:-2], chips, piece, v.shape[-1])
    bits = chips.bit_length() - 1
    far_off = lambda *dims, dtype=f32: pltpu.HBM(dims, dtype)
    local = lambda *dims, dtype=f32: pltpu.VMEM(dims, dtype)
    sides = lambda cols: [local(width // 2, cols)] * 2
    keep1, send1, hid, dsilu, gatt, gpre_uv, normed_t, events, cotangent, w_in = call(
        functools.partial(forward_kernel, rows_size, dp_size), "forward_part",
        sides(3 * width) + [
            local(tokens, 3 * width, dtype=bf16),
            local(tokens, 2 * width, dtype=bf16),
            local(tokens, width, dtype=bf16),
            local(tokens, 2 * width, dtype=bf16),
            local(width, tokens, dtype=bf16),
            local(tokens, width, dtype=bf16),
            local(tokens, width, dtype=bf16),
            local(*w_in.shape, dtype=bf16),
        ],
        (lengths, events, cotangent, w_in, w_out), 1,
        [((tokens, width), bf16), ((tokens, width), bf16), ((tokens, width), f32), ((tokens, width), f32),
         ((tokens, width), bf16), ((tokens, width), bf16), ((tokens, width), f32), ((HEADS, tokens, tokens), bf16),
         (w_out.shape, bf16)], far=4, long=True, grant=16)
    recv1 = lax.ppermute(send1, "rows", cores)
    heads = list(range(HEADS))
    (gpre_some,) = call(
        functools.partial(attention_kernel, heads[:HEADS // 2]), "attention_first", [local(tokens, width, dtype=bf16)],
        (lengths, hid, dsilu, gatt), 1, long=True, grant=10)
    half1, half2 = 3 * width // 2, width
    to_x, to_y, keep_a, keep_b = call(
        first_kernel, "first_sums", [local(2, strip, half1)] * 4, (by_dp(keep1), by_dp(after(recv1, gpre_some))))
    keep2, send2, gpre_qk = call(
        functools.partial(attention_kernel, heads[HEADS // 2:]), "attention_second",
        [local(width // 2, 2 * width)] * 2 + [local(tokens, 2 * width, dtype=bf16)],
        (lengths, hid, dsilu, after(gatt, to_x, to_y), normed_t, gpre_some), 1, long=True, grant=10)
    recv2 = lax.ppermute(send2, "rows", cores)
    pay_rows = capacity * (width // LANES) + ID_ROWS
    (send,) = call(
        events_kernel, "events_part", [local(owners, pay_rows, LANES)],
        (lengths, events, cotangent, w_in, event_slot, slot_row[0].T, gpre_uv, gpre_qk), 1,
        [((tokens, width), bf16), ((tokens, width), bf16), ((owners * capacity, width), f32)], grant=10)
    from_x, from_y = over_dp(to_x, 1), over_dp(to_y, 2)
    to_x, to_y, next_a, next_b, keep2_a, keep2_b = call(
        second_kernel, "second_sums",
        [local(strip, half1 + 2 * half2)] * 2 + [far_off(strip, half1)] * 2 + [far_off(2, strip, half2)] * 2,
        (after(keep_a, send), from_x, keep_b, from_y, by_dp(keep2), by_dp(recv2)))
    recv = lax.all_to_all(after(send, to_x, to_y), ("dp", "rows"), split_axis=0, concat_axis=0, tiled=True)
    from_x, from_y = over_dp(to_x, 1), over_dp(to_y, 2)
    send1, keep1, to_x, to_y, next_a, next_b = call(
        third_kernel, "third_sums", [local(chips // 2, piece, 2 * half1)] * 2 + [local(chips, piece, half2)] * 4,
        [by_chip(v) for v in (next_a, next_b, from_x, from_y, keep2_a, keep2_b)],
        long=True, grant=10, apart=(0, 1, 4, 5), either=(2, 3))
    first = [keep1, over_chips(send1, 0)]
    second = [next_a, next_b, over_dp(to_x, 1), over_dp(to_y, 2)]
    pieces, at = [], 1
    while second is not None:
        bit, bit2 = at if at < bits else None, at - 1 if at - 1 < bits else None
        outs = []
        if first is not None:
            outs += [local(piece, 2 * half1)] if bit is None else [local(chips >> (bit + 1), piece, 2 * half1)] * 2
        outs += [local(piece, 2 * half2)] if bit2 is None else [local(chips >> (bit2 + 1), piece, 2 * half2)] * 2
        if pieces:
            second[0] = after(second[0], *pieces)
        outs = list(call(
            functools.partial(chips_kernel, tokens, bit, bit2, first is not None), "chip_sums", outs, (first or []) + second))
        if first is not None:
            if bit is None:
                first, pieces = None, gathered(outs.pop(0))
            else:
                first = [outs[1], over_chips(outs[0], bit)]
                outs = outs[2:]
        if bit2 is None:
            second, pieces = None, pieces + gathered(outs[0])
        else:
            second = [outs[1], over_chips(outs[0], bit2)]
        at += 1
    slots = owners * capacity
    table_new, accum_new = call(
        table_kernel, "table_part", [shape(*item_table.shape), shape(*accumulator.shape)],
        (recv, item_table, accumulator), 0,
        [((slots, width), f32), ((slots, width), bf16), ((slots, width), bf16)], grant=10)
    pieces[-1] = after(pieces[-1], accum_new)
    grad_in, grad_out = call(
        gather_kernel, "gather", [shape(dp_size, piece, 4 * width), shape(dp_size, piece, width)], pieces)
    return grad_in.reshape(-1, 4 * width), grad_out.reshape(-1, width), table_new, accum_new


def solution(mesh):
    whole = P(("dp", "rows"))
    in_specs = (whole,) * 6 + (P(), P(), whole, whole)
    out_specs = (P("rows"), P("rows"), whole, whole)
    run = functools.partial(body, mesh.shape["rows"], mesh.shape["dp"])
    return jax.shard_map(run, mesh=mesh, in_specs=in_specs, out_specs=out_specs, check_vma=False)
```

```python
import functools

import jax
import jax.numpy as jnp
from jax import lax
from jax.experimental import pallas as pl
from jax.experimental.pallas import tpu as pltpu
from jax.sharding import PartitionSpec as P

HEADS = 4

norm_eps = 1e-05
adagrad_eps = 1e-10
learning_rate = 0.1

f32, bf16 = jnp.float32, jnp.bfloat16
MIB = 1024 * 1024
STEP = 256
LANES = 128
ID_ROWS = 8


def dot_nn(a, b):
    return lax.dot_general(a, b, (((1,), (0,)), ((), ())), preferred_element_type=f32)


def dot_nt(a, b):
    return lax.dot_general(a, b, (((1,), (1,)), ((), ())), preferred_element_type=f32)


def dot_tn(a, b):
    return lax.dot_general(a, b, (((0,), (0,)), ((), ())), preferred_element_type=f32)


def standardize(x):
    centered = x - jnp.mean(x, axis=-1, keepdims=True)
    inv = lax.rsqrt(jnp.mean(centered * centered, axis=-1, keepdims=True) + norm_eps)
    return centered * inv, inv


def masked_rows(cot, start, length):
    row = start + lax.broadcasted_iota(jnp.int32, cot.shape, 0)
    return jnp.where(row < length, cot.astype(f32), 0.0)


def owner_order(width, rows, dp):
    chips = rows // 2
    piece = width // (rows * dp)
    at = lax.broadcasted_iota(jnp.int32, (width, 1), 0)
    side, rest = at // (width // 2), at % (width // 2)
    part, rest = rest // (chips * piece), rest % (chips * piece)
    chip, row = rest // piece, rest % piece
    core = lax.rem(lax.axis_index("rows"), 2)
    core = jnp.where(side == 0, core, 1 - core)
    wanted = ((chip * 2 + core) * dp + part) * piece + row
    return jnp.where(lax.broadcasted_iota(jnp.int32, (width, width), 1) == wanted, 1.0, 0.0).astype(bf16)


def forward_kernel(rows_size, dp_size, len_ref, ev_hbm, cot_hbm, win_hbm, wout_hbm,
                   keep_ref, send_ref, hid_ref, dsilu_ref, gatt_ref, gpre_ref, normed_t_ref,
                   ev_ref, cot_ref, win_ref, normed_ref, user_ref, duser_ref, att_ref, mixed_ref, masked_ref, dval_ref, weights_ref,
                   wout_ref, arrived):
    tokens, width = ev_ref.shape
    copies = [pltpu.make_async_copy(ev_hbm, ev_ref, arrived.at[0])]
    for c in range(4):
        cols = pl.ds(c * width, width)
        copies.append(pltpu.make_async_copy(win_hbm.at[:, cols], win_ref.at[:, cols], arrived.at[1 + c]))
    copies.append(pltpu.make_async_copy(cot_hbm, cot_ref, arrived.at[5]))
    copies.append(pltpu.make_async_copy(wout_hbm, wout_ref, arrived.at[6]))
    for copy in copies:
        copy.start()
    hd = width // HEADS
    length = len_ref[0]
    inv_len = 1.0 / length.astype(f32)
    scale = hd ** -0.5
    steps = tokens // STEP

    copies[0].wait()
    for i in range(steps):
        rows = pl.ds(i * STEP, STEP)
        xhat, _ = standardize(ev_ref[rows, :].astype(f32))
        normed_ref[rows, :] = xhat.astype(bf16)

    def project(i, c):
        rows = pl.ds(i * STEP, STEP)
        pre = dot_nn(normed_ref[rows, :], win_ref[:, c * width:(c + 1) * width])
        sig = 0.5 + 0.5 * jnp.tanh(0.5 * pre)
        hid = pre * sig
        dsilu = sig * (1.0 + (pre - hid))
        if c == 0:
            user_ref[rows, :] = hid.astype(bf16)
            duser_ref[rows, :] = dsilu
        else:
            cols = slice((c - 1) * width, c * width)
            hid_ref[rows, cols] = hid.astype(bf16)
            if c == 1:
                dval_ref[rows, :] = dsilu
            else:
                dsilu_ref[rows, (c - 2) * width:(c - 1) * width] = dsilu.astype(bf16)

    for c in range(4):
        copies[1 + c].wait()
        for i in range(steps):
            project(i, c)

    tri = lax.broadcasted_iota(jnp.int32, (STEP, STEP), 0) >= lax.broadcasted_iota(jnp.int32, (STEP, STEP), 1)
    for h in range(HEADS):
        v_cols = slice(h * hd, (h + 1) * hd)
        q_cols = slice(width + h * hd, width + (h + 1) * hd)
        k_cols = slice(2 * width + h * hd, 2 * width + (h + 1) * hd)
        for i in range(steps):
            rows = pl.ds(i * STEP, STEP)
            query = hid_ref[rows, q_cols]
            total = None
            for j in range(i + 1):
                keys = pl.ds(j * STEP, STEP)
                half = dot_nt(query, hid_ref[keys, k_cols]) * (0.5 * scale)
                weights = (half + half * jnp.tanh(half)) * inv_len
                if i == j:
                    weights = jnp.where(tri, weights, 0.0)
                weights = weights.astype(bf16)
                weights_ref[h, rows, keys] = weights
                part = dot_nn(weights, hid_ref[keys, v_cols])
                total = part if total is None else total + part
            att_ref[rows, v_cols] = total

    copies[5].wait()
    copies[6].wait()
    for i in range(steps):
        rows = pl.ds(i * STEP, STEP)
        masked_ref[rows, :] = masked_rows(cot_ref[rows, :], i * STEP, length).astype(bf16)
        ahat, inv = standardize(att_ref[rows, :])
        user = user_ref[rows, :].astype(f32)
        mixed_ref[rows, :] = (ahat * user).astype(bf16)
        grad_mixed = dot_nt(masked_ref[rows, :], wout_ref[...])
        gpre_ref[rows, :width] = (grad_mixed * ahat * duser_ref[rows, :]).astype(bf16)
        e = grad_mixed * user
        gatt_ref[rows, :] = (inv * (e - jnp.mean(e, axis=-1, keepdims=True)
                                    - ahat * jnp.mean(e * ahat, axis=-1, keepdims=True))).astype(bf16)

    for h in range(HEADS):
        v_cols = slice(h * hd, (h + 1) * hd)
        for j in range(steps):
            keys, rest = pl.ds(j * STEP, STEP), pl.ds(j * STEP, tokens - j * STEP)
            grad_v = dot_tn(weights_ref[h, rest, keys], gatt_ref[rest, v_cols])
            gpre_ref[keys, width + h * hd:width + (h + 1) * hd] = (grad_v * dval_ref[keys, v_cols]).astype(bf16)

    order = owner_order(width, rows_size, dp_size)
    normed_t_ref[...] = dot_nt(order, normed_ref[...]).astype(bf16)
    mixed_t = dot_nt(order, mixed_ref[...]).astype(bf16)
    half = width // 2
    for ref, start in ((send_ref, half), (keep_ref, 0)):
        ref[:, :width] = dot_nn(mixed_t[start:start + half], masked_ref[...])
        ref[:, width:] = dot_nn(normed_t_ref[start:start + half, :], gpre_ref[...])


def attention_kernel(len_ref, hid_ref, dsilu_ref, gatt_ref, normed_t_ref, keep_ref, send_ref, gpre_ref):
    tokens, width = gatt_ref.shape
    hd = width // HEADS
    inv_len = 1.0 / len_ref[0].astype(f32)
    scale = hd ** -0.5
    steps = tokens // STEP

    tri = lax.broadcasted_iota(jnp.int32, (STEP, STEP), 0) <= lax.broadcasted_iota(jnp.int32, (STEP, STEP), 1)
    for h in range(HEADS):
        v_cols = slice(h * hd, (h + 1) * hd)
        q_cols = slice(width + h * hd, width + (h + 1) * hd)
        k_cols = slice(2 * width + h * hd, 2 * width + (h + 1) * hd)
        grad_q = [None] * steps
        for j in range(steps):
            keys = pl.ds(j * STEP, STEP)
            key, value = hid_ref[keys, k_cols], hid_ref[keys, v_cols]
            grad_k = None
            for i in range(j, steps):
                rows = pl.ds(i * STEP, STEP)
                query, gatt = hid_ref[rows, q_cols], gatt_ref[rows, v_cols]
                half = dot_nt(key, query) * (0.5 * scale)
                sig2 = 1.0 + jnp.tanh(half)
                silu = half * sig2
                dsilu = sig2 * ((1.0 + half) + (half - silu))
                gscore = dot_nt(value, gatt) * dsilu * (0.5 * inv_len * scale)
                if i == j:
                    gscore = jnp.where(tri, gscore, 0.0)
                gscore = gscore.astype(bf16)
                pk, pq = dot_nn(gscore, query), dot_tn(gscore, key)
                grad_k = pk if grad_k is None else grad_k + pk
                grad_q[i] = pq if grad_q[i] is None else grad_q[i] + pq
            gpre_ref[keys, q_cols] = (grad_k * dsilu_ref[keys, q_cols].astype(f32)).astype(bf16)
        for i in range(steps):
            rows = pl.ds(i * STEP, STEP)
            gpre_ref[rows, v_cols] = (grad_q[i] * dsilu_ref[rows, v_cols].astype(f32)).astype(bf16)

    half = width // 2
    for ref, start in ((send_ref, half), (keep_ref, 0)):
        ref[...] = dot_nn(normed_t_ref[start:start + half, :], gpre_ref[...])


def events_kernel(len_ref, ev_ref, cot_ref, win_ref, slot_ref, slot_row_ref, gpre_uv_ref, gpre_qk_ref,
                  send_ref, hi_ref, lo_ref, rows_ref):
    tokens, width = ev_ref.shape
    capacity, owners = slot_row_ref.shape
    length = len_ref[0]
    for i in range(tokens // STEP):
        rows = pl.ds(i * STEP, STEP)
        xhat, inv = standardize(ev_ref[rows, :].astype(f32))
        grad_normed = dot_nt(gpre_uv_ref[rows, :], win_ref[:, :2 * width]) + dot_nt(gpre_qk_ref[rows, :], win_ref[:, 2 * width:])
        grad = masked_rows(cot_ref[rows, :], i * STEP, length) + inv * (
            grad_normed - jnp.mean(grad_normed, axis=-1, keepdims=True)
            - xhat * jnp.mean(grad_normed * xhat, axis=-1, keepdims=True))
        high = grad.astype(bf16)
        hi_ref[rows, :] = high
        lo_ref[rows, :] = (grad - high.astype(f32)).astype(bf16)

    rows_ref[...] = one_hot_rows(slot_ref[...], rows_ref.shape[0], hi_ref, lo_ref)
    me = lax.axis_index(("dp", "rows"))
    lane = lax.broadcasted_iota(jnp.int32, (capacity, LANES), 1)
    place = lax.broadcasted_iota(jnp.int32, (capacity, LANES), 0) + lax.rem(me, LANES // capacity) * capacity
    spread = jnp.where(lane == place, 1.0, 0.0).astype(bf16)
    ids = slot_row_ref[...]
    ids = 16.0 * dot_tn((ids // 16).astype(bf16), spread) + dot_tn((ids % 16).astype(bf16), spread)
    tiles = width // LANES
    for o in range(owners):
        for t in range(tiles):
            send_ref[o, t * capacity:(t + 1) * capacity, :] = rows_ref[o * capacity:(o + 1) * capacity, t * LANES:(t + 1) * LANES]
        send_ref[o, tiles * capacity:, :] = jnp.broadcast_to(ids[o:o + 1, :], (ID_ROWS, LANES))


def one_hot_rows(ids, rows, hi_ref, lo_ref):
    named = lax.broadcasted_iota(jnp.int32, (rows, ids.shape[1]), 0) == ids
    onehot = jnp.where(named, 1.0, 0.0).astype(bf16)
    return dot_nn(onehot, hi_ref[...]) + dot_nn(onehot, lo_ref[...])


def table_kernel(recv_ref, table_ref, accum_ref, table_new_ref, accum_new_ref, rows_ref, hi_ref, lo_ref):
    owners = recv_ref.shape[0]
    rows, width = table_ref.shape
    tiles = width // LANES
    capacity = (recv_ref.shape[1] - ID_ROWS) // tiles
    for o in range(owners):
        for t in range(tiles):
            rows_ref[o * capacity:(o + 1) * capacity, t * LANES:(t + 1) * LANES] = recv_ref[o, t * capacity:(t + 1) * capacity, :]
    group = LANES // capacity
    ids = [sum(recv_ref[o, tiles * capacity:, :] for o in range(g, g + group)) for g in range(0, owners, group)]
    ids = jnp.concatenate(ids, axis=1)[:1, :].astype(jnp.int32)
    high = rows_ref[...].astype(bf16)
    hi_ref[...] = high
    lo_ref[...] = (rows_ref[...] - high.astype(f32)).astype(bf16)
    grad = one_hot_rows(ids, rows, hi_ref, lo_ref)
    accum = jnp.transpose(jnp.broadcast_to(accum_ref[...].reshape(1, rows), (8, rows)))[:, :1]
    accum_new = accum + jnp.mean(grad * grad, axis=-1, keepdims=True)
    accum_new_ref[...] = jnp.transpose(jnp.broadcast_to(accum_new, (rows, LANES)))[:1, :].reshape(rows)
    table_new_ref[...] = table_ref[...] - learning_rate * grad / (jnp.sqrt(accum_new) + adagrad_eps)


def place_on_dp():
    d = lax.axis_index("dp")
    return lax.rem(d, 2), d // 2


def first_kernel(keep1_ref, recv1_ref, keep2_ref, recv2_ref, to_x_ref, to_y_ref, keep_a_ref, keep_b_ref):
    x, y = place_on_dp()
    start = 0
    for keep_ref, recv_ref in ((keep1_ref, recv1_ref), (keep2_ref, recv2_ref)):
        half = keep_ref.shape[-1] // 2
        part = lambda i, j, cols: keep_ref[i, j, :, cols] + recv_ref[i, j, :, cols]
        lo, hi, out = slice(0, half), slice(half, 2 * half), slice(start, start + half)
        for s in range(2):
            to_x_ref[s, :, out] = part(s, 1 - x, lo)
            to_y_ref[s, :, out] = part(1 - y, s, hi)
            keep_a_ref[s, :, out] = part(s, x, lo)
            keep_b_ref[s, :, out] = part(y, s, hi)
        start += half


def second_kernel(keep_a_ref, from_x_ref, keep_b_ref, from_y_ref, to_y_ref, to_x_ref, next_a_ref, next_b_ref):
    x, y = place_on_dp()
    to_y_ref[...] = keep_a_ref[1 - y] + from_x_ref[1 - y]
    to_x_ref[...] = keep_b_ref[1 - x] + from_y_ref[1 - x]
    next_a_ref[...] = keep_a_ref[y] + from_x_ref[y]
    next_b_ref[...] = keep_b_ref[x] + from_y_ref[x]


def chip_bit(bit):
    return (lax.axis_index("rows") // 2) // (1 << bit) % 2


def halve(bit, send_ref, keep_ref, block):
    mine = chip_bit(bit)
    for i in range(send_ref.shape[0]):
        send_ref[i] = block(2 * i + 1 - mine)
        keep_ref[i] = block(2 * i + mine)


def chip_first_kernel(next_a_ref, from_y_ref, next_b_ref, from_x_ref, send_ref, keep_ref):
    halve(0, send_ref, keep_ref, lambda at: jnp.concatenate(
        [next_a_ref[at] + from_y_ref[at], next_b_ref[at] + from_x_ref[at]], axis=1))


def chip_kernel(bit, keep_in, recv_in, send_ref, keep_ref):
    halve(bit, send_ref, keep_ref, lambda at: keep_in[at] + recv_in[at])


def total_kernel(tokens, keep_ref, recv_ref, out_ref):
    out_ref[...] = (keep_ref[0] + recv_ref[0]) * (1.0 / tokens)


def gather_kernel(*refs):
    *pieces, grad_in_ref, grad_out_ref = refs
    d = lax.axis_index("dp")
    width = grad_out_ref.shape[-1]
    half = width // 2
    for k, piece in enumerate(pieces):
        at = jnp.bitwise_xor(d, k)
        grad_out_ref[at] = piece[:, :width]
        start = width
        for cols, first in ((half, 0), (width, 2 * width), (half, half), (width, width), (width, 3 * width)):
            grad_in_ref[at, :, first:first + cols] = piece[:, start:start + cols]
            start += cols


def vmem():
    return pl.BlockSpec(memory_space=pltpu.VMEM)


def shape(*dims, dtype=f32):
    return jax.ShapeDtypeStruct(dims, dtype)


def call(kernel, name, out_shape, args, scalars=0, scratch=(), far=0, long=False, grant=4, apart=(), either=()):
    place = [None] * scalars + [pltpu.HBM] * far + [pltpu.VMEM] * (len(args) - scalars - far)
    held = [None if i in either else pltpu.HBM if i in apart else p for i, p in enumerate(place)]
    args = [a if p is None else pltpu.with_memory_space_constraint(a, p) for a, p in zip(args, held)]
    return pl.pallas_call(
        kernel,
        name=name,
        in_specs=[pl.BlockSpec(memory_space=p or pltpu.SMEM) for p in place],
        out_specs=[vmem()] * len(out_shape),
        out_shape=list(out_shape),
        scratch_shapes=[pltpu.VMEM(dims, dtype) for dims, dtype in scratch] + [pltpu.SemaphoreType.DMA((7,))] * (far > 0),
        compiler_params=pltpu.CompilerParams(vmem_limit_bytes=grant * MIB),
        cost_estimate=pl.CostEstimate(flops=100_000_000_000 if long else 1_000_000_000, bytes_accessed=1 << 16, transcendentals=0),
    )(*args)


def body(rows_size, dp_size, events, cotangent, lengths, event_slot, slot_row, slot_count, w_in, w_out, item_table, accumulator):
    tokens, width = events.shape
    owners, capacity = slot_row.shape[1:]
    chips = rows_size // 2
    piece = width // (rows_size * dp_size)
    cores = [(i, i ^ 1) for i in range(rows_size)]
    over_dp = lambda v, bit: lax.ppermute(v, "dp", [(i, i ^ bit) for i in range(dp_size)])
    over_chips = lambda v, bit: lax.ppermute(v, "rows", [(i, i ^ (2 << bit)) for i in range(rows_size)])
    after = lambda value, *others: lax.optimization_barrier((value, *others))[0]
    strip = chips * piece

    def gathered(total):
        return [total] + [over_dp(total, k) for k in range(1, dp_size)]

    by_dp = lambda v: v.reshape(2, 2, strip, v.shape[-1])
    by_chip = lambda v: v.reshape(*v.shape[:-2], chips, piece, v.shape[-1])
    bits = chips.bit_length() - 1
    far_off = lambda *dims, dtype=f32: pltpu.HBM(dims, dtype)
    local = lambda *dims, dtype=f32: pltpu.VMEM(dims, dtype)
    sides = lambda cols: [local(width // 2, cols)] * 2
    keep1, send1, hid, dsilu, gatt, gpre_uv, normed_t, events, cotangent, w_in = call(
        functools.partial(forward_kernel, rows_size, dp_size), "forward_part",
        sides(3 * width) + [
            local(tokens, 3 * width, dtype=bf16),
            local(tokens, 2 * width, dtype=bf16),
            local(tokens, width, dtype=bf16),
            local(tokens, 2 * width, dtype=bf16),
            local(width, tokens, dtype=bf16),
            local(tokens, width, dtype=bf16),
            local(tokens, width, dtype=bf16),
            local(*w_in.shape, dtype=bf16),
        ],
        (lengths, events, cotangent, w_in, w_out), 1,
        [((tokens, width), bf16), ((tokens, width), bf16), ((tokens, width), f32), ((tokens, width), f32),
         ((tokens, width), bf16), ((tokens, width), bf16), ((tokens, width), f32), ((HEADS, tokens, tokens), bf16),
         (w_out.shape, bf16)], far=4, long=True, grant=16)
    recv1 = lax.ppermute(send1, "rows", cores)
    keep2, send2, gpre_qk = call(
        attention_kernel, "attention_part", sides(2 * width) + [local(tokens, 2 * width, dtype=bf16)],
        (lengths, hid, dsilu, gatt, normed_t), 1, long=True, grant=10)
    recv2 = lax.ppermute(send2, "rows", cores)
    pay_rows = capacity * (width // LANES) + ID_ROWS
    (send,) = call(
        events_kernel, "events_part", [local(owners, pay_rows, LANES)],
        (lengths, events, cotangent, w_in, event_slot, slot_row[0].T, gpre_uv, gpre_qk), 1,
        [((tokens, width), bf16), ((tokens, width), bf16), ((owners * capacity, width), f32)], grant=10)
    cols = w_in.shape[1] + width
    to_x, to_y, keep_a, keep_b = call(
        first_kernel, "first_sums", [local(2, strip, cols // 2)] * 2 + [far_off(2, strip, cols // 2)] * 2,
        [by_dp(v) for v in (after(keep1, send), recv1, keep2, recv2)])
    recv = lax.all_to_all(after(send, to_x, to_y), ("dp", "rows"), split_axis=0, concat_axis=0, tiled=True)
    from_x, from_y = over_dp(to_x, 1), over_dp(to_y, 2)
    to_y, to_x, next_a, next_b = call(
        second_kernel, "second_sums", [local(strip, cols // 2)] * 4, (keep_a, from_x, keep_b, from_y),
        long=True, grant=10, apart=(0, 2), either=(1, 3))
    from_y, from_x = over_dp(to_y, 2), over_dp(to_x, 1)
    send, keep = call(
        chip_first_kernel, "chip_sums", [local(chips // 2, piece, cols)] * 2,
        [by_chip(v) for v in (next_a, from_y, next_b, from_x)])
    for bit in range(1, bits):
        send, keep = call(
            functools.partial(chip_kernel, bit), "chip_sums", [local(chips >> (bit + 1), piece, cols)] * 2,
            (keep, over_chips(send, bit - 1)))
    (total,) = call(
        functools.partial(total_kernel, tokens), "total", [local(piece, cols)], (keep, over_chips(send, bits - 1)))
    pieces = gathered(total)
    slots = owners * capacity
    table_new, accum_new = call(
        table_kernel, "table_part", [shape(*item_table.shape), shape(*accumulator.shape)],
        (recv, item_table, accumulator), 0,
        [((slots, width), f32), ((slots, width), bf16), ((slots, width), bf16)], grant=10)
    pieces[-1] = after(pieces[-1], accum_new)
    grad_in, grad_out = call(
        gather_kernel, "gather", [shape(dp_size, piece, 4 * width), shape(dp_size, piece, width)], pieces)
    return grad_in.reshape(-1, 4 * width), grad_out.reshape(-1, width), table_new, accum_new


def solution(mesh):
    whole = P(("dp", "rows"))
    in_specs = (whole,) * 6 + (P(), P(), whole, whole)
    out_specs = (P("rows"), P("rows"), whole, whole)
    run = functools.partial(body, mesh.shape["rows"], mesh.shape["dp"])
    return jax.shard_map(run, mesh=mesh, in_specs=in_specs, out_specs=out_specs, check_vma=False)
```

```python
import functools

import jax
import jax.numpy as jnp
from jax import lax
from jax.experimental import pallas as pl
from jax.experimental.pallas import tpu as pltpu
from jax.sharding import PartitionSpec as P

HEADS = 4

norm_eps = 1e-05
adagrad_eps = 1e-10
learning_rate = 0.1

f32, bf16 = jnp.float32, jnp.bfloat16
MIB = 1024 * 1024
STEP = 256
LANES = 128
ID_ROWS = 8


def dot_nn(a, b):
    return lax.dot_general(a, b, (((1,), (0,)), ((), ())), preferred_element_type=f32)


def dot_nt(a, b):
    return lax.dot_general(a, b, (((1,), (1,)), ((), ())), preferred_element_type=f32)


def dot_tn(a, b):
    return lax.dot_general(a, b, (((0,), (0,)), ((), ())), preferred_element_type=f32)


def standardize(x):
    centered = x - jnp.mean(x, axis=-1, keepdims=True)
    inv = lax.rsqrt(jnp.mean(centered * centered, axis=-1, keepdims=True) + norm_eps)
    return centered * inv, inv


def masked_rows(cot, start, length):
    row = start + lax.broadcasted_iota(jnp.int32, cot.shape, 0)
    return jnp.where(row < length, cot.astype(f32), 0.0)


def owner_order(width, rows, dp):
    chips = rows // 2
    piece = width // (rows * dp)
    at = lax.broadcasted_iota(jnp.int32, (width, 1), 0)
    side, rest = at // (width // 2), at % (width // 2)
    part, rest = rest // (chips * piece), rest % (chips * piece)
    chip, row = rest // piece, rest % piece
    core = lax.rem(lax.axis_index("rows"), 2)
    core = jnp.where(side == 0, core, 1 - core)
    wanted = ((chip * 2 + core) * dp + part) * piece + row
    return jnp.where(lax.broadcasted_iota(jnp.int32, (width, width), 1) == wanted, 1.0, 0.0).astype(bf16)


def forward_kernel(rows_size, dp_size, len_ref, ev_hbm, cot_hbm, win_hbm, wout_hbm,
                   keep_ref, send_ref, hid_ref, dsilu_ref, gatt_ref, gpre_ref, normed_t_ref,
                   ev_ref, cot_ref, win_ref, normed_ref, user_ref, duser_ref, att_ref, mixed_ref, masked_ref, dval_ref, weights_ref,
                   wout_ref, arrived):
    tokens, width = ev_ref.shape
    copies = [pltpu.make_async_copy(ev_hbm, ev_ref, arrived.at[0])]
    for c in range(4):
        cols = pl.ds(c * width, width)
        copies.append(pltpu.make_async_copy(win_hbm.at[:, cols], win_ref.at[:, cols], arrived.at[1 + c]))
    copies.append(pltpu.make_async_copy(cot_hbm, cot_ref, arrived.at[5]))
    copies.append(pltpu.make_async_copy(wout_hbm, wout_ref, arrived.at[6]))
    for copy in copies:
        copy.start()
    hd = width // HEADS
    length = len_ref[0]
    inv_len = 1.0 / length.astype(f32)
    scale = hd ** -0.5
    steps = tokens // STEP

    copies[0].wait()
    for i in range(steps):
        rows = pl.ds(i * STEP, STEP)
        xhat, _ = standardize(ev_ref[rows, :].astype(f32))
        normed_ref[rows, :] = xhat.astype(bf16)

    def project(i, c):
        rows = pl.ds(i * STEP, STEP)
        pre = dot_nn(normed_ref[rows, :], win_ref[:, c * width:(c + 1) * width])
        sig = 0.5 + 0.5 * jnp.tanh(0.5 * pre)
        hid = pre * sig
        dsilu = sig * (1.0 + (pre - hid))
        if c == 0:
            user_ref[rows, :] = hid.astype(bf16)
            duser_ref[rows, :] = dsilu
        else:
            cols = slice((c - 1) * width, c * width)
            hid_ref[rows, cols] = hid.astype(bf16)
            if c == 1:
                dval_ref[rows, :] = dsilu
            else:
                dsilu_ref[rows, (c - 2) * width:(c - 1) * width] = dsilu.astype(bf16)

    for c in range(4):
        copies[1 + c].wait()
        for i in range(steps):
            project(i, c)

    tri = lax.broadcasted_iota(jnp.int32, (STEP, STEP), 0) >= lax.broadcasted_iota(jnp.int32, (STEP, STEP), 1)
    for h in range(HEADS):
        v_cols = slice(h * hd, (h + 1) * hd)
        q_cols = slice(width + h * hd, width + (h + 1) * hd)
        k_cols = slice(2 * width + h * hd, 2 * width + (h + 1) * hd)
        for i in range(steps):
            rows = pl.ds(i * STEP, STEP)
            query = hid_ref[rows, q_cols]
            total = None
            for j in range(i + 1):
                keys = pl.ds(j * STEP, STEP)
                half = dot_nt(query, hid_ref[keys, k_cols]) * (0.5 * scale)
                weights = (half + half * jnp.tanh(half)) * inv_len
                if i == j:
                    weights = jnp.where(tri, weights, 0.0)
                weights = weights.astype(bf16)
                weights_ref[h, rows, keys] = weights
                part = dot_nn(weights, hid_ref[keys, v_cols])
                total = part if total is None else total + part
            att_ref[rows, v_cols] = total

    copies[5].wait()
    copies[6].wait()
    for i in range(steps):
        rows = pl.ds(i * STEP, STEP)
        masked_ref[rows, :] = masked_rows(cot_ref[rows, :], i * STEP, length).astype(bf16)
        ahat, inv = standardize(att_ref[rows, :])
        user = user_ref[rows, :].astype(f32)
        mixed_ref[rows, :] = (ahat * user).astype(bf16)
        grad_mixed = dot_nt(masked_ref[rows, :], wout_ref[...])
        gpre_ref[rows, :width] = (grad_mixed * ahat * duser_ref[rows, :]).astype(bf16)
        e = grad_mixed * user
        gatt_ref[rows, :] = (inv * (e - jnp.mean(e, axis=-1, keepdims=True)
                                    - ahat * jnp.mean(e * ahat, axis=-1, keepdims=True))).astype(bf16)

    for h in range(HEADS):
        v_cols = slice(h * hd, (h + 1) * hd)
        for j in range(steps):
            keys, rest = pl.ds(j * STEP, STEP), pl.ds(j * STEP, tokens - j * STEP)
            grad_v = dot_tn(weights_ref[h, rest, keys], gatt_ref[rest, v_cols])
            gpre_ref[keys, width + h * hd:width + (h + 1) * hd] = (grad_v * dval_ref[keys, v_cols]).astype(bf16)

    order = owner_order(width, rows_size, dp_size)
    normed_t_ref[...] = dot_nt(order, normed_ref[...]).astype(bf16)
    mixed_t = dot_nt(order, mixed_ref[...]).astype(bf16)
    half = width // 2
    for ref, start in ((send_ref, half), (keep_ref, 0)):
        ref[:, :width] = dot_nn(mixed_t[start:start + half], masked_ref[...])
        ref[:, width:] = dot_nn(normed_t_ref[start:start + half, :], gpre_ref[...])


def attention_kernel(len_ref, hid_ref, dsilu_ref, gatt_ref, normed_t_ref, keep_ref, send_ref, gpre_ref):
    tokens, width = gatt_ref.shape
    hd = width // HEADS
    inv_len = 1.0 / len_ref[0].astype(f32)
    scale = hd ** -0.5
    steps = tokens // STEP

    tri = lax.broadcasted_iota(jnp.int32, (STEP, STEP), 0) <= lax.broadcasted_iota(jnp.int32, (STEP, STEP), 1)
    for h in range(HEADS):
        v_cols = slice(h * hd, (h + 1) * hd)
        q_cols = slice(width + h * hd, width + (h + 1) * hd)
        k_cols = slice(2 * width + h * hd, 2 * width + (h + 1) * hd)
        grad_q = [None] * steps
        for j in range(steps):
            keys = pl.ds(j * STEP, STEP)
            key, value = hid_ref[keys, k_cols], hid_ref[keys, v_cols]
            grad_k = None
            for i in range(j, steps):
                rows = pl.ds(i * STEP, STEP)
                query, gatt = hid_ref[rows, q_cols], gatt_ref[rows, v_cols]
                half = dot_nt(key, query) * (0.5 * scale)
                sig2 = 1.0 + jnp.tanh(half)
                silu = half * sig2
                dsilu = sig2 * ((1.0 + half) + (half - silu))
                gscore = dot_nt(value, gatt) * dsilu * (0.5 * inv_len * scale)
                if i == j:
                    gscore = jnp.where(tri, gscore, 0.0)
                gscore = gscore.astype(bf16)
                pk, pq = dot_nn(gscore, query), dot_tn(gscore, key)
                grad_k = pk if grad_k is None else grad_k + pk
                grad_q[i] = pq if grad_q[i] is None else grad_q[i] + pq
            gpre_ref[keys, q_cols] = (grad_k * dsilu_ref[keys, q_cols].astype(f32)).astype(bf16)
        for i in range(steps):
            rows = pl.ds(i * STEP, STEP)
            gpre_ref[rows, v_cols] = (grad_q[i] * dsilu_ref[rows, v_cols].astype(f32)).astype(bf16)

    half = width // 2
    for ref, start in ((send_ref, half), (keep_ref, 0)):
        ref[...] = dot_nn(normed_t_ref[start:start + half, :], gpre_ref[...])


def slots_in_order(position, capacity, dp, rows):
    chips = rows // 2
    owner, place = position // capacity, position % capacity
    ahead, core, part = owner // (2 * dp), (owner // dp) % 2, owner % dp
    chip = (lax.axis_index("rows") // 2 + ahead) % chips
    return part * rows + chip * 2 + core, place


def events_kernel(rows_size, dp_size, len_ref, ev_ref, cot_ref, win_ref, slot_ref, slot_row_ref, gpre_uv_ref, gpre_qk_ref, *refs):
    *send_refs, hi_ref, lo_ref, rows_ref = refs
    tokens, width = ev_ref.shape
    capacity, owners = slot_row_ref.shape
    length = len_ref[0]
    for i in range(tokens // STEP):
        rows = pl.ds(i * STEP, STEP)
        xhat, inv = standardize(ev_ref[rows, :].astype(f32))
        grad_normed = dot_nt(gpre_uv_ref[rows, :], win_ref[:, :2 * width]) + dot_nt(gpre_qk_ref[rows, :], win_ref[:, 2 * width:])
        grad = masked_rows(cot_ref[rows, :], i * STEP, length) + inv * (
            grad_normed - jnp.mean(grad_normed, axis=-1, keepdims=True)
            - xhat * jnp.mean(grad_normed * xhat, axis=-1, keepdims=True))
        high = grad.astype(bf16)
        hi_ref[rows, :] = high
        lo_ref[rows, :] = (grad - high.astype(f32)).astype(bf16)

    slots = rows_ref.shape[0]
    owner, place = slots_in_order(lax.broadcasted_iota(jnp.int32, (slots, 1), 0), capacity, dp_size, rows_size)
    rows_ref[...] = one_hot_rows(slot_ref[...], owner * capacity + place, hi_ref, lo_ref)
    owner, place = slots_in_order(lax.broadcasted_iota(jnp.int32, (1, slots), 1), capacity, dp_size, rows_size)
    chosen = lax.broadcasted_iota(jnp.int32, (owners, slots), 0) == owner
    mine = lax.broadcasted_iota(jnp.int32, (capacity, slots), 0) == place
    ids = whole_numbers(slot_row_ref[...], chosen, mine)
    tiles = width // LANES
    blocks = 2 * dp_size
    for k, send_ref in enumerate(send_refs):
        for i in range(blocks):
            at = (k * blocks + i) * capacity
            for t in range(tiles):
                send_ref[(i * tiles + t) * capacity:(i * tiles + t + 1) * capacity, :] = rows_ref[at:at + capacity, t * LANES:(t + 1) * LANES]
        tile = k * blocks * capacity // LANES * LANES
        send_ref[blocks * tiles * capacity:, :] = jnp.broadcast_to(ids[:, tile:tile + LANES], (ID_ROWS, LANES))


def whole_numbers(values, chosen, mine):
    pick = jnp.where(chosen, 1.0, 0.0).astype(bf16)
    found = 16.0 * dot_nn((values // 16).astype(bf16), pick) + dot_nn((values % 16).astype(bf16), pick)
    return jnp.sum(jnp.where(mine, found, 0.0), axis=0, keepdims=True)


def id_rows(chips):
    return max(ID_ROWS, chips)


def by_part_kernel(dp, block, *refs):
    ins, outs = refs[:-dp], refs[-dp:]
    d = lax.axis_index("dp")
    for j, out_ref in enumerate(outs):
        part = jnp.bitwise_xor(d, j)
        for k, in_ref in enumerate(ins):
            for core in range(2):
                start = pl.multiple_of((core * dp + part) * block, block)
                out_ref[(k * 2 + core) * block:(k * 2 + core + 1) * block, :] = in_ref[pl.ds(start, block), :]
        ids = [in_ref[2 * dp * block:2 * dp * block + 1, :] for in_ref in ins]
        ids += [jnp.zeros((1, LANES), f32)] * (id_rows(len(ins)) - len(ins))
        out_ref[2 * len(ins) * block:, :] = jnp.concatenate(ids, axis=0)


def by_core_kernel(chips, block, *refs):
    *ins, keep_ref, send_ref = refs
    core = lax.rem(lax.axis_index("rows"), 2)
    for out_ref, to in ((send_ref, 1 - core), (keep_ref, core)):
        for j, in_ref in enumerate(ins):
            for k in range(chips):
                start = pl.multiple_of((k * 2 + to) * block, block)
                out_ref[(j * chips + k) * block:(j * chips + k + 1) * block, :] = in_ref[pl.ds(start, block), :]
            at = len(ins) * chips * block + j * id_rows(chips)
            out_ref[at:at + id_rows(chips), :] = in_ref[2 * chips * block:, :]


def one_hot_rows(ids, wanted, hi_ref, lo_ref):
    onehot = jnp.where(wanted == ids, 1.0, 0.0).astype(bf16)
    return dot_nn(onehot, hi_ref[...]) + dot_nn(onehot, lo_ref[...])


def table_kernel(dp, chips, keep_ref, recv_ref, table_ref, accum_ref, table_new_ref, accum_new_ref, rows_ref, hi_ref, lo_ref):
    rows, width = table_ref.shape
    tiles = width // LANES
    sources = dp * chips
    capacity = rows_ref.shape[0] // (2 * sources)
    count = sources * capacity
    r = lax.axis_index("rows")
    block = lax.rem(r, 2) * dp + lax.axis_index("dp")
    ids = []
    for side, ref in enumerate((keep_ref, recv_ref)):
        for i in range(sources):
            at = side * count + i * capacity
            for t in range(tiles):
                rows_ref[at:at + capacity, t * LANES:(t + 1) * LANES] = ref[(i * tiles + t) * capacity:(i * tiles + t + 1) * capacity, :]
        values = ref[sources * tiles * capacity:, :].astype(jnp.int32)
        position = lax.broadcasted_iota(jnp.int32, (1, count), 1)
        source, place = position // capacity, position % capacity
        part, ahead = source // chips, source % chips
        lane = ahead * (2 * dp * capacity) % LANES + block * capacity + place
        chosen = lax.broadcasted_iota(jnp.int32, (LANES, count), 0) == lane
        mine = lax.broadcasted_iota(jnp.int32, (values.shape[0], count), 0) == part * id_rows(chips) + ahead
        ids.append(whole_numbers(values, chosen, mine))
    ids = jnp.concatenate(ids, axis=1).astype(jnp.int32)
    high = rows_ref[...].astype(bf16)
    hi_ref[...] = high
    lo_ref[...] = (rows_ref[...] - high.astype(f32)).astype(bf16)
    grad = one_hot_rows(ids, lax.broadcasted_iota(jnp.int32, (rows, 1), 0), hi_ref, lo_ref)
    accum = jnp.transpose(jnp.broadcast_to(accum_ref[...].reshape(1, rows), (8, rows)))[:, :1]
    accum_new = accum + jnp.mean(grad * grad, axis=-1, keepdims=True)
    accum_new_ref[...] = jnp.transpose(jnp.broadcast_to(accum_new, (rows, LANES)))[:1, :].reshape(rows)
    table_new_ref[...] = table_ref[...] - learning_rate * grad / (jnp.sqrt(accum_new) + adagrad_eps)


def place_on_dp():
    d = lax.axis_index("dp")
    return lax.rem(d, 2), d // 2


def first_kernel(keep1_ref, recv1_ref, keep2_ref, recv2_ref, to_x_ref, to_y_ref, keep_a_ref, keep_b_ref):
    x, y = place_on_dp()
    start = 0
    for keep_ref, recv_ref in ((keep1_ref, recv1_ref), (keep2_ref, recv2_ref)):
        half = keep_ref.shape[-1] // 2
        part = lambda i, j, cols: keep_ref[i, j, :, cols] + recv_ref[i, j, :, cols]
        lo, hi, out = slice(0, half), slice(half, 2 * half), slice(start, start + half)
        for s in range(2):
            to_x_ref[s, :, out] = part(s, 1 - x, lo)
            to_y_ref[s, :, out] = part(1 - y, s, hi)
            keep_a_ref[s, :, out] = part(s, x, lo)
            keep_b_ref[s, :, out] = part(y, s, hi)
        start += half


def second_kernel(keep_a_ref, from_x_ref, keep_b_ref, from_y_ref, to_y_ref, to_x_ref, next_a_ref, next_b_ref):
    x, y = place_on_dp()
    to_y_ref[...] = keep_a_ref[1 - y] + from_x_ref[1 - y]
    to_x_ref[...] = keep_b_ref[1 - x] + from_y_ref[1 - x]
    next_a_ref[...] = keep_a_ref[y] + from_x_ref[y]
    next_b_ref[...] = keep_b_ref[x] + from_y_ref[x]


def chip_bit(bit):
    return (lax.axis_index("rows") // 2) // (1 << bit) % 2


def halve(bit, send_ref, keep_ref, block):
    mine = chip_bit(bit)
    for i in range(send_ref.shape[0]):
        send_ref[i] = block(2 * i + 1 - mine)
        keep_ref[i] = block(2 * i + mine)


def chip_first_kernel(next_a_ref, from_y_ref, next_b_ref, from_x_ref, send_ref, keep_ref):
    halve(0, send_ref, keep_ref, lambda at: jnp.concatenate(
        [next_a_ref[at] + from_y_ref[at], next_b_ref[at] + from_x_ref[at]], axis=1))


def chip_kernel(bit, keep_in, recv_in, send_ref, keep_ref):
    halve(bit, send_ref, keep_ref, lambda at: keep_in[at] + recv_in[at])


def total_kernel(tokens, keep_ref, recv_ref, out_ref):
    out_ref[...] = (keep_ref[0] + recv_ref[0]) * (1.0 / tokens)


def gather_kernel(*refs):
    *pieces, grad_in_ref, grad_out_ref = refs
    d = lax.axis_index("dp")
    width = grad_out_ref.shape[-1]
    half = width // 2
    for k, piece in enumerate(pieces):
        at = jnp.bitwise_xor(d, k)
        grad_out_ref[at] = piece[:, :width]
        start = width
        for cols, first in ((half, 0), (width, 2 * width), (half, half), (width, width), (width, 3 * width)):
            grad_in_ref[at, :, first:first + cols] = piece[:, start:start + cols]
            start += cols


def vmem():
    return pl.BlockSpec(memory_space=pltpu.VMEM)


def shape(*dims, dtype=f32):
    return jax.ShapeDtypeStruct(dims, dtype)


def call(kernel, name, out_shape, args, scalars=0, scratch=(), far=0, long=False, grant=4, apart=(), either=()):
    place = [None] * scalars + [pltpu.HBM] * far + [pltpu.VMEM] * (len(args) - scalars - far)
    held = [None if i in either else pltpu.HBM if i in apart else p for i, p in enumerate(place)]
    args = [a if p is None else pltpu.with_memory_space_constraint(a, p) for a, p in zip(args, held)]
    return pl.pallas_call(
        kernel,
        name=name,
        in_specs=[pl.BlockSpec(memory_space=p or pltpu.SMEM) for p in place],
        out_specs=[vmem()] * len(out_shape),
        out_shape=list(out_shape),
        scratch_shapes=[pltpu.VMEM(dims, dtype) for dims, dtype in scratch] + [pltpu.SemaphoreType.DMA((7,))] * (far > 0),
        compiler_params=pltpu.CompilerParams(vmem_limit_bytes=grant * MIB),
        cost_estimate=pl.CostEstimate(flops=100_000_000_000 if long else 1_000_000_000, bytes_accessed=1 << 16, transcendentals=0),
    )(*args)


def body(rows_size, dp_size, events, cotangent, lengths, event_slot, slot_row, slot_count, w_in, w_out, item_table, accumulator):
    tokens, width = events.shape
    owners, capacity = slot_row.shape[1:]
    chips = rows_size // 2
    piece = width // (rows_size * dp_size)
    cores = [(i, i ^ 1) for i in range(rows_size)]
    over_dp = lambda v, bit: lax.ppermute(v, "dp", [(i, i ^ bit) for i in range(dp_size)])
    over_chips = lambda v, bit: lax.ppermute(v, "rows", [(i, i ^ (2 << bit)) for i in range(rows_size)])
    after = lambda value, *others: lax.optimization_barrier((value, *others))[0]
    strip = chips * piece

    def gathered(total):
        return [total] + [over_dp(total, k) for k in range(1, dp_size)]

    by_dp = lambda v: v.reshape(2, 2, strip, v.shape[-1])
    by_chip = lambda v: v.reshape(*v.shape[:-2], chips, piece, v.shape[-1])
    bits = chips.bit_length() - 1
    far_off = lambda *dims, dtype=f32: pltpu.HBM(dims, dtype)
    local = lambda *dims, dtype=f32: pltpu.VMEM(dims, dtype)
    sides = lambda cols: [local(width // 2, cols)] * 2
    keep1, send1, hid, dsilu, gatt, gpre_uv, normed_t, events, cotangent, w_in = call(
        functools.partial(forward_kernel, rows_size, dp_size), "forward_part",
        sides(3 * width) + [
            local(tokens, 3 * width, dtype=bf16),
            local(tokens, 2 * width, dtype=bf16),
            local(tokens, width, dtype=bf16),
            local(tokens, 2 * width, dtype=bf16),
            local(width, tokens, dtype=bf16),
            local(tokens, width, dtype=bf16),
            local(tokens, width, dtype=bf16),
            local(*w_in.shape, dtype=bf16),
        ],
        (lengths, events, cotangent, w_in, w_out), 1,
        [((tokens, width), bf16), ((tokens, width), bf16), ((tokens, width), f32), ((tokens, width), f32),
         ((tokens, width), bf16), ((tokens, width), bf16), ((tokens, width), f32), ((HEADS, tokens, tokens), bf16),
         (w_out.shape, bf16)], far=4, long=True, grant=16)
    recv1 = lax.ppermute(send1, "rows", cores)
    keep2, send2, gpre_qk = call(
        attention_kernel, "attention_part", sides(2 * width) + [local(tokens, 2 * width, dtype=bf16)],
        (lengths, hid, dsilu, gatt, normed_t), 1, long=True, grant=10)
    recv2 = lax.ppermute(send2, "rows", cores)
    block = capacity * (width // LANES)
    sends = call(
        functools.partial(events_kernel, rows_size, dp_size), "events_part",
        [local(2 * dp_size * block + ID_ROWS, LANES)] * chips,
        (lengths, events, cotangent, w_in, event_slot, slot_row[0].T, gpre_uv, gpre_qk), 1,
        [((tokens, width), bf16), ((tokens, width), bf16), ((owners * capacity, width), f32)], grant=10, long=True)
    ahead = lambda v, k: lax.ppermute(v, "rows", [(i, (i + 2 * k) % rows_size) for i in range(rows_size)])
    came = [sends[0]] + [ahead(sends[k], k) for k in range(1, chips)]
    cols = w_in.shape[1] + width
    to_x, to_y, keep_a, keep_b = call(
        first_kernel, "first_sums", [local(2, strip, cols // 2)] * 4,
        [by_dp(v) for v in (after(keep1, *sends), recv1, keep2, recv2)])
    from_x, from_y = over_dp(to_x, 1), over_dp(to_y, 2)
    to_y, to_x, next_a, next_b = call(
        second_kernel, "second_sums", [local(strip, cols // 2)] * 4, (keep_a, from_x, keep_b, from_y),
        long=True)
    from_y, from_x = over_dp(to_y, 2), over_dp(to_x, 1)
    came[0] = after(came[0], to_y, to_x)
    parts = call(
        functools.partial(by_part_kernel, dp_size, block), "by_part",
        [local(2 * chips * block + id_rows(chips), LANES)] * dp_size, came, long=True)
    next_a = after(next_a, *parts)
    send, keep = call(
        chip_first_kernel, "chip_sums", [local(chips // 2, piece, cols)] * 2,
        [by_chip(v) for v in (next_a, from_y, next_b, from_x)])
    parts = [parts[0]] + [over_dp(parts[k], k) for k in range(1, dp_size)]
    for bit in range(1, bits):
        send, keep = call(
            functools.partial(chip_kernel, bit), "chip_sums", [local(chips >> (bit + 1), piece, cols)] * 2,
            (keep, over_chips(send, bit - 1)), long=bit == 1)
    (total,) = call(
        functools.partial(total_kernel, tokens), "total", [local(piece, cols)], (keep, over_chips(send, bits - 1)))
    pieces = gathered(total)
    parts[0] = after(parts[0], total)
    keep, send = call(
        functools.partial(by_core_kernel, chips, block), "by_core",
        [local(dp_size * (chips * block + id_rows(chips)), LANES)] * 2, parts, long=True)
    recv = lax.ppermute(send, "rows", cores)
    slots = owners * capacity
    table_new, accum_new = call(
        functools.partial(table_kernel, dp_size, chips), "table_part", [shape(*item_table.shape), shape(*accumulator.shape)],
        (keep, recv, item_table, accumulator), 0,
        [((slots, width), f32), ((slots, width), bf16), ((slots, width), bf16)], grant=10)
    pieces[-1] = after(pieces[-1], accum_new)
    grad_in, grad_out = call(
        gather_kernel, "gather", [shape(dp_size, piece, 4 * width), shape(dp_size, piece, width)], pieces)
    return grad_in.reshape(-1, 4 * width), grad_out.reshape(-1, width), table_new, accum_new


def solution(mesh):
    whole = P(("dp", "rows"))
    in_specs = (whole,) * 6 + (P(), P(), whole, whole)
    out_specs = (P("rows"), P("rows"), whole, whole)
    run = functools.partial(body, mesh.shape["rows"], mesh.shape["dp"])
    return jax.shard_map(run, mesh=mesh, in_specs=in_specs, out_specs=out_specs, check_vma=False)
```

```python
import functools

import jax
import jax.numpy as jnp
from jax import lax
from jax.experimental import pallas as pl
from jax.experimental.pallas import tpu as pltpu
from jax.sharding import PartitionSpec as P

HEADS = 4

norm_eps = 1e-05
adagrad_eps = 1e-10
learning_rate = 0.1

f32, bf16 = jnp.float32, jnp.bfloat16
MIB = 1024 * 1024
STEP = 256
LANES = 128
ID_ROWS = 8


def dot_nn(a, b):
    return lax.dot_general(a, b, (((1,), (0,)), ((), ())), preferred_element_type=f32)


def dot_nt(a, b):
    return lax.dot_general(a, b, (((1,), (1,)), ((), ())), preferred_element_type=f32)


def dot_tn(a, b):
    return lax.dot_general(a, b, (((0,), (0,)), ((), ())), preferred_element_type=f32)


def standardize(x):
    centered = x - jnp.mean(x, axis=-1, keepdims=True)
    inv = lax.rsqrt(jnp.mean(centered * centered, axis=-1, keepdims=True) + norm_eps)
    return centered * inv, inv


def masked_rows(cot, start, length):
    row = start + lax.broadcasted_iota(jnp.int32, cot.shape, 0)
    return jnp.where(row < length, cot.astype(f32), 0.0)


def owner_order(width, rows, dp):
    chips = rows // 2
    piece = width // (rows * dp)
    at = lax.broadcasted_iota(jnp.int32, (width, 1), 0)
    side, rest = at // (width // 2), at % (width // 2)
    part, rest = rest // (chips * piece), rest % (chips * piece)
    chip, row = rest // piece, rest % piece
    core = lax.rem(lax.axis_index("rows"), 2)
    core = jnp.where(side == 0, core, 1 - core)
    wanted = ((chip * 2 + core) * dp + part) * piece + row
    return jnp.where(lax.broadcasted_iota(jnp.int32, (width, width), 1) == wanted, 1.0, 0.0).astype(bf16)


def forward_kernel(rows_size, dp_size, len_ref, ev_hbm, cot_hbm, win_hbm, wout_hbm,
                   keep_ref, send_ref, hid_ref, dsilu_ref, gatt_ref, gpre_ref, normed_t_ref,
                   ev_ref, cot_ref, win_ref, normed_ref, user_ref, duser_ref, att_ref, mixed_ref, masked_ref, dval_ref, weights_ref,
                   wout_ref, arrived):
    tokens, width = ev_ref.shape
    copies = [pltpu.make_async_copy(ev_hbm, ev_ref, arrived.at[0])]
    for c in range(4):
        cols = pl.ds(c * width, width)
        copies.append(pltpu.make_async_copy(win_hbm.at[:, cols], win_ref.at[:, cols], arrived.at[1 + c]))
    copies.append(pltpu.make_async_copy(cot_hbm, cot_ref, arrived.at[5]))
    copies.append(pltpu.make_async_copy(wout_hbm, wout_ref, arrived.at[6]))
    for copy in copies:
        copy.start()
    hd = width // HEADS
    length = len_ref[0]
    inv_len = 1.0 / length.astype(f32)
    scale = hd ** -0.5
    steps = tokens // STEP

    copies[0].wait()
    for i in range(steps):
        rows = pl.ds(i * STEP, STEP)
        xhat, _ = standardize(ev_ref[rows, :].astype(f32))
        normed_ref[rows, :] = xhat.astype(bf16)

    def project(i, c):
        rows = pl.ds(i * STEP, STEP)
        pre = dot_nn(normed_ref[rows, :], win_ref[:, c * width:(c + 1) * width])
        sig = 0.5 + 0.5 * jnp.tanh(0.5 * pre)
        hid = pre * sig
        dsilu = sig * (1.0 + (pre - hid))
        if c == 0:
            user_ref[rows, :] = hid.astype(bf16)
            duser_ref[rows, :] = dsilu
        else:
            cols = slice((c - 1) * width, c * width)
            hid_ref[rows, cols] = hid.astype(bf16)
            if c == 1:
                dval_ref[rows, :] = dsilu
            else:
                dsilu_ref[rows, (c - 2) * width:(c - 1) * width] = dsilu.astype(bf16)

    for c in range(4):
        copies[1 + c].wait()
        for i in range(steps):
            project(i, c)

    tri = lax.broadcasted_iota(jnp.int32, (STEP, STEP), 0) >= lax.broadcasted_iota(jnp.int32, (STEP, STEP), 1)
    for h in range(HEADS):
        v_cols = slice(h * hd, (h + 1) * hd)
        q_cols = slice(width + h * hd, width + (h + 1) * hd)
        k_cols = slice(2 * width + h * hd, 2 * width + (h + 1) * hd)
        for i in range(steps):
            rows = pl.ds(i * STEP, STEP)
            query = hid_ref[rows, q_cols]
            total = None
            for j in range(i + 1):
                keys = pl.ds(j * STEP, STEP)
                half = dot_nt(query, hid_ref[keys, k_cols]) * (0.5 * scale)
                weights = (half + half * jnp.tanh(half)) * inv_len
                if i == j:
                    weights = jnp.where(tri, weights, 0.0)
                weights = weights.astype(bf16)
                weights_ref[h, rows, keys] = weights
                part = dot_nn(weights, hid_ref[keys, v_cols])
                total = part if total is None else total + part
            att_ref[rows, v_cols] = total

    copies[5].wait()
    copies[6].wait()
    for i in range(steps):
        rows = pl.ds(i * STEP, STEP)
        masked_ref[rows, :] = masked_rows(cot_ref[rows, :], i * STEP, length).astype(bf16)
        ahat, inv = standardize(att_ref[rows, :])
        user = user_ref[rows, :].astype(f32)
        mixed_ref[rows, :] = (ahat * user).astype(bf16)
        grad_mixed = dot_nt(masked_ref[rows, :], wout_ref[...])
        gpre_ref[rows, :width] = (grad_mixed * ahat * duser_ref[rows, :]).astype(bf16)
        e = grad_mixed * user
        gatt_ref[rows, :] = (inv * (e - jnp.mean(e, axis=-1, keepdims=True)
                                    - ahat * jnp.mean(e * ahat, axis=-1, keepdims=True))).astype(bf16)

    for h in range(HEADS):
        v_cols = slice(h * hd, (h + 1) * hd)
        for j in range(steps):
            keys, rest = pl.ds(j * STEP, STEP), pl.ds(j * STEP, tokens - j * STEP)
            grad_v = dot_tn(weights_ref[h, rest, keys], gatt_ref[rest, v_cols])
            gpre_ref[keys, width + h * hd:width + (h + 1) * hd] = (grad_v * dval_ref[keys, v_cols]).astype(bf16)

    order = owner_order(width, rows_size, dp_size)
    normed_t_ref[...] = dot_nt(order, normed_ref[...]).astype(bf16)
    mixed_t = dot_nt(order, mixed_ref[...]).astype(bf16)
    half = width // 2
    for ref, start in ((send_ref, half), (keep_ref, 0)):
        ref[:, :width] = dot_nn(mixed_t[start:start + half], masked_ref[...])
        ref[:, width:] = dot_nn(normed_t_ref[start:start + half, :], gpre_ref[...])


def attention_kernel(len_ref, hid_ref, dsilu_ref, gatt_ref, normed_t_ref, keep_ref, send_ref, gpre_ref):
    tokens, width = gatt_ref.shape
    hd = width // HEADS
    inv_len = 1.0 / len_ref[0].astype(f32)
    scale = hd ** -0.5
    steps = tokens // STEP

    tri = lax.broadcasted_iota(jnp.int32, (STEP, STEP), 0) <= lax.broadcasted_iota(jnp.int32, (STEP, STEP), 1)
    for h in range(HEADS):
        v_cols = slice(h * hd, (h + 1) * hd)
        q_cols = slice(width + h * hd, width + (h + 1) * hd)
        k_cols = slice(2 * width + h * hd, 2 * width + (h + 1) * hd)
        grad_q = [None] * steps
        for j in range(steps):
            keys = pl.ds(j * STEP, STEP)
            key, value = hid_ref[keys, k_cols], hid_ref[keys, v_cols]
            grad_k = None
            for i in range(j, steps):
                rows = pl.ds(i * STEP, STEP)
                query, gatt = hid_ref[rows, q_cols], gatt_ref[rows, v_cols]
                half = dot_nt(key, query) * (0.5 * scale)
                sig2 = 1.0 + jnp.tanh(half)
                silu = half * sig2
                dsilu = sig2 * ((1.0 + half) + (half - silu))
                gscore = dot_nt(value, gatt) * dsilu * (0.5 * inv_len * scale)
                if i == j:
                    gscore = jnp.where(tri, gscore, 0.0)
                gscore = gscore.astype(bf16)
                pk, pq = dot_nn(gscore, query), dot_tn(gscore, key)
                grad_k = pk if grad_k is None else grad_k + pk
                grad_q[i] = pq if grad_q[i] is None else grad_q[i] + pq
            gpre_ref[keys, q_cols] = (grad_k * dsilu_ref[keys, q_cols].astype(f32)).astype(bf16)
        for i in range(steps):
            rows = pl.ds(i * STEP, STEP)
            gpre_ref[rows, v_cols] = (grad_q[i] * dsilu_ref[rows, v_cols].astype(f32)).astype(bf16)

    half = width // 2
    for ref, start in ((send_ref, half), (keep_ref, 0)):
        ref[...] = dot_nn(normed_t_ref[start:start + half, :], gpre_ref[...])


def slots_in_order(position, capacity, dp, rows):
    chips = rows // 2
    owner, place = position // capacity, position % capacity
    ahead, core, part = owner // (2 * dp), (owner // dp) % 2, owner % dp
    chip = (lax.axis_index("rows") // 2 + ahead) % chips
    return part * rows + chip * 2 + core, place


def events_kernel(rows_size, dp_size, len_ref, ev_ref, cot_ref, win_ref, slot_ref, slot_row_ref, gpre_uv_ref, gpre_qk_ref, *refs):
    *send_refs, hi_ref, lo_ref, rows_ref = refs
    tokens, width = ev_ref.shape
    capacity, owners = slot_row_ref.shape
    length = len_ref[0]
    for i in range(tokens // STEP):
        rows = pl.ds(i * STEP, STEP)
        xhat, inv = standardize(ev_ref[rows, :].astype(f32))
        grad_normed = dot_nt(gpre_uv_ref[rows, :], win_ref[:, :2 * width]) + dot_nt(gpre_qk_ref[rows, :], win_ref[:, 2 * width:])
        grad = masked_rows(cot_ref[rows, :], i * STEP, length) + inv * (
            grad_normed - jnp.mean(grad_normed, axis=-1, keepdims=True)
            - xhat * jnp.mean(grad_normed * xhat, axis=-1, keepdims=True))
        high = grad.astype(bf16)
        hi_ref[rows, :] = high
        lo_ref[rows, :] = (grad - high.astype(f32)).astype(bf16)

    slots = rows_ref.shape[0]
    owner, place = slots_in_order(lax.broadcasted_iota(jnp.int32, (slots, 1), 0), capacity, dp_size, rows_size)
    rows_ref[...] = one_hot_rows(slot_ref[...], owner * capacity + place, hi_ref, lo_ref)
    owner, place = slots_in_order(lax.broadcasted_iota(jnp.int32, (1, slots), 1), capacity, dp_size, rows_size)
    chosen = lax.broadcasted_iota(jnp.int32, (owners, slots), 0) == owner
    mine = lax.broadcasted_iota(jnp.int32, (capacity, slots), 0) == place
    ids = whole_numbers(slot_row_ref[...], chosen, mine)
    tiles = width // LANES
    blocks = 2 * dp_size
    for k, send_ref in enumerate(send_refs):
        for i in range(blocks):
            at = (k * blocks + i) * capacity
            for t in range(tiles):
                send_ref[(i * tiles + t) * capacity:(i * tiles + t + 1) * capacity, :] = rows_ref[at:at + capacity, t * LANES:(t + 1) * LANES]
        tile = k * blocks * capacity // LANES * LANES
        send_ref[blocks * tiles * capacity:, :] = jnp.broadcast_to(ids[:, tile:tile + LANES], (ID_ROWS, LANES))


def whole_numbers(values, chosen, mine):
    pick = jnp.where(chosen, 1.0, 0.0).astype(bf16)
    found = 16.0 * dot_nn((values // 16).astype(bf16), pick) + dot_nn((values % 16).astype(bf16), pick)
    return jnp.sum(jnp.where(mine, found, 0.0), axis=0, keepdims=True)


def id_rows(chips):
    return max(ID_ROWS, chips)


def by_part_kernel(dp, block, *refs):
    ins, outs = refs[:-dp], refs[-dp:]
    d = lax.axis_index("dp")
    for j, out_ref in enumerate(outs):
        part = jnp.bitwise_xor(d, j)
        for k, in_ref in enumerate(ins):
            for core in range(2):
                start = pl.multiple_of((core * dp + part) * block, block)
                out_ref[(k * 2 + core) * block:(k * 2 + core + 1) * block, :] = in_ref[pl.ds(start, block), :]
        ids = [in_ref[2 * dp * block:2 * dp * block + 1, :] for in_ref in ins]
        ids += [jnp.zeros((1, LANES), f32)] * (id_rows(len(ins)) - len(ins))
        out_ref[2 * len(ins) * block:, :] = jnp.concatenate(ids, axis=0)


def by_core_kernel(chips, block, *refs):
    *ins, keep_ref, send_ref = refs
    core = lax.rem(lax.axis_index("rows"), 2)
    for out_ref, to in ((send_ref, 1 - core), (keep_ref, core)):
        for j, in_ref in enumerate(ins):
            for k in range(chips):
                start = pl.multiple_of((k * 2 + to) * block, block)
                out_ref[(j * chips + k) * block:(j * chips + k + 1) * block, :] = in_ref[pl.ds(start, block), :]
            at = len(ins) * chips * block + j * id_rows(chips)
            out_ref[at:at + id_rows(chips), :] = in_ref[2 * chips * block:, :]


def one_hot_rows(ids, wanted, hi_ref, lo_ref):
    onehot = jnp.where(wanted == ids, 1.0, 0.0).astype(bf16)
    return dot_nn(onehot, hi_ref[...]) + dot_nn(onehot, lo_ref[...])


def table_kernel(dp, chips, keep_ref, recv_ref, table_ref, accum_ref, table_new_ref, accum_new_ref, rows_ref, hi_ref, lo_ref):
    rows, width = table_ref.shape
    tiles = width // LANES
    sources = dp * chips
    capacity = rows_ref.shape[0] // (2 * sources)
    count = sources * capacity
    r = lax.axis_index("rows")
    block = lax.rem(r, 2) * dp + lax.axis_index("dp")
    ids = []
    for side, ref in enumerate((keep_ref, recv_ref)):
        for i in range(sources):
            at = side * count + i * capacity
            for t in range(tiles):
                rows_ref[at:at + capacity, t * LANES:(t + 1) * LANES] = ref[(i * tiles + t) * capacity:(i * tiles + t + 1) * capacity, :]
        values = ref[sources * tiles * capacity:, :].astype(jnp.int32)
        position = lax.broadcasted_iota(jnp.int32, (1, count), 1)
        source, place = position // capacity, position % capacity
        part, ahead = source // chips, source % chips
        lane = ahead * (2 * dp * capacity) % LANES + block * capacity + place
        chosen = lax.broadcasted_iota(jnp.int32, (LANES, count), 0) == lane
        mine = lax.broadcasted_iota(jnp.int32, (values.shape[0], count), 0) == part * id_rows(chips) + ahead
        ids.append(whole_numbers(values, chosen, mine))
    ids = jnp.concatenate(ids, axis=1).astype(jnp.int32)
    high = rows_ref[...].astype(bf16)
    hi_ref[...] = high
    lo_ref[...] = (rows_ref[...] - high.astype(f32)).astype(bf16)
    grad = one_hot_rows(ids, lax.broadcasted_iota(jnp.int32, (rows, 1), 0), hi_ref, lo_ref)
    accum = jnp.transpose(jnp.broadcast_to(accum_ref[...].reshape(1, rows), (8, rows)))[:, :1]
    accum_new = accum + jnp.mean(grad * grad, axis=-1, keepdims=True)
    accum_new_ref[...] = jnp.transpose(jnp.broadcast_to(accum_new, (rows, LANES)))[:1, :].reshape(rows)
    table_new_ref[...] = table_ref[...] - learning_rate * grad / (jnp.sqrt(accum_new) + adagrad_eps)


def place_on_dp():
    d = lax.axis_index("dp")
    return lax.rem(d, 2), d // 2


def first_kernel(keep1_ref, recv1_ref, keep2_ref, recv2_ref, to_x_ref, to_y_ref, keep_a_ref, keep_b_ref):
    x, y = place_on_dp()
    start = 0
    for keep_ref, recv_ref in ((keep1_ref, recv1_ref), (keep2_ref, recv2_ref)):
        half = keep_ref.shape[-1] // 2
        part = lambda i, j, cols: keep_ref[i, j, :, cols] + recv_ref[i, j, :, cols]
        lo, hi, out = slice(0, half), slice(half, 2 * half), slice(start, start + half)
        for s in range(2):
            to_x_ref[s, :, out] = part(s, 1 - x, lo)
            to_y_ref[s, :, out] = part(1 - y, s, hi)
            keep_a_ref[s, :, out] = part(s, x, lo)
            keep_b_ref[s, :, out] = part(y, s, hi)
        start += half


def second_kernel(keep_a_ref, from_x_ref, keep_b_ref, from_y_ref, to_y_ref, to_x_ref, next_a_ref, next_b_ref):
    x, y = place_on_dp()
    to_y_ref[...] = keep_a_ref[1 - y] + from_x_ref[1 - y]
    to_x_ref[...] = keep_b_ref[1 - x] + from_y_ref[1 - x]
    next_a_ref[...] = keep_a_ref[y] + from_x_ref[y]
    next_b_ref[...] = keep_b_ref[x] + from_y_ref[x]


def chips_kernel(next_a_ref, from_y_ref, next_b_ref, from_x_ref, *out_refs):
    chips = len(out_refs)
    chip = lax.axis_index("rows") // 2
    half = next_a_ref.shape[-1]
    for k, out_ref in enumerate(out_refs):
        at = lax.rem(chip + k, chips)
        out_ref[:, :half] = next_a_ref[at] + from_y_ref[at]
        out_ref[:, half:] = next_b_ref[at] + from_x_ref[at]


def total_kernel(tokens, *refs):
    total = refs[0][...]
    for ref in refs[1:-1]:
        total = total + ref[...]
    refs[-1][...] = total * (1.0 / tokens)


def gather_kernel(*refs):
    *pieces, grad_in_ref, grad_out_ref = refs
    d = lax.axis_index("dp")
    width = grad_out_ref.shape[-1]
    half = width // 2
    for k, piece in enumerate(pieces):
        at = jnp.bitwise_xor(d, k)
        grad_out_ref[at] = piece[:, :width]
        start = width
        for cols, first in ((half, 0), (width, 2 * width), (half, half), (width, width), (width, 3 * width)):
            grad_in_ref[at, :, first:first + cols] = piece[:, start:start + cols]
            start += cols


def vmem():
    return pl.BlockSpec(memory_space=pltpu.VMEM)


def shape(*dims, dtype=f32):
    return jax.ShapeDtypeStruct(dims, dtype)


def call(kernel, name, out_shape, args, scalars=0, scratch=(), far=0, long=False, grant=4, apart=(), either=()):
    place = [None] * scalars + [pltpu.HBM] * far + [pltpu.VMEM] * (len(args) - scalars - far)
    held = [None if i in either else pltpu.HBM if i in apart else p for i, p in enumerate(place)]
    args = [a if p is None else pltpu.with_memory_space_constraint(a, p) for a, p in zip(args, held)]
    return pl.pallas_call(
        kernel,
        name=name,
        in_specs=[pl.BlockSpec(memory_space=p or pltpu.SMEM) for p in place],
        out_specs=[vmem()] * len(out_shape),
        out_shape=list(out_shape),
        scratch_shapes=[pltpu.VMEM(dims, dtype) for dims, dtype in scratch] + [pltpu.SemaphoreType.DMA((7,))] * (far > 0),
        compiler_params=pltpu.CompilerParams(vmem_limit_bytes=grant * MIB),
        cost_estimate=pl.CostEstimate(flops=100_000_000_000 if long else 1_000_000_000, bytes_accessed=1 << 16, transcendentals=0),
    )(*args)


def body(rows_size, dp_size, events, cotangent, lengths, event_slot, slot_row, slot_count, w_in, w_out, item_table, accumulator):
    tokens, width = events.shape
    owners, capacity = slot_row.shape[1:]
    chips = rows_size // 2
    piece = width // (rows_size * dp_size)
    cores = [(i, i ^ 1) for i in range(rows_size)]
    over_dp = lambda v, bit: lax.ppermute(v, "dp", [(i, i ^ bit) for i in range(dp_size)])
    after = lambda value, *others: lax.optimization_barrier((value, *others))[0]
    strip = chips * piece

    def gathered(total):
        return [total] + [over_dp(total, k) for k in range(1, dp_size)]

    by_dp = lambda v: v.reshape(2, 2, strip, v.shape[-1])
    by_chip = lambda v: v.reshape(*v.shape[:-2], chips, piece, v.shape[-1])
    local = lambda *dims, dtype=f32: pltpu.VMEM(dims, dtype)
    sides = lambda cols: [local(width // 2, cols)] * 2
    keep1, send1, hid, dsilu, gatt, gpre_uv, normed_t, events, cotangent, w_in = call(
        functools.partial(forward_kernel, rows_size, dp_size), "forward_part",
        sides(3 * width) + [
            local(tokens, 3 * width, dtype=bf16),
            local(tokens, 2 * width, dtype=bf16),
            local(tokens, width, dtype=bf16),
            local(tokens, 2 * width, dtype=bf16),
            local(width, tokens, dtype=bf16),
            local(tokens, width, dtype=bf16),
            local(tokens, width, dtype=bf16),
            local(*w_in.shape, dtype=bf16),
        ],
        (lengths, events, cotangent, w_in, w_out), 1,
        [((tokens, width), bf16), ((tokens, width), bf16), ((tokens, width), f32), ((tokens, width), f32),
         ((tokens, width), bf16), ((tokens, width), bf16), ((tokens, width), f32), ((HEADS, tokens, tokens), bf16),
         (w_out.shape, bf16)], far=4, long=True, grant=16)
    recv1 = lax.ppermute(send1, "rows", cores)
    keep2, send2, gpre_qk = call(
        attention_kernel, "attention_part", sides(2 * width) + [local(tokens, 2 * width, dtype=bf16)],
        (lengths, hid, dsilu, gatt, normed_t), 1, long=True, grant=10)
    recv2 = lax.ppermute(send2, "rows", cores)
    block = capacity * (width // LANES)
    gpre_uv = after(gpre_uv, recv1)
    sends = call(
        functools.partial(events_kernel, rows_size, dp_size), "events_part",
        [local(2 * dp_size * block + ID_ROWS, LANES)] * chips,
        (lengths, events, cotangent, w_in, event_slot, slot_row[0].T, gpre_uv, gpre_qk), 1,
        [((tokens, width), bf16), ((tokens, width), bf16), ((owners * capacity, width), f32)], grant=10, long=True)
    ahead = lambda v, k: lax.ppermute(v, "rows", [(i, (i + 2 * k) % rows_size) for i in range(rows_size)])
    came = [sends[0]] + [ahead(sends[k], k) for k in range(1, chips)]
    cols = w_in.shape[1] + width
    to_x, to_y, keep_a, keep_b = call(
        first_kernel, "first_sums", [local(2, strip, cols // 2)] * 4,
        [by_dp(v) for v in (after(keep1, *sends), recv1, keep2, recv2)])
    from_x, from_y = over_dp(to_x, 1), over_dp(to_y, 2)
    to_y, to_x, next_a, next_b = call(
        second_kernel, "second_sums", [local(strip, cols // 2)] * 4, (keep_a, from_x, keep_b, from_y),
        long=True)
    from_y, from_x = over_dp(to_y, 2), over_dp(to_x, 1)
    came[0] = after(came[0], to_y, to_x)
    parts = call(
        functools.partial(by_part_kernel, dp_size, block), "by_part",
        [local(2 * chips * block + id_rows(chips), LANES)] * dp_size, came, long=True)
    next_a = after(next_a, *parts)
    sums = call(
        chips_kernel, "chip_sums", [local(piece, cols)] * chips,
        [by_chip(v) for v in (next_a, from_y, next_b, from_x)])
    parts = [parts[0]] + [over_dp(parts[k], k) for k in range(1, dp_size)]
    sums = [sums[0]] + [ahead(sums[k], k) for k in range(1, chips)]
    (total,) = call(
        functools.partial(total_kernel, tokens), "total", [local(piece, cols)], sums, long=True)
    pieces = gathered(total)
    parts[0] = after(parts[0], total)
    keep, send = call(
        functools.partial(by_core_kernel, chips, block), "by_core",
        [local(dp_size * (chips * block + id_rows(chips)), LANES)] * 2, parts, long=True)
    recv = lax.ppermute(send, "rows", cores)
    slots = owners * capacity
    table_new, accum_new = call(
        functools.partial(table_kernel, dp_size, chips), "table_part", [shape(*item_table.shape), shape(*accumulator.shape)],
        (keep, recv, item_table, accumulator), 0,
        [((slots, width), f32), ((slots, width), bf16), ((slots, width), bf16)], grant=10)
    pieces[-1] = after(pieces[-1], accum_new)
    grad_in, grad_out = call(
        gather_kernel, "gather", [shape(dp_size, piece, 4 * width), shape(dp_size, piece, width)], pieces)
    return grad_in.reshape(-1, 4 * width), grad_out.reshape(-1, width), table_new, accum_new


def solution(mesh):
    whole = P(("dp", "rows"))
    in_specs = (whole,) * 6 + (P(), P(), whole, whole)
    out_specs = (P("rows"), P("rows"), whole, whole)
    run = functools.partial(body, mesh.shape["rows"], mesh.shape["dp"])
    return jax.shard_map(run, mesh=mesh, in_specs=in_specs, out_specs=out_specs, check_vma=False)
```

```python
import functools

import jax
import jax.numpy as jnp
from jax import lax
from jax.experimental import pallas as pl
from jax.experimental.pallas import tpu as pltpu
from jax.sharding import PartitionSpec as P

HEADS = 4

norm_eps = 1e-05
adagrad_eps = 1e-10
learning_rate = 0.1

f32, bf16 = jnp.float32, jnp.bfloat16
MIB = 1024 * 1024
STEP = 256
LANES = 128
ID_ROWS = 8


def dot_nn(a, b):
    return lax.dot_general(a, b, (((1,), (0,)), ((), ())), preferred_element_type=f32)


def dot_nt(a, b):
    return lax.dot_general(a, b, (((1,), (1,)), ((), ())), preferred_element_type=f32)


def dot_tn(a, b):
    return lax.dot_general(a, b, (((0,), (0,)), ((), ())), preferred_element_type=f32)


def over(value, n):
    return value >> (n.bit_length() - 1) if n & (n - 1) == 0 else value // n


def rest(value, n):
    return value & (n - 1) if n & (n - 1) == 0 else value % n


def standardize(x):
    centered = x - jnp.mean(x, axis=-1, keepdims=True)
    inv = lax.rsqrt(jnp.mean(centered * centered, axis=-1, keepdims=True) + norm_eps)
    return centered * inv, inv


def masked_rows(cot, start, length):
    row = start + lax.broadcasted_iota(jnp.int32, cot.shape, 0)
    return jnp.where(row < length, cot.astype(f32), 0.0)


def owner_order(width, rows, dp):
    chips = rows // 2
    piece = width // (rows * dp)
    at = lax.broadcasted_iota(jnp.int32, (width, 1), 0)
    side, part = over(at, width // 2), rest(over(at, chips * piece), dp)
    chip, row = rest(over(at, piece), chips), rest(at, piece)
    core = lax.rem(lax.axis_index("rows"), 2)
    core = jnp.where(side == 0, core, 1 - core)
    wanted = ((chip * 2 + core) * dp + part) * piece + row
    return jnp.where(lax.broadcasted_iota(jnp.int32, (width, width), 1) == wanted, 1.0, 0.0).astype(bf16)


def forward_kernel(rows_size, dp_size, len_ref, ev_hbm, cot_hbm, win_hbm, wout_hbm,
                   keep_ref, send_ref, hid_ref, dsilu_ref, gatt_ref, gpre_ref, normed_t_ref,
                   ev_ref, cot_ref, win_ref, normed_ref, user_ref, duser_ref, att_ref, mixed_ref, masked_ref, dval_ref, weights_ref,
                   wout_ref, order_ref, arrived):
    tokens, width = ev_ref.shape
    copies = [pltpu.make_async_copy(ev_hbm, ev_ref, arrived.at[0])]
    for c in range(4):
        cols = pl.ds(c * width, width)
        copies.append(pltpu.make_async_copy(win_hbm.at[:, cols], win_ref.at[:, cols], arrived.at[1 + c]))
    copies.append(pltpu.make_async_copy(cot_hbm, cot_ref, arrived.at[5]))
    copies.append(pltpu.make_async_copy(wout_hbm, wout_ref, arrived.at[6]))
    for copy in copies:
        copy.start()
    order_ref[...] = owner_order(width, rows_size, dp_size)
    hd = width // HEADS
    length = len_ref[0]
    inv_len = 1.0 / length.astype(f32)
    scale = hd ** -0.5
    steps = tokens // STEP

    copies[0].wait()
    for i in range(steps):
        rows = pl.ds(i * STEP, STEP)
        xhat, _ = standardize(ev_ref[rows, :].astype(f32))
        normed_ref[rows, :] = xhat.astype(bf16)

    def project(i, c):
        rows = pl.ds(i * STEP, STEP)
        pre = dot_nn(normed_ref[rows, :], win_ref[:, c * width:(c + 1) * width])
        sig = 0.5 + 0.5 * jnp.tanh(0.5 * pre)
        hid = pre * sig
        dsilu = sig * (1.0 + (pre - hid))
        if c == 0:
            user_ref[rows, :] = hid.astype(bf16)
            duser_ref[rows, :] = dsilu
        else:
            cols = slice((c - 1) * width, c * width)
            hid_ref[rows, cols] = hid.astype(bf16)
            if c == 1:
                dval_ref[rows, :] = dsilu
            else:
                dsilu_ref[rows, (c - 2) * width:(c - 1) * width] = dsilu.astype(bf16)

    for c in range(4):
        copies[1 + c].wait()
        for i in range(steps):
            project(i, c)

    tri = lax.broadcasted_iota(jnp.int32, (STEP, STEP), 0) >= lax.broadcasted_iota(jnp.int32, (STEP, STEP), 1)
    for h in range(HEADS):
        v_cols = slice(h * hd, (h + 1) * hd)
        q_cols = slice(width + h * hd, width + (h + 1) * hd)
        k_cols = slice(2 * width + h * hd, 2 * width + (h + 1) * hd)
        for i in range(steps):
            rows = pl.ds(i * STEP, STEP)
            query = hid_ref[rows, q_cols]
            total = None
            for j in range(i + 1):
                keys = pl.ds(j * STEP, STEP)
                half = dot_nt(query, hid_ref[keys, k_cols]) * (0.5 * scale)
                weights = (half + half * jnp.tanh(half)) * inv_len
                if i == j:
                    weights = jnp.where(tri, weights, 0.0)
                weights = weights.astype(bf16)
                weights_ref[h, rows, keys] = weights
                part = dot_nn(weights, hid_ref[keys, v_cols])
                total = part if total is None else total + part
            att_ref[rows, v_cols] = total

    copies[5].wait()
    copies[6].wait()
    for i in range(steps):
        rows = pl.ds(i * STEP, STEP)
        masked_ref[rows, :] = masked_rows(cot_ref[rows, :], i * STEP, length).astype(bf16)
        ahat, inv = standardize(att_ref[rows, :])
        user = user_ref[rows, :].astype(f32)
        mixed_ref[rows, :] = (ahat * user).astype(bf16)
        grad_mixed = dot_nt(masked_ref[rows, :], wout_ref[...])
        gpre_ref[rows, :width] = (grad_mixed * ahat * duser_ref[rows, :]).astype(bf16)
        e = grad_mixed * user
        gatt_ref[rows, :] = (inv * (e - jnp.mean(e, axis=-1, keepdims=True)
                                    - ahat * jnp.mean(e * ahat, axis=-1, keepdims=True))).astype(bf16)

    for h in range(HEADS):
        v_cols = slice(h * hd, (h + 1) * hd)
        for j in range(steps):
            keys, rest = pl.ds(j * STEP, STEP), pl.ds(j * STEP, tokens - j * STEP)
            grad_v = dot_tn(weights_ref[h, rest, keys], gatt_ref[rest, v_cols])
            gpre_ref[keys, width + h * hd:width + (h + 1) * hd] = (grad_v * dval_ref[keys, v_cols]).astype(bf16)

    order = order_ref[...]
    normed_t_ref[...] = dot_nt(order, normed_ref[...]).astype(bf16)
    mixed_t = dot_nt(order, mixed_ref[...]).astype(bf16)
    half = width // 2
    for ref, start in ((send_ref, half), (keep_ref, 0)):
        ref[:, :width] = dot_nn(mixed_t[start:start + half], masked_ref[...])
        ref[:, width:] = dot_nn(normed_t_ref[start:start + half, :], gpre_ref[...])


def attention_kernel(len_ref, hid_ref, dsilu_ref, gatt_ref, normed_t_ref, keep_ref, send_ref, gpre_ref):
    tokens, width = gatt_ref.shape
    hd = width // HEADS
    inv_len = 1.0 / len_ref[0].astype(f32)
    scale = hd ** -0.5
    steps = tokens // STEP

    factor = 0.5 * inv_len * scale
    tri = lax.broadcasted_iota(jnp.int32, (STEP, STEP), 0) <= lax.broadcasted_iota(jnp.int32, (STEP, STEP), 1)
    for h in range(HEADS):
        v_cols = slice(h * hd, (h + 1) * hd)
        q_cols = slice(width + h * hd, width + (h + 1) * hd)
        k_cols = slice(2 * width + h * hd, 2 * width + (h + 1) * hd)
        grad_q = [None] * steps
        for j in range(steps):
            keys = pl.ds(j * STEP, STEP)
            key, value = hid_ref[keys, k_cols], hid_ref[keys, v_cols]
            grad_k = None
            for i in range(j, steps):
                rows = pl.ds(i * STEP, STEP)
                query, gatt = hid_ref[rows, q_cols], gatt_ref[rows, v_cols]
                half = dot_nt(key, query) * (0.5 * scale)
                gate = jnp.tanh(half)
                dsilu = (1.0 + gate) * (1.0 + half * (1.0 - gate))
                gscore = dot_nt(value, gatt) * dsilu
                if i == j:
                    gscore = jnp.where(tri, gscore, 0.0)
                gscore = gscore.astype(bf16)
                pk, pq = dot_nn(gscore, query), dot_tn(gscore, key)
                grad_k = pk if grad_k is None else grad_k + pk
                grad_q[i] = pq if grad_q[i] is None else grad_q[i] + pq
            gpre_ref[keys, q_cols] = (grad_k * (dsilu_ref[keys, q_cols].astype(f32) * factor)).astype(bf16)
        for i in range(steps):
            rows = pl.ds(i * STEP, STEP)
            gpre_ref[rows, v_cols] = (grad_q[i] * (dsilu_ref[rows, v_cols].astype(f32) * factor)).astype(bf16)

    half = width // 2
    for ref, start in ((send_ref, half), (keep_ref, 0)):
        ref[...] = dot_nn(normed_t_ref[start:start + half, :], gpre_ref[...])


def slots_in_order(position, capacity, dp, rows):
    chips = rows // 2
    owner, place = over(position, capacity), rest(position, capacity)
    ahead, core, part = over(owner, 2 * dp), rest(over(owner, dp), 2), rest(owner, dp)
    chip = rest(lax.axis_index("rows") // 2 + ahead, chips)
    return part * rows + chip * 2 + core, place


def events_kernel(rows_size, dp_size, len_ref, ev_ref, cot_ref, win_ref, slot_ref, slot_row_ref, gpre_uv_ref, gpre_qk_ref, *refs):
    *send_refs, hi_ref, lo_ref, rows_ref = refs
    tokens, width = ev_ref.shape
    capacity, owners = slot_row_ref.shape
    length = len_ref[0]
    for i in range(tokens // STEP):
        rows = pl.ds(i * STEP, STEP)
        xhat, inv = standardize(ev_ref[rows, :].astype(f32))
        grad_normed = dot_nt(gpre_uv_ref[rows, :], win_ref[:, :2 * width]) + dot_nt(gpre_qk_ref[rows, :], win_ref[:, 2 * width:])
        grad = masked_rows(cot_ref[rows, :], i * STEP, length) + inv * (
            grad_normed - jnp.mean(grad_normed, axis=-1, keepdims=True)
            - xhat * jnp.mean(grad_normed * xhat, axis=-1, keepdims=True))
        high = grad.astype(bf16)
        hi_ref[rows, :] = high
        lo_ref[rows, :] = (grad - high.astype(f32)).astype(bf16)

    slots = rows_ref.shape[0]
    owner, place = slots_in_order(lax.broadcasted_iota(jnp.int32, (slots, 1), 0), capacity, dp_size, rows_size)
    rows_ref[...] = one_hot_rows(slot_ref[...], owner * capacity + place, hi_ref, lo_ref)
    owner, place = slots_in_order(lax.broadcasted_iota(jnp.int32, (1, slots), 1), capacity, dp_size, rows_size)
    chosen = lax.broadcasted_iota(jnp.int32, (owners, slots), 0) == owner
    mine = lax.broadcasted_iota(jnp.int32, (capacity, slots), 0) == place
    ids = whole_numbers(slot_row_ref[...], chosen, mine)
    tiles = width // LANES
    blocks = 2 * dp_size
    for k, send_ref in enumerate(send_refs):
        for i in range(blocks):
            at = (k * blocks + i) * capacity
            for t in range(tiles):
                send_ref[(i * tiles + t) * capacity:(i * tiles + t + 1) * capacity, :] = rows_ref[at:at + capacity, t * LANES:(t + 1) * LANES]
        tile = k * blocks * capacity // LANES * LANES
        send_ref[blocks * tiles * capacity:, :] = jnp.broadcast_to(ids[:, tile:tile + LANES], (ID_ROWS, LANES))


def whole_numbers(values, chosen, mine):
    pick = jnp.where(chosen, 1.0, 0.0).astype(bf16)
    found = 16.0 * dot_nn(over(values, 16).astype(bf16), pick) + dot_nn(rest(values, 16).astype(bf16), pick)
    return jnp.sum(jnp.where(mine, found, 0.0), axis=0, keepdims=True)


def id_rows(chips):
    return max(ID_ROWS, chips)


def by_part_kernel(dp, block, *refs):
    ins, outs = refs[:-dp], refs[-dp:]
    d = lax.axis_index("dp")
    for j, out_ref in enumerate(outs):
        part = jnp.bitwise_xor(d, j)
        for k, in_ref in enumerate(ins):
            for core in range(2):
                start = pl.multiple_of((core * dp + part) * block, block)
                out_ref[(k * 2 + core) * block:(k * 2 + core + 1) * block, :] = in_ref[pl.ds(start, block), :]
        ids = [in_ref[2 * dp * block:2 * dp * block + 1, :] for in_ref in ins]
        ids += [jnp.zeros((1, LANES), f32)] * (id_rows(len(ins)) - len(ins))
        out_ref[2 * len(ins) * block:, :] = jnp.concatenate(ids, axis=0)


def by_core_kernel(chips, block, *refs):
    *ins, keep_ref, send_ref = refs
    core = lax.rem(lax.axis_index("rows"), 2)
    for out_ref, to in ((send_ref, 1 - core), (keep_ref, core)):
        for j, in_ref in enumerate(ins):
            for k in range(chips):
                start = pl.multiple_of((k * 2 + to) * block, block)
                out_ref[(j * chips + k) * block:(j * chips + k + 1) * block, :] = in_ref[pl.ds(start, block), :]
            at = len(ins) * chips * block + j * id_rows(chips)
            out_ref[at:at + id_rows(chips), :] = in_ref[2 * chips * block:, :]


def one_hot_rows(ids, wanted, hi_ref, lo_ref):
    onehot = jnp.where(wanted == ids, 1.0, 0.0).astype(bf16)
    return dot_nn(onehot, hi_ref[...]) + dot_nn(onehot, lo_ref[...])


def table_kernel(dp, chips, keep_ref, recv_ref, table_ref, accum_ref, table_new_ref, accum_new_ref, rows_ref, hi_ref, lo_ref):
    rows, width = table_ref.shape
    tiles = width // LANES
    sources = dp * chips
    capacity = rows_ref.shape[0] // (2 * sources)
    count = sources * capacity
    r = lax.axis_index("rows")
    block = lax.rem(r, 2) * dp + lax.axis_index("dp")
    ids = []
    for side, ref in enumerate((keep_ref, recv_ref)):
        for i in range(sources):
            at = side * count + i * capacity
            for t in range(tiles):
                rows_ref[at:at + capacity, t * LANES:(t + 1) * LANES] = ref[(i * tiles + t) * capacity:(i * tiles + t + 1) * capacity, :]
        values = ref[sources * tiles * capacity:, :].astype(jnp.int32)
        position = lax.broadcasted_iota(jnp.int32, (1, count), 1)
        source, place = over(position, capacity), rest(position, capacity)
        part, ahead = over(source, chips), rest(source, chips)
        lane = rest(ahead * (2 * dp * capacity), LANES) + block * capacity + place
        chosen = lax.broadcasted_iota(jnp.int32, (LANES, count), 0) == lane
        mine = lax.broadcasted_iota(jnp.int32, (values.shape[0], count), 0) == part * id_rows(chips) + ahead
        ids.append(whole_numbers(values, chosen, mine))
    ids = jnp.concatenate(ids, axis=1).astype(jnp.int32)
    high = rows_ref[...].astype(bf16)
    hi_ref[...] = high
    lo_ref[...] = (rows_ref[...] - high.astype(f32)).astype(bf16)
    grad = one_hot_rows(ids, lax.broadcasted_iota(jnp.int32, (rows, 1), 0), hi_ref, lo_ref)
    accum = jnp.transpose(jnp.broadcast_to(accum_ref[...].reshape(1, rows), (8, rows)))[:, :1]
    accum_new = accum + jnp.mean(grad * grad, axis=-1, keepdims=True)
    accum_new_ref[...] = jnp.transpose(jnp.broadcast_to(accum_new, (rows, LANES)))[:1, :].reshape(rows)
    table_new_ref[...] = table_ref[...] - learning_rate * grad / (jnp.sqrt(accum_new) + adagrad_eps)


def place_on_dp():
    d = lax.axis_index("dp")
    return lax.rem(d, 2), d // 2


def first_kernel(keep1_ref, recv1_ref, keep2_ref, recv2_ref, to_x_ref, to_y_ref, keep_a_ref, keep_b_ref):
    x, y = place_on_dp()
    start = 0
    for keep_ref, recv_ref in ((keep1_ref, recv1_ref), (keep2_ref, recv2_ref)):
        half = keep_ref.shape[-1] // 2
        part = lambda i, j, cols: keep_ref[i, j, :, cols] + recv_ref[i, j, :, cols]
        lo, hi, out = slice(0, half), slice(half, 2 * half), slice(start, start + half)
        for s in range(2):
            to_x_ref[s, :, out] = part(s, 1 - x, lo)
            to_y_ref[s, :, out] = part(1 - y, s, hi)
            keep_a_ref[s, :, out] = part(s, x, lo)
            keep_b_ref[s, :, out] = part(y, s, hi)
        start += half


def second_kernel(keep_a_ref, from_x_ref, keep_b_ref, from_y_ref, to_y_ref, to_x_ref, next_a_ref, next_b_ref):
    x, y = place_on_dp()
    to_y_ref[...] = keep_a_ref[1 - y] + from_x_ref[1 - y]
    to_x_ref[...] = keep_b_ref[1 - x] + from_y_ref[1 - x]
    next_a_ref[...] = keep_a_ref[y] + from_x_ref[y]
    next_b_ref[...] = keep_b_ref[x] + from_y_ref[x]


def chips_kernel(next_a_ref, from_y_ref, next_b_ref, from_x_ref, *out_refs):
    chips = len(out_refs)
    chip = lax.axis_index("rows") // 2
    half = next_a_ref.shape[-1]
    for k, out_ref in enumerate(out_refs):
        at = lax.rem(chip + k, chips)
        out_ref[:, :half] = next_a_ref[at] + from_y_ref[at]
        out_ref[:, half:] = next_b_ref[at] + from_x_ref[at]


def total_kernel(tokens, *refs):
    total = refs[0][...]
    for ref in refs[1:-1]:
        total = total + ref[...]
    refs[-1][...] = total * (1.0 / tokens)


def gather_kernel(*refs):
    *pieces, grad_in_ref, grad_out_ref = refs
    d = lax.axis_index("dp")
    width = grad_out_ref.shape[-1]
    half = width // 2
    for k, piece in enumerate(pieces):
        at = jnp.bitwise_xor(d, k)
        grad_out_ref[at] = piece[:, :width]
        start = width
        for cols, first in ((half, 0), (width, 2 * width), (half, half), (width, width), (width, 3 * width)):
            grad_in_ref[at, :, first:first + cols] = piece[:, start:start + cols]
            start += cols


def vmem():
    return pl.BlockSpec(memory_space=pltpu.VMEM)


def shape(*dims, dtype=f32):
    return jax.ShapeDtypeStruct(dims, dtype)


def call(kernel, name, out_shape, args, scalars=0, scratch=(), far=0, long=False, grant=4, apart=(), either=()):
    place = [None] * scalars + [pltpu.HBM] * far + [pltpu.VMEM] * (len(args) - scalars - far)
    held = [None if i in either else pltpu.HBM if i in apart else p for i, p in enumerate(place)]
    args = [a if p is None else pltpu.with_memory_space_constraint(a, p) for a, p in zip(args, held)]
    return pl.pallas_call(
        kernel,
        name=name,
        in_specs=[pl.BlockSpec(memory_space=p or pltpu.SMEM) for p in place],
        out_specs=[vmem()] * len(out_shape),
        out_shape=list(out_shape),
        scratch_shapes=[pltpu.VMEM(dims, dtype) for dims, dtype in scratch] + [pltpu.SemaphoreType.DMA((7,))] * (far > 0),
        compiler_params=pltpu.CompilerParams(vmem_limit_bytes=grant * MIB),
        cost_estimate=pl.CostEstimate(flops=100_000_000_000 if long else 1_000_000_000, bytes_accessed=1 << 16, transcendentals=0),
    )(*args)


def body(rows_size, dp_size, events, cotangent, lengths, event_slot, slot_row, slot_count, w_in, w_out, item_table, accumulator):
    tokens, width = events.shape
    owners, capacity = slot_row.shape[1:]
    chips = rows_size // 2
    piece = width // (rows_size * dp_size)
    cores = [(i, i ^ 1) for i in range(rows_size)]
    over_dp = lambda v, bit: lax.ppermute(v, "dp", [(i, i ^ bit) for i in range(dp_size)])
    after = lambda value, *others: lax.optimization_barrier((value, *others))[0]
    strip = chips * piece

    def gathered(total):
        return [total] + [over_dp(total, k) for k in range(1, dp_size)]

    by_dp = lambda v: v.reshape(2, 2, strip, v.shape[-1])
    by_chip = lambda v: v.reshape(*v.shape[:-2], chips, piece, v.shape[-1])
    local = lambda *dims, dtype=f32: pltpu.VMEM(dims, dtype)
    sides = lambda cols: [local(width // 2, cols)] * 2
    keep1, send1, hid, dsilu, gatt, gpre_uv, normed_t, events, cotangent, w_in = call(
        functools.partial(forward_kernel, rows_size, dp_size), "forward_part",
        sides(3 * width) + [
            local(tokens, 3 * width, dtype=bf16),
            local(tokens, 2 * width, dtype=bf16),
            local(tokens, width, dtype=bf16),
            local(tokens, 2 * width, dtype=bf16),
            local(width, tokens, dtype=bf16),
            local(tokens, width, dtype=bf16),
            local(tokens, width, dtype=bf16),
            local(*w_in.shape, dtype=bf16),
        ],
        (lengths, events, cotangent, w_in, w_out), 1,
        [((tokens, width), bf16), ((tokens, width), bf16), ((tokens, width), f32), ((tokens, width), f32),
         ((tokens, width), bf16), ((tokens, width), bf16), ((tokens, width), f32), ((HEADS, tokens, tokens), bf16),
         (w_out.shape, bf16), ((width, width), bf16)], far=4, long=True, grant=16)
    recv1 = lax.ppermute(send1, "rows", cores)
    keep2, send2, gpre_qk = call(
        attention_kernel, "attention_part", sides(2 * width) + [local(tokens, 2 * width, dtype=bf16)],
        (lengths, hid, dsilu, gatt, normed_t), 1, long=True, grant=10)
    recv2 = lax.ppermute(send2, "rows", cores)
    block = capacity * (width // LANES)
    gpre_uv = after(gpre_uv, recv1)
    sends = call(
        functools.partial(events_kernel, rows_size, dp_size), "events_part",
        [local(2 * dp_size * block + ID_ROWS, LANES)] * chips,
        (lengths, events, cotangent, w_in, event_slot, slot_row[0].T, gpre_uv, gpre_qk), 1,
        [((tokens, width), bf16), ((tokens, width), bf16), ((owners * capacity, width), f32)], grant=10, long=True)
    ahead = lambda v, k: lax.ppermute(v, "rows", [(i, (i + 2 * k) % rows_size) for i in range(rows_size)])
    came = [sends[0]] + [ahead(sends[k], k) for k in range(1, chips)]
    cols = w_in.shape[1] + width
    to_x, to_y, keep_a, keep_b = call(
        first_kernel, "first_sums", [local(2, strip, cols // 2)] * 4,
        [by_dp(v) for v in (after(keep1, *sends), recv1, keep2, recv2)])
    from_x, from_y = over_dp(to_x, 1), over_dp(to_y, 2)
    to_y, to_x, next_a, next_b = call(
        second_kernel, "second_sums", [local(strip, cols // 2)] * 4, (keep_a, from_x, keep_b, from_y),
        long=True)
    from_y, from_x = over_dp(to_y, 2), over_dp(to_x, 1)
    came[0] = after(came[0], to_y, to_x)
    parts = call(
        functools.partial(by_part_kernel, dp_size, block), "by_part",
        [local(2 * chips * block + id_rows(chips), LANES)] * dp_size, came, long=True)
    next_a = after(next_a, *parts)
    sums = call(
        chips_kernel, "chip_sums", [local(piece, cols)] * chips,
        [by_chip(v) for v in (next_a, from_y, next_b, from_x)])
    parts = [parts[0]] + [over_dp(parts[k], k) for k in range(1, dp_size)]
    sums = [sums[0]] + [ahead(sums[k], k) for k in range(1, chips)]
    (total,) = call(
        functools.partial(total_kernel, tokens), "total", [local(piece, cols)], sums, long=True)
    pieces = gathered(total)
    parts[0] = after(parts[0], total)
    keep, send = call(
        functools.partial(by_core_kernel, chips, block), "by_core",
        [local(dp_size * (chips * block + id_rows(chips)), LANES)] * 2, parts, long=True)
    recv = lax.ppermute(send, "rows", cores)
    slots = owners * capacity
    table_new, accum_new = call(
        functools.partial(table_kernel, dp_size, chips), "table_part", [shape(*item_table.shape), shape(*accumulator.shape)],
        (keep, recv, item_table, accumulator), 0,
        [((slots, width), f32), ((slots, width), bf16), ((slots, width), bf16)], grant=10)
    pieces[-1] = after(pieces[-1], accum_new)
    grad_in, grad_out = call(
        gather_kernel, "gather", [shape(dp_size, piece, 4 * width), shape(dp_size, piece, width)], pieces)
    return grad_in.reshape(-1, 4 * width), grad_out.reshape(-1, width), table_new, accum_new


def solution(mesh):
    whole = P(("dp", "rows"))
    in_specs = (whole,) * 6 + (P(), P(), whole, whole)
    out_specs = (P("rows"), P("rows"), whole, whole)
    run = functools.partial(body, mesh.shape["rows"], mesh.shape["dp"])
    return jax.shard_map(run, mesh=mesh, in_specs=in_specs, out_specs=out_specs, check_vma=False)
```

```python
import functools

import jax
import jax.numpy as jnp
from jax import lax
from jax.experimental import pallas as pl
from jax.experimental.pallas import tpu as pltpu
from jax.sharding import PartitionSpec as P

HEADS = 4

norm_eps = 1e-05
adagrad_eps = 1e-10
learning_rate = 0.1

f32, bf16 = jnp.float32, jnp.bfloat16
MIB = 1024 * 1024
STEP = 256
LANES = 128
ID_ROWS = 8


def dot_nn(a, b):
    return lax.dot_general(a, b, (((1,), (0,)), ((), ())), preferred_element_type=f32)


def dot_nt(a, b):
    return lax.dot_general(a, b, (((1,), (1,)), ((), ())), preferred_element_type=f32)


def dot_tn(a, b):
    return lax.dot_general(a, b, (((0,), (0,)), ((), ())), preferred_element_type=f32)


def over(value, n):
    return value >> (n.bit_length() - 1) if n & (n - 1) == 0 else value // n


def rest(value, n):
    return value & (n - 1) if n & (n - 1) == 0 else value % n


def standardize(x):
    centered = x - jnp.mean(x, axis=-1, keepdims=True)
    inv = lax.rsqrt(jnp.mean(centered * centered, axis=-1, keepdims=True) + norm_eps)
    return centered * inv, inv


def masked_rows(cot, start, length):
    row = start + lax.broadcasted_iota(jnp.int32, cot.shape, 0)
    return jnp.where(row < length, cot.astype(f32), 0.0)


def owner_order(width, rows, dp):
    chips = rows // 2
    piece = width // (rows * dp)
    at = lax.broadcasted_iota(jnp.int32, (width, 1), 0)
    side, part = over(at, width // 2), rest(over(at, chips * piece), dp)
    chip, row = rest(over(at, piece), chips), rest(at, piece)
    core = lax.rem(lax.axis_index("rows"), 2)
    core = jnp.where(side == 0, core, 1 - core)
    wanted = ((chip * 2 + core) * dp + part) * piece + row
    return jnp.where(lax.broadcasted_iota(jnp.int32, (width, width), 1) == wanted, 1.0, 0.0).astype(bf16)


def forward_kernel(rows_size, dp_size, len_ref, ev_hbm, cot_hbm, win_hbm, wout_hbm,
                   keep_ref, send_ref, hid_ref, dsilu_ref, gatt_ref, gpre_ref, normed_t_ref,
                   ev_ref, cot_ref, win_ref, normed_ref, user_ref, duser_ref, att_ref, mixed_ref, masked_ref, dval_ref, weights_ref,
                   wout_ref, order_ref, grad_mixed_ref, arrived):
    tokens, width = ev_ref.shape
    copies = [pltpu.make_async_copy(ev_hbm, ev_ref, arrived.at[0])]
    for c in range(4):
        cols = pl.ds(c * width, width)
        copies.append(pltpu.make_async_copy(win_hbm.at[:, cols], win_ref.at[:, cols], arrived.at[1 + c]))
    copies.append(pltpu.make_async_copy(cot_hbm, cot_ref, arrived.at[5]))
    copies.append(pltpu.make_async_copy(wout_hbm, wout_ref, arrived.at[6]))
    for copy in copies:
        copy.start()
    order_ref[...] = owner_order(width, rows_size, dp_size)
    hd = width // HEADS
    length = len_ref[0]
    inv_len = 1.0 / length.astype(f32)
    scale = hd ** -0.5
    steps = tokens // STEP

    copies[0].wait()
    for i in range(steps):
        rows = pl.ds(i * STEP, STEP)
        xhat, _ = standardize(ev_ref[rows, :].astype(f32))
        normed_ref[rows, :] = xhat.astype(bf16)

    def project(i, c):
        rows = pl.ds(i * STEP, STEP)
        pre = dot_nn(normed_ref[rows, :], win_ref[:, c * width:(c + 1) * width])
        sig = 0.5 + 0.5 * jnp.tanh(0.5 * pre)
        hid = pre * sig
        dsilu = sig * (1.0 + (pre - hid))
        if c == 0:
            user_ref[rows, :] = hid.astype(bf16)
            duser_ref[rows, :] = dsilu
        else:
            cols = slice((c - 1) * width, c * width)
            hid_ref[rows, cols] = hid.astype(bf16)
            if c == 1:
                dval_ref[rows, :] = dsilu
            else:
                dsilu_ref[rows, (c - 2) * width:(c - 1) * width] = dsilu.astype(bf16)

    for c in range(4):
        copies[1 + c].wait()
        for i in range(steps):
            project(i, c)

    copies[5].wait()
    copies[6].wait()
    tri = lax.broadcasted_iota(jnp.int32, (STEP, STEP), 0) >= lax.broadcasted_iota(jnp.int32, (STEP, STEP), 1)
    for h in range(HEADS):
        v_cols = slice(h * hd, (h + 1) * hd)
        q_cols = slice(width + h * hd, width + (h + 1) * hd)
        k_cols = slice(2 * width + h * hd, 2 * width + (h + 1) * hd)
        for i in range(steps):
            rows = pl.ds(i * STEP, STEP)
            query = hid_ref[rows, q_cols]
            total = None
            for j in range(i + 1):
                keys = pl.ds(j * STEP, STEP)
                half = dot_nt(query, hid_ref[keys, k_cols]) * (0.5 * scale)
                weights = (half + half * jnp.tanh(half)) * inv_len
                if i == j:
                    weights = jnp.where(tri, weights, 0.0)
                weights = weights.astype(bf16)
                weights_ref[h, rows, keys] = weights
                part = dot_nn(weights, hid_ref[keys, v_cols])
                total = part if total is None else total + part
            att_ref[rows, v_cols] = total
        for i in range(h, steps, HEADS):
            rows = pl.ds(i * STEP, STEP)
            normed_t_ref[rows, :] = dot_nt(order_ref[rows, :], normed_ref[...]).astype(bf16)
        for i in range(h - HEADS // 2, steps, HEADS):
            if i >= 0:
                rows = pl.ds(i * STEP, STEP)
                masked_ref[rows, :] = masked_rows(cot_ref[rows, :], i * STEP, length).astype(bf16)
                grad_mixed_ref[rows, :] = dot_nt(masked_ref[rows, :], wout_ref[...])

    for i in range(steps):
        rows = pl.ds(i * STEP, STEP)
        ahat, inv = standardize(att_ref[rows, :])
        user = user_ref[rows, :].astype(f32)
        mixed_ref[rows, :] = (ahat * user).astype(bf16)
        grad_mixed = grad_mixed_ref[rows, :]
        gpre_ref[rows, :width] = (grad_mixed * ahat * duser_ref[rows, :]).astype(bf16)
        e = grad_mixed * user
        gatt_ref[rows, :] = (inv * (e - jnp.mean(e, axis=-1, keepdims=True)
                                    - ahat * jnp.mean(e * ahat, axis=-1, keepdims=True))).astype(bf16)

    for h in range(HEADS):
        v_cols = slice(h * hd, (h + 1) * hd)
        for j in range(steps):
            keys, rest = pl.ds(j * STEP, STEP), pl.ds(j * STEP, tokens - j * STEP)
            grad_v = dot_tn(weights_ref[h, rest, keys], gatt_ref[rest, v_cols])
            gpre_ref[keys, width + h * hd:width + (h + 1) * hd] = (grad_v * dval_ref[keys, v_cols]).astype(bf16)

    mixed_t = dot_nt(order_ref[...], mixed_ref[...]).astype(bf16)
    half = width // 2
    for ref, start in ((send_ref, half), (keep_ref, 0)):
        ref[:, :width] = dot_nn(mixed_t[start:start + half], masked_ref[...])
        ref[:, width:] = dot_nn(normed_t_ref[start:start + half, :], gpre_ref[...])


def attention_kernel(len_ref, hid_ref, dsilu_ref, gatt_ref, normed_t_ref, keep_ref, send_ref, gpre_ref):
    tokens, width = gatt_ref.shape
    hd = width // HEADS
    inv_len = 1.0 / len_ref[0].astype(f32)
    scale = hd ** -0.5
    steps = tokens // STEP

    factor = 0.5 * inv_len * scale
    tri = lax.broadcasted_iota(jnp.int32, (STEP, STEP), 0) <= lax.broadcasted_iota(jnp.int32, (STEP, STEP), 1)
    for h in range(HEADS):
        v_cols = slice(h * hd, (h + 1) * hd)
        q_cols = slice(width + h * hd, width + (h + 1) * hd)
        k_cols = slice(2 * width + h * hd, 2 * width + (h + 1) * hd)
        grad_q = [None] * steps
        for j in range(steps):
            keys = pl.ds(j * STEP, STEP)
            key, value = hid_ref[keys, k_cols], hid_ref[keys, v_cols]
            grad_k = None
            for i in range(j, steps):
                rows = pl.ds(i * STEP, STEP)
                query, gatt = hid_ref[rows, q_cols], gatt_ref[rows, v_cols]
                half = dot_nt(key, query) * (0.5 * scale)
                gate = jnp.tanh(half)
                dsilu = (1.0 + gate) * (1.0 + half * (1.0 - gate))
                gscore = dot_nt(value, gatt) * dsilu
                if i == j:
                    gscore = jnp.where(tri, gscore, 0.0)
                gscore = gscore.astype(bf16)
                pk, pq = dot_nn(gscore, query), dot_tn(gscore, key)
                grad_k = pk if grad_k is None else grad_k + pk
                grad_q[i] = pq if grad_q[i] is None else grad_q[i] + pq
            gpre_ref[keys, q_cols] = (grad_k * (dsilu_ref[keys, q_cols].astype(f32) * factor)).astype(bf16)
        for i in range(steps):
            rows = pl.ds(i * STEP, STEP)
            gpre_ref[rows, v_cols] = (grad_q[i] * (dsilu_ref[rows, v_cols].astype(f32) * factor)).astype(bf16)

    half = width // 2
    for ref, start in ((send_ref, half), (keep_ref, 0)):
        ref[...] = dot_nn(normed_t_ref[start:start + half, :], gpre_ref[...])


def slots_in_order(position, capacity, dp, rows):
    chips = rows // 2
    owner, place = over(position, capacity), rest(position, capacity)
    ahead, core, part = over(owner, 2 * dp), rest(over(owner, dp), 2), rest(owner, dp)
    chip = rest(lax.axis_index("rows") // 2 + ahead, chips)
    return part * rows + chip * 2 + core, place


def events_kernel(rows_size, dp_size, len_ref, ev_ref, cot_ref, win_ref, slot_ref, slot_row_ref, gpre_uv_ref, gpre_qk_ref, *refs):
    *send_refs, hi_ref, lo_ref, rows_ref = refs
    tokens, width = ev_ref.shape
    capacity, owners = slot_row_ref.shape
    length = len_ref[0]
    for i in range(tokens // STEP):
        rows = pl.ds(i * STEP, STEP)
        xhat, inv = standardize(ev_ref[rows, :].astype(f32))
        grad_normed = dot_nt(gpre_uv_ref[rows, :], win_ref[:, :2 * width]) + dot_nt(gpre_qk_ref[rows, :], win_ref[:, 2 * width:])
        grad = masked_rows(cot_ref[rows, :], i * STEP, length) + inv * (
            grad_normed - jnp.mean(grad_normed, axis=-1, keepdims=True)
            - xhat * jnp.mean(grad_normed * xhat, axis=-1, keepdims=True))
        high = grad.astype(bf16)
        hi_ref[rows, :] = high
        lo_ref[rows, :] = (grad - high.astype(f32)).astype(bf16)

    slots = rows_ref.shape[0]
    owner, place = slots_in_order(lax.broadcasted_iota(jnp.int32, (slots, 1), 0), capacity, dp_size, rows_size)
    rows_ref[...] = one_hot_rows(slot_ref[...], owner * capacity + place, hi_ref, lo_ref)
    owner, place = slots_in_order(lax.broadcasted_iota(jnp.int32, (1, slots), 1), capacity, dp_size, rows_size)
    chosen = lax.broadcasted_iota(jnp.int32, (owners, slots), 0) == owner
    mine = lax.broadcasted_iota(jnp.int32, (capacity, slots), 0) == place
    ids = whole_numbers(slot_row_ref[...], chosen, mine)
    tiles = width // LANES
    blocks = 2 * dp_size
    for k, send_ref in enumerate(send_refs):
        for i in range(blocks):
            at = (k * blocks + i) * capacity
            for t in range(tiles):
                send_ref[(i * tiles + t) * capacity:(i * tiles + t + 1) * capacity, :] = rows_ref[at:at + capacity, t * LANES:(t + 1) * LANES]
        tile = k * blocks * capacity // LANES * LANES
        send_ref[blocks * tiles * capacity:, :] = jnp.broadcast_to(ids[:, tile:tile + LANES], (ID_ROWS, LANES))


def whole_numbers(values, chosen, mine):
    pick = jnp.where(chosen, 1.0, 0.0).astype(bf16)
    found = 16.0 * dot_nn(over(values, 16).astype(bf16), pick) + dot_nn(rest(values, 16).astype(bf16), pick)
    return jnp.sum(jnp.where(mine, found, 0.0), axis=0, keepdims=True)


def id_rows(chips):
    return max(ID_ROWS, chips)


def by_part_kernel(dp, block, *refs):
    ins, outs = refs[:-dp], refs[-dp:]
    d = lax.axis_index("dp")
    for j, out_ref in enumerate(outs):
        part = jnp.bitwise_xor(d, j)
        for k, in_ref in enumerate(ins):
            for core in range(2):
                start = pl.multiple_of((core * dp + part) * block, block)
                out_ref[(k * 2 + core) * block:(k * 2 + core + 1) * block, :] = in_ref[pl.ds(start, block), :]
        ids = [in_ref[2 * dp * block:2 * dp * block + 1, :] for in_ref in ins]
        ids += [jnp.zeros((1, LANES), f32)] * (id_rows(len(ins)) - len(ins))
        out_ref[2 * len(ins) * block:, :] = jnp.concatenate(ids, axis=0)


def by_core_kernel(chips, block, *refs):
    *ins, keep_ref, send_ref = refs
    core = lax.rem(lax.axis_index("rows"), 2)
    for out_ref, to in ((send_ref, 1 - core), (keep_ref, core)):
        for j, in_ref in enumerate(ins):
            for k in range(chips):
                start = pl.multiple_of((k * 2 + to) * block, block)
                out_ref[(j * chips + k) * block:(j * chips + k + 1) * block, :] = in_ref[pl.ds(start, block), :]
            at = len(ins) * chips * block + j * id_rows(chips)
            out_ref[at:at + id_rows(chips), :] = in_ref[2 * chips * block:, :]


def one_hot_rows(ids, wanted, hi_ref, lo_ref):
    onehot = jnp.where(wanted == ids, 1.0, 0.0).astype(bf16)
    return dot_nn(onehot, hi_ref[...]) + dot_nn(onehot, lo_ref[...])


def table_kernel(dp, chips, keep_ref, recv_ref, table_ref, accum_ref, table_new_ref, accum_new_ref, rows_ref, hi_ref, lo_ref):
    rows, width = table_ref.shape
    tiles = width // LANES
    sources = dp * chips
    capacity = rows_ref.shape[0] // (2 * sources)
    count = sources * capacity
    r = lax.axis_index("rows")
    block = lax.rem(r, 2) * dp + lax.axis_index("dp")
    ids = []
    for side, ref in enumerate((keep_ref, recv_ref)):
        for i in range(sources):
            at = side * count + i * capacity
            for t in range(tiles):
                rows_ref[at:at + capacity, t * LANES:(t + 1) * LANES] = ref[(i * tiles + t) * capacity:(i * tiles + t + 1) * capacity, :]
        values = ref[sources * tiles * capacity:, :].astype(jnp.int32)
        position = lax.broadcasted_iota(jnp.int32, (1, count), 1)
        source, place = over(position, capacity), rest(position, capacity)
        part, ahead = over(source, chips), rest(source, chips)
        lane = rest(ahead * (2 * dp * capacity), LANES) + block * capacity + place
        chosen = lax.broadcasted_iota(jnp.int32, (LANES, count), 0) == lane
        mine = lax.broadcasted_iota(jnp.int32, (values.shape[0], count), 0) == part * id_rows(chips) + ahead
        ids.append(whole_numbers(values, chosen, mine))
    ids = jnp.concatenate(ids, axis=1).astype(jnp.int32)
    high = rows_ref[...].astype(bf16)
    hi_ref[...] = high
    lo_ref[...] = (rows_ref[...] - high.astype(f32)).astype(bf16)
    grad = one_hot_rows(ids, lax.broadcasted_iota(jnp.int32, (rows, 1), 0), hi_ref, lo_ref)
    accum = jnp.transpose(jnp.broadcast_to(accum_ref[...].reshape(1, rows), (8, rows)))[:, :1]
    accum_new = accum + jnp.mean(grad * grad, axis=-1, keepdims=True)
    accum_new_ref[...] = jnp.transpose(jnp.broadcast_to(accum_new, (rows, LANES)))[:1, :].reshape(rows)
    table_new_ref[...] = table_ref[...] - learning_rate * grad / (jnp.sqrt(accum_new) + adagrad_eps)


def place_on_dp():
    d = lax.axis_index("dp")
    return lax.rem(d, 2), d // 2


def first_kernel(keep1_ref, recv1_ref, keep2_ref, recv2_ref, to_x_ref, to_y_ref, keep_a_ref, keep_b_ref):
    x, y = place_on_dp()
    start = 0
    for keep_ref, recv_ref in ((keep1_ref, recv1_ref), (keep2_ref, recv2_ref)):
        half = keep_ref.shape[-1] // 2
        part = lambda i, j, cols: keep_ref[i, j, :, cols] + recv_ref[i, j, :, cols]
        lo, hi, out = slice(0, half), slice(half, 2 * half), slice(start, start + half)
        for s in range(2):
            to_x_ref[s, :, out] = part(s, 1 - x, lo)
            to_y_ref[s, :, out] = part(1 - y, s, hi)
            keep_a_ref[s, :, out] = part(s, x, lo)
            keep_b_ref[s, :, out] = part(y, s, hi)
        start += half


def second_kernel(keep_a_ref, from_x_ref, keep_b_ref, from_y_ref, to_y_ref, to_x_ref, next_a_ref, next_b_ref):
    x, y = place_on_dp()
    to_y_ref[...] = keep_a_ref[1 - y] + from_x_ref[1 - y]
    to_x_ref[...] = keep_b_ref[1 - x] + from_y_ref[1 - x]
    next_a_ref[...] = keep_a_ref[y] + from_x_ref[y]
    next_b_ref[...] = keep_b_ref[x] + from_y_ref[x]


def halve(bit, send_ref, keep_ref, keep_in, recv_in):
    mine = rest(lax.axis_index("rows") // 2 >> bit, 2)
    for i in range(send_ref.shape[0]):
        send_ref[i] = keep_in[2 * i + 1 - mine] + recv_in[2 * i + 1 - mine]
        keep_ref[i] = keep_in[2 * i + mine] + recv_in[2 * i + mine]


def chip_first_kernel(next_a_ref, from_y_ref, next_b_ref, from_x_ref, send_a_ref, keep_a_ref, send_b_ref, keep_b_ref):
    halve(0, send_a_ref, keep_a_ref, next_a_ref, from_y_ref)
    halve(0, send_b_ref, keep_b_ref, next_b_ref, from_x_ref)


def chip_kernel(bit, keep_in, recv_in, send_ref, keep_ref):
    halve(bit, send_ref, keep_ref, keep_in, recv_in)


def total_kernel(tokens, keep_a_ref, recv_a_ref, keep_b_ref, recv_b_ref, out_ref):
    half = keep_a_ref.shape[-1]
    out_ref[:, :half] = (keep_a_ref[0] + recv_a_ref[0]) * (1.0 / tokens)
    out_ref[:, half:] = (keep_b_ref[0] + recv_b_ref[0]) * (1.0 / tokens)


def gather_kernel(*refs):
    *pieces, grad_in_ref, grad_out_ref = refs
    d = lax.axis_index("dp")
    width = grad_out_ref.shape[-1]
    half = width // 2
    for k, piece in enumerate(pieces):
        at = jnp.bitwise_xor(d, k)
        grad_out_ref[at] = piece[:, :width]
        start = width
        for cols, first in ((half, 0), (width, 2 * width), (half, half), (width, width), (width, 3 * width)):
            grad_in_ref[at, :, first:first + cols] = piece[:, start:start + cols]
            start += cols


def vmem():
    return pl.BlockSpec(memory_space=pltpu.VMEM)


def shape(*dims, dtype=f32):
    return jax.ShapeDtypeStruct(dims, dtype)


def call(kernel, name, out_shape, args, scalars=0, scratch=(), far=0, long=False, grant=4, apart=(), either=()):
    place = [None] * scalars + [pltpu.HBM] * far + [pltpu.VMEM] * (len(args) - scalars - far)
    held = [None if i in either else pltpu.HBM if i in apart else p for i, p in enumerate(place)]
    args = [a if p is None else pltpu.with_memory_space_constraint(a, p) for a, p in zip(args, held)]
    return pl.pallas_call(
        kernel,
        name=name,
        in_specs=[pl.BlockSpec(memory_space=p or pltpu.SMEM) for p in place],
        out_specs=[vmem()] * len(out_shape),
        out_shape=list(out_shape),
        scratch_shapes=[pltpu.VMEM(dims, dtype) for dims, dtype in scratch] + [pltpu.SemaphoreType.DMA((7,))] * (far > 0),
        compiler_params=pltpu.CompilerParams(vmem_limit_bytes=grant * MIB),
        cost_estimate=pl.CostEstimate(flops=100_000_000_000 if long else 1_000_000_000, bytes_accessed=1 << 16, transcendentals=0),
    )(*args)


def body(rows_size, dp_size, events, cotangent, lengths, event_slot, slot_row, slot_count, w_in, w_out, item_table, accumulator):
    tokens, width = events.shape
    owners, capacity = slot_row.shape[1:]
    chips = rows_size // 2
    piece = width // (rows_size * dp_size)
    cores = [(i, i ^ 1) for i in range(rows_size)]
    over_dp = lambda v, bit: lax.ppermute(v, "dp", [(i, i ^ bit) for i in range(dp_size)])
    after = lambda value, *others: lax.optimization_barrier((value, *others))[0]
    strip = chips * piece

    def gathered(total):
        return [total] + [over_dp(total, k) for k in range(1, dp_size)]

    by_dp = lambda v: v.reshape(2, 2, strip, v.shape[-1])
    by_chip = lambda v: v.reshape(*v.shape[:-2], chips, piece, v.shape[-1])
    local = lambda *dims, dtype=f32: pltpu.VMEM(dims, dtype)
    sides = lambda cols: [local(width // 2, cols)] * 2
    keep1, send1, hid, dsilu, gatt, gpre_uv, normed_t, events, cotangent, w_in = call(
        functools.partial(forward_kernel, rows_size, dp_size), "forward_part",
        sides(3 * width) + [
            local(tokens, 3 * width, dtype=bf16),
            local(tokens, 2 * width, dtype=bf16),
            local(tokens, width, dtype=bf16),
            local(tokens, 2 * width, dtype=bf16),
            local(width, tokens, dtype=bf16),
            local(tokens, width, dtype=bf16),
            local(tokens, width, dtype=bf16),
            local(*w_in.shape, dtype=bf16),
        ],
        (lengths, events, cotangent, w_in, w_out), 1,
        [((tokens, width), bf16), ((tokens, width), bf16), ((tokens, width), f32), ((tokens, width), f32),
         ((tokens, width), bf16), ((tokens, width), bf16), ((tokens, width), f32), ((HEADS, tokens, tokens), bf16),
         (w_out.shape, bf16), ((width, width), bf16), ((tokens, width), f32)], far=4, long=True, grant=16)
    recv1 = lax.ppermute(send1, "rows", cores)
    keep2, send2, gpre_qk = call(
        attention_kernel, "attention_part", sides(2 * width) + [local(tokens, 2 * width, dtype=bf16)],
        (lengths, hid, dsilu, gatt, normed_t), 1, long=True, grant=10)
    recv2 = lax.ppermute(send2, "rows", cores)
    block = capacity * (width // LANES)
    gpre_uv = after(gpre_uv, recv1)
    sends = call(
        functools.partial(events_kernel, rows_size, dp_size), "events_part",
        [local(2 * dp_size * block + ID_ROWS, LANES)] * chips,
        (lengths, events, cotangent, w_in, event_slot, slot_row[0].T, gpre_uv, gpre_qk), 1,
        [((tokens, width), bf16), ((tokens, width), bf16), ((owners * capacity, width), f32)], grant=10, long=True)
    ahead = lambda v, k: lax.ppermute(v, "rows", [(i, (i + 2 * k) % rows_size) for i in range(rows_size)])
    came = [sends[0]] + [ahead(sends[k], k) for k in range(1, chips)]
    cols = w_in.shape[1] + width
    to_x, to_y, keep_a, keep_b = call(
        first_kernel, "first_sums", [local(2, strip, cols // 2)] * 4,
        [by_dp(v) for v in (after(keep1, *sends), recv1, keep2, recv2)])
    from_x, from_y = over_dp(to_x, 1), over_dp(to_y, 2)
    to_y, to_x, next_a, next_b = call(
        second_kernel, "second_sums", [local(strip, cols // 2)] * 4, (keep_a, from_x, keep_b, from_y),
        long=True)
    from_y, from_x = over_dp(to_y, 2), over_dp(to_x, 1)
    came[0] = after(came[0], to_y, to_x)
    parts = call(
        functools.partial(by_part_kernel, dp_size, block), "by_part",
        [local(2 * chips * block + id_rows(chips), LANES)] * dp_size, came, long=True)
    next_a = after(next_a, *parts)
    bits = chips.bit_length() - 1
    over_chips = lambda v, bit: lax.ppermute(v, "rows", [(i, i ^ (2 << bit)) for i in range(rows_size)])
    send_a, keep_a, send_b, keep_b = call(
        chip_first_kernel, "chip_sums", [local(chips // 2, piece, cols // 2)] * 4,
        [by_chip(v) for v in (next_a, from_y, next_b, from_x)])
    halves = [[keep_a, over_chips(send_a, 0)], [keep_b, over_chips(send_b, 0)]]
    parts = [parts[0]] + [over_dp(parts[k], k) for k in range(1, dp_size)]
    for bit in range(1, bits):
        for i in range(2):
            if i == 1:
                halves[1][0] = after(halves[1][0], send, keep)
            send, keep = call(
                functools.partial(chip_kernel, bit), "chip_sums", [local(chips >> (bit + 1), piece, cols // 2)] * 2,
                halves[i], long=False)
            halves[i] = [keep, over_chips(send, bit)]
    (total,) = call(
        functools.partial(total_kernel, tokens), "total", [local(piece, cols)], halves[0] + halves[1], long=False)
    pieces = gathered(total)
    parts[0] = after(parts[0], total)
    keep, send = call(
        functools.partial(by_core_kernel, chips, block), "by_core",
        [local(dp_size * (chips * block + id_rows(chips)), LANES)] * 2, parts, long=False)
    recv = lax.ppermute(send, "rows", cores)
    slots = owners * capacity
    table_new, accum_new = call(
        functools.partial(table_kernel, dp_size, chips), "table_part", [shape(*item_table.shape), shape(*accumulator.shape)],
        (keep, recv, item_table, accumulator), 0,
        [((slots, width), f32), ((slots, width), bf16), ((slots, width), bf16)], grant=10)
    pieces[-1] = after(pieces[-1], accum_new)
    grad_in, grad_out = call(
        gather_kernel, "gather", [shape(dp_size, piece, 4 * width), shape(dp_size, piece, width)], pieces)
    return grad_in.reshape(-1, 4 * width), grad_out.reshape(-1, width), table_new, accum_new


def solution(mesh):
    whole = P(("dp", "rows"))
    in_specs = (whole,) * 6 + (P(), P(), whole, whole)
    out_specs = (P("rows"), P("rows"), whole, whole)
    run = functools.partial(body, mesh.shape["rows"], mesh.shape["dp"])
    return jax.shard_map(run, mesh=mesh, in_specs=in_specs, out_specs=out_specs, check_vma=False)
```

```python
import functools

import jax
import jax.numpy as jnp
from jax import lax
from jax.experimental import pallas as pl
from jax.experimental.pallas import tpu as pltpu
from jax.sharding import PartitionSpec as P

HEADS = 4

norm_eps = 1e-05
adagrad_eps = 1e-10
learning_rate = 0.1

f32, bf16 = jnp.float32, jnp.bfloat16
MIB = 1024 * 1024
STEP = 256
LANES = 128
ID_ROWS = 8


def dot_nn(a, b):
    return lax.dot_general(a, b, (((1,), (0,)), ((), ())), preferred_element_type=f32)


def dot_nt(a, b):
    return lax.dot_general(a, b, (((1,), (1,)), ((), ())), preferred_element_type=f32)


def dot_tn(a, b):
    return lax.dot_general(a, b, (((0,), (0,)), ((), ())), preferred_element_type=f32)


def over(value, n):
    return value >> (n.bit_length() - 1) if n & (n - 1) == 0 else value // n


def rest(value, n):
    return value & (n - 1) if n & (n - 1) == 0 else value % n


def standardize(x):
    centered = x - jnp.mean(x, axis=-1, keepdims=True)
    inv = lax.rsqrt(jnp.mean(centered * centered, axis=-1, keepdims=True) + norm_eps)
    return centered * inv, inv


def masked_rows(cot, start, length):
    row = start + lax.broadcasted_iota(jnp.int32, cot.shape, 0)
    return jnp.where(row < length, cot.astype(f32), 0.0)


def owner_order(width, rows, dp):
    chips = rows // 2
    piece = width // (rows * dp)
    at = lax.broadcasted_iota(jnp.int32, (width, 1), 0)
    side, part = over(at, width // 2), rest(over(at, chips * piece), dp)
    chip, row = rest(over(at, piece), chips), rest(at, piece)
    core = lax.rem(lax.axis_index("rows"), 2)
    core = jnp.where(side == 0, core, 1 - core)
    wanted = ((chip * 2 + core) * dp + part) * piece + row
    return jnp.where(lax.broadcasted_iota(jnp.int32, (width, width), 1) == wanted, 1.0, 0.0).astype(bf16)


def forward_kernel(rows_size, dp_size, len_ref, ev_hbm, cot_hbm, win_hbm, wout_hbm,
                   keep_ref, send_ref, hid_ref, dsilu_ref, gatt_ref, gpre_ref, normed_t_ref,
                   ev_ref, cot_ref, win_ref, normed_ref, user_ref, duser_ref, att_ref, mixed_ref, masked_ref, dval_ref, weights_ref,
                   wout_ref, order_ref, grad_mixed_ref, arrived):
    tokens, width = ev_ref.shape
    copies = [pltpu.make_async_copy(ev_hbm, ev_ref, arrived.at[0])]
    for c in range(4):
        cols = pl.ds(c * width, width)
        copies.append(pltpu.make_async_copy(win_hbm.at[:, cols], win_ref.at[:, cols], arrived.at[1 + c]))
    copies.append(pltpu.make_async_copy(cot_hbm, cot_ref, arrived.at[5]))
    copies.append(pltpu.make_async_copy(wout_hbm, wout_ref, arrived.at[6]))
    for copy in copies:
        copy.start()
    order_ref[...] = owner_order(width, rows_size, dp_size)
    hd = width // HEADS
    length = len_ref[0]
    inv_len = 1.0 / length.astype(f32)
    scale = hd ** -0.5
    steps = tokens // STEP

    copies[0].wait()
    for i in range(steps):
        rows = pl.ds(i * STEP, STEP)
        xhat, _ = standardize(ev_ref[rows, :].astype(f32))
        normed_ref[rows, :] = xhat.astype(bf16)

    def project(i, c):
        rows = pl.ds(i * STEP, STEP)
        pre = dot_nn(normed_ref[rows, :], win_ref[:, c * width:(c + 1) * width])
        sig = 0.5 + 0.5 * jnp.tanh(0.5 * pre)
        hid = pre * sig
        dsilu = sig * (1.0 + (pre - hid))
        if c == 0:
            user_ref[rows, :] = hid.astype(bf16)
            duser_ref[rows, :] = dsilu
        else:
            cols = slice((c - 1) * width, c * width)
            hid_ref[rows, cols] = hid.astype(bf16)
            if c == 1:
                dval_ref[rows, :] = dsilu
            else:
                dsilu_ref[rows, (c - 2) * width:(c - 1) * width] = dsilu.astype(bf16)

    for c in range(4):
        copies[1 + c].wait()
        for i in range(steps):
            project(i, c)

    copies[5].wait()
    copies[6].wait()
    tri = lax.broadcasted_iota(jnp.int32, (STEP, STEP), 0) >= lax.broadcasted_iota(jnp.int32, (STEP, STEP), 1)
    for h in range(HEADS):
        v_cols = slice(h * hd, (h + 1) * hd)
        q_cols = slice(width + h * hd, width + (h + 1) * hd)
        k_cols = slice(2 * width + h * hd, 2 * width + (h + 1) * hd)
        for i in range(steps):
            rows = pl.ds(i * STEP, STEP)
            query = hid_ref[rows, q_cols]
            total = None
            for j in range(i + 1):
                keys = pl.ds(j * STEP, STEP)
                half = dot_nt(query, hid_ref[keys, k_cols]) * (0.5 * scale)
                weights = (half + half * jnp.tanh(half)) * inv_len
                if i == j:
                    weights = jnp.where(tri, weights, 0.0)
                weights = weights.astype(bf16)
                weights_ref[h, rows, keys] = weights
                part = dot_nn(weights, hid_ref[keys, v_cols])
                total = part if total is None else total + part
            att_ref[rows, v_cols] = total
        for i in range(h, steps, HEADS):
            rows = pl.ds(i * STEP, STEP)
            normed_t_ref[rows, :] = dot_nt(order_ref[rows, :], normed_ref[...]).astype(bf16)
        for i in range(h - HEADS // 2, steps, HEADS):
            if i >= 0:
                rows = pl.ds(i * STEP, STEP)
                masked_ref[rows, :] = masked_rows(cot_ref[rows, :], i * STEP, length).astype(bf16)
                grad_mixed_ref[rows, :] = dot_nt(masked_ref[rows, :], wout_ref[...])

    for i in range(steps):
        rows = pl.ds(i * STEP, STEP)
        ahat, inv = standardize(att_ref[rows, :])
        user = user_ref[rows, :].astype(f32)
        mixed_ref[rows, :] = (ahat * user).astype(bf16)
        grad_mixed = grad_mixed_ref[rows, :]
        gpre_ref[rows, :width] = (grad_mixed * ahat * duser_ref[rows, :]).astype(bf16)
        e = grad_mixed * user
        gatt_ref[rows, :] = (inv * (e - jnp.mean(e, axis=-1, keepdims=True)
                                    - ahat * jnp.mean(e * ahat, axis=-1, keepdims=True))).astype(bf16)

    for h in range(HEADS):
        v_cols = slice(h * hd, (h + 1) * hd)
        for j in range(steps):
            keys, rest = pl.ds(j * STEP, STEP), pl.ds(j * STEP, tokens - j * STEP)
            grad_v = dot_tn(weights_ref[h, rest, keys], gatt_ref[rest, v_cols])
            gpre_ref[keys, width + h * hd:width + (h + 1) * hd] = (grad_v * dval_ref[keys, v_cols]).astype(bf16)

    mixed_t = dot_nt(order_ref[...], mixed_ref[...]).astype(bf16)
    half = width // 2
    for ref, start in ((send_ref, half), (keep_ref, 0)):
        ref[:, :width] = dot_nn(mixed_t[start:start + half], masked_ref[...])
        ref[:, width:] = dot_nn(normed_t_ref[start:start + half, :], gpre_ref[...])


def attention_kernel(len_ref, hid_ref, dsilu_ref, gatt_ref, normed_t_ref, keep_ref, send_ref, gpre_ref):
    tokens, width = gatt_ref.shape
    hd = width // HEADS
    inv_len = 1.0 / len_ref[0].astype(f32)
    scale = hd ** -0.5
    steps = tokens // STEP

    factor = 0.5 * inv_len * scale
    tri = lax.broadcasted_iota(jnp.int32, (STEP, STEP), 0) <= lax.broadcasted_iota(jnp.int32, (STEP, STEP), 1)
    for h in range(HEADS):
        v_cols = slice(h * hd, (h + 1) * hd)
        q_cols = slice(width + h * hd, width + (h + 1) * hd)
        k_cols = slice(2 * width + h * hd, 2 * width + (h + 1) * hd)
        grad_q = [None] * steps
        for j in range(steps):
            keys = pl.ds(j * STEP, STEP)
            key, value = hid_ref[keys, k_cols], hid_ref[keys, v_cols]
            grad_k = None
            for i in range(j, steps):
                rows = pl.ds(i * STEP, STEP)
                query, gatt = hid_ref[rows, q_cols], gatt_ref[rows, v_cols]
                half = dot_nt(key, query) * (0.5 * scale)
                gate = jnp.tanh(half)
                dsilu = (1.0 + gate) * (1.0 + half * (1.0 - gate))
                gscore = dot_nt(value, gatt) * dsilu
                if i == j:
                    gscore = jnp.where(tri, gscore, 0.0)
                gscore = gscore.astype(bf16)
                pk, pq = dot_nn(gscore, query), dot_tn(gscore, key)
                grad_k = pk if grad_k is None else grad_k + pk
                grad_q[i] = pq if grad_q[i] is None else grad_q[i] + pq
            gpre_ref[keys, q_cols] = (grad_k * (dsilu_ref[keys, q_cols].astype(f32) * factor)).astype(bf16)
        for i in range(steps):
            rows = pl.ds(i * STEP, STEP)
            gpre_ref[rows, v_cols] = (grad_q[i] * (dsilu_ref[rows, v_cols].astype(f32) * factor)).astype(bf16)

    half = width // 2
    for ref, start in ((send_ref, half), (keep_ref, 0)):
        ref[...] = dot_nn(normed_t_ref[start:start + half, :], gpre_ref[...])


def slots_in_order(position, capacity, dp, rows):
    chips = rows // 2
    owner, place = over(position, capacity), rest(position, capacity)
    ahead, core, part = over(owner, 2 * dp), rest(over(owner, dp), 2), rest(owner, dp)
    chip = rest(lax.axis_index("rows") // 2 + ahead, chips)
    return part * rows + chip * 2 + core, place


def events_kernel(rows_size, dp_size, len_ref, ev_ref, cot_ref, win_ref, slot_ref, slot_row_ref, gpre_uv_ref, gpre_qk_ref, *refs):
    *send_refs, hi_ref, lo_ref, rows_ref = refs
    tokens, width = ev_ref.shape
    capacity, owners = slot_row_ref.shape
    length = len_ref[0]
    for i in range(tokens // STEP):
        rows = pl.ds(i * STEP, STEP)
        xhat, inv = standardize(ev_ref[rows, :].astype(f32))
        grad_normed = dot_nt(gpre_uv_ref[rows, :], win_ref[:, :2 * width]) + dot_nt(gpre_qk_ref[rows, :], win_ref[:, 2 * width:])
        grad = masked_rows(cot_ref[rows, :], i * STEP, length) + inv * (
            grad_normed - jnp.mean(grad_normed, axis=-1, keepdims=True)
            - xhat * jnp.mean(grad_normed * xhat, axis=-1, keepdims=True))
        high = grad.astype(bf16)
        hi_ref[rows, :] = high
        lo_ref[rows, :] = (grad - high.astype(f32)).astype(bf16)

    slots = rows_ref.shape[0]
    owner, place = slots_in_order(lax.broadcasted_iota(jnp.int32, (slots, 1), 0), capacity, dp_size, rows_size)
    rows_ref[...] = one_hot_rows(slot_ref[...], owner * capacity + place, hi_ref, lo_ref)
    owner, place = slots_in_order(lax.broadcasted_iota(jnp.int32, (1, slots), 1), capacity, dp_size, rows_size)
    chosen = lax.broadcasted_iota(jnp.int32, (owners, slots), 0) == owner
    mine = lax.broadcasted_iota(jnp.int32, (capacity, slots), 0) == place
    ids = whole_numbers(slot_row_ref[...], chosen, mine)
    tiles = width // LANES
    blocks = 2 * dp_size
    for k, send_ref in enumerate(send_refs):
        for i in range(blocks):
            at = (k * blocks + i) * capacity
            for t in range(tiles):
                send_ref[(i * tiles + t) * capacity:(i * tiles + t + 1) * capacity, :] = rows_ref[at:at + capacity, t * LANES:(t + 1) * LANES]
        tile = k * blocks * capacity // LANES * LANES
        send_ref[blocks * tiles * capacity:, :] = jnp.broadcast_to(ids[:, tile:tile + LANES], (ID_ROWS, LANES))


def whole_numbers(values, chosen, mine):
    pick = jnp.where(chosen, 1.0, 0.0).astype(bf16)
    found = 16.0 * dot_nn(over(values, 16).astype(bf16), pick) + dot_nn(rest(values, 16).astype(bf16), pick)
    return jnp.sum(jnp.where(mine, found, 0.0), axis=0, keepdims=True)


def id_rows(chips):
    return max(ID_ROWS, chips)


def by_part_kernel(dp, block, *refs):
    ins, outs = refs[:-dp], refs[-dp:]
    d = lax.axis_index("dp")
    for j, out_ref in enumerate(outs):
        part = jnp.bitwise_xor(d, j)
        for k, in_ref in enumerate(ins):
            for core in range(2):
                start = pl.multiple_of((core * dp + part) * block, block)
                out_ref[(k * 2 + core) * block:(k * 2 + core + 1) * block, :] = in_ref[pl.ds(start, block), :]
        ids = [in_ref[2 * dp * block:2 * dp * block + 1, :] for in_ref in ins]
        ids += [jnp.zeros((1, LANES), f32)] * (id_rows(len(ins)) - len(ins))
        out_ref[2 * len(ins) * block:, :] = jnp.concatenate(ids, axis=0)


def by_core_kernel(chips, block, *refs):
    *ins, keep_ref, send_ref = refs
    core = lax.rem(lax.axis_index("rows"), 2)
    for out_ref, to in ((send_ref, 1 - core), (keep_ref, core)):
        for j, in_ref in enumerate(ins):
            for k in range(chips):
                start = pl.multiple_of((k * 2 + to) * block, block)
                out_ref[(j * chips + k) * block:(j * chips + k + 1) * block, :] = in_ref[pl.ds(start, block), :]
            at = len(ins) * chips * block + j * id_rows(chips)
            out_ref[at:at + id_rows(chips), :] = in_ref[2 * chips * block:, :]


def one_hot_rows(ids, wanted, hi_ref, lo_ref):
    onehot = jnp.where(wanted == ids, 1.0, 0.0).astype(bf16)
    return dot_nn(onehot, hi_ref[...]) + dot_nn(onehot, lo_ref[...])


def table_kernel(dp, chips, keep_ref, recv_ref, table_ref, accum_ref, table_new_ref, accum_new_ref, rows_ref, hi_ref, lo_ref):
    rows, width = table_ref.shape
    tiles = width // LANES
    sources = dp * chips
    capacity = rows_ref.shape[0] // (2 * sources)
    count = sources * capacity
    r = lax.axis_index("rows")
    block = lax.rem(r, 2) * dp + lax.axis_index("dp")
    ids = []
    for side, ref in enumerate((keep_ref, recv_ref)):
        for i in range(sources):
            at = side * count + i * capacity
            for t in range(tiles):
                rows_ref[at:at + capacity, t * LANES:(t + 1) * LANES] = ref[(i * tiles + t) * capacity:(i * tiles + t + 1) * capacity, :]
        values = ref[sources * tiles * capacity:, :].astype(jnp.int32)
        position = lax.broadcasted_iota(jnp.int32, (1, count), 1)
        source, place = over(position, capacity), rest(position, capacity)
        part, ahead = over(source, chips), rest(source, chips)
        lane = rest(ahead * (2 * dp * capacity), LANES) + block * capacity + place
        chosen = lax.broadcasted_iota(jnp.int32, (LANES, count), 0) == lane
        mine = lax.broadcasted_iota(jnp.int32, (values.shape[0], count), 0) == part * id_rows(chips) + ahead
        ids.append(whole_numbers(values, chosen, mine))
    ids = jnp.concatenate(ids, axis=1).astype(jnp.int32)
    high = rows_ref[...].astype(bf16)
    hi_ref[...] = high
    lo_ref[...] = (rows_ref[...] - high.astype(f32)).astype(bf16)
    grad = one_hot_rows(ids, lax.broadcasted_iota(jnp.int32, (rows, 1), 0), hi_ref, lo_ref)
    accum = jnp.transpose(jnp.broadcast_to(accum_ref[...].reshape(1, rows), (8, rows)))[:, :1]
    accum_new = accum + jnp.mean(grad * grad, axis=-1, keepdims=True)
    accum_new_ref[...] = jnp.transpose(jnp.broadcast_to(accum_new, (rows, LANES)))[:1, :].reshape(rows)
    table_new_ref[...] = table_ref[...] - learning_rate * grad / (jnp.sqrt(accum_new) + adagrad_eps)


def place_on_dp():
    d = lax.axis_index("dp")
    return lax.rem(d, 2), d // 2


def first_kernel(keep1_ref, recv1_ref, keep2_ref, recv2_ref, to_x_ref, to_y_ref, keep_a_ref, keep_b_ref):
    x, y = place_on_dp()
    start = 0
    for keep_ref, recv_ref in ((keep1_ref, recv1_ref), (keep2_ref, recv2_ref)):
        half = keep_ref.shape[-1] // 2
        part = lambda i, j, cols: keep_ref[i, j, :, cols] + recv_ref[i, j, :, cols]
        lo, hi, out = slice(0, half), slice(half, 2 * half), slice(start, start + half)
        for s in range(2):
            to_x_ref[s, :, out] = part(s, 1 - x, lo)
            to_y_ref[s, :, out] = part(1 - y, s, hi)
            keep_a_ref[s, :, out] = part(s, x, lo)
            keep_b_ref[s, :, out] = part(y, s, hi)
        start += half


def second_kernel(keep_a_ref, from_x_ref, keep_b_ref, from_y_ref, to_y_ref, to_x_ref, next_a_ref, next_b_ref):
    x, y = place_on_dp()
    to_y_ref[...] = keep_a_ref[1 - y] + from_x_ref[1 - y]
    to_x_ref[...] = keep_b_ref[1 - x] + from_y_ref[1 - x]
    next_a_ref[...] = keep_a_ref[y] + from_x_ref[y]
    next_b_ref[...] = keep_b_ref[x] + from_y_ref[x]


def halve(bit, send_ref, keep_ref, keep_in, recv_in):
    mine = rest(lax.axis_index("rows") // 2 >> bit, 2)
    for i in range(send_ref.shape[0]):
        send_ref[i] = keep_in[2 * i + 1 - mine] + recv_in[2 * i + 1 - mine]
        keep_ref[i] = keep_in[2 * i + mine] + recv_in[2 * i + mine]


def chip_first_kernel(next_a_ref, from_y_ref, next_b_ref, from_x_ref, send_a_ref, keep_a_ref, send_b_ref, keep_b_ref):
    halve(0, send_a_ref, keep_a_ref, next_a_ref, from_y_ref)
    halve(0, send_b_ref, keep_b_ref, next_b_ref, from_x_ref)


def chip_kernel(bit, keep_in, recv_in, send_ref, keep_ref):
    halve(bit, send_ref, keep_ref, keep_in, recv_in)


def total_kernel(tokens, keep_ref, recv_ref, out_ref):
    out_ref[...] = (keep_ref[0] + recv_ref[0]) * (1.0 / tokens)


def gather_kernel(*refs):
    *pieces, grad_in_ref, grad_out_ref = refs
    dp = len(pieces) // 2
    d = lax.axis_index("dp")
    width = grad_out_ref.shape[-1]
    half = width // 2
    for k in range(dp):
        at = jnp.bitwise_xor(d, k)
        piece, piece_b = pieces[k], pieces[dp + k]
        grad_out_ref[at] = piece[:, :width]
        grad_in_ref[at, :, :half] = piece[:, width:width + half]
        grad_in_ref[at, :, half:2 * width] = piece_b[:, :width + half]
        grad_in_ref[at, :, 2 * width:3 * width] = piece[:, width + half:]
        grad_in_ref[at, :, 3 * width:] = piece_b[:, width + half:]


def vmem():
    return pl.BlockSpec(memory_space=pltpu.VMEM)


def shape(*dims, dtype=f32):
    return jax.ShapeDtypeStruct(dims, dtype)


def call(kernel, name, out_shape, args, scalars=0, scratch=(), far=0, long=False, grant=4, apart=(), either=()):
    place = [None] * scalars + [pltpu.HBM] * far + [pltpu.VMEM] * (len(args) - scalars - far)
    held = [None if i in either else pltpu.HBM if i in apart else p for i, p in enumerate(place)]
    args = [a if p is None else pltpu.with_memory_space_constraint(a, p) for a, p in zip(args, held)]
    return pl.pallas_call(
        kernel,
        name=name,
        in_specs=[pl.BlockSpec(memory_space=p or pltpu.SMEM) for p in place],
        out_specs=[vmem()] * len(out_shape),
        out_shape=list(out_shape),
        scratch_shapes=[pltpu.VMEM(dims, dtype) for dims, dtype in scratch] + [pltpu.SemaphoreType.DMA((7,))] * (far > 0),
        compiler_params=pltpu.CompilerParams(vmem_limit_bytes=grant * MIB),
        cost_estimate=pl.CostEstimate(flops=100_000_000_000 if long else 1_000_000_000, bytes_accessed=1 << 16, transcendentals=0),
    )(*args)


def body(rows_size, dp_size, events, cotangent, lengths, event_slot, slot_row, slot_count, w_in, w_out, item_table, accumulator):
    tokens, width = events.shape
    owners, capacity = slot_row.shape[1:]
    chips = rows_size // 2
    piece = width // (rows_size * dp_size)
    cores = [(i, i ^ 1) for i in range(rows_size)]
    over_dp = lambda v, bit: lax.ppermute(v, "dp", [(i, i ^ bit) for i in range(dp_size)])
    after = lambda value, *others: lax.optimization_barrier((value, *others))[0]
    strip = chips * piece

    def gathered(total):
        return [total] + [over_dp(total, k) for k in range(1, dp_size)]

    by_dp = lambda v: v.reshape(2, 2, strip, v.shape[-1])
    by_chip = lambda v: v.reshape(*v.shape[:-2], chips, piece, v.shape[-1])
    local = lambda *dims, dtype=f32: pltpu.VMEM(dims, dtype)
    sides = lambda cols: [local(width // 2, cols)] * 2
    keep1, send1, hid, dsilu, gatt, gpre_uv, normed_t, events, cotangent, w_in = call(
        functools.partial(forward_kernel, rows_size, dp_size), "forward_part",
        sides(3 * width) + [
            local(tokens, 3 * width, dtype=bf16),
            local(tokens, 2 * width, dtype=bf16),
            local(tokens, width, dtype=bf16),
            local(tokens, 2 * width, dtype=bf16),
            local(width, tokens, dtype=bf16),
            local(tokens, width, dtype=bf16),
            local(tokens, width, dtype=bf16),
            local(*w_in.shape, dtype=bf16),
        ],
        (lengths, events, cotangent, w_in, w_out), 1,
        [((tokens, width), bf16), ((tokens, width), bf16), ((tokens, width), f32), ((tokens, width), f32),
         ((tokens, width), bf16), ((tokens, width), bf16), ((tokens, width), f32), ((HEADS, tokens, tokens), bf16),
         (w_out.shape, bf16), ((width, width), bf16), ((tokens, width), f32)], far=4, long=True, grant=16)
    recv1 = lax.ppermute(send1, "rows", cores)
    keep2, send2, gpre_qk = call(
        attention_kernel, "attention_part", sides(2 * width) + [local(tokens, 2 * width, dtype=bf16)],
        (lengths, hid, dsilu, gatt, normed_t), 1, long=True, grant=10)
    recv2 = lax.ppermute(send2, "rows", cores)
    block = capacity * (width // LANES)
    gpre_uv = after(gpre_uv, recv1)
    sends = call(
        functools.partial(events_kernel, rows_size, dp_size), "events_part",
        [local(2 * dp_size * block + ID_ROWS, LANES)] * chips,
        (lengths, events, cotangent, w_in, event_slot, slot_row[0].T, gpre_uv, gpre_qk), 1,
        [((tokens, width), bf16), ((tokens, width), bf16), ((owners * capacity, width), f32)], grant=10, long=True)
    ahead = lambda v, k: lax.ppermute(v, "rows", [(i, (i + 2 * k) % rows_size) for i in range(rows_size)])
    came = [sends[0]] + [ahead(sends[k], k) for k in range(1, chips)]
    cols = w_in.shape[1] + width
    to_x, to_y, keep_a, keep_b = call(
        first_kernel, "first_sums", [local(2, strip, cols // 2)] * 4,
        [by_dp(v) for v in (after(keep1, *sends), recv1, keep2, recv2)])
    from_x, from_y = over_dp(to_x, 1), over_dp(to_y, 2)
    to_y, to_x, next_a, next_b = call(
        second_kernel, "second_sums", [local(strip, cols // 2)] * 4, (keep_a, from_x, keep_b, from_y),
        long=True)
    from_y, from_x = over_dp(to_y, 2), over_dp(to_x, 1)
    came[0] = after(came[0], to_y, to_x)
    parts = call(
        functools.partial(by_part_kernel, dp_size, block), "by_part",
        [local(2 * chips * block + id_rows(chips), LANES)] * dp_size, came, long=True)
    next_a = after(next_a, *parts)
    bits = chips.bit_length() - 1
    over_chips = lambda v, bit: lax.ppermute(v, "rows", [(i, i ^ (2 << bit)) for i in range(rows_size)])
    send_a, keep_a, send_b, keep_b = call(
        chip_first_kernel, "chip_sums", [local(chips // 2, piece, cols // 2)] * 4,
        [by_chip(v) for v in (next_a, from_y, next_b, from_x)])
    halves = [[keep_a, over_chips(send_a, 0)], [keep_b, over_chips(send_b, 0)]]
    parts = [parts[0]] + [over_dp(parts[k], k) for k in range(1, dp_size)]
    for bit in range(1, bits):
        for i in range(2):
            if i == 1:
                halves[1][0] = after(halves[1][0], send, keep)
            send, keep = call(
                functools.partial(chip_kernel, bit), "chip_sums", [local(chips >> (bit + 1), piece, cols // 2)] * 2,
                halves[i], long=False)
            halves[i] = [keep, over_chips(send, bit)]
    total = lambda half, **how: call(
        functools.partial(total_kernel, tokens), "total", [local(piece, cols // 2)], half, **how)[0]
    pieces = gathered(total(halves[0]))
    parts[0] = after(parts[0], pieces[0])
    keep, send = call(
        functools.partial(by_core_kernel, chips, block), "by_core",
        [local(dp_size * (chips * block + id_rows(chips)), LANES)] * 2, parts)
    halves[1][0] = after(halves[1][0], keep, send, *pieces)
    pieces += gathered(total(halves[1], long=True))
    recv = lax.ppermute(send, "rows", cores)
    slots = owners * capacity
    table_new, accum_new = call(
        functools.partial(table_kernel, dp_size, chips), "table_part", [shape(*item_table.shape), shape(*accumulator.shape)],
        (keep, recv, item_table, accumulator), 0,
        [((slots, width), f32), ((slots, width), bf16), ((slots, width), bf16)], grant=10)
    pieces[-1] = after(pieces[-1], accum_new)
    grad_in, grad_out = call(
        gather_kernel, "gather", [shape(dp_size, piece, 4 * width), shape(dp_size, piece, width)], pieces)
    return grad_in.reshape(-1, 4 * width), grad_out.reshape(-1, width), table_new, accum_new


def solution(mesh):
    whole = P(("dp", "rows"))
    in_specs = (whole,) * 6 + (P(), P(), whole, whole)
    out_specs = (P("rows"), P("rows"), whole, whole)
    run = functools.partial(body, mesh.shape["rows"], mesh.shape["dp"])
    return jax.shard_map(run, mesh=mesh, in_specs=in_specs, out_specs=out_specs, check_vma=False)
```

```python
import functools

import jax
import jax.numpy as jnp
from jax import lax
from jax.experimental import pallas as pl
from jax.experimental.pallas import tpu as pltpu
from jax.sharding import PartitionSpec as P

HEADS = 4

norm_eps = 1e-05
adagrad_eps = 1e-10
learning_rate = 0.1

f32, bf16 = jnp.float32, jnp.bfloat16
MIB = 1024 * 1024
STEP = 256
TILE = 32
LANES = 128
ID_ROWS = 8


def dot_nn(a, b):
    return lax.dot_general(a, b, (((1,), (0,)), ((), ())), preferred_element_type=f32)


def dot_nt(a, b):
    return lax.dot_general(a, b, (((1,), (1,)), ((), ())), preferred_element_type=f32)


def dot_tn(a, b):
    return lax.dot_general(a, b, (((0,), (0,)), ((), ())), preferred_element_type=f32)


def over(value, n):
    return value >> (n.bit_length() - 1) if n & (n - 1) == 0 else value // n


def rest(value, n):
    return value & (n - 1) if n & (n - 1) == 0 else value % n


def standardize(x):
    centered = x - jnp.mean(x, axis=-1, keepdims=True)
    inv = lax.rsqrt(jnp.mean(centered * centered, axis=-1, keepdims=True) + norm_eps)
    return centered * inv, inv


def masked_rows(cot, start, length):
    row = start + lax.broadcasted_iota(jnp.int32, cot.shape, 0)
    return jnp.where(row < length, cot.astype(f32), 0.0)


def owner_order(width, rows, dp):
    chips = rows // 2
    piece = width // (rows * dp)
    at = lax.broadcasted_iota(jnp.int32, (width, 1), 0)
    side, part = over(at, width // 2), rest(over(at, chips * piece), dp)
    chip, row = rest(over(at, piece), chips), rest(at, piece)
    core = lax.rem(lax.axis_index("rows"), 2)
    core = jnp.where(side == 0, core, 1 - core)
    wanted = ((chip * 2 + core) * dp + part) * piece + row
    return jnp.where(lax.broadcasted_iota(jnp.int32, (width, width), 1) == wanted, 1.0, 0.0).astype(bf16)


def tiles_of(start, count, size):
    return [pl.ds(start + at, size) for at in range(0, count, size)]


def forward_kernel(rows_size, dp_size, len_ref, ev_hbm, cot_hbm, win_hbm, wout_hbm,
                   keep_ref, send_ref, hid_ref, dsilu_ref, gatt_ref, gpre_ref, normed_t_ref,
                   ev_ref, masked_ref, win_ref, inv_ref, normed_ref, user_ref, duser_ref, att_ref, mixed_ref, dval_ref,
                   weights_ref, wout_ref, order_ref, grad_mixed_ref, cot_ref, pre_ref, raw_ref, arrived):
    tokens, width = ev_ref.shape
    copies = [pltpu.make_async_copy(ev_hbm, ev_ref, arrived.at[0])]
    for c in range(4):
        cols = pl.ds(c * width, width)
        copies.append(pltpu.make_async_copy(win_hbm.at[:, cols], win_ref.at[:, cols], arrived.at[1 + c]))
    copies.append(pltpu.make_async_copy(cot_hbm, cot_ref, arrived.at[5]))
    copies.append(pltpu.make_async_copy(wout_hbm, wout_ref, arrived.at[6]))
    for copy in copies:
        copy.start()
    order_ref[...] = owner_order(width, rows_size, dp_size)
    hd = width // HEADS
    scale = hd ** -0.5
    steps = tokens // STEP

    copies[0].wait()
    for tile in tiles_of(0, tokens, TILE):
        xhat, _ = standardize(ev_ref[tile, :].astype(f32))
        normed_ref[tile, :] = xhat.astype(bf16)

    def project(i, c):
        rows = pl.ds(i * STEP, STEP)
        slot = (c * steps + i) % pre_ref.shape[0]
        pre_ref[slot] = dot_nn(normed_ref[rows, :], win_ref[:, c * width:(c + 1) * width])
        for at in range(0, STEP, TILE):
            tile = pl.ds(i * STEP + at, TILE)
            pre = pre_ref[slot, at:at + TILE, :]
            sig = 0.5 + 0.5 * jnp.tanh(0.5 * pre)
            hid = pre * sig
            dsilu = sig * (1.0 + (pre - hid))
            if c == 0:
                user_ref[tile, :] = hid.astype(bf16)
                duser_ref[tile, :] = dsilu
            else:
                hid_ref[tile, (c - 1) * width:c * width] = hid.astype(bf16)
                if c == 1:
                    dval_ref[tile, :] = dsilu
                else:
                    dsilu_ref[tile, (c - 2) * width:(c - 1) * width] = dsilu.astype(bf16)

    for c in range(4):
        copies[1 + c].wait()
        for i in range(steps):
            project(i, c)

    for copy in copies[5:]:
        copy.wait()
    length = len_ref[0]
    inv_len = 1.0 / length.astype(f32)
    inv_ref[...] = jnp.full(inv_ref.shape, inv_len, f32)
    for h in range(HEADS):
        v_cols = slice(h * hd, (h + 1) * hd)
        q_cols = slice(width + h * hd, width + (h + 1) * hd)
        k_cols = slice(2 * width + h * hd, 2 * width + (h + 1) * hd)
        for i in range(steps):
            rows = pl.ds(i * STEP, STEP)
            for j in range(i + 1):
                keys = pl.ds(j * STEP, STEP)
                slot = (h * 3 + i + j) % raw_ref.shape[0]
                raw_ref[slot] = dot_nt(hid_ref[rows, q_cols], hid_ref[keys, k_cols])
                for at in range(0, STEP, 2 * TILE):
                    half = raw_ref[slot, at:at + 2 * TILE, :] * (0.5 * scale)
                    weights = (half + half * jnp.tanh(half)) * inv_len
                    if i == j:
                        row = at + lax.broadcasted_iota(jnp.int32, weights.shape, 0)
                        weights = jnp.where(row >= lax.broadcasted_iota(jnp.int32, weights.shape, 1), weights, 0.0)
                    weights_ref[h, pl.ds(i * STEP + at, 2 * TILE), keys] = weights.astype(bf16)
            seen = pl.ds(0, (i + 1) * STEP)
            att_ref[rows, v_cols] = dot_nn(weights_ref[h, rows, seen], hid_ref[seen, v_cols])
        for i in range(h, steps, HEADS):
            rows = pl.ds(i * STEP, STEP)
            normed_t_ref[rows, :] = dot_nt(order_ref[rows, :], normed_ref[...]).astype(bf16)
        for i in range(h - HEADS // 2, steps, HEADS):
            if i >= 0:
                rows = pl.ds(i * STEP, STEP)
                for tile in tiles_of(i * STEP, STEP, TILE):
                    masked_ref[tile, :] = masked_rows(cot_ref[tile, :], tile.start, length).astype(bf16)
                grad_mixed_ref[rows, :] = dot_nt(masked_ref[rows, :], wout_ref[...])

    for tile in tiles_of(0, tokens, TILE // 2):
        ahat, inv = standardize(att_ref[tile, :])
        user = user_ref[tile, :].astype(f32)
        mixed_ref[tile, :] = (ahat * user).astype(bf16)
        grad_mixed = grad_mixed_ref[tile, :]
        gpre_ref[tile, :width] = (grad_mixed * ahat * duser_ref[tile, :]).astype(bf16)
        e = grad_mixed * user
        gatt_ref[tile, :] = (inv * (e - jnp.mean(e, axis=-1, keepdims=True)
                                    - ahat * jnp.mean(e * ahat, axis=-1, keepdims=True))).astype(bf16)

    for h in range(HEADS):
        v_cols = slice(h * hd, (h + 1) * hd)
        for j in range(steps):
            keys, later = pl.ds(j * STEP, STEP), pl.ds(j * STEP, tokens - j * STEP)
            grad_v = dot_tn(weights_ref[h, later, keys], gatt_ref[later, v_cols])
            gpre_ref[keys, width + h * hd:width + (h + 1) * hd] = (grad_v * dval_ref[keys, v_cols]).astype(bf16)

    mixed_t = dot_nt(order_ref[...], mixed_ref[...]).astype(bf16)
    half = width // 2
    for ref, start in ((send_ref, half), (keep_ref, 0)):
        ref[:, :width] = dot_nn(mixed_t[start:start + half], masked_ref[...])
        ref[:, width:] = dot_nn(normed_t_ref[start:start + half, :], gpre_ref[...])


def attention_kernel(inv_ref, hid_ref, dsilu_ref, gatt_ref, normed_t_ref, keep_ref, send_ref, gpre_ref,
                     raw_ref, weight_ref, score_ref):
    tokens, width = gatt_ref.shape
    hd = width // HEADS
    scale = hd ** -0.5
    steps = tokens // STEP
    factor = inv_ref[:1, :hd] * (0.5 * scale)

    for h in range(HEADS):
        v_cols = slice(h * hd, (h + 1) * hd)
        q_cols = slice(width + h * hd, width + (h + 1) * hd)
        k_cols = slice(2 * width + h * hd, 2 * width + (h + 1) * hd)
        for j in range(steps):
            keys = pl.ds(j * STEP, STEP)
            for i in range(j, steps):
                rows = pl.ds(i * STEP, STEP)
                slot = (h * 3 + i + j) % raw_ref.shape[0]
                raw_ref[slot] = dot_nt(hid_ref[keys, k_cols], hid_ref[rows, q_cols])
                weight_ref[slot] = dot_nt(hid_ref[keys, v_cols], gatt_ref[rows, v_cols])
                for at in range(0, STEP, TILE):
                    half = raw_ref[slot, at:at + TILE, :] * (0.5 * scale)
                    gate = jnp.tanh(half)
                    gscore = weight_ref[slot, at:at + TILE, :] * ((1.0 + gate) * (1.0 + half * (1.0 - gate)))
                    if i == j:
                        row = at + lax.broadcasted_iota(jnp.int32, gscore.shape, 0)
                        gscore = jnp.where(row <= lax.broadcasted_iota(jnp.int32, gscore.shape, 1), gscore, 0.0)
                    score_ref[h % 2, pl.ds(j * STEP + at, TILE), rows] = gscore.astype(bf16)
        for j in range(steps):
            keys, later, seen = pl.ds(j * STEP, STEP), pl.ds(j * STEP, tokens - j * STEP), pl.ds(0, (j + 1) * STEP)
            grad_k = dot_nn(score_ref[h % 2, keys, later], hid_ref[later, q_cols])
            gpre_ref[keys, q_cols] = (grad_k * (dsilu_ref[keys, q_cols].astype(f32) * factor)).astype(bf16)
            grad_q = dot_tn(score_ref[h % 2, seen, keys], hid_ref[seen, k_cols])
            gpre_ref[keys, v_cols] = (grad_q * (dsilu_ref[keys, v_cols].astype(f32) * factor)).astype(bf16)

    half = width // 2
    for ref, start in ((send_ref, half), (keep_ref, 0)):
        ref[...] = dot_nn(normed_t_ref[start:start + half, :], gpre_ref[...])


def slots_in_order(position, capacity, dp, rows):
    chips = rows // 2
    owner, place = over(position, capacity), rest(position, capacity)
    ahead, core, part = over(owner, 2 * dp), rest(over(owner, dp), 2), rest(owner, dp)
    chip = rest(lax.axis_index("rows") // 2 + ahead, chips)
    return part * rows + chip * 2 + core, place


def events_kernel(rows_size, dp_size, ev_ref, masked_ref, win_ref, slot_ref, slot_row_ref, gpre_uv_ref, gpre_qk_ref, *refs):
    *send_refs, hi_ref, lo_ref, rows_ref, grad_ref, onehot_ref = refs
    tokens, width = ev_ref.shape
    capacity, owners = slot_row_ref.shape
    for i in range(tokens // STEP):
        rows = pl.ds(i * STEP, STEP)
        grad_ref[rows, :] = dot_nt(gpre_uv_ref[rows, :], win_ref[:, :2 * width]) + dot_nt(gpre_qk_ref[rows, :], win_ref[:, 2 * width:])
        for tile in tiles_of(i * STEP, STEP, TILE // 2):
            xhat, inv = standardize(ev_ref[tile, :].astype(f32))
            grad_normed = grad_ref[tile, :]
            grad = masked_ref[tile, :].astype(f32) + inv * (
                grad_normed - jnp.mean(grad_normed, axis=-1, keepdims=True)
                - xhat * jnp.mean(grad_normed * xhat, axis=-1, keepdims=True))
            high = grad.astype(bf16)
            hi_ref[tile, :] = high
            lo_ref[tile, :] = (grad - high.astype(f32)).astype(bf16)

    slots = rows_ref.shape[0]
    owner, place = slots_in_order(lax.broadcasted_iota(jnp.int32, (slots, 1), 0), capacity, dp_size, rows_size)
    wanted = owner * capacity + place
    for at in range(0, slots, 2 * TILE):
        onehot_ref[at:at + 2 * TILE, :] = jnp.where(wanted[at:at + 2 * TILE] == slot_ref[...], 1.0, 0.0).astype(bf16)
    rows_ref[...] = dot_nn(onehot_ref[...], hi_ref[...]) + dot_nn(onehot_ref[...], lo_ref[...])
    owner, place = slots_in_order(lax.broadcasted_iota(jnp.int32, (1, slots), 1), capacity, dp_size, rows_size)
    chosen = lax.broadcasted_iota(jnp.int32, (owners, slots), 0) == owner
    mine = lax.broadcasted_iota(jnp.int32, (capacity, slots), 0) == place
    ids = whole_numbers(slot_row_ref[...], chosen, mine)
    tiles = width // LANES
    blocks = 2 * dp_size
    for k, send_ref in enumerate(send_refs):
        for i in range(blocks):
            at = (k * blocks + i) * capacity
            for t in range(tiles):
                send_ref[(i * tiles + t) * capacity:(i * tiles + t + 1) * capacity, :] = rows_ref[at:at + capacity, t * LANES:(t + 1) * LANES]
        tile = k * blocks * capacity // LANES * LANES
        send_ref[blocks * tiles * capacity:, :] = jnp.broadcast_to(ids[:, tile:tile + LANES], (ID_ROWS, LANES))


def whole_numbers(values, chosen, mine):
    pick = jnp.where(chosen, 1.0, 0.0).astype(bf16)
    found = 16.0 * dot_nn(over(values, 16).astype(bf16), pick) + dot_nn(rest(values, 16).astype(bf16), pick)
    return jnp.sum(jnp.where(mine, found, 0.0), axis=0, keepdims=True)


def id_rows(chips):
    return max(ID_ROWS, chips)


def by_part_kernel(dp, block, *refs):
    ins, outs = refs[:-dp], refs[-dp:]
    d = lax.axis_index("dp")
    for j, out_ref in enumerate(outs):
        part = jnp.bitwise_xor(d, j)
        for k, in_ref in enumerate(ins):
            for core in range(2):
                start = pl.multiple_of((core * dp + part) * block, block)
                out_ref[(k * 2 + core) * block:(k * 2 + core + 1) * block, :] = in_ref[pl.ds(start, block), :]
        ids = [in_ref[2 * dp * block:2 * dp * block + 1, :] for in_ref in ins]
        ids += [jnp.zeros((1, LANES), f32)] * (id_rows(len(ins)) - len(ins))
        out_ref[2 * len(ins) * block:, :] = jnp.concatenate(ids, axis=0)


def by_core_kernel(chips, block, *refs):
    *ins, keep_ref, send_ref = refs
    core = lax.rem(lax.axis_index("rows"), 2)
    for out_ref, to in ((send_ref, 1 - core), (keep_ref, core)):
        for j, in_ref in enumerate(ins):
            for k in range(chips):
                start = pl.multiple_of((k * 2 + to) * block, block)
                out_ref[(j * chips + k) * block:(j * chips + k + 1) * block, :] = in_ref[pl.ds(start, block), :]
            at = len(ins) * chips * block + j * id_rows(chips)
            out_ref[at:at + id_rows(chips), :] = in_ref[2 * chips * block:, :]


def one_hot_rows(ids, wanted, hi_ref, lo_ref):
    onehot = jnp.where(wanted == ids, 1.0, 0.0).astype(bf16)
    return dot_nn(onehot, hi_ref[...]) + dot_nn(onehot, lo_ref[...])


def table_kernel(dp, chips, keep_ref, recv_ref, table_ref, accum_ref, table_new_ref, accum_new_ref, rows_ref, hi_ref, lo_ref):
    rows, width = table_ref.shape
    tiles = width // LANES
    sources = dp * chips
    capacity = rows_ref.shape[0] // (2 * sources)
    count = sources * capacity
    r = lax.axis_index("rows")
    block = lax.rem(r, 2) * dp + lax.axis_index("dp")
    ids = []
    for side, ref in enumerate((keep_ref, recv_ref)):
        for i in range(sources):
            at = side * count + i * capacity
            for t in range(tiles):
                rows_ref[at:at + capacity, t * LANES:(t + 1) * LANES] = ref[(i * tiles + t) * capacity:(i * tiles + t + 1) * capacity, :]
        values = ref[sources * tiles * capacity:, :].astype(jnp.int32)
        position = lax.broadcasted_iota(jnp.int32, (1, count), 1)
        source, place = over(position, capacity), rest(position, capacity)
        part, ahead = over(source, chips), rest(source, chips)
        lane = rest(ahead * (2 * dp * capacity), LANES) + block * capacity + place
        chosen = lax.broadcasted_iota(jnp.int32, (LANES, count), 0) == lane
        mine = lax.broadcasted_iota(jnp.int32, (values.shape[0], count), 0) == part * id_rows(chips) + ahead
        ids.append(whole_numbers(values, chosen, mine))
    ids = jnp.concatenate(ids, axis=1).astype(jnp.int32)
    high = rows_ref[...].astype(bf16)
    hi_ref[...] = high
    lo_ref[...] = (rows_ref[...] - high.astype(f32)).astype(bf16)
    grad = one_hot_rows(ids, lax.broadcasted_iota(jnp.int32, (rows, 1), 0), hi_ref, lo_ref)
    accum = jnp.transpose(jnp.broadcast_to(accum_ref[...].reshape(1, rows), (8, rows)))[:, :1]
    accum_new = accum + jnp.mean(grad * grad, axis=-1, keepdims=True)
    accum_new_ref[...] = jnp.transpose(jnp.broadcast_to(accum_new, (rows, LANES)))[:1, :].reshape(rows)
    table_new_ref[...] = table_ref[...] - learning_rate * grad / (jnp.sqrt(accum_new) + adagrad_eps)


def place_on_dp():
    d = lax.axis_index("dp")
    return lax.rem(d, 2), d // 2


def first_kernel(keep1_ref, recv1_ref, keep2_ref, recv2_ref, to_x_ref, to_y_ref, keep_a_ref, keep_b_ref):
    x, y = place_on_dp()
    start = 0
    for keep_ref, recv_ref in ((keep1_ref, recv1_ref), (keep2_ref, recv2_ref)):
        half = keep_ref.shape[-1] // 2
        part = lambda i, j, cols: keep_ref[i, j, :, cols] + recv_ref[i, j, :, cols]
        lo, hi, out = slice(0, half), slice(half, 2 * half), slice(start, start + half)
        for s in range(2):
            to_x_ref[s, :, out] = part(s, 1 - x, lo)
            to_y_ref[s, :, out] = part(1 - y, s, hi)
            keep_a_ref[s, :, out] = part(s, x, lo)
            keep_b_ref[s, :, out] = part(y, s, hi)
        start += half


def second_kernel(keep_a_ref, from_x_ref, keep_b_ref, from_y_ref, to_y_ref, to_x_ref, next_a_ref, next_b_ref):
    x, y = place_on_dp()
    to_y_ref[...] = keep_a_ref[1 - y] + from_x_ref[1 - y]
    to_x_ref[...] = keep_b_ref[1 - x] + from_y_ref[1 - x]
    next_a_ref[...] = keep_a_ref[y] + from_x_ref[y]
    next_b_ref[...] = keep_b_ref[x] + from_y_ref[x]


def halve(bit, send_ref, keep_ref, keep_in, recv_in):
    mine = rest(lax.axis_index("rows") // 2 >> bit, 2)
    for i in range(send_ref.shape[0]):
        send_ref[i] = keep_in[2 * i + 1 - mine] + recv_in[2 * i + 1 - mine]
        keep_ref[i] = keep_in[2 * i + mine] + recv_in[2 * i + mine]


def chip_first_kernel(next_a_ref, from_y_ref, next_b_ref, from_x_ref, send_a_ref, keep_a_ref, send_b_ref, keep_b_ref):
    halve(0, send_a_ref, keep_a_ref, next_a_ref, from_y_ref)
    halve(0, send_b_ref, keep_b_ref, next_b_ref, from_x_ref)


def chip_kernel(bit, keep_in, recv_in, send_ref, keep_ref):
    halve(bit, send_ref, keep_ref, keep_in, recv_in)


def total_kernel(tokens, keep_a_ref, recv_a_ref, keep_b_ref, recv_b_ref, out_ref):
    half = keep_a_ref.shape[-1]
    out_ref[:, :half] = (keep_a_ref[0] + recv_a_ref[0]) * (1.0 / tokens)
    out_ref[:, half:] = (keep_b_ref[0] + recv_b_ref[0]) * (1.0 / tokens)


def gather_kernel(*refs):
    *pieces, grad_in_ref, grad_out_ref = refs
    d = lax.axis_index("dp")
    width = grad_out_ref.shape[-1]
    half = width // 2
    for k, piece in enumerate(pieces):
        at = jnp.bitwise_xor(d, k)
        grad_out_ref[at] = piece[:, :width]
        start = width
        for cols, first in ((half, 0), (width, 2 * width), (half, half), (width, width), (width, 3 * width)):
            grad_in_ref[at, :, first:first + cols] = piece[:, start:start + cols]
            start += cols


def vmem():
    return pl.BlockSpec(memory_space=pltpu.VMEM)


def shape(*dims, dtype=f32):
    return jax.ShapeDtypeStruct(dims, dtype)


def call(kernel, name, out_shape, args, scratch=(), far=0, long=False, grant=4):
    place = [pltpu.SMEM if a.size == 1 else pltpu.HBM if i < far else pltpu.VMEM for i, a in enumerate(args)]
    args = [a if p is pltpu.SMEM else pltpu.with_memory_space_constraint(a, p) for a, p in zip(args, place)]
    return pl.pallas_call(
        kernel,
        name=name,
        in_specs=[pl.BlockSpec(memory_space=p) for p in place],
        out_specs=[vmem()] * len(out_shape),
        out_shape=list(out_shape),
        scratch_shapes=[pltpu.VMEM(dims, dtype) for dims, dtype in scratch]
        + [pltpu.SemaphoreType.DMA((7,))] * (far > 0),
        compiler_params=pltpu.CompilerParams(vmem_limit_bytes=grant * MIB),
        cost_estimate=pl.CostEstimate(flops=100_000_000_000 if long else 1_000_000_000, bytes_accessed=1 << 16, transcendentals=0),
    )(*args)


def body(rows_size, dp_size, events, cotangent, lengths, event_slot, slot_row, slot_count, w_in, w_out, item_table, accumulator):
    tokens, width = events.shape
    owners, capacity = slot_row.shape[1:]
    chips = rows_size // 2
    piece = width // (rows_size * dp_size)
    cores = [(i, i ^ 1) for i in range(rows_size)]
    over_dp = lambda v, bit: lax.ppermute(v, "dp", [(i, i ^ bit) for i in range(dp_size)])
    after = lambda value, *others: lax.optimization_barrier((value, *others))[0]
    strip = chips * piece

    def gathered(total):
        return [total] + [over_dp(total, k) for k in range(1, dp_size)]

    by_dp = lambda v: v.reshape(2, 2, strip, v.shape[-1])
    by_chip = lambda v: v.reshape(*v.shape[:-2], chips, piece, v.shape[-1])
    local = lambda *dims, dtype=f32: pltpu.VMEM(dims, dtype)
    sides = lambda cols: [local(width // 2, cols)] * 2
    keep1, send1, hid, dsilu, gatt, gpre_uv, normed_t, events, masked, w_in, inv_len = call(
        functools.partial(forward_kernel, rows_size, dp_size), "forward_part",
        sides(3 * width) + [
            local(tokens, 3 * width, dtype=bf16),
            local(tokens, 2 * width, dtype=bf16),
            local(tokens, width, dtype=bf16),
            local(tokens, 2 * width, dtype=bf16),
            local(width, tokens, dtype=bf16),
            local(tokens, width, dtype=bf16),
            local(tokens, width, dtype=bf16),
            local(*w_in.shape, dtype=bf16),
            local(8, LANES),
        ],
        (lengths, events, cotangent, w_in, w_out),
        [((tokens, width), bf16), ((tokens, width), bf16), ((tokens, width), f32), ((tokens, width), f32),
         ((tokens, width), bf16), ((tokens, width), f32), ((HEADS, tokens, tokens), bf16),
         (w_out.shape, bf16), ((width, width), bf16), ((tokens, width), f32), ((tokens, width), bf16),
         ((4, STEP, width), f32), ((4, STEP, STEP), f32)], far=5, long=True, grant=22)
    recv1 = lax.ppermute(send1, "rows", cores)
    keep2, send2, gpre_qk = call(
        attention_kernel, "attention_part", sides(2 * width) + [local(tokens, 2 * width, dtype=bf16)],
        (inv_len, hid, dsilu, gatt, normed_t),
        [((4, STEP, STEP), f32), ((4, STEP, STEP), f32), ((2, tokens, tokens), bf16)], long=True, grant=12)
    recv2 = lax.ppermute(send2, "rows", cores)
    block = capacity * (width // LANES)
    gpre_uv = after(gpre_uv, recv1)
    sends = call(
        functools.partial(events_kernel, rows_size, dp_size), "events_part",
        [local(2 * dp_size * block + ID_ROWS, LANES)] * chips,
        (events, masked, w_in, event_slot, slot_row[0].T, gpre_uv, gpre_qk),
        [((tokens, width), bf16), ((tokens, width), bf16), ((owners * capacity, width), f32), ((tokens, width), f32),
         ((owners * capacity, tokens), bf16)], grant=12, long=True)
    ahead = lambda v, k: lax.ppermute(v, "rows", [(i, (i + 2 * k) % rows_size) for i in range(rows_size)])
    came = [sends[0]] + [ahead(sends[k], k) for k in range(1, chips)]
    cols = w_in.shape[1] + width
    to_x, to_y, keep_a, keep_b = call(
        first_kernel, "first_sums", [local(2, strip, cols // 2)] * 4,
        [by_dp(v) for v in (after(keep1, *sends), recv1, keep2, recv2)])
    from_x, from_y = over_dp(to_x, 1), over_dp(to_y, 2)
    to_y, to_x, next_a, next_b = call(
        second_kernel, "second_sums", [local(strip, cols // 2)] * 4, (keep_a, from_x, keep_b, from_y),
        long=True)
    from_y, from_x = over_dp(to_y, 2), over_dp(to_x, 1)
    came[0] = after(came[0], to_y, to_x)
    parts = call(
        functools.partial(by_part_kernel, dp_size, block), "by_part",
        [local(2 * chips * block + id_rows(chips), LANES)] * dp_size, came, long=True)
    next_a = after(next_a, *parts)
    bits = chips.bit_length() - 1
    over_chips = lambda v, bit: lax.ppermute(v, "rows", [(i, i ^ (2 << bit)) for i in range(rows_size)])
    send_a, keep_a, send_b, keep_b = call(
        chip_first_kernel, "chip_sums", [local(chips // 2, piece, cols // 2)] * 4,
        [by_chip(v) for v in (next_a, from_y, next_b, from_x)])
    halves = [[keep_a, over_chips(send_a, 0)], [keep_b, over_chips(send_b, 0)]]
    parts = [parts[0]] + [over_dp(parts[k], k) for k in range(1, dp_size)]
    for bit in range(1, bits):
        for i in range(2):
            if i == 1:
                halves[1][0] = after(halves[1][0], send, keep)
            send, keep = call(
                functools.partial(chip_kernel, bit), "chip_sums", [local(chips >> (bit + 1), piece, cols // 2)] * 2,
                halves[i], long=False)
            halves[i] = [keep, over_chips(send, bit)]
    (total,) = call(
        functools.partial(total_kernel, tokens), "total", [local(piece, cols)], halves[0] + halves[1], long=False)
    pieces = gathered(total)
    parts[0] = after(parts[0], total)
    keep, send = call(
        functools.partial(by_core_kernel, chips, block), "by_core",
        [local(dp_size * (chips * block + id_rows(chips)), LANES)] * 2, parts, long=False)
    recv = lax.ppermute(send, "rows", cores)
    slots = owners * capacity
    table_new, accum_new = call(
        functools.partial(table_kernel, dp_size, chips), "table_part", [shape(*item_table.shape), shape(*accumulator.shape)],
        (keep, recv, item_table, accumulator),
        [((slots, width), f32), ((slots, width), bf16), ((slots, width), bf16)], grant=10)
    pieces[-1] = after(pieces[-1], accum_new)
    grad_in, grad_out = call(
        gather_kernel, "gather", [shape(dp_size, piece, 4 * width), shape(dp_size, piece, width)], pieces)
    return grad_in.reshape(-1, 4 * width), grad_out.reshape(-1, width), table_new, accum_new


def solution(mesh):
    whole = P(("dp", "rows"))
    in_specs = (whole,) * 6 + (P(), P(), whole, whole)
    out_specs = (P("rows"), P("rows"), whole, whole)
    run = functools.partial(body, mesh.shape["rows"], mesh.shape["dp"])
    return jax.shard_map(run, mesh=mesh, in_specs=in_specs, out_specs=out_specs, check_vma=False)
```

```python
import functools

import jax
import jax.numpy as jnp
from jax import lax
from jax.experimental import pallas as pl
from jax.experimental.pallas import tpu as pltpu
from jax.sharding import PartitionSpec as P

HEADS = 4

norm_eps = 1e-05
adagrad_eps = 1e-10
learning_rate = 0.1

f32, bf16 = jnp.float32, jnp.bfloat16
MIB = 1024 * 1024
STEP = 256
TILE = 32
LANES = 128
ID_ROWS = 8


def dot_nn(a, b):
    return lax.dot_general(a, b, (((1,), (0,)), ((), ())), preferred_element_type=f32)


def dot_nt(a, b):
    return lax.dot_general(a, b, (((1,), (1,)), ((), ())), preferred_element_type=f32)


def dot_tn(a, b):
    return lax.dot_general(a, b, (((0,), (0,)), ((), ())), preferred_element_type=f32)


def over(value, n):
    return value >> (n.bit_length() - 1) if n & (n - 1) == 0 else value // n


def rest(value, n):
    return value & (n - 1) if n & (n - 1) == 0 else value % n


def standardize(x):
    centered = x - jnp.mean(x, axis=-1, keepdims=True)
    inv = lax.rsqrt(jnp.mean(centered * centered, axis=-1, keepdims=True) + norm_eps)
    return centered * inv, inv


def masked_rows(cot, start, length):
    row = start + lax.broadcasted_iota(jnp.int32, cot.shape, 0)
    return jnp.where(row < length, cot.astype(f32), 0.0)


def owner_order(width, rows, dp):
    chips = rows // 2
    piece = width // (rows * dp)
    at = lax.broadcasted_iota(jnp.int32, (width, 1), 0)
    side, part = over(at, width // 2), rest(over(at, chips * piece), dp)
    chip, row = rest(over(at, piece), chips), rest(at, piece)
    core = lax.rem(lax.axis_index("rows"), 2)
    core = jnp.where(side == 0, core, 1 - core)
    wanted = ((chip * 2 + core) * dp + part) * piece + row
    return jnp.where(lax.broadcasted_iota(jnp.int32, (width, width), 1) == wanted, 1.0, 0.0).astype(bf16)


def tiles_of(start, count, size):
    return [pl.ds(start + at, size) for at in range(0, count, size)]


def forward_kernel(rows_size, dp_size, len_ref, ev_hbm, cot_hbm, win_hbm, wout_hbm,
                   keep_ref, send_ref, hid_ref, dsilu_ref, gatt_ref, gpre_ref, normed_t_ref,
                   ev_ref, masked_ref, win_ref, inv_ref, normed_ref, user_ref, duser_ref, att_ref, mixed_ref, dval_ref,
                   weights_ref, wout_ref, order_ref, grad_mixed_ref, cot_ref, pre_ref, raw_ref, mixed_t_ref, arrived):
    tokens, width = ev_ref.shape
    parts = [pl.ds(i * STEP, STEP) for i in range(tokens // STEP)]
    early = [pltpu.make_async_copy(ev_hbm.at[part, :], ev_ref.at[part, :], arrived.at[7 + i]) for i, part in enumerate(parts)]
    copies = [None]
    for c in range(4):
        cols = pl.ds(c * width, width)
        copies.append(pltpu.make_async_copy(win_hbm.at[:, cols], win_ref.at[:, cols], arrived.at[1 + c]))
    copies.append(pltpu.make_async_copy(cot_hbm, cot_ref, arrived.at[5]))
    copies.append(pltpu.make_async_copy(wout_hbm, wout_ref, arrived.at[6]))
    for copy in early + copies[1:]:
        copy.start()
    order_ref[...] = owner_order(width, rows_size, dp_size)
    hd = width // HEADS
    scale = hd ** -0.5
    steps = tokens // STEP

    for i in range(steps):
        early[i].wait()
        for tile in tiles_of(i * STEP, STEP, TILE // 2):
            xhat, _ = standardize(ev_ref[tile, :].astype(f32))
            normed_ref[tile, :] = xhat.astype(bf16)

    def project(i, c):
        rows = pl.ds(i * STEP, STEP)
        slot = (c * steps + i) % pre_ref.shape[0]
        pre_ref[slot] = dot_nn(normed_ref[rows, :], win_ref[:, c * width:(c + 1) * width])
        for at in range(0, STEP, TILE // 2):
            tile = pl.ds(i * STEP + at, TILE // 2)
            pre = pre_ref[slot, at:at + TILE // 2, :]
            sig = 0.5 + 0.5 * jnp.tanh(0.5 * pre)
            hid = pre * sig
            dsilu = sig * (1.0 + (pre - hid))
            if c == 0:
                user_ref[tile, :] = hid.astype(bf16)
                duser_ref[tile, :] = dsilu
            else:
                hid_ref[tile, (c - 1) * width:c * width] = hid.astype(bf16)
                if c == 1:
                    dval_ref[tile, :] = dsilu
                else:
                    dsilu_ref[tile, (c - 2) * width:(c - 1) * width] = dsilu.astype(bf16)

    for c in range(4):
        copies[1 + c].wait()
        for i in range(steps):
            project(i, c)

    for copy in copies[5:]:
        copy.wait()
    length = len_ref[0]
    inv_len = 1.0 / length.astype(f32)
    inv_ref[...] = jnp.full(inv_ref.shape, inv_len, f32)
    for h in range(HEADS):
        v_cols = slice(h * hd, (h + 1) * hd)
        q_cols = slice(width + h * hd, width + (h + 1) * hd)
        k_cols = slice(2 * width + h * hd, 2 * width + (h + 1) * hd)
        for i in range(steps):
            rows = pl.ds(i * STEP, STEP)
            for j in range(i + 1):
                keys = pl.ds(j * STEP, STEP)
                slot = (h * 3 + i + j) % raw_ref.shape[0]
                raw_ref[slot] = dot_nt(hid_ref[rows, q_cols], hid_ref[keys, k_cols])
                for at in range(0, STEP, TILE):
                    half = raw_ref[slot, at:at + TILE, :] * (0.5 * scale)
                    weights = (half + half * jnp.tanh(half)) * inv_len
                    if i == j:
                        row = at + lax.broadcasted_iota(jnp.int32, weights.shape, 0)
                        weights = jnp.where(row >= lax.broadcasted_iota(jnp.int32, weights.shape, 1), weights, 0.0)
                    weights_ref[h, pl.ds(i * STEP + at, TILE), keys] = weights.astype(bf16)
            seen = pl.ds(0, (i + 1) * STEP)
            att_ref[rows, v_cols] = dot_nn(weights_ref[h, rows, seen], hid_ref[seen, v_cols])
        for i in range(h, steps, HEADS):
            rows = pl.ds(i * STEP, STEP)
            normed_t_ref[rows, :] = dot_nt(order_ref[rows, :], normed_ref[...]).astype(bf16)
        for i in range(h - HEADS // 2, steps, HEADS):
            if i >= 0:
                rows = pl.ds(i * STEP, STEP)
                for tile in tiles_of(i * STEP, STEP, TILE):
                    masked_ref[tile, :] = masked_rows(cot_ref[tile, :], tile.start, length).astype(bf16)
                grad_mixed_ref[rows, :] = dot_nt(masked_ref[rows, :], wout_ref[...])

    for tile in tiles_of(0, tokens, TILE // 2):
        ahat, inv = standardize(att_ref[tile, :])
        user = user_ref[tile, :].astype(f32)
        mixed_ref[tile, :] = (ahat * user).astype(bf16)
        grad_mixed = grad_mixed_ref[tile, :]
        gpre_ref[tile, :width] = (grad_mixed * ahat * duser_ref[tile, :]).astype(bf16)
        e = grad_mixed * user
        gatt_ref[tile, :] = (inv * (e - jnp.mean(e, axis=-1, keepdims=True)
                                    - ahat * jnp.mean(e * ahat, axis=-1, keepdims=True))).astype(bf16)

    for h in range(HEADS):
        v_cols = slice(h * hd, (h + 1) * hd)
        for j in range(steps):
            keys, later = pl.ds(j * STEP, STEP), pl.ds(j * STEP, tokens - j * STEP)
            grad_v = dot_tn(weights_ref[h, later, keys], gatt_ref[later, v_cols])
            gpre_ref[keys, width + h * hd:width + (h + 1) * hd] = (grad_v * dval_ref[keys, v_cols]).astype(bf16)

    half = width // 2
    for ref, start in ((send_ref, half), (keep_ref, 0)):
        mixed_t_ref[...] = dot_nt(order_ref[start:start + half, :], mixed_ref[...]).astype(bf16)
        ref[:, :width] = dot_nn(mixed_t_ref[...], masked_ref[...])
        ref[:, width:] = dot_nn(normed_t_ref[start:start + half, :], gpre_ref[...])


def attention_kernel(inv_ref, hid_ref, dsilu_ref, gatt_ref, normed_t_ref, keep_ref, send_ref, gpre_ref,
                     raw_ref, weight_ref, score_ref):
    tokens, width = gatt_ref.shape
    hd = width // HEADS
    scale = hd ** -0.5
    steps = tokens // STEP
    factor = inv_ref[:1, :hd] * (0.5 * scale)

    for h in range(HEADS):
        v_cols = slice(h * hd, (h + 1) * hd)
        q_cols = slice(width + h * hd, width + (h + 1) * hd)
        k_cols = slice(2 * width + h * hd, 2 * width + (h + 1) * hd)
        for j in range(steps):
            keys = pl.ds(j * STEP, STEP)
            for i in range(j, steps):
                rows = pl.ds(i * STEP, STEP)
                slot = (h * 3 + i + j) % raw_ref.shape[0]
                raw_ref[slot] = dot_nt(hid_ref[keys, k_cols], hid_ref[rows, q_cols])
                weight_ref[slot] = dot_nt(hid_ref[keys, v_cols], gatt_ref[rows, v_cols])
                for at in range(0, STEP, TILE):
                    half = raw_ref[slot, at:at + TILE, :] * (0.5 * scale)
                    gate = jnp.tanh(half)
                    gscore = weight_ref[slot, at:at + TILE, :] * ((1.0 + gate) * (1.0 + half * (1.0 - gate)))
                    if i == j:
                        row = at + lax.broadcasted_iota(jnp.int32, gscore.shape, 0)
                        gscore = jnp.where(row <= lax.broadcasted_iota(jnp.int32, gscore.shape, 1), gscore, 0.0)
                    score_ref[h % 2, pl.ds(j * STEP + at, TILE), rows] = gscore.astype(bf16)
        for j in range(steps):
            keys, later, seen = pl.ds(j * STEP, STEP), pl.ds(j * STEP, tokens - j * STEP), pl.ds(0, (j + 1) * STEP)
            grad_k = dot_nn(score_ref[h % 2, keys, later], hid_ref[later, q_cols])
            gpre_ref[keys, q_cols] = (grad_k * (dsilu_ref[keys, q_cols].astype(f32) * factor)).astype(bf16)
            grad_q = dot_tn(score_ref[h % 2, seen, keys], hid_ref[seen, k_cols])
            gpre_ref[keys, v_cols] = (grad_q * (dsilu_ref[keys, v_cols].astype(f32) * factor)).astype(bf16)

    half = width // 2
    for ref, start in ((send_ref, half), (keep_ref, 0)):
        ref[...] = dot_nn(normed_t_ref[start:start + half, :], gpre_ref[...])


def slots_in_order(position, capacity, dp, rows):
    chips = rows // 2
    owner, place = over(position, capacity), rest(position, capacity)
    ahead, core, part = over(owner, 2 * dp), rest(over(owner, dp), 2), rest(owner, dp)
    chip = rest(lax.axis_index("rows") // 2 + ahead, chips)
    return part * rows + chip * 2 + core, place


def events_kernel(rows_size, dp_size, ev_ref, masked_ref, win_ref, slot_ref, slot_row_ref, gpre_uv_ref, gpre_qk_ref, *refs):
    *send_refs, hi_ref, lo_ref, rows_ref, grad_ref, onehot_ref = refs
    tokens, width = ev_ref.shape
    capacity, owners = slot_row_ref.shape
    for i in range(tokens // STEP):
        rows = pl.ds(i * STEP, STEP)
        grad_ref[rows, :] = dot_nt(gpre_uv_ref[rows, :], win_ref[:, :2 * width]) + dot_nt(gpre_qk_ref[rows, :], win_ref[:, 2 * width:])
        for tile in tiles_of(i * STEP, STEP, TILE // 2):
            xhat, inv = standardize(ev_ref[tile, :].astype(f32))
            grad_normed = grad_ref[tile, :]
            grad = masked_ref[tile, :].astype(f32) + inv * (
                grad_normed - jnp.mean(grad_normed, axis=-1, keepdims=True)
                - xhat * jnp.mean(grad_normed * xhat, axis=-1, keepdims=True))
            high = grad.astype(bf16)
            hi_ref[tile, :] = high
            lo_ref[tile, :] = (grad - high.astype(f32)).astype(bf16)

    slots = rows_ref.shape[0]
    owner, place = slots_in_order(lax.broadcasted_iota(jnp.int32, (slots, 1), 0), capacity, dp_size, rows_size)
    wanted = owner * capacity + place
    for at in range(0, slots, 2 * TILE):
        onehot_ref[at:at + 2 * TILE, :] = jnp.where(wanted[at:at + 2 * TILE] == slot_ref[...], 1.0, 0.0).astype(bf16)
    rows_ref[...] = dot_nn(onehot_ref[...], hi_ref[...]) + dot_nn(onehot_ref[...], lo_ref[...])
    owner, place = slots_in_order(lax.broadcasted_iota(jnp.int32, (1, slots), 1), capacity, dp_size, rows_size)
    chosen = lax.broadcasted_iota(jnp.int32, (owners, slots), 0) == owner
    mine = lax.broadcasted_iota(jnp.int32, (capacity, slots), 0) == place
    ids = whole_numbers(slot_row_ref[...], chosen, mine)
    tiles = width // LANES
    blocks = 2 * dp_size
    for k, send_ref in enumerate(send_refs):
        for i in range(blocks):
            at = (k * blocks + i) * capacity
            for t in range(tiles):
                send_ref[(i * tiles + t) * capacity:(i * tiles + t + 1) * capacity, :] = rows_ref[at:at + capacity, t * LANES:(t + 1) * LANES]
        tile = k * blocks * capacity // LANES * LANES
        send_ref[blocks * tiles * capacity:, :] = jnp.broadcast_to(ids[:, tile:tile + LANES], (ID_ROWS, LANES))


def whole_numbers(values, chosen, mine):
    pick = jnp.where(chosen, 1.0, 0.0).astype(bf16)
    found = 16.0 * dot_nn(over(values, 16).astype(bf16), pick) + dot_nn(rest(values, 16).astype(bf16), pick)
    return jnp.sum(jnp.where(mine, found, 0.0), axis=0, keepdims=True)


def id_rows(chips):
    return max(ID_ROWS, chips)


def by_part_kernel(dp, block, *refs):
    ins, outs = refs[:-dp], refs[-dp:]
    d = lax.axis_index("dp")
    for j, out_ref in enumerate(outs):
        part = jnp.bitwise_xor(d, j)
        for k, in_ref in enumerate(ins):
            for core in range(2):
                start = pl.multiple_of((core * dp + part) * block, block)
                out_ref[(k * 2 + core) * block:(k * 2 + core + 1) * block, :] = in_ref[pl.ds(start, block), :]
        ids = [in_ref[2 * dp * block:2 * dp * block + 1, :] for in_ref in ins]
        ids += [jnp.zeros((1, LANES), f32)] * (id_rows(len(ins)) - len(ins))
        out_ref[2 * len(ins) * block:, :] = jnp.concatenate(ids, axis=0)


def by_core_kernel(chips, block, *refs):
    *ins, keep_ref, send_ref = refs
    core = lax.rem(lax.axis_index("rows"), 2)
    for out_ref, to in ((send_ref, 1 - core), (keep_ref, core)):
        for j, in_ref in enumerate(ins):
            for k in range(chips):
                start = pl.multiple_of((k * 2 + to) * block, block)
                out_ref[(j * chips + k) * block:(j * chips + k + 1) * block, :] = in_ref[pl.ds(start, block), :]
            at = len(ins) * chips * block + j * id_rows(chips)
            out_ref[at:at + id_rows(chips), :] = in_ref[2 * chips * block:, :]


def one_hot_rows(ids, wanted, hi_ref, lo_ref):
    onehot = jnp.where(wanted == ids, 1.0, 0.0).astype(bf16)
    return dot_nn(onehot, hi_ref[...]) + dot_nn(onehot, lo_ref[...])


def table_kernel(dp, chips, keep_ref, recv_ref, table_ref, accum_ref, table_new_ref, accum_new_ref, rows_ref, hi_ref, lo_ref):
    rows, width = table_ref.shape
    tiles = width // LANES
    sources = dp * chips
    capacity = rows_ref.shape[0] // (2 * sources)
    count = sources * capacity
    r = lax.axis_index("rows")
    block = lax.rem(r, 2) * dp + lax.axis_index("dp")
    ids = []
    for side, ref in enumerate((keep_ref, recv_ref)):
        for i in range(sources):
            at = side * count + i * capacity
            for t in range(tiles):
                rows_ref[at:at + capacity, t * LANES:(t + 1) * LANES] = ref[(i * tiles + t) * capacity:(i * tiles + t + 1) * capacity, :]
        values = ref[sources * tiles * capacity:, :].astype(jnp.int32)
        position = lax.broadcasted_iota(jnp.int32, (1, count), 1)
        source, place = over(position, capacity), rest(position, capacity)
        part, ahead = over(source, chips), rest(source, chips)
        lane = rest(ahead * (2 * dp * capacity), LANES) + block * capacity + place
        chosen = lax.broadcasted_iota(jnp.int32, (LANES, count), 0) == lane
        mine = lax.broadcasted_iota(jnp.int32, (values.shape[0], count), 0) == part * id_rows(chips) + ahead
        ids.append(whole_numbers(values, chosen, mine))
    ids = jnp.concatenate(ids, axis=1).astype(jnp.int32)
    high = rows_ref[...].astype(bf16)
    hi_ref[...] = high
    lo_ref[...] = (rows_ref[...] - high.astype(f32)).astype(bf16)
    grad = one_hot_rows(ids, lax.broadcasted_iota(jnp.int32, (rows, 1), 0), hi_ref, lo_ref)
    accum = jnp.transpose(jnp.broadcast_to(accum_ref[...].reshape(1, rows), (8, rows)))[:, :1]
    accum_new = accum + jnp.mean(grad * grad, axis=-1, keepdims=True)
    accum_new_ref[...] = jnp.transpose(jnp.broadcast_to(accum_new, (rows, LANES)))[:1, :].reshape(rows)
    table_new_ref[...] = table_ref[...] - learning_rate * grad / (jnp.sqrt(accum_new) + adagrad_eps)


def place_on_dp():
    d = lax.axis_index("dp")
    return lax.rem(d, 2), d // 2


def first_kernel(keep1_ref, recv1_ref, keep2_ref, recv2_ref, to_x_ref, to_y_ref, keep_a_ref, keep_b_ref):
    x, y = place_on_dp()
    start = 0
    for keep_ref, recv_ref in ((keep1_ref, recv1_ref), (keep2_ref, recv2_ref)):
        half = keep_ref.shape[-1] // 2
        part = lambda i, j, cols: keep_ref[i, j, :, cols] + recv_ref[i, j, :, cols]
        lo, hi, out = slice(0, half), slice(half, 2 * half), slice(start, start + half)
        for s in range(2):
            to_x_ref[s, :, out] = part(s, 1 - x, lo)
            to_y_ref[s, :, out] = part(1 - y, s, hi)
            keep_a_ref[s, :, out] = part(s, x, lo)
            keep_b_ref[s, :, out] = part(y, s, hi)
        start += half


def second_kernel(keep_a_ref, from_x_ref, keep_b_ref, from_y_ref, to_y_ref, to_x_ref, next_a_ref, next_b_ref):
    x, y = place_on_dp()
    to_y_ref[...] = keep_a_ref[1 - y] + from_x_ref[1 - y]
    to_x_ref[...] = keep_b_ref[1 - x] + from_y_ref[1 - x]
    next_a_ref[...] = keep_a_ref[y] + from_x_ref[y]
    next_b_ref[...] = keep_b_ref[x] + from_y_ref[x]


def halve(bit, send_ref, keep_ref, keep_in, recv_in):
    mine = rest(lax.axis_index("rows") // 2 >> bit, 2)
    for i in range(send_ref.shape[0]):
        send_ref[i] = keep_in[2 * i + 1 - mine] + recv_in[2 * i + 1 - mine]
        keep_ref[i] = keep_in[2 * i + mine] + recv_in[2 * i + mine]


def chip_first_kernel(next_a_ref, from_y_ref, next_b_ref, from_x_ref, send_a_ref, keep_a_ref, send_b_ref, keep_b_ref):
    halve(0, send_a_ref, keep_a_ref, next_a_ref, from_y_ref)
    halve(0, send_b_ref, keep_b_ref, next_b_ref, from_x_ref)


def chip_kernel(bit, keep_in, recv_in, send_ref, keep_ref):
    halve(bit, send_ref, keep_ref, keep_in, recv_in)


def total_kernel(tokens, keep_a_ref, recv_a_ref, keep_b_ref, recv_b_ref, out_ref):
    half = keep_a_ref.shape[-1]
    out_ref[:, :half] = (keep_a_ref[0] + recv_a_ref[0]) * (1.0 / tokens)
    out_ref[:, half:] = (keep_b_ref[0] + recv_b_ref[0]) * (1.0 / tokens)


def gather_kernel(*refs):
    *pieces, grad_in_ref, grad_out_ref = refs
    d = lax.axis_index("dp")
    width = grad_out_ref.shape[-1]
    half = width // 2
    for k, piece in enumerate(pieces):
        at = jnp.bitwise_xor(d, k)
        grad_out_ref[at] = piece[:, :width]
        start = width
        for cols, first in ((half, 0), (width, 2 * width), (half, half), (width, width), (width, 3 * width)):
            grad_in_ref[at, :, first:first + cols] = piece[:, start:start + cols]
            start += cols


def vmem():
    return pl.BlockSpec(memory_space=pltpu.VMEM)


def shape(*dims, dtype=f32):
    return jax.ShapeDtypeStruct(dims, dtype)


def call(kernel, name, out_shape, args, scratch=(), far=0, long=False, grant=4):
    place = [pltpu.SMEM if a.size == 1 else pltpu.HBM if i < far else pltpu.VMEM for i, a in enumerate(args)]
    args = [a if p is pltpu.SMEM else pltpu.with_memory_space_constraint(a, p) for a, p in zip(args, place)]
    return pl.pallas_call(
        kernel,
        name=name,
        in_specs=[pl.BlockSpec(memory_space=p) for p in place],
        out_specs=[vmem()] * len(out_shape),
        out_shape=list(out_shape),
        scratch_shapes=[pltpu.VMEM(dims, dtype) for dims, dtype in scratch]
        + [pltpu.SemaphoreType.DMA((16,))] * (far > 0),
        compiler_params=pltpu.CompilerParams(vmem_limit_bytes=grant * MIB),
        cost_estimate=pl.CostEstimate(flops=100_000_000_000 if long else 1_000_000_000, bytes_accessed=1 << 16, transcendentals=0),
    )(*args)


def body(rows_size, dp_size, events, cotangent, lengths, event_slot, slot_row, slot_count, w_in, w_out, item_table, accumulator):
    tokens, width = events.shape
    owners, capacity = slot_row.shape[1:]
    chips = rows_size // 2
    piece = width // (rows_size * dp_size)
    cores = [(i, i ^ 1) for i in range(rows_size)]
    over_dp = lambda v, bit: lax.ppermute(v, "dp", [(i, i ^ bit) for i in range(dp_size)])
    after = lambda value, *others: lax.optimization_barrier((value, *others))[0]
    strip = chips * piece

    def gathered(total):
        return [total] + [over_dp(total, k) for k in range(1, dp_size)]

    by_dp = lambda v: v.reshape(2, 2, strip, v.shape[-1])
    by_chip = lambda v: v.reshape(*v.shape[:-2], chips, piece, v.shape[-1])
    local = lambda *dims, dtype=f32: pltpu.VMEM(dims, dtype)
    sides = lambda cols: [local(width // 2, cols)] * 2
    keep1, send1, hid, dsilu, gatt, gpre_uv, normed_t, events, masked, w_in, inv_len = call(
        functools.partial(forward_kernel, rows_size, dp_size), "forward_part",
        sides(3 * width) + [
            local(tokens, 3 * width, dtype=bf16),
            local(tokens, 2 * width, dtype=bf16),
            local(tokens, width, dtype=bf16),
            local(tokens, 2 * width, dtype=bf16),
            local(width, tokens, dtype=bf16),
            local(tokens, width, dtype=bf16),
            local(tokens, width, dtype=bf16),
            local(*w_in.shape, dtype=bf16),
            local(8, LANES),
        ],
        (lengths, events, cotangent, w_in, w_out),
        [((tokens, width), bf16), ((tokens, width), bf16), ((tokens, width), f32), ((tokens, width), f32),
         ((tokens, width), bf16), ((tokens, width), f32), ((HEADS, tokens, tokens), bf16),
         (w_out.shape, bf16), ((width, width), bf16), ((tokens, width), f32), ((tokens, width), bf16),
         ((4, STEP, width), f32), ((4, STEP, STEP), f32), ((width // 2, tokens), bf16)], far=5, long=True, grant=22)
    recv1 = lax.ppermute(send1, "rows", cores)
    keep2, send2, gpre_qk = call(
        attention_kernel, "attention_part", sides(2 * width) + [local(tokens, 2 * width, dtype=bf16)],
        (inv_len, hid, dsilu, gatt, normed_t),
        [((4, STEP, STEP), f32), ((4, STEP, STEP), f32), ((2, tokens, tokens), bf16)], long=True, grant=12)
    recv2 = lax.ppermute(send2, "rows", cores)
    block = capacity * (width // LANES)
    gpre_uv = after(gpre_uv, recv1)
    sends = call(
        functools.partial(events_kernel, rows_size, dp_size), "events_part",
        [local(2 * dp_size * block + ID_ROWS, LANES)] * chips,
        (events, masked, w_in, event_slot, slot_row[0].T, gpre_uv, gpre_qk),
        [((tokens, width), bf16), ((tokens, width), bf16), ((owners * capacity, width), f32), ((tokens, width), f32),
         ((owners * capacity, tokens), bf16)], grant=12, long=True)
    ahead = lambda v, k: lax.ppermute(v, "rows", [(i, (i + 2 * k) % rows_size) for i in range(rows_size)])
    came = [sends[0]] + [ahead(sends[k], k) for k in range(1, chips)]
    cols = w_in.shape[1] + width
    to_x, to_y, keep_a, keep_b = call(
        first_kernel, "first_sums", [local(2, strip, cols // 2)] * 4,
        [by_dp(v) for v in (after(keep1, *sends), recv1, keep2, recv2)])
    from_x, from_y = over_dp(to_x, 1), over_dp(to_y, 2)
    to_y, to_x, next_a, next_b = call(
        second_kernel, "second_sums", [local(strip, cols // 2)] * 4, (keep_a, from_x, keep_b, from_y),
        long=True)
    from_y, from_x = over_dp(to_y, 2), over_dp(to_x, 1)
    came[0] = after(came[0], to_y, to_x)
    parts = call(
        functools.partial(by_part_kernel, dp_size, block), "by_part",
        [local(2 * chips * block + id_rows(chips), LANES)] * dp_size, came, long=True)
    next_a = after(next_a, *parts)
    bits = chips.bit_length() - 1
    over_chips = lambda v, bit: lax.ppermute(v, "rows", [(i, i ^ (2 << bit)) for i in range(rows_size)])
    send_a, keep_a, send_b, keep_b = call(
        chip_first_kernel, "chip_sums", [local(chips // 2, piece, cols // 2)] * 4,
        [by_chip(v) for v in (next_a, from_y, next_b, from_x)])
    halves = [[keep_a, over_chips(send_a, 0)], [keep_b, over_chips(send_b, 0)]]
    parts = [parts[0]] + [over_dp(parts[k], k) for k in range(1, dp_size)]
    for bit in range(1, bits):
        for i in range(2):
            if i == 1:
                halves[1][0] = after(halves[1][0], send, keep)
            send, keep = call(
                functools.partial(chip_kernel, bit), "chip_sums", [local(chips >> (bit + 1), piece, cols // 2)] * 2,
                halves[i], long=False)
            halves[i] = [keep, over_chips(send, bit)]
    (total,) = call(
        functools.partial(total_kernel, tokens), "total", [local(piece, cols)], halves[0] + halves[1], long=False)
    pieces = gathered(total)
    parts[0] = after(parts[0], total)
    keep, send = call(
        functools.partial(by_core_kernel, chips, block), "by_core",
        [local(dp_size * (chips * block + id_rows(chips)), LANES)] * 2, parts, long=False)
    recv = lax.ppermute(send, "rows", cores)
    slots = owners * capacity
    table_new, accum_new = call(
        functools.partial(table_kernel, dp_size, chips), "table_part", [shape(*item_table.shape), shape(*accumulator.shape)],
        (keep, recv, item_table, accumulator),
        [((slots, width), f32), ((slots, width), bf16), ((slots, width), bf16)], grant=10)
    pieces[-1] = after(pieces[-1], accum_new)
    grad_in, grad_out = call(
        gather_kernel, "gather", [shape(dp_size, piece, 4 * width), shape(dp_size, piece, width)], pieces)
    return grad_in.reshape(-1, 4 * width), grad_out.reshape(-1, width), table_new, accum_new


def solution(mesh):
    whole = P(("dp", "rows"))
    in_specs = (whole,) * 6 + (P(), P(), whole, whole)
    out_specs = (P("rows"), P("rows"), whole, whole)
    run = functools.partial(body, mesh.shape["rows"], mesh.shape["dp"])
    return jax.shard_map(run, mesh=mesh, in_specs=in_specs, out_specs=out_specs, check_vma=False)
```

```python
import functools

import jax
import jax.numpy as jnp
from jax import lax
from jax.experimental import pallas as pl
from jax.experimental.pallas import tpu as pltpu
from jax.sharding import PartitionSpec as P

HEADS = 4

norm_eps = 1e-05
adagrad_eps = 1e-10
learning_rate = 0.1

f32, bf16 = jnp.float32, jnp.bfloat16
MIB = 1024 * 1024
STEP = 256
TILE = 32
LANES = 128
ID_ROWS = 8


def dot_nn(a, b):
    return lax.dot_general(a, b, (((1,), (0,)), ((), ())), preferred_element_type=f32)


def dot_nt(a, b):
    return lax.dot_general(a, b, (((1,), (1,)), ((), ())), preferred_element_type=f32)


def dot_tn(a, b):
    return lax.dot_general(a, b, (((0,), (0,)), ((), ())), preferred_element_type=f32)


def over(value, n):
    return value >> (n.bit_length() - 1) if n & (n - 1) == 0 else value // n


def rest(value, n):
    return value & (n - 1) if n & (n - 1) == 0 else value % n


def standardize(x):
    centered = x - jnp.mean(x, axis=-1, keepdims=True)
    inv = lax.rsqrt(jnp.mean(centered * centered, axis=-1, keepdims=True) + norm_eps)
    return centered * inv, inv


def masked_rows(cot, start, length):
    row = start + lax.broadcasted_iota(jnp.int32, cot.shape, 0)
    return jnp.where(row < length, cot.astype(f32), 0.0)


def owner_order(width, rows, dp):
    chips = rows // 2
    piece = width // (rows * dp)
    at = lax.broadcasted_iota(jnp.int32, (width, 1), 0)
    side, part = over(at, width // 2), rest(over(at, chips * piece), dp)
    chip, row = rest(over(at, piece), chips), rest(at, piece)
    core = lax.rem(lax.axis_index("rows"), 2)
    core = jnp.where(side == 0, core, 1 - core)
    wanted = ((chip * 2 + core) * dp + part) * piece + row
    return jnp.where(lax.broadcasted_iota(jnp.int32, (width, width), 1) == wanted, 1.0, 0.0).astype(bf16)


def tiles_of(start, count, size):
    return [pl.ds(start + at, size) for at in range(0, count, size)]


def forward_kernel(rows_size, dp_size, len_ref, ev_hbm, cot_hbm, win_hbm, wout_hbm,
                   keep_ref, send_ref, hid_ref, dsilu_ref, gatt_ref, gpre_ref, normed_t_ref,
                   ev_ref, masked_ref, win_ref, inv_ref, normed_ref, user_ref, duser_ref, att_ref, mixed_ref, dval_ref,
                   weights_ref, wout_ref, order_ref, grad_mixed_ref, cot_ref, pre_ref, raw_ref, arrived):
    tokens, width = ev_ref.shape
    copies = [pltpu.make_async_copy(ev_hbm, ev_ref, arrived.at[0])]
    for c in range(4):
        cols = pl.ds(c * width, width)
        copies.append(pltpu.make_async_copy(win_hbm.at[:, cols], win_ref.at[:, cols], arrived.at[1 + c]))
    copies.append(pltpu.make_async_copy(cot_hbm, cot_ref, arrived.at[5]))
    copies.append(pltpu.make_async_copy(wout_hbm, wout_ref, arrived.at[6]))
    for copy in copies:
        copy.start()
    order_ref[...] = owner_order(width, rows_size, dp_size)
    hd = width // HEADS
    scale = hd ** -0.5
    steps = tokens // STEP

    copies[0].wait()
    for tile in tiles_of(0, tokens, TILE):
        xhat, _ = standardize(ev_ref[tile, :].astype(f32))
        normed_ref[tile, :] = xhat.astype(bf16)

    def project(n):
        c, i = n // steps, n % steps
        if i == 0:
            copies[1 + c].wait()
        pre_ref[n % pre_ref.shape[0]] = dot_nn(normed_ref[pl.ds(i * STEP, STEP), :], win_ref[:, c * width:(c + 1) * width])

    def gate(n):
        c, i = n // steps, n % steps
        for at in range(0, STEP, TILE):
            tile = pl.ds(i * STEP + at, TILE)
            pre = pre_ref[n % pre_ref.shape[0], at:at + TILE, :]
            sig = 0.5 + 0.5 * jnp.tanh(0.5 * pre)
            hid = pre * sig
            dsilu = sig * (1.0 + (pre - hid))
            if c == 0:
                user_ref[tile, :] = hid.astype(bf16)
                duser_ref[tile, :] = dsilu
            else:
                hid_ref[tile, (c - 1) * width:c * width] = hid.astype(bf16)
                if c == 1:
                    dval_ref[tile, :] = dsilu
                else:
                    dsilu_ref[tile, (c - 2) * width:(c - 1) * width] = dsilu.astype(bf16)

    project(0)
    for n in range(4 * steps):
        if n + 1 < 4 * steps:
            project(n + 1)
        gate(n)

    for copy in copies[5:]:
        copy.wait()
    length = len_ref[0]
    inv_len = 1.0 / length.astype(f32)
    inv_ref[...] = jnp.full(inv_ref.shape, inv_len, f32)
    blocks = [(h, i, j) for h in range(HEADS) for i in range(steps) for j in range(i + 1)]

    def score(n):
        h, i, j = blocks[n]
        query = hid_ref[pl.ds(i * STEP, STEP), width + h * hd:width + (h + 1) * hd]
        key = hid_ref[pl.ds(j * STEP, STEP), 2 * width + h * hd:2 * width + (h + 1) * hd]
        raw_ref[n % raw_ref.shape[0]] = dot_nt(query, key)

    score(0)
    for n, (h, i, j) in enumerate(blocks):
        if n + 1 < len(blocks):
            score(n + 1)
        for at in range(0, STEP, 2 * TILE):
            half = raw_ref[n % raw_ref.shape[0], at:at + 2 * TILE, :] * (0.5 * scale)
            weights = (half + half * jnp.tanh(half)) * inv_len
            if i == j:
                row = at + lax.broadcasted_iota(jnp.int32, weights.shape, 0)
                weights = jnp.where(row >= lax.broadcasted_iota(jnp.int32, weights.shape, 1), weights, 0.0)
            weights_ref[h, pl.ds(i * STEP + at, 2 * TILE), pl.ds(j * STEP, STEP)] = weights.astype(bf16)
        if j == i:
            rows, seen, v_cols = pl.ds(i * STEP, STEP), pl.ds(0, (i + 1) * STEP), slice(h * hd, (h + 1) * hd)
            att_ref[rows, v_cols] = dot_nn(weights_ref[h, rows, seen], hid_ref[seen, v_cols])
        if i < steps - 1 or j < i:
            continue
        for i in range(h, steps, HEADS):
            rows = pl.ds(i * STEP, STEP)
            normed_t_ref[rows, :] = dot_nt(order_ref[rows, :], normed_ref[...]).astype(bf16)
        for i in range(h - HEADS // 2, steps, HEADS):
            if i >= 0:
                rows = pl.ds(i * STEP, STEP)
                for tile in tiles_of(i * STEP, STEP, TILE):
                    masked_ref[tile, :] = masked_rows(cot_ref[tile, :], tile.start, length).astype(bf16)
                grad_mixed_ref[rows, :] = dot_nt(masked_ref[rows, :], wout_ref[...])

    for tile in tiles_of(0, tokens, TILE // 2):
        ahat, inv = standardize(att_ref[tile, :])
        user = user_ref[tile, :].astype(f32)
        mixed_ref[tile, :] = (ahat * user).astype(bf16)
        grad_mixed = grad_mixed_ref[tile, :]
        gpre_ref[tile, :width] = (grad_mixed * ahat * duser_ref[tile, :]).astype(bf16)
        e = grad_mixed * user
        gatt_ref[tile, :] = (inv * (e - jnp.mean(e, axis=-1, keepdims=True)
                                    - ahat * jnp.mean(e * ahat, axis=-1, keepdims=True))).astype(bf16)

    for h in range(HEADS):
        v_cols = slice(h * hd, (h + 1) * hd)
        for j in range(steps):
            keys, later = pl.ds(j * STEP, STEP), pl.ds(j * STEP, tokens - j * STEP)
            grad_v = dot_tn(weights_ref[h, later, keys], gatt_ref[later, v_cols])
            gpre_ref[keys, width + h * hd:width + (h + 1) * hd] = (grad_v * dval_ref[keys, v_cols]).astype(bf16)

    mixed_t = dot_nt(order_ref[...], mixed_ref[...]).astype(bf16)
    half = width // 2
    for ref, start in ((send_ref, half), (keep_ref, 0)):
        ref[:, :width] = dot_nn(mixed_t[start:start + half], masked_ref[...])
        ref[:, width:] = dot_nn(normed_t_ref[start:start + half, :], gpre_ref[...])


def attention_kernel(inv_ref, hid_ref, dsilu_ref, gatt_ref, normed_t_ref, keep_ref, send_ref, gpre_ref,
                     raw_ref, weight_ref, score_ref):
    tokens, width = gatt_ref.shape
    hd = width // HEADS
    scale = hd ** -0.5
    steps = tokens // STEP
    factor = inv_ref[:1, :hd] * (0.5 * scale)

    blocks = [(h, j, i) for h in range(HEADS) for j in range(steps) for i in range(j, steps)]
    slots = raw_ref.shape[0]

    def score(n):
        h, j, i = blocks[n]
        keys, rows, v_cols = pl.ds(j * STEP, STEP), pl.ds(i * STEP, STEP), slice(h * hd, (h + 1) * hd)
        raw_ref[n % slots] = dot_nt(
            hid_ref[keys, 2 * width + h * hd:2 * width + (h + 1) * hd], hid_ref[rows, width + h * hd:width + (h + 1) * hd])
        weight_ref[n % slots] = dot_nt(hid_ref[keys, v_cols], gatt_ref[rows, v_cols])

    score(0)
    for n, (h, j, i) in enumerate(blocks):
        if n + 1 < len(blocks):
            score(n + 1)
        for at in range(0, STEP, TILE):
            half = raw_ref[n % slots, at:at + TILE, :] * (0.5 * scale)
            gate = jnp.tanh(half)
            gscore = weight_ref[n % slots, at:at + TILE, :] * ((1.0 + gate) * (1.0 + half * (1.0 - gate)))
            if i == j:
                row = at + lax.broadcasted_iota(jnp.int32, gscore.shape, 0)
                gscore = jnp.where(row <= lax.broadcasted_iota(jnp.int32, gscore.shape, 1), gscore, 0.0)
            score_ref[h % 2, pl.ds(j * STEP + at, TILE), pl.ds(i * STEP, STEP)] = gscore.astype(bf16)
        if j < steps - 1:
            continue
        v_cols = slice(h * hd, (h + 1) * hd)
        q_cols = slice(width + h * hd, width + (h + 1) * hd)
        k_cols = slice(2 * width + h * hd, 2 * width + (h + 1) * hd)
        for j in range(steps):
            keys, later, seen = pl.ds(j * STEP, STEP), pl.ds(j * STEP, tokens - j * STEP), pl.ds(0, (j + 1) * STEP)
            grad_k = dot_nn(score_ref[h % 2, keys, later], hid_ref[later, q_cols])
            gpre_ref[keys, q_cols] = (grad_k * (dsilu_ref[keys, q_cols].astype(f32) * factor)).astype(bf16)
            grad_q = dot_tn(score_ref[h % 2, seen, keys], hid_ref[seen, k_cols])
            gpre_ref[keys, v_cols] = (grad_q * (dsilu_ref[keys, v_cols].astype(f32) * factor)).astype(bf16)

    half = width // 2
    for ref, start in ((send_ref, half), (keep_ref, 0)):
        ref[...] = dot_nn(normed_t_ref[start:start + half, :], gpre_ref[...])


def slots_in_order(position, capacity, dp, rows):
    chips = rows // 2
    owner, place = over(position, capacity), rest(position, capacity)
    ahead, core, part = over(owner, 2 * dp), rest(over(owner, dp), 2), rest(owner, dp)
    chip = rest(lax.axis_index("rows") // 2 + ahead, chips)
    return part * rows + chip * 2 + core, place


def events_kernel(rows_size, dp_size, ev_ref, masked_ref, win_ref, slot_ref, slot_row_ref, gpre_uv_ref, gpre_qk_ref, *refs):
    *send_refs, hi_ref, lo_ref, rows_ref, grad_ref, onehot_ref = refs
    tokens, width = ev_ref.shape
    capacity, owners = slot_row_ref.shape
    for i in range(tokens // STEP):
        rows = pl.ds(i * STEP, STEP)
        grad_ref[rows, :] = dot_nt(gpre_uv_ref[rows, :], win_ref[:, :2 * width]) + dot_nt(gpre_qk_ref[rows, :], win_ref[:, 2 * width:])
        for tile in tiles_of(i * STEP, STEP, TILE // 2):
            xhat, inv = standardize(ev_ref[tile, :].astype(f32))
            grad_normed = grad_ref[tile, :]
            grad = masked_ref[tile, :].astype(f32) + inv * (
                grad_normed - jnp.mean(grad_normed, axis=-1, keepdims=True)
                - xhat * jnp.mean(grad_normed * xhat, axis=-1, keepdims=True))
            high = grad.astype(bf16)
            hi_ref[tile, :] = high
            lo_ref[tile, :] = (grad - high.astype(f32)).astype(bf16)

    slots = rows_ref.shape[0]
    owner, place = slots_in_order(lax.broadcasted_iota(jnp.int32, (slots, 1), 0), capacity, dp_size, rows_size)
    wanted = owner * capacity + place
    for at in range(0, slots, 2 * TILE):
        onehot_ref[at:at + 2 * TILE, :] = jnp.where(wanted[at:at + 2 * TILE] == slot_ref[...], 1.0, 0.0).astype(bf16)
    rows_ref[...] = dot_nn(onehot_ref[...], hi_ref[...]) + dot_nn(onehot_ref[...], lo_ref[...])
    owner, place = slots_in_order(lax.broadcasted_iota(jnp.int32, (1, slots), 1), capacity, dp_size, rows_size)
    chosen = lax.broadcasted_iota(jnp.int32, (owners, slots), 0) == owner
    mine = lax.broadcasted_iota(jnp.int32, (capacity, slots), 0) == place
    ids = whole_numbers(slot_row_ref[...], chosen, mine)
    tiles = width // LANES
    blocks = 2 * dp_size
    for k, send_ref in enumerate(send_refs):
        for i in range(blocks):
            at = (k * blocks + i) * capacity
            for t in range(tiles):
                send_ref[(i * tiles + t) * capacity:(i * tiles + t + 1) * capacity, :] = rows_ref[at:at + capacity, t * LANES:(t + 1) * LANES]
        tile = k * blocks * capacity // LANES * LANES
        send_ref[blocks * tiles * capacity:, :] = jnp.broadcast_to(ids[:, tile:tile + LANES], (ID_ROWS, LANES))


def whole_numbers(values, chosen, mine):
    pick = jnp.where(chosen, 1.0, 0.0).astype(bf16)
    found = 16.0 * dot_nn(over(values, 16).astype(bf16), pick) + dot_nn(rest(values, 16).astype(bf16), pick)
    return jnp.sum(jnp.where(mine, found, 0.0), axis=0, keepdims=True)


def id_rows(chips):
    return max(ID_ROWS, chips)


def by_part_kernel(dp, block, *refs):
    ins, outs = refs[:-dp], refs[-dp:]
    d = lax.axis_index("dp")
    for j, out_ref in enumerate(outs):
        part = jnp.bitwise_xor(d, j)
        for k, in_ref in enumerate(ins):
            for core in range(2):
                start = pl.multiple_of((core * dp + part) * block, block)
                out_ref[(k * 2 + core) * block:(k * 2 + core + 1) * block, :] = in_ref[pl.ds(start, block), :]
        ids = [in_ref[2 * dp * block:2 * dp * block + 1, :] for in_ref in ins]
        ids += [jnp.zeros((1, LANES), f32)] * (id_rows(len(ins)) - len(ins))
        out_ref[2 * len(ins) * block:, :] = jnp.concatenate(ids, axis=0)


def by_core_kernel(chips, block, *refs):
    *ins, keep_ref, send_ref = refs
    core = lax.rem(lax.axis_index("rows"), 2)
    for out_ref, to in ((send_ref, 1 - core), (keep_ref, core)):
        for j, in_ref in enumerate(ins):
            for k in range(chips):
                start = pl.multiple_of((k * 2 + to) * block, block)
                out_ref[(j * chips + k) * block:(j * chips + k + 1) * block, :] = in_ref[pl.ds(start, block), :]
            at = len(ins) * chips * block + j * id_rows(chips)
            out_ref[at:at + id_rows(chips), :] = in_ref[2 * chips * block:, :]


def one_hot_rows(ids, wanted, hi_ref, lo_ref):
    onehot = jnp.where(wanted == ids, 1.0, 0.0).astype(bf16)
    return dot_nn(onehot, hi_ref[...]) + dot_nn(onehot, lo_ref[...])


def table_kernel(dp, chips, keep_ref, recv_ref, table_ref, accum_ref, table_new_ref, accum_new_ref, rows_ref, hi_ref, lo_ref):
    rows, width = table_ref.shape
    tiles = width // LANES
    sources = dp * chips
    capacity = rows_ref.shape[0] // (2 * sources)
    count = sources * capacity
    r = lax.axis_index("rows")
    block = lax.rem(r, 2) * dp + lax.axis_index("dp")
    ids = []
    for side, ref in enumerate((keep_ref, recv_ref)):
        for i in range(sources):
            at = side * count + i * capacity
            for t in range(tiles):
                rows_ref[at:at + capacity, t * LANES:(t + 1) * LANES] = ref[(i * tiles + t) * capacity:(i * tiles + t + 1) * capacity, :]
        values = ref[sources * tiles * capacity:, :].astype(jnp.int32)
        position = lax.broadcasted_iota(jnp.int32, (1, count), 1)
        source, place = over(position, capacity), rest(position, capacity)
        part, ahead = over(source, chips), rest(source, chips)
        lane = rest(ahead * (2 * dp * capacity), LANES) + block * capacity + place
        chosen = lax.broadcasted_iota(jnp.int32, (LANES, count), 0) == lane
        mine = lax.broadcasted_iota(jnp.int32, (values.shape[0], count), 0) == part * id_rows(chips) + ahead
        ids.append(whole_numbers(values, chosen, mine))
    ids = jnp.concatenate(ids, axis=1).astype(jnp.int32)
    high = rows_ref[...].astype(bf16)
    hi_ref[...] = high
    lo_ref[...] = (rows_ref[...] - high.astype(f32)).astype(bf16)
    grad = one_hot_rows(ids, lax.broadcasted_iota(jnp.int32, (rows, 1), 0), hi_ref, lo_ref)
    accum = jnp.transpose(jnp.broadcast_to(accum_ref[...].reshape(1, rows), (8, rows)))[:, :1]
    accum_new = accum + jnp.mean(grad * grad, axis=-1, keepdims=True)
    accum_new_ref[...] = jnp.transpose(jnp.broadcast_to(accum_new, (rows, LANES)))[:1, :].reshape(rows)
    table_new_ref[...] = table_ref[...] - learning_rate * grad / (jnp.sqrt(accum_new) + adagrad_eps)


def place_on_dp():
    d = lax.axis_index("dp")
    return lax.rem(d, 2), d // 2


def first_kernel(keep1_ref, recv1_ref, keep2_ref, recv2_ref, to_x_ref, to_y_ref, keep_a_ref, keep_b_ref):
    x, y = place_on_dp()
    start = 0
    for keep_ref, recv_ref in ((keep1_ref, recv1_ref), (keep2_ref, recv2_ref)):
        half = keep_ref.shape[-1] // 2
        part = lambda i, j, cols: keep_ref[i, j, :, cols] + recv_ref[i, j, :, cols]
        lo, hi, out = slice(0, half), slice(half, 2 * half), slice(start, start + half)
        for s in range(2):
            to_x_ref[s, :, out] = part(s, 1 - x, lo)
            to_y_ref[s, :, out] = part(1 - y, s, hi)
            keep_a_ref[s, :, out] = part(s, x, lo)
            keep_b_ref[s, :, out] = part(y, s, hi)
        start += half


def second_kernel(keep_a_ref, from_x_ref, keep_b_ref, from_y_ref, to_y_ref, to_x_ref, next_a_ref, next_b_ref):
    x, y = place_on_dp()
    to_y_ref[...] = keep_a_ref[1 - y] + from_x_ref[1 - y]
    to_x_ref[...] = keep_b_ref[1 - x] + from_y_ref[1 - x]
    next_a_ref[...] = keep_a_ref[y] + from_x_ref[y]
    next_b_ref[...] = keep_b_ref[x] + from_y_ref[x]


def halve(bit, send_ref, keep_ref, keep_in, recv_in):
    mine = rest(lax.axis_index("rows") // 2 >> bit, 2)
    for i in range(send_ref.shape[0]):
        send_ref[i] = keep_in[2 * i + 1 - mine] + recv_in[2 * i + 1 - mine]
        keep_ref[i] = keep_in[2 * i + mine] + recv_in[2 * i + mine]


def chip_first_kernel(next_a_ref, from_y_ref, next_b_ref, from_x_ref, send_a_ref, keep_a_ref, send_b_ref, keep_b_ref):
    halve(0, send_a_ref, keep_a_ref, next_a_ref, from_y_ref)
    halve(0, send_b_ref, keep_b_ref, next_b_ref, from_x_ref)


def chip_kernel(bit, keep_in, recv_in, send_ref, keep_ref):
    halve(bit, send_ref, keep_ref, keep_in, recv_in)


def total_kernel(tokens, keep_a_ref, recv_a_ref, keep_b_ref, recv_b_ref, out_ref):
    half = keep_a_ref.shape[-1]
    out_ref[:, :half] = (keep_a_ref[0] + recv_a_ref[0]) * (1.0 / tokens)
    out_ref[:, half:] = (keep_b_ref[0] + recv_b_ref[0]) * (1.0 / tokens)


def gather_kernel(*refs):
    *pieces, grad_in_ref, grad_out_ref = refs
    d = lax.axis_index("dp")
    width = grad_out_ref.shape[-1]
    half = width // 2
    for k, piece in enumerate(pieces):
        at = jnp.bitwise_xor(d, k)
        grad_out_ref[at] = piece[:, :width]
        start = width
        for cols, first in ((half, 0), (width, 2 * width), (half, half), (width, width), (width, 3 * width)):
            grad_in_ref[at, :, first:first + cols] = piece[:, start:start + cols]
            start += cols


def vmem():
    return pl.BlockSpec(memory_space=pltpu.VMEM)


def shape(*dims, dtype=f32):
    return jax.ShapeDtypeStruct(dims, dtype)


def call(kernel, name, out_shape, args, scratch=(), far=0, long=False, grant=4):
    place = [pltpu.SMEM if a.size == 1 else pltpu.HBM if i < far else pltpu.VMEM for i, a in enumerate(args)]
    args = [a if p is pltpu.SMEM else pltpu.with_memory_space_constraint(a, p) for a, p in zip(args, place)]
    return pl.pallas_call(
        kernel,
        name=name,
        in_specs=[pl.BlockSpec(memory_space=p) for p in place],
        out_specs=[vmem()] * len(out_shape),
        out_shape=list(out_shape),
        scratch_shapes=[pltpu.VMEM(dims, dtype) for dims, dtype in scratch]
        + [pltpu.SemaphoreType.DMA((7,))] * (far > 0),
        compiler_params=pltpu.CompilerParams(vmem_limit_bytes=grant * MIB),
        cost_estimate=pl.CostEstimate(flops=100_000_000_000 if long else 1_000_000_000, bytes_accessed=1 << 16, transcendentals=0),
    )(*args)


def body(rows_size, dp_size, events, cotangent, lengths, event_slot, slot_row, slot_count, w_in, w_out, item_table, accumulator):
    tokens, width = events.shape
    owners, capacity = slot_row.shape[1:]
    chips = rows_size // 2
    piece = width // (rows_size * dp_size)
    cores = [(i, i ^ 1) for i in range(rows_size)]
    over_dp = lambda v, bit: lax.ppermute(v, "dp", [(i, i ^ bit) for i in range(dp_size)])
    after = lambda value, *others: lax.optimization_barrier((value, *others))[0]
    strip = chips * piece

    def gathered(total):
        return [total] + [over_dp(total, k) for k in range(1, dp_size)]

    by_dp = lambda v: v.reshape(2, 2, strip, v.shape[-1])
    by_chip = lambda v: v.reshape(*v.shape[:-2], chips, piece, v.shape[-1])
    local = lambda *dims, dtype=f32: pltpu.VMEM(dims, dtype)
    sides = lambda cols: [local(width // 2, cols)] * 2
    keep1, send1, hid, dsilu, gatt, gpre_uv, normed_t, events, masked, w_in, inv_len = call(
        functools.partial(forward_kernel, rows_size, dp_size), "forward_part",
        sides(3 * width) + [
            local(tokens, 3 * width, dtype=bf16),
            local(tokens, 2 * width, dtype=bf16),
            local(tokens, width, dtype=bf16),
            local(tokens, 2 * width, dtype=bf16),
            local(width, tokens, dtype=bf16),
            local(tokens, width, dtype=bf16),
            local(tokens, width, dtype=bf16),
            local(*w_in.shape, dtype=bf16),
            local(8, LANES),
        ],
        (lengths, events, cotangent, w_in, w_out),
        [((tokens, width), bf16), ((tokens, width), bf16), ((tokens, width), f32), ((tokens, width), f32),
         ((tokens, width), bf16), ((tokens, width), f32), ((HEADS, tokens, tokens), bf16),
         (w_out.shape, bf16), ((width, width), bf16), ((tokens, width), f32), ((tokens, width), bf16),
         ((4, STEP, width), f32), ((4, STEP, STEP), f32)], far=5, long=True, grant=22)
    recv1 = lax.ppermute(send1, "rows", cores)
    keep2, send2, gpre_qk = call(
        attention_kernel, "attention_part", sides(2 * width) + [local(tokens, 2 * width, dtype=bf16)],
        (inv_len, hid, dsilu, gatt, normed_t),
        [((4, STEP, STEP), f32), ((4, STEP, STEP), f32), ((2, tokens, tokens), bf16)], long=True, grant=12)
    recv2 = lax.ppermute(send2, "rows", cores)
    block = capacity * (width // LANES)
    gpre_uv = after(gpre_uv, recv1)
    sends = call(
        functools.partial(events_kernel, rows_size, dp_size), "events_part",
        [local(2 * dp_size * block + ID_ROWS, LANES)] * chips,
        (events, masked, w_in, event_slot, slot_row[0].T, gpre_uv, gpre_qk),
        [((tokens, width), bf16), ((tokens, width), bf16), ((owners * capacity, width), f32), ((tokens, width), f32),
         ((owners * capacity, tokens), bf16)], grant=12, long=True)
    ahead = lambda v, k: lax.ppermute(v, "rows", [(i, (i + 2 * k) % rows_size) for i in range(rows_size)])
    came = [sends[0]] + [ahead(sends[k], k) for k in range(1, chips)]
    cols = w_in.shape[1] + width
    to_x, to_y, keep_a, keep_b = call(
        first_kernel, "first_sums", [local(2, strip, cols // 2)] * 4,
        [by_dp(v) for v in (after(keep1, *sends), recv1, keep2, recv2)])
    from_x, from_y = over_dp(to_x, 1), over_dp(to_y, 2)
    to_y, to_x, next_a, next_b = call(
        second_kernel, "second_sums", [local(strip, cols // 2)] * 4, (keep_a, from_x, keep_b, from_y),
        long=True)
    from_y, from_x = over_dp(to_y, 2), over_dp(to_x, 1)
    came[0] = after(came[0], to_y, to_x)
    parts = call(
        functools.partial(by_part_kernel, dp_size, block), "by_part",
        [local(2 * chips * block + id_rows(chips), LANES)] * dp_size, came, long=True)
    next_a = after(next_a, *parts)
    bits = chips.bit_length() - 1
    over_chips = lambda v, bit: lax.ppermute(v, "rows", [(i, i ^ (2 << bit)) for i in range(rows_size)])
    send_a, keep_a, send_b, keep_b = call(
        chip_first_kernel, "chip_sums", [local(chips // 2, piece, cols // 2)] * 4,
        [by_chip(v) for v in (next_a, from_y, next_b, from_x)])
    halves = [[keep_a, over_chips(send_a, 0)], [keep_b, over_chips(send_b, 0)]]
    parts = [parts[0]] + [over_dp(parts[k], k) for k in range(1, dp_size)]
    for bit in range(1, bits):
        for i in range(2):
            if i == 1:
                halves[1][0] = after(halves[1][0], send, keep)
            send, keep = call(
                functools.partial(chip_kernel, bit), "chip_sums", [local(chips >> (bit + 1), piece, cols // 2)] * 2,
                halves[i], long=False)
            halves[i] = [keep, over_chips(send, bit)]
    (total,) = call(
        functools.partial(total_kernel, tokens), "total", [local(piece, cols)], halves[0] + halves[1], long=False)
    pieces = gathered(total)
    parts[0] = after(parts[0], total)
    keep, send = call(
        functools.partial(by_core_kernel, chips, block), "by_core",
        [local(dp_size * (chips * block + id_rows(chips)), LANES)] * 2, parts, long=False)
    recv = lax.ppermute(send, "rows", cores)
    slots = owners * capacity
    table_new, accum_new = call(
        functools.partial(table_kernel, dp_size, chips), "table_part", [shape(*item_table.shape), shape(*accumulator.shape)],
        (keep, recv, item_table, accumulator),
        [((slots, width), f32), ((slots, width), bf16), ((slots, width), bf16)], grant=10)
    pieces[-1] = after(pieces[-1], accum_new)
    grad_in, grad_out = call(
        gather_kernel, "gather", [shape(dp_size, piece, 4 * width), shape(dp_size, piece, width)], pieces)
    return grad_in.reshape(-1, 4 * width), grad_out.reshape(-1, width), table_new, accum_new


def solution(mesh):
    whole = P(("dp", "rows"))
    in_specs = (whole,) * 6 + (P(), P(), whole, whole)
    out_specs = (P("rows"), P("rows"), whole, whole)
    run = functools.partial(body, mesh.shape["rows"], mesh.shape["dp"])
    return jax.shard_map(run, mesh=mesh, in_specs=in_specs, out_specs=out_specs, check_vma=False)
```

```python
import functools

import jax
import jax.numpy as jnp
from jax import lax
from jax.experimental import pallas as pl
from jax.experimental.pallas import tpu as pltpu
from jax.sharding import PartitionSpec as P

HEADS = 4

norm_eps = 1e-05
adagrad_eps = 1e-10
learning_rate = 0.1

f32, bf16 = jnp.float32, jnp.bfloat16
MIB = 1024 * 1024
STEP = 256
TILE = 32
LANES = 128
ID_ROWS = 8


def dot_nn(a, b):
    return lax.dot_general(a, b, (((1,), (0,)), ((), ())), preferred_element_type=f32)


def dot_nt(a, b):
    return lax.dot_general(a, b, (((1,), (1,)), ((), ())), preferred_element_type=f32)


def dot_tn(a, b):
    return lax.dot_general(a, b, (((0,), (0,)), ((), ())), preferred_element_type=f32)


def over(value, n):
    return value >> (n.bit_length() - 1) if n & (n - 1) == 0 else value // n


def rest(value, n):
    return value & (n - 1) if n & (n - 1) == 0 else value % n


def standardize(x):
    centered = x - jnp.mean(x, axis=-1, keepdims=True)
    inv = lax.rsqrt(jnp.mean(centered * centered, axis=-1, keepdims=True) + norm_eps)
    return centered * inv, inv


def masked_rows(cot, start, length):
    row = start + lax.broadcasted_iota(jnp.int32, cot.shape, 0)
    return jnp.where(row < length, cot.astype(f32), 0.0)


def owner_order(width, rows, dp):
    chips = rows // 2
    piece = width // (rows * dp)
    at = lax.broadcasted_iota(jnp.int32, (width, 1), 0)
    side, part = over(at, width // 2), rest(over(at, chips * piece), dp)
    chip, row = rest(over(at, piece), chips), rest(at, piece)
    core = lax.rem(lax.axis_index("rows"), 2)
    core = jnp.where(side == 0, core, 1 - core)
    wanted = ((chip * 2 + core) * dp + part) * piece + row
    return jnp.where(lax.broadcasted_iota(jnp.int32, (width, width), 1) == wanted, 1.0, 0.0).astype(bf16)


def at_block(index, size):
    return pl.ds(pl.multiple_of(index * size, size), size)


def repeat(count, body, unroll=1):
    lax.fori_loop(0, count, lambda i, _: (body(i), None)[1], None, unroll=unroll)


def tiles_of(start, count, size):
    return [pl.ds(start + at, size) for at in range(0, count, size)]


def forward_kernel(rows_size, dp_size, len_ref, ev_hbm, cot_hbm, win_hbm, wout_hbm,
                   keep_ref, send_ref, hid_ref, dsilu_ref, gatt_ref, gpre_ref, normed_t_ref,
                   ev_ref, masked_ref, win_ref, inv_ref, normed_ref, att_ref, mixed_ref,
                   weights_ref, wout_ref, order_ref, grad_mixed_ref, cot_ref, pre_ref, raw_ref, arrived):
    tokens, width = ev_ref.shape
    copies = [pltpu.make_async_copy(ev_hbm, ev_ref, arrived.at[0])]
    for c in range(4):
        cols = pl.ds(c * width, width)
        copies.append(pltpu.make_async_copy(win_hbm.at[:, cols], win_ref.at[:, cols], arrived.at[1 + c]))
    copies.append(pltpu.make_async_copy(cot_hbm, cot_ref, arrived.at[5]))
    copies.append(pltpu.make_async_copy(wout_hbm, wout_ref, arrived.at[6]))
    for copy in copies:
        copy.start()
    order_ref[...] = owner_order(width, rows_size, dp_size)
    hd = width // HEADS
    scale = hd ** -0.5
    steps = tokens // STEP

    copies[0].wait()

    def normalize(t):
        tile = at_block(t, TILE // 2)
        xhat, _ = standardize(ev_ref[tile, :].astype(f32))
        normed_ref[tile, :] = xhat.astype(bf16)

    repeat(tokens // (TILE // 2), normalize, unroll=4)

    def project(c):
        cols = at_block(c, width)
        pltpu.make_async_copy(win_hbm.at[:, cols], win_ref.at[:, cols], arrived.at[1 + c]).wait()
        for i in range(steps):
            pre_ref[i] = dot_nn(normed_ref[pl.ds(i * STEP, STEP), :], win_ref[:, cols])
            for at in range(0, STEP, TILE):
                tile = pl.ds(i * STEP + at, TILE)
                pre = pre_ref[i, at:at + TILE, :]
                sig = 0.5 + 0.5 * jnp.tanh(0.5 * pre)
                hid = pre * sig
                hid_ref[tile, cols] = hid.astype(bf16)
                dsilu_ref[tile, cols] = (sig * (1.0 + (pre - hid))).astype(bf16)

    repeat(4, project)

    for copy in copies[5:]:
        copy.wait()
    length = len_ref[0]
    inv_len = 1.0 / length.astype(f32)
    inv_ref[...] = jnp.full(inv_ref.shape, inv_len, f32)

    def attend(h):
        v_cols, q_cols, k_cols = (at_block(part * HEADS + h, hd) for part in (1, 2, 3))
        for i in range(steps):
            rows = pl.ds(i * STEP, STEP)
            for j in range(i + 1):
                keys = pl.ds(j * STEP, STEP)
                raw_ref[i + j] = dot_nt(hid_ref[rows, q_cols], hid_ref[keys, k_cols])
                for at in range(0, STEP, 2 * TILE):
                    half = raw_ref[i + j, at:at + 2 * TILE, :] * (0.5 * scale)
                    weights = (half + half * jnp.tanh(half)) * inv_len
                    if i == j:
                        row = at + lax.broadcasted_iota(jnp.int32, weights.shape, 0)
                        weights = jnp.where(row >= lax.broadcasted_iota(jnp.int32, weights.shape, 1), weights, 0.0)
                    weights_ref[h, pl.ds(i * STEP + at, 2 * TILE), keys] = weights.astype(bf16)
            seen = pl.ds(0, (i + 1) * STEP)
            att_ref[rows, at_block(h, hd)] = dot_nn(weights_ref[h, rows, seen], hid_ref[seen, v_cols])

    repeat(HEADS, attend)

    def mask(t):
        tile = at_block(t, TILE)
        masked_ref[tile, :] = masked_rows(cot_ref[tile, :], t * TILE, length).astype(bf16)

    repeat(tokens // TILE, mask, unroll=4)
    normed_t_ref[...] = dot_nt(order_ref[...], normed_ref[...]).astype(bf16)
    grad_mixed_ref[...] = dot_nt(masked_ref[...], wout_ref[...])

    def gate(t):
        tile = at_block(t, TILE // 2)
        ahat, inv = standardize(att_ref[tile, :])
        user = hid_ref[tile, :width].astype(f32)
        mixed_ref[tile, :] = (ahat * user).astype(bf16)
        grad_mixed = grad_mixed_ref[tile, :]
        gpre_ref[tile, :width] = (grad_mixed * ahat * dsilu_ref[tile, :width].astype(f32)).astype(bf16)
        e = grad_mixed * user
        gatt_ref[tile, :] = (inv * (e - jnp.mean(e, axis=-1, keepdims=True)
                                    - ahat * jnp.mean(e * ahat, axis=-1, keepdims=True))).astype(bf16)

    repeat(tokens // (TILE // 2), gate, unroll=4)

    def value_grads(h):
        v_cols, out_cols = at_block(h, hd), at_block(HEADS + h, hd)
        for j in range(steps):
            keys, later = pl.ds(j * STEP, STEP), pl.ds(j * STEP, tokens - j * STEP)
            grad_v = dot_tn(weights_ref[h, later, keys], gatt_ref[later, v_cols])
            gpre_ref[keys, out_cols] = (grad_v * dsilu_ref[keys, out_cols].astype(f32)).astype(bf16)

    repeat(HEADS, value_grads)

    mixed_t = dot_nt(order_ref[...], mixed_ref[...]).astype(bf16)
    half = width // 2
    for ref, start in ((send_ref, half), (keep_ref, 0)):
        ref[:, :width] = dot_nn(mixed_t[start:start + half], masked_ref[...])
        ref[:, width:] = dot_nn(normed_t_ref[start:start + half, :], gpre_ref[...])


def attention_kernel(inv_ref, hid_ref, dsilu_ref, gatt_ref, normed_t_ref, keep_ref, send_ref, gpre_ref,
                     raw_ref, weight_ref, score_ref):
    tokens, width = gatt_ref.shape
    hd = width // HEADS
    scale = hd ** -0.5
    steps = tokens // STEP
    factor = inv_ref[:1, :hd] * (0.5 * scale)

    def attend(h):
        a_cols, v_cols, q_cols, k_cols = (at_block(part * HEADS + h, hd) for part in range(4))
        for j in range(steps):
            keys = pl.ds(j * STEP, STEP)
            for i in range(j, steps):
                rows = pl.ds(i * STEP, STEP)
                raw_ref[i + j] = dot_nt(hid_ref[keys, k_cols], hid_ref[rows, q_cols])
                weight_ref[i + j] = dot_nt(hid_ref[keys, v_cols], gatt_ref[rows, a_cols])
                for at in range(0, STEP, TILE):
                    half = raw_ref[i + j, at:at + TILE, :] * (0.5 * scale)
                    gate = jnp.tanh(half)
                    gscore = weight_ref[i + j, at:at + TILE, :] * ((1.0 + gate) * (1.0 + half * (1.0 - gate)))
                    if i == j:
                        row = at + lax.broadcasted_iota(jnp.int32, gscore.shape, 0)
                        gscore = jnp.where(row <= lax.broadcasted_iota(jnp.int32, gscore.shape, 1), gscore, 0.0)
                    score_ref[pl.ds(j * STEP + at, TILE), rows] = gscore.astype(bf16)
        for j in range(steps):
            keys, later, seen = pl.ds(j * STEP, STEP), pl.ds(j * STEP, tokens - j * STEP), pl.ds(0, (j + 1) * STEP)
            grad_k = dot_nn(score_ref[keys, later], hid_ref[later, q_cols])
            gpre_ref[keys, v_cols] = (grad_k * (dsilu_ref[keys, k_cols].astype(f32) * factor)).astype(bf16)
            grad_q = dot_tn(score_ref[seen, keys], hid_ref[seen, k_cols])
            gpre_ref[keys, a_cols] = (grad_q * (dsilu_ref[keys, q_cols].astype(f32) * factor)).astype(bf16)

    repeat(HEADS, attend)

    half = width // 2
    for ref, start in ((send_ref, half), (keep_ref, 0)):
        ref[...] = dot_nn(normed_t_ref[start:start + half, :], gpre_ref[...])


def slots_in_order(position, capacity, dp, rows):
    chips = rows // 2
    owner, place = over(position, capacity), rest(position, capacity)
    ahead, core, part = over(owner, 2 * dp), rest(over(owner, dp), 2), rest(owner, dp)
    chip = rest(lax.axis_index("rows") // 2 + ahead, chips)
    return part * rows + chip * 2 + core, place


def events_kernel(rows_size, dp_size, ev_ref, masked_ref, win_ref, slot_ref, slot_row_ref, gpre_uv_ref, gpre_qk_ref, *refs):
    *send_refs, hi_ref, lo_ref, rows_ref, grad_ref, onehot_ref = refs
    tokens, width = ev_ref.shape
    capacity, owners = slot_row_ref.shape
    for i in range(tokens // STEP):
        rows = pl.ds(i * STEP, STEP)
        grad_ref[rows, :] = dot_nt(gpre_uv_ref[rows, :], win_ref[:, :2 * width]) + dot_nt(gpre_qk_ref[rows, :], win_ref[:, 2 * width:])

    def event_grads(t):
        tile = at_block(t, TILE // 2)
        xhat, inv = standardize(ev_ref[tile, :].astype(f32))
        grad_normed = grad_ref[tile, :]
        grad = masked_ref[tile, :].astype(f32) + inv * (
            grad_normed - jnp.mean(grad_normed, axis=-1, keepdims=True)
            - xhat * jnp.mean(grad_normed * xhat, axis=-1, keepdims=True))
        high = grad.astype(bf16)
        hi_ref[tile, :] = high
        lo_ref[tile, :] = (grad - high.astype(f32)).astype(bf16)

    repeat(tokens // (TILE // 2), event_grads, unroll=4)

    slots = rows_ref.shape[0]
    owner, place = slots_in_order(lax.broadcasted_iota(jnp.int32, (slots, 1), 0), capacity, dp_size, rows_size)
    wanted = owner * capacity + place
    for at in range(0, slots, 2 * TILE):
        onehot_ref[at:at + 2 * TILE, :] = jnp.where(wanted[at:at + 2 * TILE] == slot_ref[...], 1.0, 0.0).astype(bf16)
    rows_ref[...] = dot_nn(onehot_ref[...], hi_ref[...]) + dot_nn(onehot_ref[...], lo_ref[...])
    owner, place = slots_in_order(lax.broadcasted_iota(jnp.int32, (1, slots), 1), capacity, dp_size, rows_size)
    chosen = lax.broadcasted_iota(jnp.int32, (owners, slots), 0) == owner
    mine = lax.broadcasted_iota(jnp.int32, (capacity, slots), 0) == place
    ids = whole_numbers(slot_row_ref[...], chosen, mine)
    tiles = width // LANES
    blocks = 2 * dp_size
    for k, send_ref in enumerate(send_refs):
        for i in range(blocks):
            at = (k * blocks + i) * capacity
            for t in range(tiles):
                send_ref[(i * tiles + t) * capacity:(i * tiles + t + 1) * capacity, :] = rows_ref[at:at + capacity, t * LANES:(t + 1) * LANES]
        tile = k * blocks * capacity // LANES * LANES
        send_ref[blocks * tiles * capacity:, :] = jnp.broadcast_to(ids[:, tile:tile + LANES], (ID_ROWS, LANES))


def whole_numbers(values, chosen, mine):
    pick = jnp.where(chosen, 1.0, 0.0).astype(bf16)
    found = 16.0 * dot_nn(over(values, 16).astype(bf16), pick) + dot_nn(rest(values, 16).astype(bf16), pick)
    return jnp.sum(jnp.where(mine, found, 0.0), axis=0, keepdims=True)


def id_rows(chips):
    return max(ID_ROWS, chips)


def by_part_kernel(dp, block, *refs):
    ins, outs = refs[:-dp], refs[-dp:]
    d = lax.axis_index("dp")
    for j, out_ref in enumerate(outs):
        part = jnp.bitwise_xor(d, j)
        for k, in_ref in enumerate(ins):
            for core in range(2):
                start = pl.multiple_of((core * dp + part) * block, block)
                out_ref[(k * 2 + core) * block:(k * 2 + core + 1) * block, :] = in_ref[pl.ds(start, block), :]
        ids = [in_ref[2 * dp * block:2 * dp * block + 1, :] for in_ref in ins]
        ids += [jnp.zeros((1, LANES), f32)] * (id_rows(len(ins)) - len(ins))
        out_ref[2 * len(ins) * block:, :] = jnp.concatenate(ids, axis=0)


def by_core_kernel(chips, block, *refs):
    *ins, keep_ref, send_ref = refs
    core = lax.rem(lax.axis_index("rows"), 2)
    for out_ref, to in ((send_ref, 1 - core), (keep_ref, core)):
        for j, in_ref in enumerate(ins):
            for k in range(chips):
                start = pl.multiple_of((k * 2 + to) * block, block)
                out_ref[(j * chips + k) * block:(j * chips + k + 1) * block, :] = in_ref[pl.ds(start, block), :]
            at = len(ins) * chips * block + j * id_rows(chips)
            out_ref[at:at + id_rows(chips), :] = in_ref[2 * chips * block:, :]


def one_hot_rows(ids, wanted, hi_ref, lo_ref):
    onehot = jnp.where(wanted == ids, 1.0, 0.0).astype(bf16)
    return dot_nn(onehot, hi_ref[...]) + dot_nn(onehot, lo_ref[...])


def table_kernel(dp, chips, keep_ref, recv_ref, table_ref, accum_ref, table_new_ref, accum_new_ref, rows_ref, hi_ref, lo_ref):
    rows, width = table_ref.shape
    tiles = width // LANES
    sources = dp * chips
    capacity = rows_ref.shape[0] // (2 * sources)
    count = sources * capacity
    r = lax.axis_index("rows")
    block = lax.rem(r, 2) * dp + lax.axis_index("dp")
    ids = []
    for side, ref in enumerate((keep_ref, recv_ref)):
        for i in range(sources):
            at = side * count + i * capacity
            for t in range(tiles):
                rows_ref[at:at + capacity, t * LANES:(t + 1) * LANES] = ref[(i * tiles + t) * capacity:(i * tiles + t + 1) * capacity, :]
        values = ref[sources * tiles * capacity:, :].astype(jnp.int32)
        position = lax.broadcasted_iota(jnp.int32, (1, count), 1)
        source, place = over(position, capacity), rest(position, capacity)
        part, ahead = over(source, chips), rest(source, chips)
        lane = rest(ahead * (2 * dp * capacity), LANES) + block * capacity + place
        chosen = lax.broadcasted_iota(jnp.int32, (LANES, count), 0) == lane
        mine = lax.broadcasted_iota(jnp.int32, (values.shape[0], count), 0) == part * id_rows(chips) + ahead
        ids.append(whole_numbers(values, chosen, mine))
    ids = jnp.concatenate(ids, axis=1).astype(jnp.int32)
    high = rows_ref[...].astype(bf16)
    hi_ref[...] = high
    lo_ref[...] = (rows_ref[...] - high.astype(f32)).astype(bf16)
    grad = one_hot_rows(ids, lax.broadcasted_iota(jnp.int32, (rows, 1), 0), hi_ref, lo_ref)
    accum = jnp.transpose(jnp.broadcast_to(accum_ref[...].reshape(1, rows), (8, rows)))[:, :1]
    accum_new = accum + jnp.mean(grad * grad, axis=-1, keepdims=True)
    accum_new_ref[...] = jnp.transpose(jnp.broadcast_to(accum_new, (rows, LANES)))[:1, :].reshape(rows)
    table_new_ref[...] = table_ref[...] - learning_rate * grad / (jnp.sqrt(accum_new) + adagrad_eps)


def place_on_dp():
    d = lax.axis_index("dp")
    return lax.rem(d, 2), d // 2


def first_kernel(keep1_ref, recv1_ref, keep2_ref, recv2_ref, to_x_ref, to_y_ref, keep_a_ref, keep_b_ref):
    x, y = place_on_dp()
    start = 0
    for keep_ref, recv_ref in ((keep1_ref, recv1_ref), (keep2_ref, recv2_ref)):
        half = keep_ref.shape[-1] // 2
        part = lambda i, j, cols: keep_ref[i, j, :, cols] + recv_ref[i, j, :, cols]
        lo, hi, out = slice(0, half), slice(half, 2 * half), slice(start, start + half)
        for s in range(2):
            to_x_ref[s, :, out] = part(s, 1 - x, lo)
            to_y_ref[s, :, out] = part(1 - y, s, hi)
            keep_a_ref[s, :, out] = part(s, x, lo)
            keep_b_ref[s, :, out] = part(y, s, hi)
        start += half


def second_kernel(keep_a_ref, from_x_ref, keep_b_ref, from_y_ref, to_y_ref, to_x_ref, next_a_ref, next_b_ref):
    x, y = place_on_dp()
    to_y_ref[...] = keep_a_ref[1 - y] + from_x_ref[1 - y]
    to_x_ref[...] = keep_b_ref[1 - x] + from_y_ref[1 - x]
    next_a_ref[...] = keep_a_ref[y] + from_x_ref[y]
    next_b_ref[...] = keep_b_ref[x] + from_y_ref[x]


def halve(bit, send_ref, keep_ref, keep_in, recv_in):
    mine = rest(lax.axis_index("rows") // 2 >> bit, 2)
    for i in range(send_ref.shape[0]):
        send_ref[i] = keep_in[2 * i + 1 - mine] + recv_in[2 * i + 1 - mine]
        keep_ref[i] = keep_in[2 * i + mine] + recv_in[2 * i + mine]


def chip_first_kernel(next_a_ref, from_y_ref, next_b_ref, from_x_ref, send_a_ref, keep_a_ref, send_b_ref, keep_b_ref):
    halve(0, send_a_ref, keep_a_ref, next_a_ref, from_y_ref)
    halve(0, send_b_ref, keep_b_ref, next_b_ref, from_x_ref)


def chip_kernel(bit, keep_in, recv_in, send_ref, keep_ref):
    halve(bit, send_ref, keep_ref, keep_in, recv_in)


def total_kernel(tokens, keep_a_ref, recv_a_ref, keep_b_ref, recv_b_ref, out_ref):
    half = keep_a_ref.shape[-1]
    out_ref[:, :half] = (keep_a_ref[0] + recv_a_ref[0]) * (1.0 / tokens)
    out_ref[:, half:] = (keep_b_ref[0] + recv_b_ref[0]) * (1.0 / tokens)


def gather_kernel(*refs):
    *pieces, grad_in_ref, grad_out_ref = refs
    d = lax.axis_index("dp")
    width = grad_out_ref.shape[-1]
    half = width // 2
    for k, piece in enumerate(pieces):
        at = jnp.bitwise_xor(d, k)
        grad_out_ref[at] = piece[:, :width]
        start = width
        for cols, first in ((half, 0), (width, 2 * width), (half, half), (width, width), (width, 3 * width)):
            grad_in_ref[at, :, first:first + cols] = piece[:, start:start + cols]
            start += cols


def vmem():
    return pl.BlockSpec(memory_space=pltpu.VMEM)


def shape(*dims, dtype=f32):
    return jax.ShapeDtypeStruct(dims, dtype)


def call(kernel, name, out_shape, args, scratch=(), far=0, long=False, grant=4):
    place = [pltpu.SMEM if a.size == 1 else pltpu.HBM if i < far else pltpu.VMEM for i, a in enumerate(args)]
    args = [a if p is pltpu.SMEM else pltpu.with_memory_space_constraint(a, p) for a, p in zip(args, place)]
    return pl.pallas_call(
        kernel,
        name=name,
        in_specs=[pl.BlockSpec(memory_space=p) for p in place],
        out_specs=[vmem()] * len(out_shape),
        out_shape=list(out_shape),
        scratch_shapes=[pltpu.VMEM(dims, dtype) for dims, dtype in scratch]
        + [pltpu.SemaphoreType.DMA((7,))] * (far > 0),
        compiler_params=pltpu.CompilerParams(vmem_limit_bytes=grant * MIB),
        cost_estimate=pl.CostEstimate(flops=100_000_000_000 if long else 1_000_000_000, bytes_accessed=1 << 16, transcendentals=0),
    )(*args)


def body(rows_size, dp_size, events, cotangent, lengths, event_slot, slot_row, slot_count, w_in, w_out, item_table, accumulator):
    tokens, width = events.shape
    owners, capacity = slot_row.shape[1:]
    chips = rows_size // 2
    piece = width // (rows_size * dp_size)
    cores = [(i, i ^ 1) for i in range(rows_size)]
    over_dp = lambda v, bit: lax.ppermute(v, "dp", [(i, i ^ bit) for i in range(dp_size)])
    after = lambda value, *others: lax.optimization_barrier((value, *others))[0]
    strip = chips * piece

    def gathered(total):
        return [total] + [over_dp(total, k) for k in range(1, dp_size)]

    by_dp = lambda v: v.reshape(2, 2, strip, v.shape[-1])
    by_chip = lambda v: v.reshape(*v.shape[:-2], chips, piece, v.shape[-1])
    local = lambda *dims, dtype=f32: pltpu.VMEM(dims, dtype)
    sides = lambda cols: [local(width // 2, cols)] * 2
    keep1, send1, hid, dsilu, gatt, gpre_uv, normed_t, events, masked, w_in, inv_len = call(
        functools.partial(forward_kernel, rows_size, dp_size), "forward_part",
        sides(3 * width) + [
            local(tokens, 4 * width, dtype=bf16),
            local(tokens, 4 * width, dtype=bf16),
            local(tokens, width, dtype=bf16),
            local(tokens, 2 * width, dtype=bf16),
            local(width, tokens, dtype=bf16),
            local(tokens, width, dtype=bf16),
            local(tokens, width, dtype=bf16),
            local(*w_in.shape, dtype=bf16),
            local(8, LANES),
        ],
        (lengths, events, cotangent, w_in, w_out),
        [((tokens, width), bf16), ((tokens, width), f32), ((tokens, width), bf16), ((HEADS, tokens, tokens), bf16),
         (w_out.shape, bf16), ((width, width), bf16), ((tokens, width), f32), ((tokens, width), bf16),
         ((4, STEP, width), f32), ((4, STEP, STEP), f32)], far=5, long=True, grant=22)
    recv1 = lax.ppermute(send1, "rows", cores)
    keep2, send2, gpre_qk = call(
        attention_kernel, "attention_part", sides(2 * width) + [local(tokens, 2 * width, dtype=bf16)],
        (inv_len, hid, dsilu, gatt, normed_t),
        [((4, STEP, STEP), f32), ((4, STEP, STEP), f32), ((tokens, tokens), bf16)], long=True, grant=12)
    recv2 = lax.ppermute(send2, "rows", cores)
    block = capacity * (width // LANES)
    gpre_uv = after(gpre_uv, recv1)
    sends = call(
        functools.partial(events_kernel, rows_size, dp_size), "events_part",
        [local(2 * dp_size * block + ID_ROWS, LANES)] * chips,
        (events, masked, w_in, event_slot, slot_row[0].T, gpre_uv, gpre_qk),
        [((tokens, width), bf16), ((tokens, width), bf16), ((owners * capacity, width), f32), ((tokens, width), f32),
         ((owners * capacity, tokens), bf16)], grant=12, long=True)
    ahead = lambda v, k: lax.ppermute(v, "rows", [(i, (i + 2 * k) % rows_size) for i in range(rows_size)])
    came = [sends[0]] + [ahead(sends[k], k) for k in range(1, chips)]
    cols = w_in.shape[1] + width
    to_x, to_y, keep_a, keep_b = call(
        first_kernel, "first_sums", [local(2, strip, cols // 2)] * 4,
        [by_dp(v) for v in (after(keep1, *sends), recv1, keep2, recv2)])
    from_x, from_y = over_dp(to_x, 1), over_dp(to_y, 2)
    to_y, to_x, next_a, next_b = call(
        second_kernel, "second_sums", [local(strip, cols // 2)] * 4, (keep_a, from_x, keep_b, from_y),
        long=True)
    from_y, from_x = over_dp(to_y, 2), over_dp(to_x, 1)
    came[0] = after(came[0], to_y, to_x)
    parts = call(
        functools.partial(by_part_kernel, dp_size, block), "by_part",
        [local(2 * chips * block + id_rows(chips), LANES)] * dp_size, came, long=True)
    next_a = after(next_a, *parts)
    bits = chips.bit_length() - 1
    over_chips = lambda v, bit: lax.ppermute(v, "rows", [(i, i ^ (2 << bit)) for i in range(rows_size)])
    send_a, keep_a, send_b, keep_b = call(
        chip_first_kernel, "chip_sums", [local(chips // 2, piece, cols // 2)] * 4,
        [by_chip(v) for v in (next_a, from_y, next_b, from_x)])
    halves = [[keep_a, over_chips(send_a, 0)], [keep_b, over_chips(send_b, 0)]]
    parts = [parts[0]] + [over_dp(parts[k], k) for k in range(1, dp_size)]
    for bit in range(1, bits):
        for i in range(2):
            if i == 1:
                halves[1][0] = after(halves[1][0], send, keep)
            send, keep = call(
                functools.partial(chip_kernel, bit), "chip_sums", [local(chips >> (bit + 1), piece, cols // 2)] * 2,
                halves[i], long=False)
            halves[i] = [keep, over_chips(send, bit)]
    (total,) = call(
        functools.partial(total_kernel, tokens), "total", [local(piece, cols)], halves[0] + halves[1], long=False)
    pieces = gathered(total)
    parts[0] = after(parts[0], total)
    keep, send = call(
        functools.partial(by_core_kernel, chips, block), "by_core",
        [local(dp_size * (chips * block + id_rows(chips)), LANES)] * 2, parts, long=False)
    recv = lax.ppermute(send, "rows", cores)
    slots = owners * capacity
    table_new, accum_new = call(
        functools.partial(table_kernel, dp_size, chips), "table_part", [shape(*item_table.shape), shape(*accumulator.shape)],
        (keep, recv, item_table, accumulator),
        [((slots, width), f32), ((slots, width), bf16), ((slots, width), bf16)], grant=10)
    pieces[-1] = after(pieces[-1], accum_new)
    grad_in, grad_out = call(
        gather_kernel, "gather", [shape(dp_size, piece, 4 * width), shape(dp_size, piece, width)], pieces)
    return grad_in.reshape(-1, 4 * width), grad_out.reshape(-1, width), table_new, accum_new


def solution(mesh):
    whole = P(("dp", "rows"))
    in_specs = (whole,) * 6 + (P(), P(), whole, whole)
    out_specs = (P("rows"), P("rows"), whole, whole)
    run = functools.partial(body, mesh.shape["rows"], mesh.shape["dp"])
    return jax.shard_map(run, mesh=mesh, in_specs=in_specs, out_specs=out_specs, check_vma=False)
```

```python
import functools

import jax
import jax.numpy as jnp
from jax import lax
from jax.experimental import pallas as pl
from jax.experimental.pallas import tpu as pltpu
from jax.sharding import PartitionSpec as P

HEADS = 4

norm_eps = 1e-05
adagrad_eps = 1e-10
learning_rate = 0.1

f32, bf16 = jnp.float32, jnp.bfloat16
MIB = 1024 * 1024
STEP = 256
TILE = 32
LANES = 128
ID_ROWS = 8


def dot_nn(a, b):
    return lax.dot_general(a, b, (((1,), (0,)), ((), ())), preferred_element_type=f32)


def dot_nt(a, b):
    return lax.dot_general(a, b, (((1,), (1,)), ((), ())), preferred_element_type=f32)


def dot_tn(a, b):
    return lax.dot_general(a, b, (((0,), (0,)), ((), ())), preferred_element_type=f32)


def over(value, n):
    return value >> (n.bit_length() - 1) if n & (n - 1) == 0 else value // n


def rest(value, n):
    return value & (n - 1) if n & (n - 1) == 0 else value % n


def standardize(x):
    centered = x - jnp.mean(x, axis=-1, keepdims=True)
    inv = lax.rsqrt(jnp.mean(centered * centered, axis=-1, keepdims=True) + norm_eps)
    return centered * inv, inv


def masked_rows(cot, start, length):
    row = start + lax.broadcasted_iota(jnp.int32, cot.shape, 0)
    return jnp.where(row < length, cot.astype(f32), 0.0)


def owner_order(width, rows, dp):
    chips = rows // 2
    piece = width // (rows * dp)
    at = lax.broadcasted_iota(jnp.int32, (width, 1), 0)
    side, part = over(at, width // 2), rest(over(at, chips * piece), dp)
    chip, row = rest(over(at, piece), chips), rest(at, piece)
    core = lax.rem(lax.axis_index("rows"), 2)
    core = jnp.where(side == 0, core, 1 - core)
    wanted = ((chip * 2 + core) * dp + part) * piece + row
    return jnp.where(lax.broadcasted_iota(jnp.int32, (width, width), 1) == wanted, 1.0, 0.0).astype(bf16)


def tiles_of(start, count, size):
    return [pl.ds(start + at, size) for at in range(0, count, size)]


def forward_kernel(rows_size, dp_size, len_ref, ev_hbm, cot_hbm, win_hbm, wout_hbm,
                   keep_ref, send_ref, hid_ref, dsilu_ref, gatt_ref, gpre_ref, normed_t_ref,
                   ev_ref, masked_ref, win_ref, inv_ref, normed_ref, user_ref, duser_ref, att_ref, mixed_ref, dval_ref,
                   weights_ref, wout_ref, order_ref, grad_mixed_ref, cot_ref, pre_ref, raw_ref, arrived):
    tokens, width = ev_ref.shape
    copies = [pltpu.make_async_copy(ev_hbm, ev_ref, arrived.at[0])]
    for c in range(4):
        cols = pl.ds(c * width, width)
        copies.append(pltpu.make_async_copy(win_hbm.at[:, cols], win_ref.at[:, cols], arrived.at[1 + c]))
    copies.append(pltpu.make_async_copy(cot_hbm, cot_ref, arrived.at[5]))
    copies.append(pltpu.make_async_copy(wout_hbm, wout_ref, arrived.at[6]))
    for copy in copies:
        copy.start()
    order_ref[...] = owner_order(width, rows_size, dp_size)
    hd = width // HEADS
    scale = hd ** -0.5
    steps = tokens // STEP

    copies[0].wait()
    for tile in tiles_of(0, tokens, TILE):
        xhat, _ = standardize(ev_ref[tile, :].astype(f32))
        normed_ref[tile, :] = xhat.astype(bf16)

    def project(i, c):
        rows = pl.ds(i * STEP, STEP)
        slot = (c * steps + i) % pre_ref.shape[0]
        pre_ref[slot] = dot_nn(normed_ref[rows, :], win_ref[:, c * width:(c + 1) * width])
        for at in range(0, STEP, TILE):
            tile = pl.ds(i * STEP + at, TILE)
            pre = pre_ref[slot, at:at + TILE, :]
            sig = 0.5 + 0.5 * jnp.tanh(0.5 * pre)
            hid = pre * sig
            dsilu = sig * (1.0 + (pre - hid))
            if c == 0:
                user_ref[tile, :] = hid.astype(bf16)
                duser_ref[tile, :] = dsilu
            else:
                hid_ref[tile, (c - 1) * width:c * width] = hid.astype(bf16)
                if c == 1:
                    dval_ref[tile, :] = dsilu
                else:
                    dsilu_ref[tile, (c - 2) * width:(c - 1) * width] = dsilu.astype(bf16)

    for c in range(4):
        copies[1 + c].wait()
        for i in range(steps):
            project(i, c)

    for copy in copies[5:]:
        copy.wait()
    length = len_ref[0]
    inv_len = 1.0 / length.astype(f32)
    inv_ref[...] = jnp.full(inv_ref.shape, inv_len, f32)
    for h in range(HEADS):
        v_cols = slice(h * hd, (h + 1) * hd)
        q_cols = slice(width + h * hd, width + (h + 1) * hd)
        k_cols = slice(2 * width + h * hd, 2 * width + (h + 1) * hd)
        for i in range(steps):
            rows = pl.ds(i * STEP, STEP)
            for j in range(i + 1):
                keys = pl.ds(j * STEP, STEP)
                slot = (h * 3 + i + j) % raw_ref.shape[0]
                raw_ref[slot] = dot_nt(hid_ref[rows, q_cols], hid_ref[keys, k_cols])
                for at in range(0, STEP, 2 * TILE):
                    half = raw_ref[slot, at:at + 2 * TILE, :] * (0.5 * scale)
                    weights = (half + half * jnp.tanh(half)) * inv_len
                    if i == j:
                        row = at + lax.broadcasted_iota(jnp.int32, weights.shape, 0)
                        weights = jnp.where(row >= lax.broadcasted_iota(jnp.int32, weights.shape, 1), weights, 0.0)
                    weights_ref[h, pl.ds(i * STEP + at, 2 * TILE), keys] = weights.astype(bf16)
            seen = pl.ds(0, (i + 1) * STEP)
            att_ref[rows, v_cols] = dot_nn(weights_ref[h, rows, seen], hid_ref[seen, v_cols])
        for i in range(h, steps, HEADS):
            rows = pl.ds(i * STEP, STEP)
            normed_t_ref[rows, :] = dot_nt(order_ref[rows, :], normed_ref[...]).astype(bf16)
        for i in range(h - HEADS // 2, steps, HEADS):
            if i >= 0:
                rows = pl.ds(i * STEP, STEP)
                for tile in tiles_of(i * STEP, STEP, TILE):
                    masked_ref[tile, :] = masked_rows(cot_ref[tile, :], tile.start, length).astype(bf16)
                grad_mixed_ref[rows, :] = dot_nt(masked_ref[rows, :], wout_ref[...])

    for tile in tiles_of(0, tokens, TILE // 2):
        ahat, inv = standardize(att_ref[tile, :])
        user = user_ref[tile, :].astype(f32)
        mixed_ref[tile, :] = (ahat * user).astype(bf16)
        grad_mixed = grad_mixed_ref[tile, :]
        gpre_ref[tile, :width] = (grad_mixed * ahat * duser_ref[tile, :]).astype(bf16)
        e = grad_mixed * user
        gatt_ref[tile, :] = (inv * (e - jnp.mean(e, axis=-1, keepdims=True)
                                    - ahat * jnp.mean(e * ahat, axis=-1, keepdims=True))).astype(bf16)

    for h in range(HEADS):
        v_cols = slice(h * hd, (h + 1) * hd)
        for j in range(steps):
            keys, later = pl.ds(j * STEP, STEP), pl.ds(j * STEP, tokens - j * STEP)
            grad_v = dot_tn(weights_ref[h, later, keys], gatt_ref[later, v_cols])
            gpre_ref[keys, width + h * hd:width + (h + 1) * hd] = (grad_v * dval_ref[keys, v_cols]).astype(bf16)

    mixed_t = dot_nt(order_ref[...], mixed_ref[...]).astype(bf16)
    half = width // 2
    for ref, start in ((send_ref, half), (keep_ref, 0)):
        ref[:, :width] = dot_nn(mixed_t[start:start + half], masked_ref[...])
        ref[:, width:] = dot_nn(normed_t_ref[start:start + half, :], gpre_ref[...])


def attention_kernel(inv_ref, hid_ref, dsilu_ref, gatt_ref, normed_t_ref, keep_ref, send_ref, gpre_ref,
                     raw_ref, weight_ref, score_ref):
    tokens, width = gatt_ref.shape
    hd = width // HEADS
    scale = hd ** -0.5
    steps = tokens // STEP
    factor = inv_ref[:1, :hd] * (0.5 * scale)

    for h in range(HEADS):
        v_cols = slice(h * hd, (h + 1) * hd)
        q_cols = slice(width + h * hd, width + (h + 1) * hd)
        k_cols = slice(2 * width + h * hd, 2 * width + (h + 1) * hd)
        for j in range(steps):
            keys = pl.ds(j * STEP, STEP)
            for i in range(j, steps):
                rows = pl.ds(i * STEP, STEP)
                slot = (h * 3 + i + j) % raw_ref.shape[0]
                raw_ref[slot] = dot_nt(hid_ref[keys, k_cols], hid_ref[rows, q_cols])
                weight_ref[slot] = dot_nt(hid_ref[keys, v_cols], gatt_ref[rows, v_cols])
                for at in range(0, STEP, TILE):
                    half = raw_ref[slot, at:at + TILE, :] * (0.5 * scale)
                    gate = jnp.tanh(half)
                    gscore = weight_ref[slot, at:at + TILE, :] * ((1.0 + gate) * (1.0 + half * (1.0 - gate)))
                    if i == j:
                        row = at + lax.broadcasted_iota(jnp.int32, gscore.shape, 0)
                        gscore = jnp.where(row <= lax.broadcasted_iota(jnp.int32, gscore.shape, 1), gscore, 0.0)
                    score_ref[h % 2, pl.ds(j * STEP + at, TILE), rows] = gscore.astype(bf16)
        for j in range(steps):
            keys, later, seen = pl.ds(j * STEP, STEP), pl.ds(j * STEP, tokens - j * STEP), pl.ds(0, (j + 1) * STEP)
            grad_k = dot_nn(score_ref[h % 2, keys, later], hid_ref[later, q_cols])
            gpre_ref[keys, q_cols] = (grad_k * (dsilu_ref[keys, q_cols].astype(f32) * factor)).astype(bf16)
            grad_q = dot_tn(score_ref[h % 2, seen, keys], hid_ref[seen, k_cols])
            gpre_ref[keys, v_cols] = (grad_q * (dsilu_ref[keys, v_cols].astype(f32) * factor)).astype(bf16)

    half = width // 2
    for ref, start in ((send_ref, half), (keep_ref, 0)):
        ref[...] = dot_nn(normed_t_ref[start:start + half, :], gpre_ref[...])


def slots_in_order(position, capacity, dp, rows):
    chips = rows // 2
    owner, place = over(position, capacity), rest(position, capacity)
    ahead, core, part = over(owner, 2 * dp), rest(over(owner, dp), 2), rest(owner, dp)
    chip = rest(lax.axis_index("rows") // 2 + ahead, chips)
    return part * rows + chip * 2 + core, place


def events_kernel(rows_size, dp_size, ev_ref, masked_ref, win_ref, slot_ref, slot_row_ref, gpre_uv_ref, gpre_qk_ref, *refs):
    *send_refs, hi_ref, lo_ref, rows_ref, grad_ref, onehot_ref = refs
    tokens, width = ev_ref.shape
    capacity, owners = slot_row_ref.shape
    for i in range(tokens // STEP):
        rows = pl.ds(i * STEP, STEP)
        grad_ref[rows, :] = dot_nt(gpre_uv_ref[rows, :], win_ref[:, :2 * width]) + dot_nt(gpre_qk_ref[rows, :], win_ref[:, 2 * width:])
        for tile in tiles_of(i * STEP, STEP, TILE // 2):
            xhat, inv = standardize(ev_ref[tile, :].astype(f32))
            grad_normed = grad_ref[tile, :]
            grad = masked_ref[tile, :].astype(f32) + inv * (
                grad_normed - jnp.mean(grad_normed, axis=-1, keepdims=True)
                - xhat * jnp.mean(grad_normed * xhat, axis=-1, keepdims=True))
            high = grad.astype(bf16)
            hi_ref[tile, :] = high
            lo_ref[tile, :] = (grad - high.astype(f32)).astype(bf16)

    slots = rows_ref.shape[0]
    owner, place = slots_in_order(lax.broadcasted_iota(jnp.int32, (slots, 1), 0), capacity, dp_size, rows_size)
    wanted = owner * capacity + place
    for at in range(0, slots, 2 * TILE):
        onehot_ref[at:at + 2 * TILE, :] = jnp.where(wanted[at:at + 2 * TILE] == slot_ref[...], 1.0, 0.0).astype(bf16)
    rows_ref[...] = dot_nn(onehot_ref[...], hi_ref[...]) + dot_nn(onehot_ref[...], lo_ref[...])
    owner, place = slots_in_order(lax.broadcasted_iota(jnp.int32, (1, slots), 1), capacity, dp_size, rows_size)
    chosen = lax.broadcasted_iota(jnp.int32, (owners, slots), 0) == owner
    mine = lax.broadcasted_iota(jnp.int32, (capacity, slots), 0) == place
    ids = whole_numbers(slot_row_ref[...], chosen, mine)
    tiles = width // LANES
    blocks = 2 * dp_size
    for k, send_ref in enumerate(send_refs):
        for i in range(blocks):
            at = (k * blocks + i) * capacity
            for t in range(tiles):
                send_ref[(i * tiles + t) * capacity:(i * tiles + t + 1) * capacity, :] = rows_ref[at:at + capacity, t * LANES:(t + 1) * LANES]
        tile = k * blocks * capacity // LANES * LANES
        send_ref[blocks * tiles * capacity:, :] = jnp.broadcast_to(ids[:, tile:tile + LANES], (ID_ROWS, LANES))


def whole_numbers(values, chosen, mine):
    pick = jnp.where(chosen, 1.0, 0.0).astype(bf16)
    found = 16.0 * dot_nn(over(values, 16).astype(bf16), pick) + dot_nn(rest(values, 16).astype(bf16), pick)
    return jnp.sum(jnp.where(mine, found, 0.0), axis=0, keepdims=True)


def id_rows(chips):
    return max(ID_ROWS, chips)


def by_part_kernel(dp, block, *refs):
    ins, outs = refs[:-dp], refs[-dp:]
    d = lax.axis_index("dp")
    for j, out_ref in enumerate(outs):
        part = jnp.bitwise_xor(d, j)
        for k, in_ref in enumerate(ins):
            for core in range(2):
                start = pl.multiple_of((core * dp + part) * block, block)
                out_ref[(k * 2 + core) * block:(k * 2 + core + 1) * block, :] = in_ref[pl.ds(start, block), :]
        ids = [in_ref[2 * dp * block:2 * dp * block + 1, :] for in_ref in ins]
        ids += [jnp.zeros((1, LANES), f32)] * (id_rows(len(ins)) - len(ins))
        out_ref[2 * len(ins) * block:, :] = jnp.concatenate(ids, axis=0)


def by_core_kernel(chips, block, *refs):
    *ins, keep_ref, send_ref = refs
    core = lax.rem(lax.axis_index("rows"), 2)
    for out_ref, to in ((send_ref, 1 - core), (keep_ref, core)):
        for j, in_ref in enumerate(ins):
            for k in range(chips):
                start = pl.multiple_of((k * 2 + to) * block, block)
                out_ref[(j * chips + k) * block:(j * chips + k + 1) * block, :] = in_ref[pl.ds(start, block), :]
            at = len(ins) * chips * block + j * id_rows(chips)
            out_ref[at:at + id_rows(chips), :] = in_ref[2 * chips * block:, :]


def one_hot_rows(ids, wanted, hi_ref, lo_ref):
    onehot = jnp.where(wanted == ids, 1.0, 0.0).astype(bf16)
    return dot_nn(onehot, hi_ref[...]) + dot_nn(onehot, lo_ref[...])


def table_kernel(dp, chips, keep_ref, recv_ref, table_ref, accum_ref, table_new_ref, accum_new_ref, rows_ref, hi_ref, lo_ref):
    rows, width = table_ref.shape
    tiles = width // LANES
    sources = dp * chips
    capacity = rows_ref.shape[0] // (2 * sources)
    count = sources * capacity
    r = lax.axis_index("rows")
    block = lax.rem(r, 2) * dp + lax.axis_index("dp")
    ids = []
    for side, ref in enumerate((keep_ref, recv_ref)):
        for i in range(sources):
            at = side * count + i * capacity
            for t in range(tiles):
                rows_ref[at:at + capacity, t * LANES:(t + 1) * LANES] = ref[(i * tiles + t) * capacity:(i * tiles + t + 1) * capacity, :]
        values = ref[sources * tiles * capacity:, :].astype(jnp.int32)
        position = lax.broadcasted_iota(jnp.int32, (1, count), 1)
        source, place = over(position, capacity), rest(position, capacity)
        part, ahead = over(source, chips), rest(source, chips)
        lane = rest(ahead * (2 * dp * capacity), LANES) + block * capacity + place
        chosen = lax.broadcasted_iota(jnp.int32, (LANES, count), 0) == lane
        mine = lax.broadcasted_iota(jnp.int32, (values.shape[0], count), 0) == part * id_rows(chips) + ahead
        ids.append(whole_numbers(values, chosen, mine))
    ids = jnp.concatenate(ids, axis=1).astype(jnp.int32)
    high = rows_ref[...].astype(bf16)
    hi_ref[...] = high
    lo_ref[...] = (rows_ref[...] - high.astype(f32)).astype(bf16)
    grad = one_hot_rows(ids, lax.broadcasted_iota(jnp.int32, (rows, 1), 0), hi_ref, lo_ref)
    accum = jnp.transpose(jnp.broadcast_to(accum_ref[...].reshape(1, rows), (8, rows)))[:, :1]
    accum_new = accum + jnp.mean(grad * grad, axis=-1, keepdims=True)
    accum_new_ref[...] = jnp.transpose(jnp.broadcast_to(accum_new, (rows, LANES)))[:1, :].reshape(rows)
    table_new_ref[...] = table_ref[...] - learning_rate * grad / (jnp.sqrt(accum_new) + adagrad_eps)


def place_on_dp():
    d = lax.axis_index("dp")
    return lax.rem(d, 2), d // 2


def first_kernel(keep1_ref, recv1_ref, keep2_ref, recv2_ref, to_x_ref, to_y_ref, keep_a_ref, keep_b_ref):
    x, y = place_on_dp()
    start = 0
    for keep_ref, recv_ref in ((keep1_ref, recv1_ref), (keep2_ref, recv2_ref)):
        half = keep_ref.shape[-1] // 2
        part = lambda i, j, cols: keep_ref[i, j, :, cols] + recv_ref[i, j, :, cols]
        lo, hi, out = slice(0, half), slice(half, 2 * half), slice(start, start + half)
        for s in range(2):
            to_x_ref[s, :, out] = part(s, 1 - x, lo)
            to_y_ref[s, :, out] = part(1 - y, s, hi)
            keep_a_ref[s, :, out] = part(s, x, lo)
            keep_b_ref[s, :, out] = part(y, s, hi)
        start += half


def second_kernel(keep_a_ref, from_x_ref, keep_b_ref, from_y_ref, to_y_ref, to_x_ref, next_a_ref, next_b_ref):
    x, y = place_on_dp()
    to_y_ref[...] = keep_a_ref[1 - y] + from_x_ref[1 - y]
    to_x_ref[...] = keep_b_ref[1 - x] + from_y_ref[1 - x]
    next_a_ref[...] = keep_a_ref[y] + from_x_ref[y]
    next_b_ref[...] = keep_b_ref[x] + from_y_ref[x]


def halve(bit, send_ref, keep_ref, keep_in, recv_in):
    mine = rest(lax.axis_index("rows") // 2 >> bit, 2)
    for i in range(send_ref.shape[0]):
        send_ref[i] = keep_in[2 * i + 1 - mine] + recv_in[2 * i + 1 - mine]
        keep_ref[i] = keep_in[2 * i + mine] + recv_in[2 * i + mine]


def chip_first_kernel(next_a_ref, from_y_ref, next_b_ref, from_x_ref, send_a_ref, keep_a_ref, send_b_ref, keep_b_ref):
    halve(0, send_a_ref, keep_a_ref, next_a_ref, from_y_ref)
    halve(0, send_b_ref, keep_b_ref, next_b_ref, from_x_ref)


def chip_kernel(bit, keep_in, recv_in, send_ref, keep_ref):
    halve(bit, send_ref, keep_ref, keep_in, recv_in)


def total_kernel(tokens, keep_a_ref, recv_a_ref, keep_b_ref, recv_b_ref, out_ref):
    half = keep_a_ref.shape[-1]
    out_ref[:, :half] = (keep_a_ref[0] + recv_a_ref[0]) * (1.0 / tokens)
    out_ref[:, half:] = (keep_b_ref[0] + recv_b_ref[0]) * (1.0 / tokens)


def gather_kernel(*refs):
    *pieces, grad_in_ref, grad_out_ref = refs
    d = lax.axis_index("dp")
    width = grad_out_ref.shape[-1]
    half = width // 2
    for k, piece in enumerate(pieces):
        at = jnp.bitwise_xor(d, k)
        grad_out_ref[at] = piece[:, :width]
        start = width
        for cols, first in ((half, 0), (width, 2 * width), (half, half), (width, width), (width, 3 * width)):
            grad_in_ref[at, :, first:first + cols] = piece[:, start:start + cols]
            start += cols


def vmem():
    return pl.BlockSpec(memory_space=pltpu.VMEM)


def shape(*dims, dtype=f32):
    return jax.ShapeDtypeStruct(dims, dtype)


def call(kernel, name, out_shape, args, scratch=(), far=0, long=False, grant=4):
    place = [pltpu.SMEM if a.size == 1 else pltpu.HBM if i < far else pltpu.VMEM for i, a in enumerate(args)]
    args = [a if p is pltpu.SMEM else pltpu.with_memory_space_constraint(a, p) for a, p in zip(args, place)]
    return pl.pallas_call(
        kernel,
        name=name,
        in_specs=[pl.BlockSpec(memory_space=p) for p in place],
        out_specs=[vmem()] * len(out_shape),
        out_shape=list(out_shape),
        scratch_shapes=[pltpu.VMEM(dims, dtype) for dims, dtype in scratch]
        + [pltpu.SemaphoreType.DMA((7,))] * (far > 0),
        compiler_params=pltpu.CompilerParams(vmem_limit_bytes=grant * MIB),
        cost_estimate=pl.CostEstimate(flops=100_000_000_000 if long else 1_000_000_000, bytes_accessed=1 << 16, transcendentals=0),
    )(*args)


def body(rows_size, dp_size, events, cotangent, lengths, event_slot, slot_row, slot_count, w_in, w_out, item_table, accumulator):
    tokens, width = events.shape
    owners, capacity = slot_row.shape[1:]
    chips = rows_size // 2
    piece = width // (rows_size * dp_size)
    cores = [(i, i ^ 1) for i in range(rows_size)]
    over_dp = lambda v, bit: lax.ppermute(v, "dp", [(i, i ^ bit) for i in range(dp_size)])
    after = lambda value, *others: lax.optimization_barrier((value, *others))[0]
    strip = chips * piece

    def gathered(total):
        return [total] + [over_dp(total, k) for k in range(1, dp_size)]

    by_dp = lambda v: v.reshape(2, 2, strip, v.shape[-1])
    by_chip = lambda v: v.reshape(*v.shape[:-2], chips, piece, v.shape[-1])
    local = lambda *dims, dtype=f32: pltpu.VMEM(dims, dtype)
    sides = lambda cols: [local(width // 2, cols)] * 2
    keep1, send1, hid, dsilu, gatt, gpre_uv, normed_t, events, masked, w_in, inv_len = call(
        functools.partial(forward_kernel, rows_size, dp_size), "forward_part",
        sides(3 * width) + [
            local(tokens, 3 * width, dtype=bf16),
            local(tokens, 2 * width, dtype=bf16),
            local(tokens, width, dtype=bf16),
            local(tokens, 2 * width, dtype=bf16),
            local(width, tokens, dtype=bf16),
            local(tokens, width, dtype=bf16),
            local(tokens, width, dtype=bf16),
            local(*w_in.shape, dtype=bf16),
            local(8, LANES),
        ],
        (lengths, events, cotangent, w_in, w_out),
        [((tokens, width), bf16), ((tokens, width), bf16), ((tokens, width), f32), ((tokens, width), f32),
         ((tokens, width), bf16), ((tokens, width), f32), ((HEADS, tokens, tokens), bf16),
         (w_out.shape, bf16), ((width, width), bf16), ((tokens, width), f32), ((tokens, width), bf16),
         ((4, STEP, width), f32), ((4, STEP, STEP), f32)], far=5, long=True, grant=22)
    recv1 = lax.ppermute(send1, "rows", cores)
    keep2, send2, gpre_qk = call(
        attention_kernel, "attention_part", sides(2 * width) + [local(tokens, 2 * width, dtype=bf16)],
        (inv_len, hid, dsilu, gatt, normed_t),
        [((4, STEP, STEP), f32), ((4, STEP, STEP), f32), ((2, tokens, tokens), bf16)], long=True, grant=12)
    recv2 = lax.ppermute(send2, "rows", cores)
    block = capacity * (width // LANES)
    gpre_uv = after(gpre_uv, recv1)
    sends = call(
        functools.partial(events_kernel, rows_size, dp_size), "events_part",
        [local(2 * dp_size * block + ID_ROWS, LANES)] * chips,
        (events, masked, w_in, event_slot, slot_row[0].T, gpre_uv, gpre_qk),
        [((tokens, width), bf16), ((tokens, width), bf16), ((owners * capacity, width), f32), ((tokens, width), f32),
         ((owners * capacity, tokens), bf16)], grant=12, long=True)
    ahead = lambda v, k: lax.ppermute(v, "rows", [(i, (i + 2 * k) % rows_size) for i in range(rows_size)])
    came = [sends[0]] + [ahead(sends[k], k) for k in range(1, chips)]
    cols = w_in.shape[1] + width
    to_x, to_y, keep_a, keep_b = call(
        first_kernel, "first_sums", [local(2, strip, cols // 2)] * 4,
        [by_dp(v) for v in (after(keep1, *sends), recv1, keep2, recv2)])
    from_x, from_y = over_dp(to_x, 1), over_dp(to_y, 2)
    to_y, to_x, next_a, next_b = call(
        second_kernel, "second_sums", [local(strip, cols // 2)] * 4, (keep_a, from_x, keep_b, from_y),
        long=True)
    from_y, from_x = over_dp(to_y, 2), over_dp(to_x, 1)
    came[0] = after(came[0], to_y, to_x)
    parts = call(
        functools.partial(by_part_kernel, dp_size, block), "by_part",
        [local(2 * chips * block + id_rows(chips), LANES)] * dp_size, came, long=True)
    next_a = after(next_a, *parts)
    bits = chips.bit_length() - 1
    over_chips = lambda v, bit: lax.ppermute(v, "rows", [(i, i ^ (2 << bit)) for i in range(rows_size)])
    send_a, keep_a, send_b, keep_b = call(
        chip_first_kernel, "chip_sums", [local(chips // 2, piece, cols // 2)] * 4,
        [by_chip(v) for v in (next_a, from_y, next_b, from_x)])
    halves = [[keep_a, over_chips(send_a, 0)], [keep_b, over_chips(send_b, 0)]]
    parts = [parts[0]] + [over_dp(parts[k], k) for k in range(1, dp_size)]
    for bit in range(1, bits):
        for i in range(2):
            if i == 1:
                halves[1][0] = after(halves[1][0], send, keep)
            send, keep = call(
                functools.partial(chip_kernel, bit), "chip_sums", [local(chips >> (bit + 1), piece, cols // 2)] * 2,
                halves[i], long=False)
            halves[i] = [keep, over_chips(send, bit)]
    parts[0] = after(parts[0], halves[1][0])
    keep, send = call(
        functools.partial(by_core_kernel, chips, block), "by_core",
        [local(dp_size * (chips * block + id_rows(chips)), LANES)] * 2, parts, long=True)
    halves[1][0] = after(halves[1][0], keep, send)
    (total,) = call(
        functools.partial(total_kernel, tokens), "total", [local(piece, cols)], halves[0] + halves[1], long=True)
    pieces = gathered(total)
    recv = lax.ppermute(send, "rows", cores)
    slots = owners * capacity
    table_new, accum_new = call(
        functools.partial(table_kernel, dp_size, chips), "table_part", [shape(*item_table.shape), shape(*accumulator.shape)],
        (keep, recv, item_table, accumulator),
        [((slots, width), f32), ((slots, width), bf16), ((slots, width), bf16)], grant=10)
    pieces[-1] = after(pieces[-1], accum_new)
    grad_in, grad_out = call(
        gather_kernel, "gather", [shape(dp_size, piece, 4 * width), shape(dp_size, piece, width)], pieces)
    return grad_in.reshape(-1, 4 * width), grad_out.reshape(-1, width), table_new, accum_new


def solution(mesh):
    whole = P(("dp", "rows"))
    in_specs = (whole,) * 6 + (P(), P(), whole, whole)
    out_specs = (P("rows"), P("rows"), whole, whole)
    run = functools.partial(body, mesh.shape["rows"], mesh.shape["dp"])
    return jax.shard_map(run, mesh=mesh, in_specs=in_specs, out_specs=out_specs, check_vma=False)
```
